32 devices in a mesh: grp: 2 (over core), row: 4 (over y, x), col: 4 (over z).
Axes of the slice: x: 2, y: 2, z: 4, core: 2. Of those that a mesh axis runs over, the one named last changes fastest.
Arguments:
- global_state: bfloat16 [64, 1440, 384], P(('grp', 'row'), 'col'), may hold values from -6 to 6
- spec_filter: float32 [2, 720, 384], P(None, None, 'col'), may hold values from -4 to 4
- w_skip: bfloat16 [384, 384], replicated, may hold values from -0.3125 to 0.3125
- w_mix: bfloat16 [384, 384], replicated, may hold values from -0.3125 to 0.3125
- w_decode: bfloat16 [384, 26], replicated, may hold values from -0.3125 to 0.3125
- regional_state: bfloat16 [99, 128, 512], P(None, ('grp', 'row'), 'col'), may hold values from -6 to 6
- noise_draws: bfloat16 [2, 99, 128, 512], P(None, None, ('grp', 'row'), 'col'), may hold values from -6 to 6
- w_first: bfloat16 [128, 9, 125], replicated, may hold values from -0.1875 to 0.1875
- w_down: bfloat16 [256, 9, 128], replicated, may hold values from -0.1875 to 0.1875
- w_up: bfloat16 [128, 256], replicated, may hold values from -0.375 to 0.375
- w_bridge: bfloat16 [128, 128], replicated, may hold values from -0.5 to 0.5
- w_last: bfloat16 [99, 9, 128], replicated, may hold values from -0.1875 to 0.1875
- box_lat0: int32 [1], replicated, may hold values from 0 to 46
- box_lon0: int32 [1], replicated, may hold values from 0 to 1374
- stencil_lat: int32 [128, 512], P(('grp', 'row'), 'col'), may hold values from 0 to 16, as said below
- stencil_lon: int32 [128, 512], P(('grp', 'row'), 'col'), may hold values from 0 to 64, as said below
Outputs:
- global_final: bfloat16 [64, 1440, 384], P(('grp', 'row'), 'col')
- regional_final: bfloat16 [99, 128, 512], P(None, ('grp', 'row'), 'col')
The draws below stay inside these ranges and needn't reach their ends.
Inputs may be any that keep to these rules, and one draw needn't show every extreme that they name: stencil_lat[r, q] is r // 8 or r // 8 + 1. stencil_lon[r, q] is q // 8 or q // 8 + 1.
All inputs are finite; a program needn't handle non-finite values.
Results may differ from the reference program's by a relative error of at most 0.012.
Values may be sent and summed in bfloat16 or wider, within the bound.
No kernel may reach another device: no remote copies, remote signals or barrier semaphores. Data moves between devices by JAX's collectives and lax.ppermute only.
A program may use at most 128 MiB of HBM per device.

```python
import math
import jax
import jax.numpy as jnp
from jax import lax

CG = 384
NLON = 1440
MODES = 720
COND = 26
VARS = 99
CH1 = 128
CH2 = 256
RATIO = 8
HOURS = 2
NLAT = 64
NROW = 128
NCOL = 512
BOX_LAT = 18
BOX_LON = 66


def draw_stencil_lat(key, part):
    key = jax.random.fold_in(key, 11)
    jitter = jax.random.randint(key, (NROW, NCOL), 0, 2)
    rows_index = jnp.arange(NROW, dtype=jnp.int32)[:, None]
    jitter = jnp.where(rows_index == 0, 0, jnp.where(rows_index == NROW - 1, 1, jitter))
    return (rows_index // RATIO + jitter).astype(jnp.int32)


def draw_stencil_lon(key, part):
    key = jax.random.fold_in(key, 23)
    jitter = jax.random.randint(key, (NROW, NCOL), 0, 2)
    cols_index = jnp.arange(NCOL, dtype=jnp.int32)[None, :]
    jitter = jnp.where(cols_index == 0, 0, jnp.where(cols_index == NCOL - 1, 1, jitter))
    return (cols_index // RATIO + jitter).astype(jnp.int32)


def block_scale(own_key, extent, cuts, low, high):
    level = 1.0
    for dim, parts in cuts:
        heights = jax.random.uniform(jax.random.fold_in(jax.random.fold_in(own_key, 6), dim), (parts,), jnp.float32, low / len(cuts), high / len(cuts))
        level = level * jnp.repeat(jnp.exp(heights), extent[dim] // parts).reshape((-1,) + (1,) * (len(extent) - 1 - dim))
    return level


def gaussian(rng, extent, width, bound, shards=(), kind=jnp.bfloat16):
    factor_of = block_scale(rng, extent, shards, -0.22, 0.18) if shards else 1.0
    result = jax.random.normal(rng, extent, jnp.float32) * width * factor_of
    return jnp.minimum(jnp.maximum(result, -bound), bound).astype(kind)


def setup_inputs(seed: int = 0) -> dict:
    seeds = jax.random.split(jax.random.key(seed), 17)
    return {
        "global_state": gaussian(seeds[0], (NLAT, NLON, CG), 1.0, 6.0, ((0, 8), (1, 4))),
        "spec_filter": gaussian(seeds[1], (2, MODES, CG), 0.7, 4.0, ((2, 4),), jnp.float32),
        "w_skip": gaussian(seeds[2], (CG, CG), CG ** -0.5, 0.3125),
        "w_mix": gaussian(seeds[3], (CG, CG), CG ** -0.5, 0.3125),
        "w_decode": gaussian(seeds[4], (CG, COND), CG ** -0.5, 0.3125),
        "regional_state": gaussian(seeds[5], (VARS, NROW, NCOL), 1.0, 6.0, ((1, 8), (2, 4))),
        "noise_draws": gaussian(seeds[6], (HOURS, VARS, NROW, NCOL), 1.0, 6.0, ((2, 8), (3, 4))),
        "w_first": gaussian(seeds[7], (CH1, 9, VARS + COND), (9 * (VARS + COND)) ** -0.5, 0.1875),
        "w_down": gaussian(seeds[8], (CH2, 9, CH1), (9 * CH1) ** -0.5, 0.1875),
        "w_up": gaussian(seeds[9], (CH1, CH2), CH2 ** -0.5, 0.375),
        "w_bridge": gaussian(seeds[10], (CH1, CH1), CH1 ** -0.5, 0.5),
        "w_last": gaussian(seeds[11], (VARS, 9, CH1), (9 * CH1) ** -0.5, 0.1875),
        "box_lat0": jax.random.randint(seeds[12], (1,), 0, NLAT - BOX_LAT + 1).astype(jnp.int32),
        "box_lon0": jax.random.randint(seeds[13], (1,), 0, NLON - BOX_LON + 1).astype(jnp.int32),
        "stencil_lat": draw_stencil_lat(jax.random.fold_in(seeds[16], 71), 0),
        "stencil_lon": draw_stencil_lon(jax.random.fold_in(seeds[16], 71), 0),
    }


noise_level = 0.5


def fourier_tables(length, num_modes):
    position = jnp.arange(length, dtype=jnp.int32)[:, None]
    frequency = jnp.arange(num_modes, dtype=jnp.int32)[None, :]
    angle = ((position * frequency) % length).astype(jnp.float32) * (2.0 * math.pi / length)
    cosine = jnp.cos(angle)
    sine = jnp.sin(angle)
    factor = jnp.where(frequency == 0, 1.0, 2.0) / length
    forward = jnp.concatenate([cosine, -sine], axis=1).astype(jnp.bfloat16)
    inverse = jnp.concatenate([cosine * factor, -sine * factor], axis=1).T.astype(jnp.bfloat16)
    return forward, inverse


def global_hour(current, spec_filter, w_skip, w_mix, forward, inverse):
    spectrum = jnp.einsum("alc,lm->amc", current.astype(jnp.float32), forward.astype(jnp.float32))
    num_modes = spec_filter.shape[1]
    real_part = spectrum[:, :num_modes, :]
    imag_part = spectrum[:, num_modes:, :]
    filt_real = spec_filter[0][None]
    filt_imag = spec_filter[1][None]
    mixed = jnp.concatenate([real_part * filt_real - imag_part * filt_imag, real_part * filt_imag + imag_part * filt_real], axis=1).astype(jnp.bfloat16)
    spectral = jnp.einsum("amc,ml->alc", mixed.astype(jnp.float32), inverse.astype(jnp.float32)).astype(jnp.bfloat16)
    skipped = jnp.einsum("alc,cd->ald", current.astype(jnp.float32), w_skip.astype(jnp.float32))
    activated = jax.nn.gelu(spectral.astype(jnp.float32) + skipped).astype(jnp.bfloat16)
    update = jnp.einsum("ald,de->ale", activated.astype(jnp.float32), w_mix.astype(jnp.float32))
    return (current.astype(jnp.float32) + update).astype(jnp.bfloat16)


def condition_field(current, w_decode, box_lat0, box_lon0, stencil_lat, stencil_lon):
    coarse = jnp.einsum("alc,ck->kal", current.astype(jnp.float32), w_decode.astype(jnp.float32)).astype(jnp.bfloat16)
    zero_index = jnp.zeros((), jnp.int32)
    region = lax.dynamic_slice(coarse, (zero_index, box_lat0[0].astype(jnp.int32), box_lon0[0].astype(jnp.int32)), (COND, BOX_LAT, BOX_LON)).astype(jnp.float32)
    flat = region.reshape(COND, BOX_LAT * BOX_LON)
    base = stencil_lat * BOX_LON + stencil_lon
    low_left = jnp.take(flat, base, axis=1)
    low_right = jnp.take(flat, base + 1, axis=1)
    up_left = jnp.take(flat, base + BOX_LON, axis=1)
    up_right = jnp.take(flat, base + BOX_LON + 1, axis=1)
    frac_row = (((jnp.arange(NROW, dtype=jnp.int32) % RATIO).astype(jnp.float32) + 0.5) / RATIO)[:, None]
    frac_col = (((jnp.arange(NCOL, dtype=jnp.int32) % RATIO).astype(jnp.float32) + 0.5) / RATIO)[None, :]
    blended = (1.0 - frac_row) * ((1.0 - frac_col) * low_left + frac_col * low_right) + frac_row * ((1.0 - frac_col) * up_left + frac_col * up_right)
    return blended.astype(jnp.bfloat16)


def conv_taps(source, weight):
    extent_rows, extent_cols = source.shape[1], source.shape[2]
    padded = jnp.pad(source, ((0, 0), (1, 1), (1, 1)))
    accumulated = jnp.zeros((weight.shape[0], extent_rows, extent_cols), jnp.float32)
    for step_down in range(3):
        for step_side in range(3):
            accumulated = accumulated + jnp.einsum("oc,chw->ohw", weight[:, 3 * step_down + step_side, :].astype(jnp.float32), padded[:, step_down:step_down + extent_rows, step_side:step_side + extent_cols].astype(jnp.float32))
    return accumulated


def average_pool(source):
    channels, extent_rows, extent_cols = source.shape
    blocks = source.astype(jnp.float32).reshape(channels, extent_rows // 2, 2, extent_cols // 2, 2)
    return jnp.mean(blocks, axis=(2, 4)).astype(jnp.bfloat16)


def regional_hour(current, noise_now, cond_fine, w_first, w_down, w_up, w_bridge, w_last):
    noisy = (current.astype(jnp.float32) + noise_level * noise_now.astype(jnp.float32)).astype(jnp.bfloat16)
    stacked = jnp.concatenate([noisy, cond_fine], axis=0)
    first = jax.nn.silu(conv_taps(stacked, w_first)).astype(jnp.bfloat16)
    pooled = average_pool(first)
    second = jax.nn.silu(conv_taps(pooled, w_down)).astype(jnp.bfloat16)
    lifted = jnp.einsum("oc,chw->ohw", w_up.astype(jnp.float32), second.astype(jnp.float32))
    lifted = jnp.repeat(jnp.repeat(lifted, 2, axis=1), 2, axis=2)
    bridged = jnp.einsum("oc,chw->ohw", w_bridge.astype(jnp.float32), first.astype(jnp.float32))
    third = jax.nn.silu(lifted + bridged).astype(jnp.bfloat16)
    correction = conv_taps(third, w_last)
    return (noisy.astype(jnp.float32) + correction).astype(jnp.bfloat16)


def reference(global_state, spec_filter, w_skip, w_mix, w_decode, regional_state, noise_draws, w_first, w_down, w_up, w_bridge, w_last, box_lat0, box_lon0, stencil_lat, stencil_lon):
    forward, inverse = fourier_tables(NLON, MODES)
    global_now = global_state
    regional_now = regional_state
    for hour_index in range(HOURS):
        global_now = global_hour(global_now, spec_filter, w_skip, w_mix, forward, inverse)
        cond_fine = condition_field(global_now, w_decode, box_lat0, box_lon0, stencil_lat, stencil_lon)
        regional_now = regional_hour(regional_now, noise_draws[hour_index], cond_fine, w_first, w_down, w_up, w_bridge, w_last)
    return global_now, regional_now
```

```python
import functools
import math

import jax
import jax.numpy as jnp
import ml_dtypes
import numpy as np
from jax import lax
from jax.experimental import pallas as pl
from jax.experimental.pallas import tpu as pltpu
from jax.sharding import PartitionSpec as P

RATIO = 8
noise_level = 0.5
PLANE = ("grp", "row")
RIM = 9
RIM_USED = 4
LANES = 128


def fourier_tables(length, num_modes):
    position = np.arange(length, dtype=np.int64)[:, None]
    frequency = np.arange(num_modes, dtype=np.int64)[None, :]
    angle = (position * frequency % length).astype(np.float64) * (2.0 * math.pi / length)
    cosine = np.cos(angle)
    sine = np.sin(angle)
    factor = np.where(frequency == 0, 1.0, 2.0) / length
    forward = np.concatenate([cosine, -sine], axis=1).T.astype(ml_dtypes.bfloat16)
    inverse = np.concatenate([cosine * factor, -sine * factor], axis=1).astype(ml_dtypes.bfloat16)
    return jnp.asarray(forward), jnp.asarray(inverse)


def shift_pairs(count, step):
    return [(source, (source + step) % count) for source in range(count)]


def exchange(blocks, axis):
    count = lax.axis_size(axis)
    me = lax.axis_index(axis)
    pieces = []
    for step in range(1, count):
        piece = lax.dynamic_index_in_dim(blocks, (me + step) % count, 0, keepdims=True)
        pieces.append(lax.ppermute(piece, axis, shift_pairs(count, step)))
    result = blocks
    for step, piece in enumerate(pieces, 1):
        result = lax.dynamic_update_slice_in_dim(result, piece, (me - step) % count, 0)
    return result


def collect(block, axis):
    count = lax.axis_size(axis)
    me = lax.axis_index(axis)
    pieces = [
        lax.ppermute(block, axis, shift_pairs(count, step)) for step in range(1, count)
    ]
    result = jnp.broadcast_to(block[None], (count,) + block.shape)
    for step, piece in enumerate(pieces, 1):
        result = lax.dynamic_update_slice_in_dim(result, piece[None], (me - step) % count, 0)
    return result


def collect_filter(spec_filter):
    rows = 2 * spec_filter.shape[1]
    flat = spec_filter.reshape(rows, spec_filter.shape[2]).astype(jnp.bfloat16)
    grp, row = lax.axis_size("grp"), lax.axis_size("row")
    share = rows // (grp * row)
    place = lax.axis_index("row") * grp + lax.axis_index("grp")
    mine = lax.dynamic_slice_in_dim(flat, place * share, share, 0)
    wide = collect(mine, "col")
    wide = jnp.swapaxes(wide, 0, 1).reshape(share, -1)
    pair = collect(wide, "grp").reshape(grp * share, -1)
    return collect(pair, "row").reshape(rows, -1)


def latitude_kernel(
    hours, block, state_ref, forward_ref, inverse_ref, filter_ref, skip_ref, mix_ref, decode_ref,
    out_ref, coarse_ref, filtered_ref,
):
    length = state_ref.shape[0]
    modes = filter_ref.shape[0] // 2
    for hour in range(hours):
        source_ref = state_ref if hour == 0 else out_ref

        def analyse(index, carry):
            low = pl.ds(pl.multiple_of(index * block, 16), block)
            high = pl.ds(pl.multiple_of(modes + index * block, 16), block)
            state = source_ref[...]
            real = jnp.dot(forward_ref[low, :], state, preferred_element_type=jnp.float32)
            imag = jnp.dot(forward_ref[high, :], state, preferred_element_type=jnp.float32)
            gain_real = filter_ref[low, :].astype(jnp.float32)
            gain_imag = filter_ref[high, :].astype(jnp.float32)
            filtered_ref[low, :] = (real * gain_real - imag * gain_imag).astype(jnp.bfloat16)
            filtered_ref[high, :] = (real * gain_imag + imag * gain_real).astype(jnp.bfloat16)
            return carry

        lax.fori_loop(0, modes // block, analyse, 0)

        def synthesise(index, carry):
            here = pl.ds(pl.multiple_of(index * block, 16), block)
            spectral = jnp.dot(
                inverse_ref[here, :], filtered_ref[...], preferred_element_type=jnp.float32
            ).astype(jnp.bfloat16)
            state = source_ref[here, :]
            skipped = jnp.dot(state, skip_ref[...], preferred_element_type=jnp.float32)
            activated = jax.nn.gelu(spectral.astype(jnp.float32) + skipped).astype(jnp.bfloat16)
            update = jnp.dot(activated, mix_ref[...], preferred_element_type=jnp.float32)
            fresh = (state.astype(jnp.float32) + update).astype(jnp.bfloat16)
            out_ref[here, :] = fresh
            coarse_ref[hour, here, :] = jnp.dot(
                fresh, decode_ref[...], preferred_element_type=jnp.float32
            ).astype(jnp.bfloat16)
            return carry

        lax.fori_loop(0, length // block, synthesise, 0)


def advance_latitude(hours, state, forward, inverse, gains, w_skip, w_mix, decode):
    length, channels = state.shape
    modes = gains.shape[0] // 2
    block = next(b for b in (144, 48, 16) if modes % b == 0)
    flops = hours * 2 * length * channels * (4 * modes + 2 * channels + LANES)
    return pl.pallas_call(
        functools.partial(latitude_kernel, hours, block),
        out_shape=(
            jax.ShapeDtypeStruct((length, channels), jnp.bfloat16),
            jax.ShapeDtypeStruct((hours, length, LANES), jnp.bfloat16),
        ),
        scratch_shapes=[pltpu.VMEM((2 * modes, channels), jnp.bfloat16)],
        compiler_params=pltpu.CompilerParams(vmem_limit_bytes=40 * 2**20),
        cost_estimate=pl.CostEstimate(
            flops=flops, bytes_accessed=12 * 2**20, transcendentals=hours * length * channels
        ),
        name="advance_latitude",
    )(state, forward, inverse, gains, w_skip, w_mix, decode)


def global_hour(current, spec_filter, w_skip, w_mix, forward, inverse):
    longitude = lax.all_to_all(current, "col", split_axis=2, concat_axis=1, tiled=True)
    spectrum = jnp.einsum("alc,ml->amc", longitude, forward, preferred_element_type=jnp.float32)
    num_modes = spec_filter.shape[1]
    real_part = spectrum[:, :num_modes, :]
    imag_part = spectrum[:, num_modes:, :]
    filt_real = spec_filter[0][None]
    filt_imag = spec_filter[1][None]
    mixed = jnp.concatenate(
        [
            real_part * filt_real - imag_part * filt_imag,
            real_part * filt_imag + imag_part * filt_real,
        ],
        axis=1,
    ).astype(jnp.bfloat16)
    filtered = jnp.einsum("amc,lm->alc", mixed, inverse, preferred_element_type=jnp.float32).astype(
        jnp.bfloat16
    )
    spectral = lax.all_to_all(filtered, "col", split_axis=1, concat_axis=2, tiled=True)
    skipped = jnp.einsum("alc,cd->ald", current, w_skip, preferred_element_type=jnp.float32)
    activated = jax.nn.gelu(spectral.astype(jnp.float32) + skipped).astype(jnp.bfloat16)
    update = jnp.einsum("ald,de->ale", activated, w_mix, preferred_element_type=jnp.float32)
    return (current.astype(jnp.float32) + update).astype(jnp.bfloat16)


def window_extent(cells):
    return (cells + RIM - 1) // RATIO + 3 - (-RIM // RATIO)


def window_base():
    return -(-RIM // RATIO)


def global_by_latitude(
    hours, global_state, spec_filter, w_skip, w_mix, w_decode, box_lat0, box_lon0, rows_here, cols_here
):
    count = lax.axis_size("col")
    lats_here, _, channels = global_state.shape
    lon_total = global_state.shape[1] * count
    turns = lats_here // count
    forward, inverse = fourier_tables(lon_total, spec_filter.shape[1])
    conds = w_decode.shape[1]
    decode = jnp.pad(w_decode, ((0, 0), (0, LANES - conds)))
    gathered = [
        exchange(global_state[turn * count : (turn + 1) * count], "col") for turn in range(turns)
    ]
    gains = collect_filter(spec_filter)
    finals, coarses = [], []
    for turn in range(turns):
        state = gathered[turn].reshape(lon_total, channels)
        state, coarse = advance_latitude(
            hours, state, forward, inverse, gains, w_skip, w_mix, decode
        )
        finals.append(exchange(state.reshape((count, -1, channels)), "col"))
        coarses.append(coarse)
    global_final = jnp.concatenate(finals, axis=0)
    base = window_base()
    high, wide = window_extent(rows_here), window_extent(cols_here)
    coarse = jnp.stack(coarses, axis=1)[..., :conds]
    step = cols_here // RATIO
    span = (count - 1) * step + wide
    coarse = jnp.pad(coarse, ((0, 0), (0, 0), (base, span), (0, 0)))
    zero = jnp.zeros((), jnp.int32)
    strip = lax.dynamic_slice(
        coarse, (zero, zero, box_lon0[0], zero), (hours, turns, span, conds)
    )
    packed = jnp.stack(
        [strip[:, :, col * step : col * step + wide].reshape(-1) for col in range(count)]
    )
    size = packed.shape[1]
    packed = jnp.pad(packed, ((0, 0), (0, -size % 1024))).reshape(count, -1, LANES)
    plane = lax.axis_size(PLANE)
    sent = jnp.broadcast_to(packed[None], (plane,) + packed.shape).reshape(
        (plane * count,) + packed.shape[1:]
    )
    got = lax.all_to_all(sent, PLANE + ("col",), split_axis=0, concat_axis=0, tiled=True)
    got = got.reshape(plane, count, -1)[..., :size].reshape(plane, count, hours, turns, wide, conds)
    got = jnp.transpose(got, (2, 0, 3, 1, 4, 5)).reshape(hours, plane * lats_here, wide, conds)
    got = jnp.pad(got, ((0, 0), (base, high), (0, 0), (0, 0)))
    start = box_lat0[0] + lax.axis_index(PLANE) * (rows_here // RATIO)
    windows = lax.dynamic_slice_in_dim(got, start, high, 1)
    return global_final, [windows[hour].reshape(high * wide, conds) for hour in range(hours)]


def global_by_channel(
    hours, global_state, spec_filter, w_skip, w_mix, w_decode, box_lat0, box_lon0, rows_here, cols_here
):
    count = lax.axis_size("col")
    forward, inverse = fourier_tables(global_state.shape[1] * count, spec_filter.shape[1])
    base = window_base()
    high, wide = window_extent(rows_here), window_extent(cols_here)
    span = (count - 1) * (cols_here // RATIO) + wide
    lat_start = box_lat0[0] + lax.axis_index(PLANE) * (rows_here // RATIO)
    lon_start = box_lon0[0] + lax.axis_index("col") * (cols_here // RATIO)
    windows = []
    for _ in range(hours):
        global_state = global_hour(global_state, spec_filter, w_skip, w_mix, forward, inverse)
        coarse = jnp.einsum(
            "alc,ck->alk", global_state, w_decode, preferred_element_type=jnp.float32
        ).astype(jnp.bfloat16)
        coarse = lax.all_gather(coarse, "col", axis=1, tiled=True)
        coarse = jnp.pad(coarse, ((0, 0), (base, span), (0, 0)))
        coarse = lax.dynamic_slice_in_dim(coarse, box_lon0[0], base + span, 1)
        coarse = lax.all_gather(coarse, PLANE, axis=0, tiled=True)
        coarse = lax.dynamic_slice_in_dim(coarse, lon_start - box_lon0[0], wide, 1)
        coarse = jnp.pad(coarse, ((base, high), (0, 0), (0, 0)))
        coarse = lax.dynamic_slice_in_dim(coarse, lat_start, high, 0)
        windows.append(coarse.reshape(high * wide, -1))
    return global_state, windows


def with_rim(block, rim):
    for axis, dim in ((PLANE, 0), ("col", 1)):
        count = lax.axis_size(axis)
        forward = [(i, i + 1) for i in range(count - 1)]
        backward = [(target, source) for source, target in forward]
        extent = block.shape[dim]
        low = lax.ppermute(
            lax.slice_in_dim(block, extent - rim, extent, axis=dim), axis, forward
        )
        high = lax.ppermute(lax.slice_in_dim(block, 0, rim, axis=dim), axis, backward)
        block = jnp.concatenate([low, block, high], axis=dim)
    return block


def blend_matrix(lat_shift, lon_shift, inside, high, wide):
    rows, cols = lat_shift.shape[:2]
    point = jnp.arange(high * wide, dtype=jnp.int32)[None, None, :]
    row = jnp.arange(rows, dtype=jnp.int32)[:, None, None] - RIM
    col = jnp.arange(cols, dtype=jnp.int32)[None, :, None] - RIM
    from_lat = point // wide - (row // RATIO + window_base()) - lat_shift
    from_lon = point % wide - (col // RATIO + window_base()) - lon_shift
    frac_row = ((row % RATIO).astype(jnp.float32) + 0.5) / RATIO
    frac_col = ((col % RATIO).astype(jnp.float32) + 0.5) / RATIO
    weight_lat = jnp.where(from_lat == 0, 1.0 - frac_row, jnp.where(from_lat == 1, frac_row, 0.0))
    weight_lon = jnp.where(from_lon == 0, 1.0 - frac_col, jnp.where(from_lon == 1, frac_col, 0.0))
    return jnp.where(inside, weight_lat * weight_lon, 0.0).astype(jnp.bfloat16)


def convolve(source, weight):
    return lax.conv_general_dilated(
        source[None],
        weight,
        (1, 1),
        "VALID",
        dimension_numbers=("NHWC", "HWIO", "NHWC"),
        preferred_element_type=jnp.float32,
    )[0]


def trim(source, width):
    return source[width : source.shape[0] - width, width : source.shape[1] - width]


def regional_hour(noisy, cond, rim, inside_at, w_first, w_down, w_up, w_bridge, w_last):
    stacked = jnp.concatenate([noisy, cond], axis=2)
    first = jax.nn.silu(convolve(stacked, w_first)).astype(jnp.bfloat16)
    first = jnp.where(inside_at(rim - 1, 1), first, 0)
    rows, cols, channels = first.shape
    pooled = (
        jnp.mean(
            first.astype(jnp.float32).reshape(rows // 2, 2, cols // 2, 2, channels), axis=(1, 3)
        )
    ).astype(jnp.bfloat16)
    second = jax.nn.silu(convolve(pooled, w_down)).astype(jnp.bfloat16)
    lifted = jnp.einsum("hwc,co->hwo", second, w_up, preferred_element_type=jnp.float32)
    lifted = jnp.repeat(jnp.repeat(lifted, 2, axis=0), 2, axis=1)
    bridged = jnp.einsum("hwc,co->hwo", trim(first, 2), w_bridge, preferred_element_type=jnp.float32)
    third = jax.nn.silu(lifted + bridged).astype(jnp.bfloat16)
    third = jnp.where(inside_at(rim - 3, 1), third, 0)
    correction = convolve(third, w_last)
    fresh = (trim(noisy, 4).astype(jnp.float32) + correction).astype(jnp.bfloat16)
    return jnp.where(inside_at(rim - 4, 1), fresh, 0)


def shards(
    global_state,
    spec_filter,
    w_skip,
    w_mix,
    w_decode,
    regional_state,
    noise_draws,
    w_first,
    w_down,
    w_up,
    w_bridge,
    w_last,
    box_lat0,
    box_lon0,
    stencil_lat,
    stencil_lon,
):
    hours = noise_draws.shape[0]
    rows_here, cols_here = regional_state.shape[1:]
    row_start = lax.axis_index(PLANE) * rows_here
    col_start = lax.axis_index("col") * cols_here
    total_rows = rows_here * lax.axis_size(PLANE)
    total_cols = cols_here * lax.axis_size("col")
    assert hours == 2

    def inside_at(rim, stride):
        row = row_start - rim + stride * jnp.arange((rows_here + 2 * rim) // stride, dtype=jnp.int32)
        col = col_start - rim + stride * jnp.arange((cols_here + 2 * rim) // stride, dtype=jnp.int32)
        row_in = (row >= 0) & (row < total_rows)
        col_in = (col >= 0) & (col < total_cols)
        return row_in[:, None, None] & col_in[None, :, None]

    by_latitude = global_state.shape[0] % lax.axis_size("col") == 0
    global_steps = global_by_latitude if by_latitude else global_by_channel
    global_final, windows = global_steps(
        hours, global_state, spec_filter, w_skip, w_mix, w_decode, box_lat0, box_lon0,
        rows_here, cols_here,
    )

    variables = regional_state.shape[0]
    noisy = (
        regional_state.astype(jnp.float32) + noise_level * noise_draws[0].astype(jnp.float32)
    ).astype(jnp.bfloat16)
    lat_shift = stencil_lat - (row_start + jnp.arange(rows_here, dtype=jnp.int32))[:, None] // RATIO
    lon_shift = stencil_lon - (col_start + jnp.arange(cols_here, dtype=jnp.int32))[None, :] // RATIO
    packed = jnp.concatenate(
        [
            jnp.transpose(noisy, (1, 2, 0)),
            lat_shift.astype(jnp.bfloat16)[..., None],
            lon_shift.astype(jnp.bfloat16)[..., None],
            jnp.zeros((rows_here, cols_here, LANES - variables - 2), jnp.bfloat16),
        ],
        axis=2,
    )
    packed = with_rim(packed, RIM)
    later_noise = with_rim(
        jnp.pad(jnp.transpose(noise_draws[1], (1, 2, 0)), ((0, 0), (0, 0), (0, LANES - variables))),
        RIM - RIM_USED,
    )[..., :variables]
    noisy = packed[..., :variables]
    high, wide = window_extent(rows_here), window_extent(cols_here)
    blend = blend_matrix(
        packed[..., variables : variables + 1].astype(jnp.int32),
        packed[..., variables + 1 : variables + 2].astype(jnp.int32),
        inside_at(RIM, 1),
        high,
        wide,
    )

    def taps(weight):
        return jnp.transpose(weight, (1, 2, 0)).reshape(3, 3, weight.shape[2], weight.shape[0])

    weights = (taps(w_first), taps(w_down), w_up.T, w_bridge.T, taps(w_last))
    for hour in range(hours):
        rim = RIM - RIM_USED * hour
        cond = jnp.einsum(
            "hwp,pk->hwk", trim(blend, RIM - rim), windows[hour], preferred_element_type=jnp.float32
        ).astype(jnp.bfloat16)
        state = regional_hour(noisy, cond, rim, inside_at, *weights)
        if hour == 0:
            noisy = (
                state.astype(jnp.float32) + noise_level * later_noise.astype(jnp.float32)
            ).astype(jnp.bfloat16)
    regional_final = jnp.transpose(trim(state, RIM - RIM_USED * hours), (2, 0, 1))
    return global_final, regional_final


def solution(mesh):
    return jax.shard_map(
        shards,
        mesh=mesh,
        in_specs=(
            P(PLANE, "col", None),
            P(None, None, "col"),
            P(),
            P(),
            P(),
            P(None, PLANE, "col"),
            P(None, None, PLANE, "col"),
            P(),
            P(),
            P(),
            P(),
            P(),
            P(),
            P(),
            P(PLANE, "col"),
            P(PLANE, "col"),
        ),
        out_specs=(P(PLANE, "col", None), P(None, PLANE, "col")),
        check_vma=False,
    )
```

```python
import functools
import math

import jax
import jax.numpy as jnp
import ml_dtypes
import numpy as np
from jax import lax
from jax.experimental import pallas as pl
from jax.experimental.pallas import tpu as pltpu
from jax.sharding import PartitionSpec as P

RATIO = 8
noise_level = 0.5
PLANE = ("grp", "row")
RIM = 9
RIM_USED = 4
LANES = 128
RIM_COLS = 16


def fourier_tables(length, num_modes):
    position = np.arange(length, dtype=np.int64)[:, None]
    frequency = np.arange(num_modes, dtype=np.int64)[None, :]
    angle = (position * frequency % length).astype(np.float64) * (2.0 * math.pi / length)
    cosine = np.cos(angle)
    sine = np.sin(angle)
    factor = np.where(frequency == 0, 1.0, 2.0) / length
    forward = np.concatenate([cosine, -sine], axis=1).T.astype(ml_dtypes.bfloat16)
    inverse = np.concatenate([cosine * factor, -sine * factor], axis=1).astype(ml_dtypes.bfloat16)
    return jnp.asarray(forward), jnp.asarray(inverse)


def shift_pairs(count, step):
    return [(source, (source + step) % count) for source in range(count)]


def exchange(blocks, axis):
    count = lax.axis_size(axis)
    me = lax.axis_index(axis)
    pieces = []
    for step in range(1, count):
        piece = lax.dynamic_index_in_dim(blocks, (me + step) % count, 0, keepdims=True)
        pieces.append(lax.ppermute(piece, axis, shift_pairs(count, step)))
    result = blocks
    for step, piece in enumerate(pieces, 1):
        result = lax.dynamic_update_slice_in_dim(result, piece, (me - step) % count, 0)
    return result


def collect(block, axis):
    count = lax.axis_size(axis)
    me = lax.axis_index(axis)
    pieces = [
        lax.ppermute(block, axis, shift_pairs(count, step)) for step in range(1, count)
    ]
    result = jnp.broadcast_to(block[None], (count,) + block.shape)
    for step, piece in enumerate(pieces, 1):
        result = lax.dynamic_update_slice_in_dim(result, piece[None], (me - step) % count, 0)
    return result


def collect_filter(spec_filter):
    rows = 2 * spec_filter.shape[1]
    flat = spec_filter.reshape(rows, spec_filter.shape[2]).astype(jnp.bfloat16)
    grp, row = lax.axis_size("grp"), lax.axis_size("row")
    share = rows // (grp * row)
    place = lax.axis_index("row") * grp + lax.axis_index("grp")
    mine = lax.dynamic_slice_in_dim(flat, place * share, share, 0)
    wide = collect(mine, "col")
    wide = jnp.swapaxes(wide, 0, 1).reshape(share, -1)
    pair = collect(wide, "grp").reshape(grp * share, -1)
    return collect(pair, "row").reshape(rows, -1)


def latitude_kernel(
    hours, block, state_ref, forward_ref, inverse_ref, filter_ref, skip_ref, mix_ref, decode_ref,
    out_ref, coarse_ref, filtered_ref,
):
    length = state_ref.shape[0]
    modes = filter_ref.shape[0] // 2
    for hour in range(hours):
        source_ref = state_ref if hour == 0 else out_ref

        def analyse(index, carry):
            low = pl.ds(pl.multiple_of(index * block, 16), block)
            high = pl.ds(pl.multiple_of(modes + index * block, 16), block)
            state = source_ref[...]
            real = jnp.dot(forward_ref[low, :], state, preferred_element_type=jnp.float32)
            imag = jnp.dot(forward_ref[high, :], state, preferred_element_type=jnp.float32)
            gain_real = filter_ref[low, :].astype(jnp.float32)
            gain_imag = filter_ref[high, :].astype(jnp.float32)
            filtered_ref[low, :] = (real * gain_real - imag * gain_imag).astype(jnp.bfloat16)
            filtered_ref[high, :] = (real * gain_imag + imag * gain_real).astype(jnp.bfloat16)
            return carry

        lax.fori_loop(0, modes // block, analyse, 0)

        def synthesise(index, carry):
            here = pl.ds(pl.multiple_of(index * block, 16), block)
            spectral = jnp.dot(
                inverse_ref[here, :], filtered_ref[...], preferred_element_type=jnp.float32
            ).astype(jnp.bfloat16)
            state = source_ref[here, :]
            skipped = jnp.dot(state, skip_ref[...], preferred_element_type=jnp.float32)
            activated = jax.nn.gelu(spectral.astype(jnp.float32) + skipped).astype(jnp.bfloat16)
            update = jnp.dot(activated, mix_ref[...], preferred_element_type=jnp.float32)
            fresh = (state.astype(jnp.float32) + update).astype(jnp.bfloat16)
            out_ref[here, :] = fresh
            coarse_ref[hour, here, :] = jnp.dot(
                fresh, decode_ref[...], preferred_element_type=jnp.float32
            ).astype(jnp.bfloat16)
            return carry

        lax.fori_loop(0, length // block, synthesise, 0)


def advance_latitude(hours, state, forward, inverse, gains, w_skip, w_mix, decode):
    length, channels = state.shape
    modes = gains.shape[0] // 2
    block = next(b for b in (720, 240, 144, 48, 16) if modes % b == 0)
    flops = hours * 2 * length * channels * (4 * modes + 2 * channels + LANES)
    return pl.pallas_call(
        functools.partial(latitude_kernel, hours, block),
        out_shape=(
            jax.ShapeDtypeStruct((length, channels), jnp.bfloat16),
            jax.ShapeDtypeStruct((hours, length, LANES), jnp.bfloat16),
        ),
        scratch_shapes=[pltpu.VMEM((2 * modes, channels), jnp.bfloat16)],
        compiler_params=pltpu.CompilerParams(vmem_limit_bytes=40 * 2**20),
        cost_estimate=pl.CostEstimate(
            flops=flops, bytes_accessed=12 * 2**20, transcendentals=hours * length * channels
        ),
        name="advance_latitude",
    )(state, forward, inverse, gains, w_skip, w_mix, decode)


def global_hour(current, spec_filter, w_skip, w_mix, forward, inverse):
    longitude = lax.all_to_all(current, "col", split_axis=2, concat_axis=1, tiled=True)
    spectrum = jnp.einsum("alc,ml->amc", longitude, forward, preferred_element_type=jnp.float32)
    num_modes = spec_filter.shape[1]
    real_part = spectrum[:, :num_modes, :]
    imag_part = spectrum[:, num_modes:, :]
    filt_real = spec_filter[0][None]
    filt_imag = spec_filter[1][None]
    mixed = jnp.concatenate(
        [
            real_part * filt_real - imag_part * filt_imag,
            real_part * filt_imag + imag_part * filt_real,
        ],
        axis=1,
    ).astype(jnp.bfloat16)
    filtered = jnp.einsum("amc,lm->alc", mixed, inverse, preferred_element_type=jnp.float32).astype(
        jnp.bfloat16
    )
    spectral = lax.all_to_all(filtered, "col", split_axis=1, concat_axis=2, tiled=True)
    skipped = jnp.einsum("alc,cd->ald", current, w_skip, preferred_element_type=jnp.float32)
    activated = jax.nn.gelu(spectral.astype(jnp.float32) + skipped).astype(jnp.bfloat16)
    update = jnp.einsum("ald,de->ale", activated, w_mix, preferred_element_type=jnp.float32)
    return (current.astype(jnp.float32) + update).astype(jnp.bfloat16)


def window_extent(cells):
    return (cells + RIM - 1) // RATIO + 3 - (-RIM // RATIO)


def window_stride(cells):
    return -(-window_extent(cells) // 32) * 32


def window_base():
    return -(-RIM // RATIO)


def pad_windows(windows, cols_here):
    spare = window_stride(cols_here) - windows.shape[2]
    return jnp.pad(windows, ((0, 0), (0, 0), (0, spare), (0, 0)))


def global_by_latitude(
    hours, global_state, spec_filter, w_skip, w_mix, w_decode, box_lat0, box_lon0, rows_here, cols_here
):
    count = lax.axis_size("col")
    lats_here, _, channels = global_state.shape
    lon_total = global_state.shape[1] * count
    turns = lats_here // count
    forward, inverse = fourier_tables(lon_total, spec_filter.shape[1])
    conds = w_decode.shape[1]
    decode = jnp.pad(w_decode, ((0, 0), (0, LANES - conds)))
    gathered = [
        exchange(global_state[turn * count : (turn + 1) * count], "col") for turn in range(turns)
    ]
    gains = collect_filter(spec_filter)
    finals, coarses = [], []
    for turn in range(turns):
        state = gathered[turn].reshape(lon_total, channels)
        state, coarse = advance_latitude(
            hours, state, forward, inverse, gains, w_skip, w_mix, decode
        )
        finals.append(exchange(state.reshape((count, -1, channels)), "col"))
        coarses.append(coarse)
    global_final = jnp.concatenate(finals, axis=0)
    base = window_base()
    high, wide = window_extent(rows_here), window_extent(cols_here)
    coarse = jnp.stack(coarses, axis=1)[..., :conds]
    step = cols_here // RATIO
    span = (count - 1) * step + wide
    coarse = jnp.pad(coarse, ((0, 0), (0, 0), (base, span), (0, 0)))
    zero = jnp.zeros((), jnp.int32)
    strip = lax.dynamic_slice(
        coarse, (zero, zero, box_lon0[0], zero), (hours, turns, span, conds)
    )
    packed = jnp.stack(
        [strip[:, :, col * step : col * step + wide].reshape(-1) for col in range(count)]
    )
    size = packed.shape[1]
    packed = jnp.pad(packed, ((0, 0), (0, -size % 1024))).reshape(count, -1, LANES)
    plane = lax.axis_size(PLANE)
    sent = jnp.broadcast_to(packed[None], (plane,) + packed.shape).reshape(
        (plane * count,) + packed.shape[1:]
    )
    got = lax.all_to_all(sent, PLANE + ("col",), split_axis=0, concat_axis=0, tiled=True)
    got = got.reshape(plane, count, -1)[..., :size].reshape(plane, count, hours, turns, wide, conds)
    got = jnp.transpose(got, (2, 0, 3, 1, 4, 5)).reshape(hours, plane * lats_here, wide, conds)
    got = jnp.pad(got, ((0, 0), (base, high), (0, 0), (0, 0)))
    start = box_lat0[0] + lax.axis_index(PLANE) * (rows_here // RATIO)
    windows = lax.dynamic_slice_in_dim(got, start, high, 1)
    return global_final, pad_windows(windows, cols_here)


def global_by_channel(
    hours, global_state, spec_filter, w_skip, w_mix, w_decode, box_lat0, box_lon0, rows_here, cols_here
):
    count = lax.axis_size("col")
    forward, inverse = fourier_tables(global_state.shape[1] * count, spec_filter.shape[1])
    base = window_base()
    high, wide = window_extent(rows_here), window_extent(cols_here)
    span = (count - 1) * (cols_here // RATIO) + wide
    lat_start = box_lat0[0] + lax.axis_index(PLANE) * (rows_here // RATIO)
    lon_start = box_lon0[0] + lax.axis_index("col") * (cols_here // RATIO)
    windows = []
    for _ in range(hours):
        global_state = global_hour(global_state, spec_filter, w_skip, w_mix, forward, inverse)
        coarse = jnp.einsum(
            "alc,ck->alk", global_state, w_decode, preferred_element_type=jnp.float32
        ).astype(jnp.bfloat16)
        coarse = lax.all_gather(coarse, "col", axis=1, tiled=True)
        coarse = jnp.pad(coarse, ((0, 0), (base, span), (0, 0)))
        coarse = lax.dynamic_slice_in_dim(coarse, box_lon0[0], base + span, 1)
        coarse = lax.all_gather(coarse, PLANE, axis=0, tiled=True)
        coarse = lax.dynamic_slice_in_dim(coarse, lon_start - box_lon0[0], wide, 1)
        coarse = jnp.pad(coarse, ((base, high), (0, 0), (0, 0)))
        coarse = lax.dynamic_slice_in_dim(coarse, lat_start, high, 0)
        windows.append(coarse)
    return global_state, pad_windows(jnp.stack(windows), cols_here)


def next_to(low, high, axis):
    count = lax.axis_size(axis)
    forward = [(i, i + 1) for i in range(count - 1)]
    backward = [(target, source) for source, target in forward]
    return lax.ppermute(low, axis, forward), lax.ppermute(high, axis, backward)


def grid_place(start_ref, total, base, extent):
    place = start_ref + base + lax.broadcasted_iota(jnp.int32, (extent, 1), 0)
    return (place >= 0) & (place < total)


def assemble_kernel(
    rows, cols, totals, high, wide, lanes, place_ref, mid0_ref, mid1_ref, above_ref, below_ref,
    left_ref, right_ref, noisy_ref, noise_ref, blend_ref,
):
    inner = RIM - RIM_USED
    pad = (noisy_ref.shape[1] - cols) // 2
    width = noisy_ref.shape[1]
    for ref, mid_ref, rim, part in ((noisy_ref, mid0_ref, RIM, 0), (noise_ref, mid1_ref, inner, RIM)):
        ref[0:rim, pad : pad + cols, :] = above_ref[part : part + rim]
        ref[rim : rim + rows, pad : pad + cols, :] = mid_ref[...]
        ref[rim + rows :, pad : pad + cols, :] = below_ref[part : part + rim]
        first = 0 if rim == RIM else rows + 2 * RIM
        ref[:, 0:pad, :] = left_ref[first : first + rows + 2 * rim]
        ref[:, pad + cols :, :] = right_ref[first : first + rows + 2 * rim]

    base = window_base()
    col = lax.broadcasted_iota(jnp.int32, (width, 1), 0) - pad
    col_in = grid_place(place_ref[1], totals[1], -pad, width)
    frac_col = ((col % RATIO).astype(jnp.float32) + 0.5) / RATIO
    col_base = jnp.where(col_in, (col + pad) // RATIO - pad // RATIO + base, -4 * high * wide)
    point = lax.broadcasted_iota(jnp.int32, (width, high * wide), 1)
    point_lat = (point // wide).astype(jnp.float32)
    point_lon = (point % wide).astype(jnp.float32)

    def weigh(index, carry):
        row = index - RIM
        whole = (row + 2 * RATIO) // RATIO - 2
        frac_row = ((row - whole * RATIO).astype(jnp.float32) + 0.5) / RATIO
        there = place_ref[0] + row
        row_base = jnp.where((there >= 0) & (there < totals[0]), whole + base, -4 * high * wide)
        shifts = noisy_ref[index, :, :].astype(jnp.float32)
        lat = row_base.astype(jnp.float32) + shifts[:, lanes : lanes + 1]
        lon = col_base.astype(jnp.float32) + shifts[:, lanes + 1 : lanes + 2]
        from_lat = point_lat - lat
        from_lon = point_lon - lon
        weight_lat = jnp.where(
            from_lat == 0.0, 1.0 - frac_row, jnp.where(from_lat == 1.0, frac_row, 0.0)
        )
        weight_lon = jnp.where(
            from_lon == 0.0, 1.0 - frac_col, jnp.where(from_lon == 1.0, frac_col, 0.0)
        )
        blend_ref[index, :, :] = (weight_lat * weight_lon).astype(jnp.bfloat16)
        return carry

    lax.fori_loop(0, rows + 2 * RIM, weigh, 0)


def assemble(rows, cols, totals, high, wide, lanes, place, mid0, mid1, above, below, left, right):
    inner = RIM - RIM_USED
    width = cols + 2 * left.shape[1]
    channels = mid0.shape[2]
    return pl.pallas_call(
        functools.partial(assemble_kernel, rows, cols, totals, high, wide, lanes),
        out_shape=(
            jax.ShapeDtypeStruct((rows + 2 * RIM, width, channels), jnp.bfloat16),
            jax.ShapeDtypeStruct((rows + 2 * inner, width, channels), jnp.bfloat16),
            jax.ShapeDtypeStruct((rows + 2 * RIM, width, high * wide), jnp.bfloat16),
        ),
        in_specs=[pl.BlockSpec(memory_space=pltpu.SMEM)]
        + [pl.BlockSpec(memory_space=pltpu.VMEM)] * 6,
        compiler_params=pltpu.CompilerParams(vmem_limit_bytes=40 * 2**20),
        cost_estimate=pl.CostEstimate(flops=2 * 10**8, bytes_accessed=10**7, transcendentals=0),
        name="assemble",
    )(place, mid0, mid1, above, below, left, right)


def silu(x):
    return x / (1.0 + jnp.exp(-x))


def denoise_kernel(
    rows, cols, totals, variables, place_ref, noisy_ref, noise_ref, blend_ref, window_ref, first_w_ref,
    down_w_ref, up_w_ref, bridge_w_ref, last_w_ref, out_ref, stack_ref, first_ref, pooled_ref,
    lifted_ref, third_ref, pair_ref, spread_ref,
):
    width = noisy_ref.shape[1]
    half = width // 2
    pad = (width - cols) // 2
    channels = noisy_ref.shape[2]
    f32, bf16 = jnp.float32, jnp.bfloat16
    col_in = grid_place(place_ref[1], totals[1], -pad, width).astype(f32)
    lane = lax.broadcasted_iota(jnp.int32, (1, channels), 1)
    is_state = lane < variables

    def flat(start, count, unit):
        return pl.ds(pl.multiple_of(start * unit, 16), count * unit)

    def inside(row, count):
        marks = []
        for step in range(count):
            there = place_ref[0] + row + step
            marks.append(col_in * jnp.where((there >= 0) & (there < totals[0]), 1.0, 0.0))
        return jnp.concatenate(marks, axis=0)

    def conv(source_ref, row, count, unit, weight_ref):
        lhs = jnp.concatenate(
            [source_ref[flat(row + step, count, unit), :] for step in range(3)], axis=1
        )
        wide = jnp.dot(lhs, weight_ref[...], preferred_element_type=f32)
        size = weight_ref.shape[1] // 3
        span = count * unit
        return (
            pltpu.roll(wide[:, :size], 1, 0)
            + wide[:, size : 2 * size]
            + pltpu.roll(wide[:, 2 * size :], span - 1, 0)
        )

    for hour in range(2):
        rim = RIM - RIM_USED * hour
        tall = rows + 2 * rim

        def stack(index, carry, hour=hour, rim=rim):
            here = flat(index * 2, 2, width)
            weights = blend_ref[pl.ds(index * 2 + RIM - rim, 2)].reshape(2 * width, -1)
            cond = jnp.dot(weights, window_ref[hour], preferred_element_type=f32).astype(bf16)
            if hour == 0:
                own = noisy_ref[pl.ds(index * 2, 2)].reshape(2 * width, channels)
            else:
                own = stack_ref[here, :]
            stack_ref[here, :] = jnp.where(is_state, own, cond)
            return carry

        lax.fori_loop(0, tall // 2, stack, 0)

        def make_first(index, carry, rim=rim):
            row = index * 4
            value = silu(conv(stack_ref, row, 4, width, first_w_ref)) * inside(row - rim + 1, 4)
            value = value.astype(bf16)
            first_ref[flat(row, 4, width), :] = value
            value = value.astype(f32)
            for step in range(2):
                at = 2 * step * width
                pair_ref[...] = value[at : at + width] + value[at + width : at + 2 * width]
                even = pair_ref[pl.ds(0, half, stride=2), :]
                odd = pair_ref[pl.ds(1, half, stride=2), :]
                pooled_ref[flat(index * 2 + step, 1, half), :] = ((even + odd) * 0.25).astype(bf16)
            return carry

        lax.fori_loop(0, (tall - 2) // 4, make_first, 0)

        half_rows = (tall - 2) // 2 - 2

        def make_lifted(index, carry):
            value = silu(conv(pooled_ref, index * 2, 2, half, down_w_ref)).astype(bf16)
            lifted_ref[flat(index * 2, 2, half), :] = jnp.dot(
                value, up_w_ref[...], preferred_element_type=f32
            )
            return carry

        lax.fori_loop(0, half_rows // 2, make_lifted, 0)

        def make_third(index, carry, rim=rim):
            row = index * 2
            lifted = lifted_ref[flat(index, 1, half), :]
            spread_ref[pl.ds(0, half, stride=2), :] = lifted
            spread_ref[pl.ds(1, half, stride=2), :] = lifted
            bridged = jnp.dot(
                first_ref[flat(row + 2, 2, width), :], bridge_w_ref[...], preferred_element_type=f32
            )
            spread = spread_ref[...]
            value = silu(bridged + jnp.concatenate([spread, spread], axis=0))
            value = value * inside(row - rim + 3, 2)
            third_ref[flat(row, 2, width), :] = value.astype(bf16)
            return carry

        lax.fori_loop(0, half_rows, make_third, 0)

        def finish(index, carry, hour=hour, rim=rim):
            row = index * 2
            skip = 1 if hour == 1 else 0
            fresh = conv(third_ref, row + skip, 2, width, last_w_ref)
            own = stack_ref[flat(row + RIM_USED + skip, 2, width), :].astype(f32)
            fresh = (own + fresh).astype(bf16)
            if hour == 0:
                noise = noise_ref[pl.ds(row, 2)].reshape(2 * width, channels).astype(f32)
                fresh = (fresh.astype(f32) + noise_level * noise) * inside(row - rim + RIM_USED, 2)
                stack_ref[flat(row, 2, width), :] = fresh.astype(bf16)
            else:
                for step in range(2):
                    at = step * width + pad
                    out_ref[row + step] = fresh[at : at + cols]
            return carry

        lax.fori_loop(0, (tall - 2 * RIM_USED) // 2 if hour == 0 else rows // 2, finish, 0)


def denoise(rows, cols, totals, variables, place, noisy, noise, blend, windows, weights):
    width, channels = noisy.shape[1:]
    tall = rows + 2 * RIM
    bf16, f32 = jnp.bfloat16, jnp.float32
    return pl.pallas_call(
        functools.partial(denoise_kernel, rows, cols, totals, variables),
        out_shape=jax.ShapeDtypeStruct((rows, cols, channels), bf16),
        in_specs=[pl.BlockSpec(memory_space=pltpu.SMEM)]
        + [pl.BlockSpec(memory_space=pltpu.VMEM)] * 9,
        scratch_shapes=[
            pltpu.VMEM((tall * width, channels), bf16),
            pltpu.VMEM((tall * width, channels), bf16),
            pltpu.VMEM((tall // 2 * width // 2, channels), bf16),
            pltpu.VMEM((tall // 2 * width // 2, channels), f32),
            pltpu.VMEM((tall * width, channels), bf16),
            pltpu.VMEM((width, channels), f32),
            pltpu.VMEM((width, channels), f32),
        ],
        compiler_params=pltpu.CompilerParams(vmem_limit_bytes=40 * 2**20),
        cost_estimate=pl.CostEstimate(
            flops=10**10, bytes_accessed=10**7, transcendentals=4 * 10**6
        ),
        name="denoise",
    )(place, noisy, noise, blend, windows, *weights)


def conv_weight(weight, depth, width):
    out, _, given = weight.shape
    weight = weight.reshape(out, 3, 3, given)
    weight = jnp.pad(weight, ((0, width - out), (0, 0), (0, 0), (0, depth - given)))
    return jnp.transpose(weight, (1, 3, 2, 0)).reshape(3 * depth, 3 * width)


def shards(
    global_state,
    spec_filter,
    w_skip,
    w_mix,
    w_decode,
    regional_state,
    noise_draws,
    w_first,
    w_down,
    w_up,
    w_bridge,
    w_last,
    box_lat0,
    box_lon0,
    stencil_lat,
    stencil_lon,
):
    hours = noise_draws.shape[0]
    rows_here, cols_here = regional_state.shape[1:]
    row_start = lax.axis_index(PLANE) * rows_here
    col_start = lax.axis_index("col") * cols_here
    total_rows = rows_here * lax.axis_size(PLANE)
    total_cols = cols_here * lax.axis_size("col")
    assert hours == 2

    by_latitude = global_state.shape[0] % lax.axis_size("col") == 0
    global_steps = global_by_latitude if by_latitude else global_by_channel
    global_final, windows = global_steps(
        hours, global_state, spec_filter, w_skip, w_mix, w_decode, box_lat0, box_lon0,
        rows_here, cols_here,
    )

    variables = regional_state.shape[0]
    conds = w_decode.shape[1]
    lanes = variables + conds
    noisy = (
        regional_state.astype(jnp.float32) + noise_level * noise_draws[0].astype(jnp.float32)
    ).astype(jnp.bfloat16)
    lat_shift = stencil_lat - (row_start + jnp.arange(rows_here, dtype=jnp.int32))[:, None] // RATIO
    lon_shift = stencil_lon - (col_start + jnp.arange(cols_here, dtype=jnp.int32))[None, :] // RATIO
    mid0 = jnp.concatenate(
        [
            jnp.transpose(noisy, (1, 2, 0)),
            jnp.zeros((rows_here, cols_here, conds), jnp.bfloat16),
            lat_shift.astype(jnp.bfloat16)[..., None],
            lon_shift.astype(jnp.bfloat16)[..., None],
            jnp.zeros((rows_here, cols_here, LANES - lanes - 2), jnp.bfloat16),
        ],
        axis=2,
    )
    mid1 = jnp.pad(
        jnp.transpose(noise_draws[1], (1, 2, 0)), ((0, 0), (0, 0), (0, LANES - variables))
    )
    inner = RIM - RIM_USED
    above, below = next_to(
        jnp.concatenate([mid0[rows_here - RIM :], mid1[rows_here - inner :]], axis=0),
        jnp.concatenate([mid0[:RIM], mid1[:inner]], axis=0),
        PLANE,
    )

    def rim_cols(part):
        return jnp.concatenate(
            [
                above[:RIM, part], mid0[:, part], below[:RIM, part],
                above[RIM:, part], mid1[:, part], below[RIM:, part],
            ],
            axis=0,
        )

    left, right = next_to(
        rim_cols(slice(cols_here - RIM_COLS, cols_here)), rim_cols(slice(0, RIM_COLS)), "col"
    )
    high, wide = window_extent(rows_here), window_stride(cols_here)
    place = jnp.stack([row_start, col_start]).astype(jnp.int32)
    totals = (total_rows, total_cols)
    noisy, noise, blend = assemble(
        rows_here, cols_here, totals, high, wide, lanes, place, mid0, mid1, above, below, left, right
    )
    weights = (
        conv_weight(w_first, LANES, w_first.shape[0]),
        conv_weight(w_down, w_down.shape[2], w_down.shape[0]),
        w_up.T,
        w_bridge.T,
        conv_weight(w_last, w_last.shape[2], LANES),
    )
    windows = jnp.pad(windows, ((0, 0), (0, 0), (0, 0), (variables, LANES - lanes))).reshape(
        hours, high * wide, LANES
    )
    regional_final = denoise(
        rows_here, cols_here, totals, variables, place, noisy, noise, blend, windows, weights
    )
    return global_final, jnp.transpose(regional_final[:, :, :variables], (2, 0, 1))


def solution(mesh):
    return jax.shard_map(
        shards,
        mesh=mesh,
        in_specs=(
            P(PLANE, "col", None),
            P(None, None, "col"),
            P(),
            P(),
            P(),
            P(None, PLANE, "col"),
            P(None, None, PLANE, "col"),
            P(),
            P(),
            P(),
            P(),
            P(),
            P(),
            P(),
            P(PLANE, "col"),
            P(PLANE, "col"),
        ),
        out_specs=(P(PLANE, "col", None), P(None, PLANE, "col")),
        check_vma=False,
    )
```

```python
import functools
import math

import jax
import jax.numpy as jnp
import ml_dtypes
import numpy as np
from jax import lax
from jax.experimental import pallas as pl
from jax.experimental.pallas import tpu as pltpu
from jax.sharding import PartitionSpec as P

RATIO = 8
noise_level = 0.5
PLANE = ("grp", "row")
RIM = 9
RIM_USED = 4
LANES = 128
RIM_COLS = 16


def fourier_tables(length, num_modes):
    position = np.arange(length, dtype=np.int64)[:, None]
    frequency = np.arange(num_modes, dtype=np.int64)[None, :]
    angle = (position * frequency % length).astype(np.float64) * (2.0 * math.pi / length)
    cosine = np.cos(angle)
    sine = np.sin(angle)
    factor = np.where(frequency == 0, 1.0, 2.0) / length
    forward = np.concatenate([cosine, -sine], axis=1).T.astype(ml_dtypes.bfloat16)
    inverse = np.concatenate([cosine * factor, -sine * factor], axis=1).astype(ml_dtypes.bfloat16)
    return jnp.asarray(forward), jnp.asarray(inverse)


def exchange(blocks, axis):
    return lax.all_to_all(blocks, axis, split_axis=0, concat_axis=0, tiled=True)


def spread(block, axis):
    return exchange(jnp.broadcast_to(block[None], (lax.axis_size(axis),) + block.shape), axis)


def collect_filter(spec_filter):
    rows = 2 * spec_filter.shape[1]
    flat = spec_filter.reshape(rows, spec_filter.shape[2])
    share = rows // lax.axis_size(PLANE)
    mine = lax.dynamic_slice_in_dim(flat, lax.axis_index(PLANE) * share, share, 0)
    wide = spread(mine.astype(jnp.bfloat16), "col")
    wide = jnp.swapaxes(wide, 0, 1).reshape(share, -1)
    return spread(wide, PLANE).reshape(rows, -1)


def latitude_kernel(
    hours, block, state_ref, forward_ref, inverse_ref, filter_ref, skip_ref, mix_ref, decode_ref,
    out_ref, coarse_ref, filtered_ref,
):
    length = state_ref.shape[0]
    modes = filter_ref.shape[0] // 2
    for hour in range(hours):
        source_ref = state_ref if hour == 0 else out_ref

        def analyse(index, carry):
            low = pl.ds(pl.multiple_of(index * block, 16), block)
            high = pl.ds(pl.multiple_of(modes + index * block, 16), block)
            state = source_ref[...]
            real = jnp.dot(forward_ref[low, :], state, preferred_element_type=jnp.float32)
            imag = jnp.dot(forward_ref[high, :], state, preferred_element_type=jnp.float32)
            gain_real = filter_ref[low, :].astype(jnp.float32)
            gain_imag = filter_ref[high, :].astype(jnp.float32)
            filtered_ref[low, :] = (real * gain_real - imag * gain_imag).astype(jnp.bfloat16)
            filtered_ref[high, :] = (real * gain_imag + imag * gain_real).astype(jnp.bfloat16)
            return carry

        lax.fori_loop(0, modes // block, analyse, 0)

        def synthesise(index, carry):
            here = pl.ds(pl.multiple_of(index * block, 16), block)
            spectral = jnp.dot(
                inverse_ref[here, :], filtered_ref[...], preferred_element_type=jnp.float32
            ).astype(jnp.bfloat16)
            state = source_ref[here, :]
            skipped = jnp.dot(state, skip_ref[...], preferred_element_type=jnp.float32)
            activated = jax.nn.gelu(spectral.astype(jnp.float32) + skipped).astype(jnp.bfloat16)
            update = jnp.dot(activated, mix_ref[...], preferred_element_type=jnp.float32)
            fresh = (state.astype(jnp.float32) + update).astype(jnp.bfloat16)
            out_ref[here, :] = fresh
            coarse_ref[hour, here, :] = jnp.dot(
                fresh, decode_ref[...], preferred_element_type=jnp.float32
            ).astype(jnp.bfloat16)
            return carry

        lax.fori_loop(0, length // block, synthesise, 0)


def advance_latitude(hours, state, forward, inverse, gains, w_skip, w_mix, decode):
    length, channels = state.shape
    modes = gains.shape[0] // 2
    block = next(b for b in (720, 240, 144, 48, 16) if modes % b == 0)
    flops = hours * 2 * length * channels * (4 * modes + 2 * channels + LANES)
    return pl.pallas_call(
        functools.partial(latitude_kernel, hours, block),
        out_shape=(
            jax.ShapeDtypeStruct((length, channels), jnp.bfloat16),
            jax.ShapeDtypeStruct((hours, length, LANES), jnp.bfloat16),
        ),
        scratch_shapes=[pltpu.VMEM((2 * modes, channels), jnp.bfloat16)],
        compiler_params=pltpu.CompilerParams(vmem_limit_bytes=40 * 2**20),
        cost_estimate=pl.CostEstimate(
            flops=flops, bytes_accessed=12 * 2**20, transcendentals=hours * length * channels
        ),
        name="advance_latitude",
    )(state, forward, inverse, gains, w_skip, w_mix, decode)


def global_hour(current, spec_filter, w_skip, w_mix, forward, inverse):
    longitude = lax.all_to_all(current, "col", split_axis=2, concat_axis=1, tiled=True)
    spectrum = jnp.einsum("alc,ml->amc", longitude, forward, preferred_element_type=jnp.float32)
    num_modes = spec_filter.shape[1]
    real_part = spectrum[:, :num_modes, :]
    imag_part = spectrum[:, num_modes:, :]
    filt_real = spec_filter[0][None]
    filt_imag = spec_filter[1][None]
    mixed = jnp.concatenate(
        [
            real_part * filt_real - imag_part * filt_imag,
            real_part * filt_imag + imag_part * filt_real,
        ],
        axis=1,
    ).astype(jnp.bfloat16)
    filtered = jnp.einsum("amc,lm->alc", mixed, inverse, preferred_element_type=jnp.float32).astype(
        jnp.bfloat16
    )
    spectral = lax.all_to_all(filtered, "col", split_axis=1, concat_axis=2, tiled=True)
    skipped = jnp.einsum("alc,cd->ald", current, w_skip, preferred_element_type=jnp.float32)
    activated = jax.nn.gelu(spectral.astype(jnp.float32) + skipped).astype(jnp.bfloat16)
    update = jnp.einsum("ald,de->ale", activated, w_mix, preferred_element_type=jnp.float32)
    return (current.astype(jnp.float32) + update).astype(jnp.bfloat16)


def window_extent(cells):
    return (cells + RIM - 1) // RATIO + 3 - (-RIM // RATIO)


def window_stride(cells):
    return -(-window_extent(cells) // 32) * 32


def window_base():
    return -(-RIM // RATIO)


def pad_windows(windows, cols_here):
    spare = window_stride(cols_here) - windows.shape[2]
    return jnp.pad(windows, ((0, 0), (0, 0), (0, spare), (0, 0)))


def global_by_latitude(
    hours, global_state, spec_filter, w_skip, w_mix, w_decode, box_lat0, box_lon0, rows_here, cols_here
):
    count = lax.axis_size("col")
    lats_here, _, channels = global_state.shape
    lon_total = global_state.shape[1] * count
    turns = lats_here // count
    forward, inverse = fourier_tables(lon_total, spec_filter.shape[1])
    conds = w_decode.shape[1]
    decode = jnp.pad(w_decode, ((0, 0), (0, LANES - conds)))
    gathered = [
        exchange(global_state[turn * count : (turn + 1) * count], "col") for turn in range(turns)
    ]
    gains = collect_filter(spec_filter)
    finals, coarses = [], []
    for turn in range(turns):
        state = gathered[turn].reshape(lon_total, channels)
        state, coarse = advance_latitude(
            hours, state, forward, inverse, gains, w_skip, w_mix, decode
        )
        finals.append(exchange(state.reshape((count, -1, channels)), "col"))
        coarses.append(coarse)
    global_final = jnp.concatenate(finals, axis=0)
    base = window_base()
    high, wide = window_extent(rows_here), window_extent(cols_here)
    coarse = jnp.stack(coarses, axis=1)[..., :conds]
    step = cols_here // RATIO
    span = (count - 1) * step + wide
    coarse = jnp.pad(coarse, ((0, 0), (0, 0), (base, span), (0, 0)))
    zero = jnp.zeros((), jnp.int32)
    strip = lax.dynamic_slice(
        coarse, (zero, zero, box_lon0[0], zero), (hours, turns, span, conds)
    )
    packed = jnp.stack(
        [strip[:, :, col * step : col * step + wide].reshape(-1) for col in range(count)]
    )
    size = packed.shape[1]
    packed = jnp.pad(packed, ((0, 0), (0, -size % 1024))).reshape(count, -1, LANES)
    plane = lax.axis_size(PLANE)
    sent = jnp.broadcast_to(packed[None], (plane,) + packed.shape).reshape(
        (plane * count,) + packed.shape[1:]
    )
    got = lax.all_to_all(sent, PLANE + ("col",), split_axis=0, concat_axis=0, tiled=True)
    got = got.reshape(plane, count, -1)[..., :size].reshape(plane, count, hours, turns, wide, conds)
    got = jnp.transpose(got, (2, 0, 3, 1, 4, 5)).reshape(hours, plane * lats_here, wide, conds)
    got = jnp.pad(got, ((0, 0), (base, high), (0, 0), (0, 0)))
    start = box_lat0[0] + lax.axis_index(PLANE) * (rows_here // RATIO)
    windows = lax.dynamic_slice_in_dim(got, start, high, 1)
    return global_final, pad_windows(windows, cols_here)


def global_by_channel(
    hours, global_state, spec_filter, w_skip, w_mix, w_decode, box_lat0, box_lon0, rows_here, cols_here
):
    count = lax.axis_size("col")
    forward, inverse = fourier_tables(global_state.shape[1] * count, spec_filter.shape[1])
    base = window_base()
    high, wide = window_extent(rows_here), window_extent(cols_here)
    span = (count - 1) * (cols_here // RATIO) + wide
    lat_start = box_lat0[0] + lax.axis_index(PLANE) * (rows_here // RATIO)
    lon_start = box_lon0[0] + lax.axis_index("col") * (cols_here // RATIO)
    windows = []
    for _ in range(hours):
        global_state = global_hour(global_state, spec_filter, w_skip, w_mix, forward, inverse)
        coarse = jnp.einsum(
            "alc,ck->alk", global_state, w_decode, preferred_element_type=jnp.float32
        ).astype(jnp.bfloat16)
        coarse = lax.all_gather(coarse, "col", axis=1, tiled=True)
        coarse = jnp.pad(coarse, ((0, 0), (base, span), (0, 0)))
        coarse = lax.dynamic_slice_in_dim(coarse, box_lon0[0], base + span, 1)
        coarse = lax.all_gather(coarse, PLANE, axis=0, tiled=True)
        coarse = lax.dynamic_slice_in_dim(coarse, lon_start - box_lon0[0], wide, 1)
        coarse = jnp.pad(coarse, ((base, high), (0, 0), (0, 0)))
        coarse = lax.dynamic_slice_in_dim(coarse, lat_start, high, 0)
        windows.append(coarse)
    return global_state, pad_windows(jnp.stack(windows), cols_here)


def next_to(low, high, axis):
    count = lax.axis_size(axis)
    forward = [(i, i + 1) for i in range(count - 1)]
    backward = [(target, source) for source, target in forward]
    return lax.ppermute(low, axis, forward), lax.ppermute(high, axis, backward)


def grid_place(start_ref, total, base, extent):
    place = start_ref + base + lax.broadcasted_iota(jnp.int32, (extent, 1), 0)
    return (place >= 0) & (place < total)


def assemble_kernel(
    rows, cols, totals, high, wide, lanes, place_ref, mid0_ref, mid1_ref, above_ref, below_ref,
    left_ref, right_ref, noisy_ref, noise_ref, blend_ref,
):
    inner = RIM - RIM_USED
    pad = (noisy_ref.shape[1] - cols) // 2
    width = noisy_ref.shape[1]
    for ref, mid_ref, rim, part in ((noisy_ref, mid0_ref, RIM, 0), (noise_ref, mid1_ref, inner, RIM)):
        ref[0:rim, pad : pad + cols, :] = above_ref[part : part + rim]
        ref[rim : rim + rows, pad : pad + cols, :] = mid_ref[...]
        ref[rim + rows :, pad : pad + cols, :] = below_ref[part : part + rim]
        first = 0 if rim == RIM else rows + 2 * RIM
        ref[:, 0:pad, :] = left_ref[first : first + rows + 2 * rim]
        ref[:, pad + cols :, :] = right_ref[first : first + rows + 2 * rim]

    base = window_base()
    col = lax.broadcasted_iota(jnp.int32, (width, 1), 0) - pad
    col_in = grid_place(place_ref[1], totals[1], -pad, width)
    frac_col = ((col % RATIO).astype(jnp.float32) + 0.5) / RATIO
    col_base = jnp.where(col_in, (col + pad) // RATIO - pad // RATIO + base, -4 * high * wide)
    point = lax.broadcasted_iota(jnp.int32, (width, high * wide), 1)
    point_lat = (point // wide).astype(jnp.float32)
    point_lon = (point % wide).astype(jnp.float32)

    def weigh(index, carry):
        row = index - RIM
        whole = (row + 2 * RATIO) // RATIO - 2
        frac_row = ((row - whole * RATIO).astype(jnp.float32) + 0.5) / RATIO
        there = place_ref[0] + row
        row_base = jnp.where((there >= 0) & (there < totals[0]), whole + base, -4 * high * wide)
        shifts = noisy_ref[index, :, :].astype(jnp.float32)
        lat = row_base.astype(jnp.float32) + shifts[:, lanes : lanes + 1]
        lon = col_base.astype(jnp.float32) + shifts[:, lanes + 1 : lanes + 2]
        from_lat = point_lat - lat
        from_lon = point_lon - lon
        weight_lat = jnp.where(
            from_lat == 0.0, 1.0 - frac_row, jnp.where(from_lat == 1.0, frac_row, 0.0)
        )
        weight_lon = jnp.where(
            from_lon == 0.0, 1.0 - frac_col, jnp.where(from_lon == 1.0, frac_col, 0.0)
        )
        blend_ref[index, :, :] = (weight_lat * weight_lon).astype(jnp.bfloat16)
        return carry

    lax.fori_loop(0, rows + 2 * RIM, weigh, 0)


def assemble(rows, cols, totals, high, wide, lanes, place, mid0, mid1, above, below, left, right):
    inner = RIM - RIM_USED
    width = cols + 2 * left.shape[1]
    channels = mid0.shape[2]
    return pl.pallas_call(
        functools.partial(assemble_kernel, rows, cols, totals, high, wide, lanes),
        out_shape=(
            jax.ShapeDtypeStruct((rows + 2 * RIM, width, channels), jnp.bfloat16),
            jax.ShapeDtypeStruct((rows + 2 * inner, width, channels), jnp.bfloat16),
            jax.ShapeDtypeStruct((rows + 2 * RIM, width, high * wide), jnp.bfloat16),
        ),
        in_specs=[pl.BlockSpec(memory_space=pltpu.SMEM)]
        + [pl.BlockSpec(memory_space=pltpu.VMEM)] * 6,
        compiler_params=pltpu.CompilerParams(vmem_limit_bytes=40 * 2**20),
        cost_estimate=pl.CostEstimate(flops=2 * 10**8, bytes_accessed=10**7, transcendentals=0),
        name="assemble",
    )(place, mid0, mid1, above, below, left, right)


def silu(x):
    return x / (1.0 + jnp.exp(-x))


def denoise_kernel(
    rows, cols, totals, variables, place_ref, noisy_ref, noise_ref, blend_ref, window_ref, first_w_ref,
    down_w_ref, up_w_ref, bridge_w_ref, last_w_ref, out_ref, stack_ref, first_ref, pooled_ref,
    lifted_ref, third_ref, pair_ref, spread_ref,
):
    width = noisy_ref.shape[1]
    half = width // 2
    pad = (width - cols) // 2
    channels = noisy_ref.shape[2]
    f32, bf16 = jnp.float32, jnp.bfloat16
    col_in = grid_place(place_ref[1], totals[1], -pad, width).astype(f32)
    lane = lax.broadcasted_iota(jnp.int32, (1, channels), 1)
    is_state = lane < variables

    def flat(start, count, unit):
        return pl.ds(pl.multiple_of(start * unit, 16), count * unit)

    def inside(row, count):
        marks = []
        for step in range(count):
            there = place_ref[0] + row + step
            marks.append(col_in * jnp.where((there >= 0) & (there < totals[0]), 1.0, 0.0))
        return jnp.concatenate(marks, axis=0)

    def conv(source_ref, row, count, unit, weight_ref):
        lhs = jnp.concatenate(
            [source_ref[flat(row + step, count, unit), :] for step in range(3)], axis=1
        )
        wide = jnp.dot(lhs, weight_ref[...], preferred_element_type=f32)
        size = weight_ref.shape[1] // 3
        span = count * unit
        return (
            pltpu.roll(wide[:, :size], 1, 0)
            + wide[:, size : 2 * size]
            + pltpu.roll(wide[:, 2 * size :], span - 1, 0)
        )

    for hour in range(2):
        rim = RIM - RIM_USED * hour
        tall = rows + 2 * rim

        def stack(index, carry, hour=hour, rim=rim):
            here = flat(index * 2, 2, width)
            weights = blend_ref[pl.ds(index * 2 + RIM - rim, 2)].reshape(2 * width, -1)
            cond = jnp.dot(weights, window_ref[hour], preferred_element_type=f32).astype(bf16)
            if hour == 0:
                own = noisy_ref[pl.ds(index * 2, 2)].reshape(2 * width, channels)
            else:
                own = stack_ref[here, :]
            stack_ref[here, :] = jnp.where(is_state, own, cond)
            return carry

        lax.fori_loop(0, tall // 2, stack, 0)

        def make_first(index, carry, rim=rim):
            row = index * 4
            value = silu(conv(stack_ref, row, 4, width, first_w_ref)) * inside(row - rim + 1, 4)
            value = value.astype(bf16)
            first_ref[flat(row, 4, width), :] = value
            value = value.astype(f32)
            for step in range(2):
                at = 2 * step * width
                pair_ref[...] = value[at : at + width] + value[at + width : at + 2 * width]
                even = pair_ref[pl.ds(0, half, stride=2), :]
                odd = pair_ref[pl.ds(1, half, stride=2), :]
                pooled_ref[flat(index * 2 + step, 1, half), :] = ((even + odd) * 0.25).astype(bf16)
            return carry

        lax.fori_loop(0, (tall - 2) // 4, make_first, 0)

        half_rows = (tall - 2) // 2 - 2

        def make_lifted(index, carry):
            value = silu(conv(pooled_ref, index * 2, 2, half, down_w_ref)).astype(bf16)
            lifted_ref[flat(index * 2, 2, half), :] = jnp.dot(
                value, up_w_ref[...], preferred_element_type=f32
            )
            return carry

        lax.fori_loop(0, half_rows // 2, make_lifted, 0)

        def make_third(index, carry, rim=rim):
            row = index * 2
            lifted = lifted_ref[flat(index, 1, half), :]
            spread_ref[pl.ds(0, half, stride=2), :] = lifted
            spread_ref[pl.ds(1, half, stride=2), :] = lifted
            bridged = jnp.dot(
                first_ref[flat(row + 2, 2, width), :], bridge_w_ref[...], preferred_element_type=f32
            )
            spread = spread_ref[...]
            value = silu(bridged + jnp.concatenate([spread, spread], axis=0))
            value = value * inside(row - rim + 3, 2)
            third_ref[flat(row, 2, width), :] = value.astype(bf16)
            return carry

        lax.fori_loop(0, half_rows, make_third, 0)

        def finish(index, carry, hour=hour, rim=rim):
            row = index * 2
            skip = 1 if hour == 1 else 0
            fresh = conv(third_ref, row + skip, 2, width, last_w_ref)
            own = stack_ref[flat(row + RIM_USED + skip, 2, width), :].astype(f32)
            fresh = (own + fresh).astype(bf16)
            if hour == 0:
                noise = noise_ref[pl.ds(row, 2)].reshape(2 * width, channels).astype(f32)
                fresh = (fresh.astype(f32) + noise_level * noise) * inside(row - rim + RIM_USED, 2)
                stack_ref[flat(row, 2, width), :] = fresh.astype(bf16)
            else:
                for step in range(2):
                    at = step * width + pad
                    out_ref[row + step] = fresh[at : at + cols]
            return carry

        lax.fori_loop(0, (tall - 2 * RIM_USED) // 2 if hour == 0 else rows // 2, finish, 0)


def denoise(rows, cols, totals, variables, place, noisy, noise, blend, windows, weights):
    width, channels = noisy.shape[1:]
    tall = rows + 2 * RIM
    bf16, f32 = jnp.bfloat16, jnp.float32
    return pl.pallas_call(
        functools.partial(denoise_kernel, rows, cols, totals, variables),
        out_shape=jax.ShapeDtypeStruct((rows, cols, channels), bf16),
        in_specs=[pl.BlockSpec(memory_space=pltpu.SMEM)]
        + [pl.BlockSpec(memory_space=pltpu.VMEM)] * 9,
        scratch_shapes=[
            pltpu.VMEM((tall * width, channels), bf16),
            pltpu.VMEM((tall * width, channels), bf16),
            pltpu.VMEM((tall // 2 * width // 2, channels), bf16),
            pltpu.VMEM((tall // 2 * width // 2, channels), f32),
            pltpu.VMEM((tall * width, channels), bf16),
            pltpu.VMEM((width, channels), f32),
            pltpu.VMEM((width, channels), f32),
        ],
        compiler_params=pltpu.CompilerParams(vmem_limit_bytes=40 * 2**20),
        cost_estimate=pl.CostEstimate(
            flops=10**10, bytes_accessed=10**7, transcendentals=4 * 10**6
        ),
        name="denoise",
    )(place, noisy, noise, blend, windows, *weights)


def conv_weight(weight, depth, width):
    out, _, given = weight.shape
    weight = weight.reshape(out, 3, 3, given)
    weight = jnp.pad(weight, ((0, width - out), (0, 0), (0, 0), (0, depth - given)))
    return jnp.transpose(weight, (1, 3, 2, 0)).reshape(3 * depth, 3 * width)


def shards(
    global_state,
    spec_filter,
    w_skip,
    w_mix,
    w_decode,
    regional_state,
    noise_draws,
    w_first,
    w_down,
    w_up,
    w_bridge,
    w_last,
    box_lat0,
    box_lon0,
    stencil_lat,
    stencil_lon,
):
    hours = noise_draws.shape[0]
    rows_here, cols_here = regional_state.shape[1:]
    row_start = lax.axis_index(PLANE) * rows_here
    col_start = lax.axis_index("col") * cols_here
    total_rows = rows_here * lax.axis_size(PLANE)
    total_cols = cols_here * lax.axis_size("col")
    assert hours == 2

    by_latitude = global_state.shape[0] % lax.axis_size("col") == 0
    global_steps = global_by_latitude if by_latitude else global_by_channel
    global_final, windows = global_steps(
        hours, global_state, spec_filter, w_skip, w_mix, w_decode, box_lat0, box_lon0,
        rows_here, cols_here,
    )

    variables = regional_state.shape[0]
    conds = w_decode.shape[1]
    lanes = variables + conds
    noisy = (
        regional_state.astype(jnp.float32) + noise_level * noise_draws[0].astype(jnp.float32)
    ).astype(jnp.bfloat16)
    lat_shift = stencil_lat - (row_start + jnp.arange(rows_here, dtype=jnp.int32))[:, None] // RATIO
    lon_shift = stencil_lon - (col_start + jnp.arange(cols_here, dtype=jnp.int32))[None, :] // RATIO
    cells = (rows_here, cols_here)
    mids = jnp.concatenate(
        [
            noisy,
            jnp.zeros((conds,) + cells, jnp.bfloat16),
            lat_shift.astype(jnp.bfloat16)[None],
            lon_shift.astype(jnp.bfloat16)[None],
            jnp.zeros((LANES - lanes - 2,) + cells, jnp.bfloat16),
            noise_draws[1],
            jnp.zeros((LANES - variables,) + cells, jnp.bfloat16),
        ],
        axis=0,
    )
    mids = jnp.transpose(mids.reshape((2, LANES) + cells), (0, 2, 3, 1))
    mid0, mid1 = mids[0], mids[1]
    inner = RIM - RIM_USED
    above, below = next_to(
        jnp.concatenate([mid0[rows_here - RIM :], mid1[rows_here - inner :]], axis=0),
        jnp.concatenate([mid0[:RIM], mid1[:inner]], axis=0),
        PLANE,
    )

    def rim_cols(part):
        return jnp.concatenate(
            [
                above[:RIM, part], mid0[:, part], below[:RIM, part],
                above[RIM:, part], mid1[:, part], below[RIM:, part],
            ],
            axis=0,
        )

    left, right = next_to(
        rim_cols(slice(cols_here - RIM_COLS, cols_here)), rim_cols(slice(0, RIM_COLS)), "col"
    )
    high, wide = window_extent(rows_here), window_stride(cols_here)
    place = jnp.stack([row_start, col_start]).astype(jnp.int32)
    totals = (total_rows, total_cols)
    noisy, noise, blend = assemble(
        rows_here, cols_here, totals, high, wide, lanes, place, mid0, mid1, above, below, left, right
    )
    weights = (
        conv_weight(w_first, LANES, w_first.shape[0]),
        conv_weight(w_down, w_down.shape[2], w_down.shape[0]),
        w_up.T,
        w_bridge.T,
        conv_weight(w_last, w_last.shape[2], LANES),
    )
    windows = jnp.pad(windows, ((0, 0), (0, 0), (0, 0), (variables, LANES - lanes))).reshape(
        hours, high * wide, LANES
    )
    regional_final = denoise(
        rows_here, cols_here, totals, variables, place, noisy, noise, blend, windows, weights
    )
    return global_final, jnp.transpose(regional_final[:, :, :variables], (2, 0, 1))


def solution(mesh):
    return jax.shard_map(
        shards,
        mesh=mesh,
        in_specs=(
            P(PLANE, "col", None),
            P(None, None, "col"),
            P(),
            P(),
            P(),
            P(None, PLANE, "col"),
            P(None, None, PLANE, "col"),
            P(),
            P(),
            P(),
            P(),
            P(),
            P(),
            P(),
            P(PLANE, "col"),
            P(PLANE, "col"),
        ),
        out_specs=(P(PLANE, "col", None), P(None, PLANE, "col")),
        check_vma=False,
    )
```

```python
import functools
import math

import jax
import jax.numpy as jnp
import ml_dtypes
import numpy as np
from jax import lax
from jax.experimental import pallas as pl
from jax.experimental.pallas import tpu as pltpu
from jax.sharding import PartitionSpec as P

RATIO = 8
noise_level = 0.5
PLANE = ("grp", "row")
RIM = 9
RIM_USED = 4
LANES = 128
PACKED = 32
STRIP = 8
FAR = -4096
RIM_COLS = 16


def fourier_tables(length, num_modes):
    position = np.arange(length, dtype=np.int64)[:, None]
    frequency = np.arange(num_modes, dtype=np.int64)[None, :]
    angle = (position * frequency % length).astype(np.float64) * (2.0 * math.pi / length)
    cosine = np.cos(angle)
    sine = np.sin(angle)
    factor = np.where(frequency == 0, 1.0, 2.0) / length
    forward = np.concatenate([cosine, -sine], axis=1).T.astype(ml_dtypes.bfloat16)
    inverse = np.concatenate([cosine * factor, -sine * factor], axis=1).astype(ml_dtypes.bfloat16)
    return forward, inverse


def round_up(size, unit):
    return -(-size // unit) * unit


def pieced_tables(length, num_modes, count):
    forward, inverse = fourier_tables(length, num_modes)
    piece = length // count
    spare = round_up(piece, LANES) - piece
    forward = np.pad(forward.reshape(2 * num_modes, count, piece), ((0, 0), (0, 0), (0, spare)))
    inverse = np.pad(inverse.reshape(count, piece, 2 * num_modes), ((0, 0), (0, spare), (0, 0)))
    return (
        jnp.asarray(forward.reshape(2 * num_modes, -1)),
        jnp.asarray(inverse.reshape(-1, 2 * num_modes)),
    )


def exchange(blocks, axis):
    return lax.all_to_all(blocks, axis, split_axis=0, concat_axis=0, tiled=True)


def spread(block, axis):
    return exchange(jnp.broadcast_to(block[None], (lax.axis_size(axis),) + block.shape), axis)


def collect_filter(spec_filter):
    rows = 2 * spec_filter.shape[1]
    flat = spec_filter.reshape(rows, spec_filter.shape[2])
    share = rows // lax.axis_size(PLANE)
    mine = lax.dynamic_slice_in_dim(flat, lax.axis_index(PLANE) * share, share, 0)
    wide = spread(mine.astype(jnp.bfloat16), "col")
    wide = jnp.swapaxes(wide, 0, 1).reshape(share, -1)
    return spread(wide, PLANE).reshape(rows, -1)


def latitude_kernel(hours, count, block, targets, step, place_ref, *refs):
    piece_refs, refs = refs[:count], refs[count:]
    forward_ref, inverse_ref, filter_ref, skip_ref, mix_ref, decode_ref = refs[:6]
    out_refs, strip_ref = refs[6 : 6 + count], refs[6 + count]
    state_ref, filtered_ref, coarse_ref, near_ref, packed_ref = refs[7 + count :]
    piece = piece_refs[0].shape[1]
    padded = state_ref.shape[0] // count
    length = piece * count
    modes = filter_ref.shape[0] // 2
    group = LANES // PACKED
    for index in range(count):
        own = piece_refs[index][0]
        spare = jnp.zeros((padded - piece, own.shape[1]), own.dtype)
        state_ref[index * padded : (index + 1) * padded, :] = jnp.concatenate([own, spare], axis=0)

    for hour in range(hours):
        state = state_ref[...]
        real = jnp.dot(forward_ref[:modes, :], state, preferred_element_type=jnp.float32)
        imag = jnp.dot(forward_ref[modes:, :], state, preferred_element_type=jnp.float32)
        gain_real = filter_ref[:modes, :].astype(jnp.float32)
        gain_imag = filter_ref[modes:, :].astype(jnp.float32)
        filtered_ref[:modes, :] = (real * gain_real - imag * gain_imag).astype(jnp.bfloat16)
        filtered_ref[modes:, :] = (real * gain_imag + imag * gain_real).astype(jnp.bfloat16)

        def synthesise(index, carry):
            here = pl.ds(pl.multiple_of(index * block, LANES), block)
            spectral = jnp.dot(
                inverse_ref[here, :], filtered_ref[...], preferred_element_type=jnp.float32
            ).astype(jnp.bfloat16)
            state = state_ref[here, :]
            skipped = jnp.dot(state, skip_ref[...], preferred_element_type=jnp.float32)
            activated = jax.nn.gelu(spectral.astype(jnp.float32) + skipped).astype(jnp.bfloat16)
            update = jnp.dot(activated, mix_ref[...], preferred_element_type=jnp.float32)
            state_ref[here, :] = (state.astype(jnp.float32) + update).astype(jnp.bfloat16)
            return carry

        lax.fori_loop(0, count * padded // block, synthesise, 0)

        for index in range(count):
            coarse_ref[index * piece : (index + 1) * piece, :] = jnp.dot(
                state_ref[index * padded : (index + 1) * padded, :],
                decode_ref[...],
                preferred_element_type=jnp.float32,
            )[:piece]
        span = near_ref.shape[0]
        coarse_ref[length : length + span, :] = coarse_ref[:span, :]
        near_ref[...] = coarse_ref[pl.ds(place_ref[0], span), :]
        rows = span // group
        packed = near_ref[pl.ds(0, rows, stride=group), :]
        for turn in range(1, group):
            packed += pltpu.roll(near_ref[pl.ds(turn, rows, stride=group), :], turn * PACKED, 1)
        packed_ref[hour * rows : (hour + 1) * rows, :] = packed

    for index in range(count):
        out_refs[index][0] = state_ref[index * padded : index * padded + piece, :]
    rows = near_ref.shape[0] // group
    for target in range(targets):
        low = target * step // group
        strip = [
            packed_ref[hour * rows + low : hour * rows + low + STRIP, :] for hour in range(hours)
        ]
        strip_ref[target] = jnp.concatenate(strip, axis=0).astype(jnp.bfloat16)


def advance_latitude(hours, step, place, pieces, forward, inverse, gains, w_skip, w_mix, decode):
    count = len(pieces)
    _, piece, channels = pieces[0].shape
    padded = round_up(piece, LANES)
    modes = gains.shape[0] // 2
    group = LANES // PACKED
    span = round_up((count - 1) * step + STRIP * group, 8 * group)
    flops = hours * 2 * count * padded * channels * (4 * modes + 2 * channels + LANES)
    block = 2 * padded if count % 2 == 0 else padded
    results = pl.pallas_call(
        functools.partial(latitude_kernel, hours, count, block, count, step),
        out_shape=tuple(jax.ShapeDtypeStruct((1, piece, channels), jnp.bfloat16) for _ in pieces)
        + (jax.ShapeDtypeStruct((count, hours * STRIP, LANES), jnp.bfloat16),),
        in_specs=[pl.BlockSpec(memory_space=pltpu.SMEM)]
        + [pl.BlockSpec(memory_space=pltpu.VMEM)] * (count + 6),
        scratch_shapes=[
            pltpu.VMEM((count * padded, channels), jnp.bfloat16),
            pltpu.VMEM((2 * modes, channels), jnp.bfloat16),
            pltpu.VMEM((count * piece + span, LANES), jnp.float32),
            pltpu.VMEM((span, LANES), jnp.float32),
            pltpu.VMEM((hours * span // group, LANES), jnp.float32),
        ],
        compiler_params=pltpu.CompilerParams(vmem_limit_bytes=48 * 2**20),
        cost_estimate=pl.CostEstimate(
            flops=flops, bytes_accessed=14 * 2**20, transcendentals=hours * count * piece * channels
        ),
        name="advance_latitude",
    )(place, *pieces, forward, inverse, gains, w_skip, w_mix, decode)
    return results[:count], results[count]


def collate_kernel(count, place_ref, *refs):
    pieces, out_ref, sems = refs[:-2], refs[-2], refs[-1]
    copies = [
        pltpu.make_async_copy(piece, out_ref.at[pl.ds(place_ref[index], 1)], sems.at[index])
        for index, piece in enumerate(pieces)
    ]
    for copy in copies:
        copy.start()
    for copy in copies:
        copy.wait()


def collate(place, pieces):
    count = len(pieces)
    return pl.pallas_call(
        functools.partial(collate_kernel, count),
        out_shape=jax.ShapeDtypeStruct((count,) + pieces[0].shape[1:], pieces[0].dtype),
        in_specs=[pl.BlockSpec(memory_space=pltpu.SMEM)]
        + [pl.BlockSpec(memory_space=pl.ANY)] * count,
        out_specs=pl.BlockSpec(memory_space=pl.ANY),
        scratch_shapes=[pltpu.SemaphoreType.DMA((count,))],
        name="collate",
    )(place, *pieces)


def shift(block, axis, step):
    count = lax.axis_size(axis)
    return lax.ppermute(block, axis, [(source, (source + step) % count) for source in range(count)])


def global_hour(current, spec_filter, w_skip, w_mix, forward, inverse):
    longitude = lax.all_to_all(current, "col", split_axis=2, concat_axis=1, tiled=True)
    spectrum = jnp.einsum("alc,ml->amc", longitude, forward, preferred_element_type=jnp.float32)
    num_modes = spec_filter.shape[1]
    real_part = spectrum[:, :num_modes, :]
    imag_part = spectrum[:, num_modes:, :]
    filt_real = spec_filter[0][None]
    filt_imag = spec_filter[1][None]
    mixed = jnp.concatenate(
        [
            real_part * filt_real - imag_part * filt_imag,
            real_part * filt_imag + imag_part * filt_real,
        ],
        axis=1,
    ).astype(jnp.bfloat16)
    filtered = jnp.einsum("amc,lm->alc", mixed, inverse, preferred_element_type=jnp.float32).astype(
        jnp.bfloat16
    )
    spectral = lax.all_to_all(filtered, "col", split_axis=1, concat_axis=2, tiled=True)
    skipped = jnp.einsum("alc,cd->ald", current, w_skip, preferred_element_type=jnp.float32)
    activated = jax.nn.gelu(spectral.astype(jnp.float32) + skipped).astype(jnp.bfloat16)
    update = jnp.einsum("ald,de->ale", activated, w_mix, preferred_element_type=jnp.float32)
    return (current.astype(jnp.float32) + update).astype(jnp.bfloat16)


def window_extent(cells):
    return (cells + RIM - 1) // RATIO + 3 - (-RIM // RATIO)


def window_base():
    return -(-RIM // RATIO)


def global_by_latitude(
    hours, global_state, spec_filter, w_skip, w_mix, w_decode, box_lat0, box_lon0, rows_here,
    cols_here, prepare,
):
    count = lax.axis_size("col")
    me = lax.axis_index("col")
    lats_here, piece, _ = global_state.shape
    length = piece * count
    turns = lats_here // count
    forward, inverse = pieced_tables(length, spec_filter.shape[1], count)
    decode = jnp.pad(w_decode, ((0, 0), (0, LANES - w_decode.shape[1])))
    received = []
    for turn in range(turns):
        pieces = []
        for step in range(count):
            lat = turn * count + (me - step) % count
            own = lax.dynamic_slice_in_dim(global_state, lat, 1, 0)
            pieces.append(shift(own, "col", -step) if step else own)
        received.append(pieces)
    gains = collect_filter(spec_filter)
    prepared = prepare(received[0][1])
    tied = lax.optimization_barrier((received[0], gains, decode, prepared))
    received[0], gains, decode, prepared = tied
    start = ((box_lon0 - window_base() - me * piece) % length).astype(jnp.int32)
    places, finals, strips = [], [], []
    for turn in range(turns):
        pieces, strip = advance_latitude(
            hours, cols_here // RATIO, start, received[turn], forward, inverse, gains, w_skip, w_mix,
            decode,
        )
        strips.append(strip)
        for step in range(count):
            places.append(turn * count + (me - step) % count)
            finals.append(shift(pieces[step], "col", step) if step else pieces[step])
    global_final = collate(jnp.stack(places).astype(jnp.int32), finals)
    plane = lax.axis_size(PLANE)
    strips = jnp.concatenate(strips, axis=1)
    sent = jnp.broadcast_to(strips[None], (plane,) + strips.shape)
    got = exchange(sent.reshape((plane * count,) + strips.shape[1:]), PLANE + ("col",))
    got = got.reshape((plane * lats_here, -1, LANES))
    lat = box_lat0[0] - window_base() + lax.axis_index(PLANE) * (rows_here // RATIO)
    lat = jnp.clip(lat + jnp.arange(window_extent(rows_here), dtype=jnp.int32), 0, plane * lats_here - 1)
    band, lat = lat // lats_here, lat % lats_here
    pick = (band * count + lat % count) * turns + lat // count
    return global_final, got, pick.astype(jnp.int32), prepared


def global_by_channel(
    hours, global_state, spec_filter, w_skip, w_mix, w_decode, box_lat0, box_lon0, rows_here,
    cols_here, prepare,
):
    count = lax.axis_size("col")
    prepared = prepare(global_state)
    forward, inverse = fourier_tables(global_state.shape[1] * count, spec_filter.shape[1])
    base = window_base()
    high, wide = window_extent(rows_here), window_extent(cols_here)
    span = (count - 1) * (cols_here // RATIO) + wide
    lat_start = box_lat0[0] + lax.axis_index(PLANE) * (rows_here // RATIO)
    lon_start = box_lon0[0] + lax.axis_index("col") * (cols_here // RATIO)
    windows = []
    for _ in range(hours):
        global_state = global_hour(global_state, spec_filter, w_skip, w_mix, forward, inverse)
        coarse = jnp.einsum(
            "alc,ck->alk", global_state, w_decode, preferred_element_type=jnp.float32
        ).astype(jnp.bfloat16)
        coarse = lax.all_gather(coarse, "col", axis=1, tiled=True)
        coarse = jnp.pad(coarse, ((0, 0), (base, span), (0, 0)))
        coarse = lax.dynamic_slice_in_dim(coarse, box_lon0[0], base + span, 1)
        coarse = lax.all_gather(coarse, PLANE, axis=0, tiled=True)
        coarse = lax.dynamic_slice_in_dim(coarse, lon_start - box_lon0[0], wide, 1)
        coarse = jnp.pad(coarse, ((base, high), (0, 0), (0, 0)))
        coarse = lax.dynamic_slice_in_dim(coarse, lat_start, high, 0)
        windows.append(coarse)
    group = LANES // PACKED
    windows = jnp.stack(windows, axis=1)
    windows = jnp.pad(
        windows, ((0, 0), (0, 0), (0, STRIP * group - wide), (0, PACKED - windows.shape[3]))
    )
    windows = windows.reshape(high, hours * STRIP, LANES)
    return global_state, windows, jnp.arange(high, dtype=jnp.int32), prepared


def next_to(low, high, axis):
    count = lax.axis_size(axis)
    forward = [(i, i + 1) for i in range(count - 1)]
    backward = [(target, source) for source, target in forward]
    return lax.ppermute(low, axis, forward), lax.ppermute(high, axis, backward)


def grid_place(start_ref, total, base, extent):
    place = start_ref + base + lax.broadcasted_iota(jnp.int32, (extent, 1), 0)
    return (place >= 0) & (place < total)


def assemble_kernel(
    rows, cols, totals, high, lanes, place_ref, mid0_ref, mid1_ref, above_ref, below_ref,
    left_ref, right_ref, noisy_ref, noise_ref, blend_ref,
):
    inner = RIM - RIM_USED
    pad = (noisy_ref.shape[1] - cols) // 2
    width = noisy_ref.shape[1]
    for ref, mid_ref, rim, part in ((noisy_ref, mid0_ref, RIM, 0), (noise_ref, mid1_ref, inner, RIM)):
        ref[0:rim, pad : pad + cols, :] = above_ref[part : part + rim]
        ref[rim : rim + rows, pad : pad + cols, :] = mid_ref[...]
        ref[rim + rows :, pad : pad + cols, :] = below_ref[part : part + rim]
        first = 0 if rim == RIM else rows + 2 * RIM
        ref[:, 0:pad, :] = left_ref[first : first + rows + 2 * rim]
        ref[:, pad + cols :, :] = right_ref[first : first + rows + 2 * rim]

    base = window_base()
    col = lax.broadcasted_iota(jnp.int32, (width, 1), 0) - pad
    col_in = grid_place(place_ref[1], totals[1], -pad, width)
    frac_col = ((col % RATIO).astype(jnp.float32) + 0.5) / RATIO
    col_base = jnp.where(col_in, (col + pad) // RATIO - pad // RATIO + base, FAR)
    group = LANES // PACKED
    point = lax.broadcasted_iota(jnp.int32, (width, group * high * STRIP), 1)
    point_lat = (point // STRIP % high).astype(jnp.float32)
    point_lon = (point % STRIP * group + point // (STRIP * high)).astype(jnp.float32)

    def weigh(index, carry):
        row = index - RIM
        whole = (row + 2 * RATIO) // RATIO - 2
        frac_row = ((row - whole * RATIO).astype(jnp.float32) + 0.5) / RATIO
        there = place_ref[0] + row
        row_base = jnp.where((there >= 0) & (there < totals[0]), whole + base, FAR)
        shifts = noisy_ref[index, :, :].astype(jnp.float32)
        lat = row_base.astype(jnp.float32) + shifts[:, lanes : lanes + 1]
        lon = col_base.astype(jnp.float32) + shifts[:, lanes + 1 : lanes + 2]
        from_lat = point_lat - lat
        from_lon = point_lon - lon
        weight_lat = jnp.where(
            from_lat == 0.0, 1.0 - frac_row, jnp.where(from_lat == 1.0, frac_row, 0.0)
        )
        weight_lon = jnp.where(
            from_lon == 0.0, 1.0 - frac_col, jnp.where(from_lon == 1.0, frac_col, 0.0)
        )
        blend_ref[index, :, :] = (weight_lat * weight_lon).astype(jnp.bfloat16)
        return carry

    lax.fori_loop(0, rows + 2 * RIM, weigh, 0)


def assemble(rows, cols, totals, high, lanes, place, mid0, mid1, above, below, left, right):
    inner = RIM - RIM_USED
    width = cols + 2 * left.shape[1]
    channels = mid0.shape[2]
    return pl.pallas_call(
        functools.partial(assemble_kernel, rows, cols, totals, high, lanes),
        out_shape=(
            jax.ShapeDtypeStruct((rows + 2 * RIM, width, channels), jnp.bfloat16),
            jax.ShapeDtypeStruct((rows + 2 * inner, width, channels), jnp.bfloat16),
            jax.ShapeDtypeStruct(
                (rows + 2 * RIM, width, LANES // PACKED * high * STRIP), jnp.bfloat16
            ),
        ),
        in_specs=[pl.BlockSpec(memory_space=pltpu.SMEM)]
        + [pl.BlockSpec(memory_space=pltpu.VMEM)] * 6,
        compiler_params=pltpu.CompilerParams(vmem_limit_bytes=40 * 2**20),
        cost_estimate=pl.CostEstimate(flops=2 * 10**8, bytes_accessed=10**7, transcendentals=0),
        name="assemble",
    )(place, mid0, mid1, above, below, left, right)


def silu(x):
    return x / (1.0 + jnp.exp(-x))


def denoise_kernel(
    rows, cols, totals, variables, conds, place_ref, pick_ref, noisy_ref, noise_ref, blend_ref,
    strip_ref, first_w_ref, down_w_ref, up_w_ref, bridge_w_ref, last_w_ref, out_ref, stack_ref, first_ref, pooled_ref,
    lifted_ref, third_ref, pair_ref, spread_ref, window_ref,
):
    width = noisy_ref.shape[1]
    half = width // 2
    pad = (width - cols) // 2
    channels = noisy_ref.shape[2]
    f32, bf16 = jnp.float32, jnp.bfloat16
    col_in = grid_place(place_ref[1], totals[1], -pad, width).astype(f32)
    lane = lax.broadcasted_iota(jnp.int32, (1, channels), 1)
    is_state = lane < variables
    is_cond = (lane >= variables) & (lane < variables + conds)
    high = pick_ref.shape[0]
    strips = [strip_ref[pick_ref[index]].astype(f32) for index in range(high)]
    for hour in range(2):
        near = jnp.concatenate([s[hour * STRIP : (hour + 1) * STRIP] for s in strips], axis=0)
        for turn in range(LANES // PACKED):
            moved = pltpu.roll(near, (variables - turn * PACKED) % LANES, 1)
            window_ref[hour, turn * high * STRIP : (turn + 1) * high * STRIP, :] = jnp.where(
                is_cond, moved, 0.0
            ).astype(bf16)

    def flat(start, count, unit):
        return pl.ds(pl.multiple_of(start * unit, 16), count * unit)

    def inside(row, count):
        marks = []
        for step in range(count):
            there = place_ref[0] + row + step
            marks.append(col_in * jnp.where((there >= 0) & (there < totals[0]), 1.0, 0.0))
        return jnp.concatenate(marks, axis=0)

    def conv(source_ref, row, count, unit, weight_ref):
        lhs = jnp.concatenate(
            [source_ref[flat(row + step, count, unit), :] for step in range(3)], axis=1
        )
        wide = jnp.dot(lhs, weight_ref[...], preferred_element_type=f32)
        size = weight_ref.shape[1] // 3
        span = count * unit
        return (
            pltpu.roll(wide[:, :size], 1, 0)
            + wide[:, size : 2 * size]
            + pltpu.roll(wide[:, 2 * size :], span - 1, 0)
        )

    for hour in range(2):
        rim = RIM - RIM_USED * hour
        tall = rows + 2 * rim

        def stack(index, carry, hour=hour, rim=rim):
            here = flat(index * 2, 2, width)
            weights = blend_ref[pl.ds(index * 2 + RIM - rim, 2)].reshape(2 * width, -1)
            cond = jnp.dot(weights, window_ref[hour], preferred_element_type=f32).astype(bf16)
            if hour == 0:
                own = noisy_ref[pl.ds(index * 2, 2)].reshape(2 * width, channels)
            else:
                own = stack_ref[here, :]
            stack_ref[here, :] = jnp.where(is_state, own, cond)
            return carry

        lax.fori_loop(0, tall // 2, stack, 0)

        def make_first(index, carry, rim=rim):
            row = index * 4
            value = silu(conv(stack_ref, row, 4, width, first_w_ref)) * inside(row - rim + 1, 4)
            value = value.astype(bf16)
            first_ref[flat(row, 4, width), :] = value
            value = value.astype(f32)
            for step in range(2):
                at = 2 * step * width
                pair_ref[...] = value[at : at + width] + value[at + width : at + 2 * width]
                even = pair_ref[pl.ds(0, half, stride=2), :]
                odd = pair_ref[pl.ds(1, half, stride=2), :]
                pooled_ref[flat(index * 2 + step, 1, half), :] = ((even + odd) * 0.25).astype(bf16)
            return carry

        lax.fori_loop(0, (tall - 2) // 4, make_first, 0)

        half_rows = (tall - 2) // 2 - 2

        def make_lifted(index, carry):
            value = silu(conv(pooled_ref, index * 2, 2, half, down_w_ref)).astype(bf16)
            lifted_ref[flat(index * 2, 2, half), :] = jnp.dot(
                value, up_w_ref[...], preferred_element_type=f32
            )
            return carry

        lax.fori_loop(0, half_rows // 2, make_lifted, 0)

        def make_third(index, carry, rim=rim):
            row = index * 2
            lifted = lifted_ref[flat(index, 1, half), :]
            spread_ref[pl.ds(0, half, stride=2), :] = lifted
            spread_ref[pl.ds(1, half, stride=2), :] = lifted
            bridged = jnp.dot(
                first_ref[flat(row + 2, 2, width), :], bridge_w_ref[...], preferred_element_type=f32
            )
            spread = spread_ref[...]
            value = silu(bridged + jnp.concatenate([spread, spread], axis=0))
            value = value * inside(row - rim + 3, 2)
            third_ref[flat(row, 2, width), :] = value.astype(bf16)
            return carry

        lax.fori_loop(0, half_rows, make_third, 0)

        def finish(index, carry, hour=hour, rim=rim):
            row = index * 2
            skip = 1 if hour == 1 else 0
            fresh = conv(third_ref, row + skip, 2, width, last_w_ref)
            own = stack_ref[flat(row + RIM_USED + skip, 2, width), :].astype(f32)
            fresh = (own + fresh).astype(bf16)
            if hour == 0:
                noise = noise_ref[pl.ds(row, 2)].reshape(2 * width, channels).astype(f32)
                fresh = (fresh.astype(f32) + noise_level * noise) * inside(row - rim + RIM_USED, 2)
                stack_ref[flat(row, 2, width), :] = fresh.astype(bf16)
            else:
                for step in range(2):
                    at = step * width + pad
                    out_ref[row + step] = fresh[at : at + cols]
            return carry

        lax.fori_loop(0, (tall - 2 * RIM_USED) // 2 if hour == 0 else rows // 2, finish, 0)


def denoise(rows, cols, totals, variables, conds, place, pick, noisy, noise, blend, strips, weights):
    width, channels = noisy.shape[1:]
    tall = rows + 2 * RIM
    bf16, f32 = jnp.bfloat16, jnp.float32
    return pl.pallas_call(
        functools.partial(denoise_kernel, rows, cols, totals, variables, conds),
        out_shape=jax.ShapeDtypeStruct((rows, cols, channels), bf16),
        in_specs=[pl.BlockSpec(memory_space=pltpu.SMEM)] * 2
        + [pl.BlockSpec(memory_space=pltpu.VMEM)] * 9,
        scratch_shapes=[
            pltpu.VMEM((tall * width, channels), bf16),
            pltpu.VMEM((tall * width, channels), bf16),
            pltpu.VMEM((tall // 2 * width // 2, channels), bf16),
            pltpu.VMEM((tall // 2 * width // 2, channels), f32),
            pltpu.VMEM((tall * width, channels), bf16),
            pltpu.VMEM((width, channels), f32),
            pltpu.VMEM((width, channels), f32),
            pltpu.VMEM((2, blend.shape[2], channels), bf16),
        ],
        compiler_params=pltpu.CompilerParams(vmem_limit_bytes=40 * 2**20),
        cost_estimate=pl.CostEstimate(
            flops=10**10, bytes_accessed=10**7, transcendentals=4 * 10**6
        ),
        name="denoise",
    )(place, pick, noisy, noise, blend, strips, *weights)


def conv_weight(weight, depth, width):
    out, _, given = weight.shape
    weight = weight.reshape(out, 3, 3, given)
    weight = jnp.pad(weight, ((0, width - out), (0, 0), (0, 0), (0, depth - given)))
    return jnp.transpose(weight, (1, 3, 2, 0)).reshape(3 * depth, 3 * width)


def shards(
    global_state,
    spec_filter,
    w_skip,
    w_mix,
    w_decode,
    regional_state,
    noise_draws,
    w_first,
    w_down,
    w_up,
    w_bridge,
    w_last,
    box_lat0,
    box_lon0,
    stencil_lat,
    stencil_lon,
):
    hours = noise_draws.shape[0]
    rows_here, cols_here = regional_state.shape[1:]
    row_start = lax.axis_index(PLANE) * rows_here
    col_start = lax.axis_index("col") * cols_here
    total_rows = rows_here * lax.axis_size(PLANE)
    total_cols = cols_here * lax.axis_size("col")
    assert hours == 2

    variables = regional_state.shape[0]
    conds = w_decode.shape[1]
    lanes = variables + conds
    noisy = (
        regional_state.astype(jnp.float32) + noise_level * noise_draws[0].astype(jnp.float32)
    ).astype(jnp.bfloat16)
    lat_shift = stencil_lat - (row_start + jnp.arange(rows_here, dtype=jnp.int32))[:, None] // RATIO
    lon_shift = stencil_lon - (col_start + jnp.arange(cols_here, dtype=jnp.int32))[None, :] // RATIO
    cells = (rows_here, cols_here)
    mids = jnp.concatenate(
        [
            noisy,
            jnp.zeros((conds,) + cells, jnp.bfloat16),
            lat_shift.astype(jnp.bfloat16)[None],
            lon_shift.astype(jnp.bfloat16)[None],
            jnp.zeros((LANES - lanes - 2,) + cells, jnp.bfloat16),
            noise_draws[1],
            jnp.zeros((LANES - variables,) + cells, jnp.bfloat16),
        ],
        axis=0,
    )
    mids = jnp.transpose(mids.reshape((2, LANES) + cells), (0, 2, 3, 1))
    mid0, mid1 = mids[0], mids[1]
    inner = RIM - RIM_USED
    high = window_extent(rows_here)
    place = jnp.stack([row_start, col_start]).astype(jnp.int32)
    totals = (total_rows, total_cols)

    def prepare(after):
        lows = jnp.concatenate([mid0[rows_here - RIM :], mid1[rows_here - inner :]], axis=0)
        highs = jnp.concatenate([mid0[:RIM], mid1[:inner]], axis=0)
        lows, highs, _ = lax.optimization_barrier((lows, highs, after))
        above, below = next_to(lows, highs, PLANE)
        weights = (
            conv_weight(w_first, LANES, w_first.shape[0]),
            conv_weight(w_down, w_down.shape[2], w_down.shape[0]),
            w_up.T,
            w_bridge.T,
            conv_weight(w_last, w_last.shape[2], LANES),
        )
        return above, below, weights

    by_latitude = global_state.shape[0] % lax.axis_size("col") == 0
    global_steps = global_by_latitude if by_latitude else global_by_channel
    global_final, strips, pick, (above, below, weights) = global_steps(
        hours, global_state, spec_filter, w_skip, w_mix, w_decode, box_lat0, box_lon0,
        rows_here, cols_here, prepare,
    )

    def rim_cols(part):
        return jnp.concatenate(
            [
                above[:RIM, part], mid0[:, part], below[:RIM, part],
                above[RIM:, part], mid1[:, part], below[RIM:, part],
            ],
            axis=0,
        )

    left, right = next_to(
        rim_cols(slice(cols_here - RIM_COLS, cols_here)), rim_cols(slice(0, RIM_COLS)), "col"
    )
    noisy, noise, blend = assemble(
        rows_here, cols_here, totals, high, lanes, place, mid0, mid1, above, below, left, right
    )
    regional_final = denoise(
        rows_here, cols_here, totals, variables, conds, place, pick, noisy, noise, blend, strips, weights
    )
    return global_final, jnp.transpose(regional_final[:, :, :variables], (2, 0, 1))


def solution(mesh):
    return jax.shard_map(
        shards,
        mesh=mesh,
        in_specs=(
            P(PLANE, "col", None),
            P(None, None, "col"),
            P(),
            P(),
            P(),
            P(None, PLANE, "col"),
            P(None, None, PLANE, "col"),
            P(),
            P(),
            P(),
            P(),
            P(),
            P(),
            P(),
            P(PLANE, "col"),
            P(PLANE, "col"),
        ),
        out_specs=(P(PLANE, "col", None), P(None, PLANE, "col")),
        check_vma=False,
    )
```

```python
import functools
import math

import jax
import jax.numpy as jnp
import ml_dtypes
import numpy as np
from jax import lax
from jax.experimental import pallas as pl
from jax.experimental.pallas import tpu as pltpu
from jax.sharding import PartitionSpec as P

RATIO = 8
noise_level = 0.5
PLANE = ("grp", "row")
RIM = 9
RIM_USED = 4
LANES = 128
PACKED = 32
MODE_TILE = 64
STRIP = 8
FAR = -4096
RIM_COLS = 16


def fourier_tables(length, num_modes):
    position = np.arange(length, dtype=np.int64)[:, None]
    frequency = np.arange(num_modes, dtype=np.int64)[None, :]
    angle = (position * frequency % length).astype(np.float64) * (2.0 * math.pi / length)
    cosine = np.cos(angle)
    sine = np.sin(angle)
    factor = np.where(frequency == 0, 1.0, 2.0) / length
    forward = np.concatenate([cosine, -sine], axis=1).T.astype(ml_dtypes.bfloat16)
    inverse = np.concatenate([cosine * factor, -sine * factor], axis=1).astype(ml_dtypes.bfloat16)
    return forward, inverse


def round_up(size, unit):
    return -(-size // unit) * unit


def split_tables(length, num_modes):
    piece = length // 4
    place = np.arange(piece, dtype=np.int64)[:, None]

    def waves(mode):
        angle = (place * mode[None, :] % length).astype(np.float64) * (2.0 * math.pi / length)
        return np.cos(angle), np.sin(angle), np.where(mode == 0, 1.0, 2.0)[None, :] / length

    def padded(blocks, unit_rows, unit_cols):
        rows = []
        for row in blocks:
            cols = []
            for block in row:
                spare = [(0, -block.shape[0] % unit_rows), (0, -block.shape[1] % unit_cols)]
                cols.append(np.pad(block, spare))
            rows.append(np.concatenate(cols, axis=1))
        return np.concatenate(rows, axis=0).astype(ml_dtypes.bfloat16)

    forward, inverse = [], []
    for residue in (0, 2):
        cosine, sine, factor = waves(np.arange(residue, num_modes, 4))
        forward.append(padded([[cosine.T], [-sine.T]], MODE_TILE, LANES))
        inverse.append(padded([[cosine * factor, -sine * factor]], LANES, MODE_TILE))
    mode = np.arange(1, num_modes, 2)
    cosine, sine, factor = waves(mode)
    sign = np.where(mode % 4 == 1, 1.0, -1.0)[None, :]
    odd_forward = padded(
        [[cosine.T, (-sign * sine).T], [-sine.T, (-sign * cosine).T]], 2 * MODE_TILE, LANES
    )
    odd_inverse = padded(
        [
            [cosine * factor, -sine * factor],
            [-sign * sine * factor, -sign * cosine * factor],
        ],
        LANES,
        2 * MODE_TILE,
    )
    return tuple(
        jnp.asarray(table)
        for table in (np.stack(forward), odd_forward, np.stack(inverse), odd_inverse)
    )


def sort_modes(spec_filter):
    parts = []
    for low, step, unit in ((0, 4, MODE_TILE), (2, 4, MODE_TILE), (1, 2, 2 * MODE_TILE)):
        part = spec_filter[:, low::step].astype(jnp.bfloat16)
        part = jnp.pad(part, ((0, 0), (0, -part.shape[1] % unit), (0, 0)))
        parts.append(part.reshape(-1, part.shape[2]))
    return jnp.concatenate(parts, axis=0)


def exchange(blocks, axis):
    return lax.all_to_all(blocks, axis, split_axis=0, concat_axis=0, tiled=True)


def spread(block, axis):
    return exchange(jnp.broadcast_to(block[None], (lax.axis_size(axis),) + block.shape), axis)


def collect_filter(spec_filter):
    flat = sort_modes(spec_filter)
    rows = flat.shape[0]
    share = rows // lax.axis_size(PLANE)
    mine = lax.dynamic_slice_in_dim(flat, lax.axis_index(PLANE) * share, share, 0)
    wide = spread(mine, "col")
    wide = jnp.swapaxes(wide, 0, 1).reshape(share, -1)
    return spread(wide, PLANE).reshape(rows, -1)


def latitude_kernel(hours, turns, step, place_ref, *refs):
    piece_refs, refs = refs[:4], refs[4:]
    even_forward_ref, odd_forward_ref, even_inverse_ref, odd_inverse_ref = refs[:4]
    filter_ref, skip_ref, mix_ref, decode_ref = refs[4:8]
    out_refs, strip_ref = refs[8:12], refs[12]
    state_ref, spectral_ref, coarse_ref, near_ref, packed_ref = refs[13:]
    f32, bf16 = jnp.float32, jnp.bfloat16
    piece, channels = piece_refs[0].shape[1:]
    padded = state_ref.shape[0] // 4
    group = LANES // PACKED
    span = near_ref.shape[0]
    rows = span // group
    spare = jnp.zeros((padded - piece, channels), bf16)
    for index in range(4):
        for turn in range(turns):
            state_ref[
                index * padded : (index + 1) * padded, turn * channels : (turn + 1) * channels
            ] = jnp.concatenate([piece_refs[index][turn], spare], axis=0)

    def gain(spectrum, low):
        half = spectrum.shape[0] // 2
        real, imag = spectrum[:half], spectrum[half:]
        gain_real = filter_ref[low : low + half, :].astype(f32)
        gain_imag = filter_ref[low + half : low + 2 * half, :].astype(f32)
        gain_real = jnp.concatenate([gain_real] * turns, axis=1)
        gain_imag = jnp.concatenate([gain_imag] * turns, axis=1)
        return jnp.concatenate(
            [
                (real * gain_real - imag * gain_imag).astype(bf16),
                (real * gain_imag + imag * gain_real).astype(bf16),
            ],
            axis=0,
        )

    def dot(left, right):
        return jnp.dot(left, right, preferred_element_type=f32)

    def advance(hour, carry):
        pieces = [
            state_ref[index * padded : (index + 1) * padded, :].astype(f32) for index in range(4)
        ]
        both, other = pieces[0] + pieces[2], pieces[1] + pieces[3]
        low = 0
        shares = []
        for index, mixed in enumerate((both + other, both - other)):
            spectrum = dot(even_forward_ref[index], mixed.astype(bf16))
            shares.append(dot(even_inverse_ref[index], gain(spectrum, low)))
            low += spectrum.shape[0]
        mixed = jnp.concatenate([pieces[0] - pieces[2], pieces[1] - pieces[3]], axis=0)
        odd = gain(dot(odd_forward_ref[...], mixed.astype(bf16)), low)
        odd = dot(odd_inverse_ref[...], odd)
        for index in range(4):
            even = shares[0] + shares[1] if index % 2 == 0 else shares[0] - shares[1]
            part = odd[:padded] if index % 2 == 0 else odd[padded:]
            total = even + part if index < 2 else even - part
            spectral_ref[index * padded : (index + 1) * padded, :] = total.astype(bf16)

        def mix(index, carry):
            here = pl.ds(pl.multiple_of(index * padded, LANES), padded)
            for turn in range(turns):
                lanes = slice(turn * channels, (turn + 1) * channels)
                state = state_ref[here, lanes]
                summed = spectral_ref[here, lanes].astype(f32) + dot(state, skip_ref[...])
                activated = jax.nn.gelu(summed).astype(bf16)
                update = dot(activated, mix_ref[...])
                state_ref[here, lanes] = (state.astype(f32) + update).astype(bf16)
            return carry

        lax.fori_loop(0, 4, mix, 0)

        for index in range(2):
            here = pl.ds(pl.multiple_of(place_ref[index] * padded, LANES), padded)
            coarse = dot(state_ref[here, :], decode_ref[...])
            for turn in range(turns):
                coarse_ref[turn, index * piece : (index + 1) * piece, :] = coarse[
                    :piece, turn * LANES : (turn + 1) * LANES
                ]
        for turn in range(turns):
            near_ref[...] = coarse_ref[turn, pl.ds(place_ref[2], span), :]
            packed = near_ref[pl.ds(0, rows, stride=group), :]
            for sub in range(1, group):
                packed += pltpu.roll(near_ref[pl.ds(sub, rows, stride=group), :], sub * PACKED, 1)
            packed_ref[turn, pl.ds(pl.multiple_of(hour * rows, 8), rows), :] = packed
        return carry

    lax.fori_loop(0, hours, advance, 0)
    for index in range(4):
        for turn in range(turns):
            out_refs[index][turn] = state_ref[
                index * padded : index * padded + piece, turn * channels : (turn + 1) * channels
            ]
    for target in range(4):
        low = target * step // group
        for turn in range(turns):
            strip = [
                packed_ref[turn, hour * rows + low : hour * rows + low + STRIP, :]
                for hour in range(hours)
            ]
            strip_ref[target, turn * hours * STRIP : (turn + 1) * hours * STRIP, :] = jnp.concatenate(
                strip, axis=0
            ).astype(bf16)


def advance_latitudes(hours, step, place, pieces, tables, gains, w_skip, w_mix, w_decode):
    turns, piece, channels = pieces[0].shape
    padded = round_up(piece, LANES)
    group = LANES // PACKED
    span = round_up(3 * step + STRIP * group, 8 * group)
    decode = jnp.pad(w_decode, ((0, 0), (0, LANES - w_decode.shape[1])))
    decode = jnp.concatenate(
        [jnp.pad(decode, ((0, 0), (t * LANES, (turns - 1 - t) * LANES))) for t in range(turns)], axis=0
    )
    modes = gains.shape[0] // 2
    flops = hours * turns * 8 * padded * channels * (3 * modes // 4 + 2 * channels)
    results = pl.pallas_call(
        functools.partial(latitude_kernel, hours, turns, step),
        out_shape=tuple(
            jax.ShapeDtypeStruct((turns, piece, channels), jnp.bfloat16) for _ in pieces
        )
        + (jax.ShapeDtypeStruct((4, turns * hours * STRIP, LANES), jnp.bfloat16),),
        in_specs=[pl.BlockSpec(memory_space=pltpu.SMEM)]
        + [pl.BlockSpec(memory_space=pltpu.VMEM)] * 12,
        scratch_shapes=[
            pltpu.VMEM((4 * padded, turns * channels), jnp.bfloat16),
            pltpu.VMEM((4 * padded, turns * channels), jnp.bfloat16),
            pltpu.VMEM((turns, 2 * piece, LANES), jnp.float32),
            pltpu.VMEM((span, LANES), jnp.float32),
            pltpu.VMEM((turns, hours * span // group, LANES), jnp.float32),
        ],
        compiler_params=pltpu.CompilerParams(vmem_limit_bytes=48 * 2**20),
        cost_estimate=pl.CostEstimate(
            flops=flops,
            bytes_accessed=12 * 2**20,
            transcendentals=hours * turns * 4 * piece * channels,
        ),
        name="advance_latitudes",
    )(place, *pieces, *tables, gains, w_skip, w_mix, decode)
    return results[:4], results[4]


def collate_kernel(count, place_ref, *refs):
    pieces, out_ref, sems = refs[:count], refs[count], refs[count + 1]
    copies = [
        pltpu.make_async_copy(
            piece, out_ref.at[pl.ds(place_ref[index], piece.shape[0])], sems.at[index]
        )
        for index, piece in enumerate(pieces)
    ]
    for copy in copies:
        copy.start()
    for copy in copies:
        copy.wait()


def collate(place, pieces):
    count = len(pieces)
    turns, piece, channels = pieces[0].shape
    return pl.pallas_call(
        functools.partial(collate_kernel, count),
        out_shape=jax.ShapeDtypeStruct((count * turns, piece, channels), pieces[0].dtype),
        in_specs=[pl.BlockSpec(memory_space=pltpu.SMEM)]
        + [pl.BlockSpec(memory_space=pltpu.VMEM)] * count,
        out_specs=pl.BlockSpec(memory_space=pl.ANY),
        scratch_shapes=[pltpu.SemaphoreType.DMA((count,))],
        name="collate",
    )(place, *pieces)


def shift(block, axis, step):
    count = lax.axis_size(axis)
    return lax.ppermute(block, axis, [(source, (source + step) % count) for source in range(count)])


def global_hour(current, spec_filter, w_skip, w_mix, forward, inverse):
    longitude = lax.all_to_all(current, "col", split_axis=2, concat_axis=1, tiled=True)
    spectrum = jnp.einsum("alc,ml->amc", longitude, forward, preferred_element_type=jnp.float32)
    num_modes = spec_filter.shape[1]
    real_part = spectrum[:, :num_modes, :]
    imag_part = spectrum[:, num_modes:, :]
    filt_real = spec_filter[0][None]
    filt_imag = spec_filter[1][None]
    mixed = jnp.concatenate(
        [
            real_part * filt_real - imag_part * filt_imag,
            real_part * filt_imag + imag_part * filt_real,
        ],
        axis=1,
    ).astype(jnp.bfloat16)
    filtered = jnp.einsum("amc,lm->alc", mixed, inverse, preferred_element_type=jnp.float32).astype(
        jnp.bfloat16
    )
    spectral = lax.all_to_all(filtered, "col", split_axis=1, concat_axis=2, tiled=True)
    skipped = jnp.einsum("alc,cd->ald", current, w_skip, preferred_element_type=jnp.float32)
    activated = jax.nn.gelu(spectral.astype(jnp.float32) + skipped).astype(jnp.bfloat16)
    update = jnp.einsum("ald,de->ale", activated, w_mix, preferred_element_type=jnp.float32)
    return (current.astype(jnp.float32) + update).astype(jnp.bfloat16)


def window_extent(cells):
    return (cells + RIM - 1) // RATIO + 3 - (-RIM // RATIO)


def window_base():
    return -(-RIM // RATIO)


def global_by_latitude(
    hours, global_state, spec_filter, w_skip, w_mix, w_decode, box_lat0, box_lon0, rows_here,
    cols_here, prepare,
):
    count = lax.axis_size("col")
    me = lax.axis_index("col")
    lats_here, piece, _ = global_state.shape
    turns = lats_here // count
    tables = split_tables(piece * count, spec_filter.shape[1])
    owners = [(me - step) % count * turns for step in range(count)]
    received = []
    for step, owner in enumerate(owners):
        own = lax.dynamic_slice_in_dim(global_state, owner, turns, 0)
        received.append(shift(own, "col", -step) if step else own)
    gains = collect_filter(spec_filter)
    prepared = prepare(received[1])
    received, gains, prepared = lax.optimization_barrier((received, gains, prepared))
    start = (box_lon0[0] - window_base() - me * piece) % (piece * count)
    place = jnp.stack([start // piece, (start // piece + 1) % count, start % piece])
    pieces, strips = advance_latitudes(
        hours, cols_here // RATIO, place.astype(jnp.int32), received, tables, gains, w_skip, w_mix,
        w_decode,
    )
    plane = lax.axis_size(PLANE)
    sent = jnp.broadcast_to(strips[None], (plane,) + strips.shape)
    got = exchange(sent.reshape((plane * count,) + strips.shape[1:]), PLANE + ("col",))
    got = got.reshape((plane * lats_here, -1, LANES))
    lat = box_lat0[0] - window_base() + lax.axis_index(PLANE) * (rows_here // RATIO)
    lat = jnp.clip(lat + jnp.arange(window_extent(rows_here), dtype=jnp.int32), 0, plane * lats_here - 1)
    finals = [shift(block, "col", step) if step else block for step, block in enumerate(pieces)]

    def finish(after):
        blocks, after = lax.optimization_barrier((finals, after))
        return collate(jnp.stack(owners).astype(jnp.int32), blocks), after

    return finish, got, lat.astype(jnp.int32), prepared


def global_by_channel(
    hours, global_state, spec_filter, w_skip, w_mix, w_decode, box_lat0, box_lon0, rows_here,
    cols_here, prepare,
):
    count = lax.axis_size("col")
    prepared = prepare(global_state)
    forward, inverse = fourier_tables(global_state.shape[1] * count, spec_filter.shape[1])
    base = window_base()
    high, wide = window_extent(rows_here), window_extent(cols_here)
    span = (count - 1) * (cols_here // RATIO) + wide
    lat_start = box_lat0[0] + lax.axis_index(PLANE) * (rows_here // RATIO)
    lon_start = box_lon0[0] + lax.axis_index("col") * (cols_here // RATIO)
    windows = []
    for _ in range(hours):
        global_state = global_hour(global_state, spec_filter, w_skip, w_mix, forward, inverse)
        coarse = jnp.einsum(
            "alc,ck->alk", global_state, w_decode, preferred_element_type=jnp.float32
        ).astype(jnp.bfloat16)
        coarse = lax.all_gather(coarse, "col", axis=1, tiled=True)
        coarse = jnp.pad(coarse, ((0, 0), (base, span), (0, 0)))
        coarse = lax.dynamic_slice_in_dim(coarse, box_lon0[0], base + span, 1)
        coarse = lax.all_gather(coarse, PLANE, axis=0, tiled=True)
        coarse = lax.dynamic_slice_in_dim(coarse, lon_start - box_lon0[0], wide, 1)
        coarse = jnp.pad(coarse, ((base, high), (0, 0), (0, 0)))
        coarse = lax.dynamic_slice_in_dim(coarse, lat_start, high, 0)
        windows.append(coarse)
    group = LANES // PACKED
    windows = jnp.stack(windows, axis=1)
    windows = jnp.pad(
        windows, ((0, 0), (0, 0), (0, STRIP * group - wide), (0, PACKED - windows.shape[3]))
    )
    windows = windows.reshape(high, hours * STRIP, LANES)
    return lambda after: (global_state, after), windows, jnp.arange(high, dtype=jnp.int32), prepared


def next_to(low, high, axis):
    count = lax.axis_size(axis)
    forward = [(i, i + 1) for i in range(count - 1)]
    backward = [(target, source) for source, target in forward]
    return lax.ppermute(low, axis, forward), lax.ppermute(high, axis, backward)


def grid_place(start_ref, total, base, extent):
    place = start_ref + base + lax.broadcasted_iota(jnp.int32, (extent, 1), 0)
    return (place >= 0) & (place < total)


def assemble_kernel(
    rows, cols, totals, high, lanes, place_ref, mid0_ref, mid1_ref, above_ref, below_ref,
    left_ref, right_ref, noisy_ref, noise_ref, blend_ref,
):
    inner = RIM - RIM_USED
    pad = (noisy_ref.shape[1] - cols) // 2
    width = noisy_ref.shape[1]
    for ref, mid_ref, rim, part in ((noisy_ref, mid0_ref, RIM, 0), (noise_ref, mid1_ref, inner, RIM)):
        ref[0:rim, pad : pad + cols, :] = above_ref[part : part + rim]
        ref[rim : rim + rows, pad : pad + cols, :] = mid_ref[...]
        ref[rim + rows :, pad : pad + cols, :] = below_ref[part : part + rim]
        first = 0 if rim == RIM else rows + 2 * RIM
        ref[:, 0:pad, :] = left_ref[first : first + rows + 2 * rim]
        ref[:, pad + cols :, :] = right_ref[first : first + rows + 2 * rim]

    base = window_base()
    col = lax.broadcasted_iota(jnp.int32, (width, 1), 0) - pad
    col_in = grid_place(place_ref[1], totals[1], -pad, width)
    frac_col = ((col % RATIO).astype(jnp.float32) + 0.5) / RATIO
    col_base = jnp.where(col_in, (col + pad) // RATIO - pad // RATIO + base, FAR)
    group = LANES // PACKED
    point = lax.broadcasted_iota(jnp.int32, (width, group * high * STRIP), 1)
    point_lat = (point // STRIP % high).astype(jnp.float32)
    point_lon = (point % STRIP * group + point // (STRIP * high)).astype(jnp.float32)

    def weigh(index, carry):
        row = index - RIM
        whole = (row + 2 * RATIO) // RATIO - 2
        frac_row = ((row - whole * RATIO).astype(jnp.float32) + 0.5) / RATIO
        there = place_ref[0] + row
        row_base = jnp.where((there >= 0) & (there < totals[0]), whole + base, FAR)
        shifts = noisy_ref[index, :, :].astype(jnp.float32)
        lat = row_base.astype(jnp.float32) + shifts[:, lanes : lanes + 1]
        lon = col_base.astype(jnp.float32) + shifts[:, lanes + 1 : lanes + 2]
        from_lat = point_lat - lat
        from_lon = point_lon - lon
        weight_lat = jnp.where(
            from_lat == 0.0, 1.0 - frac_row, jnp.where(from_lat == 1.0, frac_row, 0.0)
        )
        weight_lon = jnp.where(
            from_lon == 0.0, 1.0 - frac_col, jnp.where(from_lon == 1.0, frac_col, 0.0)
        )
        blend_ref[index, :, :] = (weight_lat * weight_lon).astype(jnp.bfloat16)
        return carry

    lax.fori_loop(0, rows + 2 * RIM, weigh, 0)


def assemble(rows, cols, totals, high, lanes, place, mid0, mid1, above, below, left, right):
    inner = RIM - RIM_USED
    width = cols + 2 * left.shape[1]
    channels = mid0.shape[2]
    return pl.pallas_call(
        functools.partial(assemble_kernel, rows, cols, totals, high, lanes),
        out_shape=(
            jax.ShapeDtypeStruct((rows + 2 * RIM, width, channels), jnp.bfloat16),
            jax.ShapeDtypeStruct((rows + 2 * inner, width, channels), jnp.bfloat16),
            jax.ShapeDtypeStruct(
                (rows + 2 * RIM, width, LANES // PACKED * high * STRIP), jnp.bfloat16
            ),
        ),
        in_specs=[pl.BlockSpec(memory_space=pltpu.SMEM)]
        + [pl.BlockSpec(memory_space=pltpu.VMEM)] * 6,
        compiler_params=pltpu.CompilerParams(vmem_limit_bytes=40 * 2**20),
        cost_estimate=pl.CostEstimate(flops=2 * 10**8, bytes_accessed=10**7, transcendentals=0),
        name="assemble",
    )(place, mid0, mid1, above, below, left, right)


def silu(x):
    half = 0.5 * x
    return half + half * jnp.tanh(half)


def denoise_kernel(
    rows, cols, totals, variables, conds, place_ref, pick_ref, noisy_ref, noise_ref, blend_ref,
    strip_ref, first_w_ref, down_w_ref, up_w_ref, bridge_w_ref, last_w_ref, out_ref, stack_ref, first_ref, pooled_ref,
    lifted_ref, third_ref, pair_ref, spread_ref, window_ref,
):
    width = noisy_ref.shape[1]
    half = width // 2
    pad = (width - cols) // 2
    channels = noisy_ref.shape[2]
    f32, bf16 = jnp.float32, jnp.bfloat16
    col_in = grid_place(place_ref[1], totals[1], -pad, width).astype(f32)
    lane = lax.broadcasted_iota(jnp.int32, (1, channels), 1)
    is_state = lane < variables
    is_cond = (lane >= variables) & (lane < variables + conds)
    high = pick_ref.shape[0]
    strips = [strip_ref[pick_ref[index]].astype(f32) for index in range(high)]
    for hour in range(2):
        near = jnp.concatenate([s[hour * STRIP : (hour + 1) * STRIP] for s in strips], axis=0)
        for turn in range(LANES // PACKED):
            moved = pltpu.roll(near, (variables - turn * PACKED) % LANES, 1)
            window_ref[hour, turn * high * STRIP : (turn + 1) * high * STRIP, :] = jnp.where(
                is_cond, moved, 0.0
            ).astype(bf16)

    def flat(start, count, unit):
        return pl.ds(pl.multiple_of(start * unit, 16), count * unit)

    def inside(row, count):
        marks = []
        for step in range(count):
            there = place_ref[0] + row + step
            marks.append(col_in * jnp.where((there >= 0) & (there < totals[0]), 1.0, 0.0))
        return jnp.concatenate(marks, axis=0)

    def conv(source_ref, row, count, unit, weight_ref):
        lhs = jnp.concatenate(
            [source_ref[flat(row + step, count, unit), :] for step in range(3)], axis=1
        )
        wide = jnp.dot(lhs, weight_ref[...], preferred_element_type=f32)
        size = weight_ref.shape[1] // 3
        span = count * unit
        return (
            pltpu.roll(wide[:, :size], 1, 0)
            + wide[:, size : 2 * size]
            + pltpu.roll(wide[:, 2 * size :], span - 1, 0)
        )

    for hour in range(2):
        rim = RIM - RIM_USED * hour
        tall = rows + 2 * rim

        def stack(index, carry, hour=hour, rim=rim):
            here = flat(index * 2, 2, width)
            weights = blend_ref[pl.ds(index * 2 + RIM - rim, 2)].reshape(2 * width, -1)
            cond = jnp.dot(weights, window_ref[hour], preferred_element_type=f32).astype(bf16)
            if hour == 0:
                own = noisy_ref[pl.ds(index * 2, 2)].reshape(2 * width, channels)
            else:
                own = stack_ref[here, :]
            stack_ref[here, :] = jnp.where(is_state, own, cond)
            return carry

        lax.fori_loop(0, tall // 2, stack, 0)

        def make_first(index, carry, rim=rim):
            row = index * 8
            value = silu(conv(stack_ref, row, 8, width, first_w_ref)) * inside(row - rim + 1, 8)
            value = value.astype(bf16)
            first_ref[flat(row, 8, width), :] = value
            value = value.astype(f32)
            for step in range(4):
                at = 2 * step * width
                pair_ref[step] = value[at : at + width] + value[at + width : at + 2 * width]
                even = pair_ref[step, pl.ds(0, half, stride=2), :]
                odd = pair_ref[step, pl.ds(1, half, stride=2), :]
                pooled_ref[flat(index * 4 + step, 1, half), :] = ((even + odd) * 0.25).astype(bf16)
            return carry

        lax.fori_loop(0, (tall - 2) // 8, make_first, 0)

        half_rows = (tall - 2) // 2 - 2

        def make_lifted(index, carry, part=half_rows // 2):
            value = silu(conv(pooled_ref, index * part, part, half, down_w_ref)).astype(bf16)
            lifted_ref[flat(index * part, part, half), :] = jnp.dot(
                value, up_w_ref[...], preferred_element_type=f32
            )
            return carry

        lax.fori_loop(0, 2, make_lifted, 0)

        def make_third(index, carry, rim=rim):
            row = index * 4
            spreads = []
            for step in range(2):
                lifted = lifted_ref[flat(index * 2 + step, 1, half), :]
                spread_ref[step, pl.ds(0, half, stride=2), :] = lifted
                spread_ref[step, pl.ds(1, half, stride=2), :] = lifted
                spreads += [spread_ref[step]] * 2
            bridged = jnp.dot(
                first_ref[flat(row + 2, 4, width), :], bridge_w_ref[...], preferred_element_type=f32
            )
            value = silu(bridged + jnp.concatenate(spreads, axis=0))
            value = value * inside(row - rim + 3, 4)
            third_ref[flat(row, 4, width), :] = value.astype(bf16)
            return carry

        lax.fori_loop(0, half_rows // 2, make_third, 0)

        part = (rows + 2 * (rim - RIM_USED)) // 2 if hour == 0 else rows // 2

        def finish(index, carry, hour=hour, rim=rim, part=part):
            row = index * part
            skip = 1 if hour == 1 else 0
            fresh = conv(third_ref, row + skip, part, width, last_w_ref)
            own = stack_ref[flat(row + RIM_USED + skip, part, width), :].astype(f32)
            fresh = (own + fresh).astype(bf16)
            if hour == 0:
                noise = noise_ref[pl.ds(row, part)].reshape(part * width, channels).astype(f32)
                fresh = (fresh.astype(f32) + noise_level * noise) * inside(row - rim + RIM_USED, part)
                stack_ref[flat(row, part, width), :] = fresh.astype(bf16)
            else:
                for step in range(part):
                    at = step * width + pad
                    out_ref[row + step] = fresh[at : at + cols]
            return carry

        lax.fori_loop(0, 2, finish, 0)


def denoise(rows, cols, totals, variables, conds, place, pick, noisy, noise, blend, strips, weights):
    width, channels = noisy.shape[1:]
    tall = rows + 2 * RIM
    bf16, f32 = jnp.bfloat16, jnp.float32
    return pl.pallas_call(
        functools.partial(denoise_kernel, rows, cols, totals, variables, conds),
        out_shape=jax.ShapeDtypeStruct((rows, cols, channels), bf16),
        in_specs=[pl.BlockSpec(memory_space=pltpu.SMEM)] * 2
        + [pl.BlockSpec(memory_space=pltpu.VMEM)] * 9,
        scratch_shapes=[
            pltpu.VMEM((tall * width, channels), bf16),
            pltpu.VMEM((tall * width, channels), bf16),
            pltpu.VMEM((tall // 2 * width // 2, channels), bf16),
            pltpu.VMEM((tall // 2 * width // 2, channels), f32),
            pltpu.VMEM((tall * width, channels), bf16),
            pltpu.VMEM((4, width, channels), f32),
            pltpu.VMEM((2, width, channels), f32),
            pltpu.VMEM((2, blend.shape[2], channels), bf16),
        ],
        compiler_params=pltpu.CompilerParams(vmem_limit_bytes=40 * 2**20),
        cost_estimate=pl.CostEstimate(
            flops=10**10, bytes_accessed=10**7, transcendentals=4 * 10**6
        ),
        name="denoise",
    )(place, pick, noisy, noise, blend, strips, *weights)


def conv_weight(weight, depth, width):
    out, _, given = weight.shape
    weight = weight.reshape(out, 3, 3, given)
    weight = jnp.pad(weight, ((0, width - out), (0, 0), (0, 0), (0, depth - given)))
    return jnp.transpose(weight, (1, 3, 2, 0)).reshape(3 * depth, 3 * width)


def shards(
    global_state,
    spec_filter,
    w_skip,
    w_mix,
    w_decode,
    regional_state,
    noise_draws,
    w_first,
    w_down,
    w_up,
    w_bridge,
    w_last,
    box_lat0,
    box_lon0,
    stencil_lat,
    stencil_lon,
):
    hours = noise_draws.shape[0]
    rows_here, cols_here = regional_state.shape[1:]
    row_start = lax.axis_index(PLANE) * rows_here
    col_start = lax.axis_index("col") * cols_here
    total_rows = rows_here * lax.axis_size(PLANE)
    total_cols = cols_here * lax.axis_size("col")
    assert hours == 2

    variables = regional_state.shape[0]
    conds = w_decode.shape[1]
    lanes = variables + conds
    noisy = (
        regional_state.astype(jnp.float32) + noise_level * noise_draws[0].astype(jnp.float32)
    ).astype(jnp.bfloat16)
    lat_shift = stencil_lat - (row_start + jnp.arange(rows_here, dtype=jnp.int32))[:, None] // RATIO
    lon_shift = stencil_lon - (col_start + jnp.arange(cols_here, dtype=jnp.int32))[None, :] // RATIO
    cells = (rows_here, cols_here)
    mids = jnp.concatenate(
        [
            noisy,
            jnp.zeros((conds,) + cells, jnp.bfloat16),
            lat_shift.astype(jnp.bfloat16)[None],
            lon_shift.astype(jnp.bfloat16)[None],
            jnp.zeros((LANES - lanes - 2,) + cells, jnp.bfloat16),
            noise_draws[1],
            jnp.zeros((LANES - variables,) + cells, jnp.bfloat16),
        ],
        axis=0,
    )
    mids = jnp.transpose(mids.reshape((2, LANES) + cells), (0, 2, 3, 1))
    mid0, mid1 = mids[0], mids[1]
    inner = RIM - RIM_USED
    high = window_extent(rows_here)
    place = jnp.stack([row_start, col_start]).astype(jnp.int32)
    totals = (total_rows, total_cols)

    def prepare(after):
        lows = jnp.concatenate([mid0[rows_here - RIM :], mid1[rows_here - inner :]], axis=0)
        highs = jnp.concatenate([mid0[:RIM], mid1[:inner]], axis=0)
        above, below = next_to(lows, highs, PLANE)

        def rim_cols(part):
            return jnp.concatenate(
                [
                    above[:RIM, part], mid0[:, part], below[:RIM, part],
                    above[RIM:, part], mid1[:, part], below[RIM:, part],
                ],
                axis=0,
            )

        left, right = next_to(
            rim_cols(slice(cols_here - RIM_COLS, cols_here)), rim_cols(slice(0, RIM_COLS)), "col"
        )
        weights = (
            conv_weight(w_first, LANES, w_first.shape[0]),
            conv_weight(w_down, w_down.shape[2], w_down.shape[0]),
            w_up.T,
            w_bridge.T,
            conv_weight(w_last, w_last.shape[2], LANES),
        )
        return (mid0, mid1, above, below, left, right), weights

    by_latitude = lax.axis_size("col") == 4 and global_state.shape[0] % 4 == 0
    global_steps = global_by_latitude if by_latitude else global_by_channel
    finish, strips, pick, (parts, weights) = global_steps(
        hours, global_state, spec_filter, w_skip, w_mix, w_decode, box_lat0, box_lon0,
        rows_here, cols_here, prepare,
    )
    noisy, noise, blend = assemble(rows_here, cols_here, totals, high, lanes, place, *parts)
    regional_final = denoise(
        rows_here, cols_here, totals, variables, conds, place, pick, noisy, noise, blend, strips, weights
    )
    regional_final = jnp.transpose(regional_final[:, :, :variables], (2, 0, 1))
    return finish(regional_final)


def solution(mesh):
    return jax.shard_map(
        shards,
        mesh=mesh,
        in_specs=(
            P(PLANE, "col", None),
            P(None, None, "col"),
            P(),
            P(),
            P(),
            P(None, PLANE, "col"),
            P(None, None, PLANE, "col"),
            P(),
            P(),
            P(),
            P(),
            P(),
            P(),
            P(),
            P(PLANE, "col"),
            P(PLANE, "col"),
        ),
        out_specs=(P(PLANE, "col", None), P(None, PLANE, "col")),
        check_vma=False,
    )
```

```python
import functools
import math

import jax
import jax.numpy as jnp
import ml_dtypes
import numpy as np
from jax import lax
from jax.experimental import pallas as pl
from jax.experimental.pallas import tpu as pltpu
from jax.sharding import PartitionSpec as P

RATIO = 8
noise_level = 0.5
PLANE = ("grp", "row")
RIM = 9
RIM_USED = 4
LANES = 128
PACKED = 32
MODE_TILE = 64
STRIP = 8
FAR = -4096
RIM_COLS = 16


def fourier_tables(length, num_modes):
    position = np.arange(length, dtype=np.int64)[:, None]
    frequency = np.arange(num_modes, dtype=np.int64)[None, :]
    angle = (position * frequency % length).astype(np.float64) * (2.0 * math.pi / length)
    cosine = np.cos(angle)
    sine = np.sin(angle)
    factor = np.where(frequency == 0, 1.0, 2.0) / length
    forward = np.concatenate([cosine, -sine], axis=1).T.astype(ml_dtypes.bfloat16)
    inverse = np.concatenate([cosine * factor, -sine * factor], axis=1).astype(ml_dtypes.bfloat16)
    return forward, inverse


def round_up(size, unit):
    return -(-size // unit) * unit


def split_tables(length, num_modes):
    piece = length // 4
    place = np.arange(piece, dtype=np.int64)[:, None]

    def waves(mode):
        angle = (place * mode[None, :] % length).astype(np.float64) * (2.0 * math.pi / length)
        return np.cos(angle), np.sin(angle), np.where(mode == 0, 1.0, 2.0)[None, :] / length

    def padded(blocks, unit_rows, unit_cols):
        rows = []
        for row in blocks:
            cols = []
            for block in row:
                spare = [(0, -block.shape[0] % unit_rows), (0, -block.shape[1] % unit_cols)]
                cols.append(np.pad(block, spare))
            rows.append(np.concatenate(cols, axis=1))
        return np.concatenate(rows, axis=0).astype(ml_dtypes.bfloat16)

    forward, inverse = [], []
    for residue in (0, 2):
        cosine, sine, factor = waves(np.arange(residue, num_modes, 4))
        forward.append(padded([[cosine.T], [-sine.T]], MODE_TILE, LANES))
        inverse.append(padded([[cosine * factor, -sine * factor]], LANES, MODE_TILE))
    mode = np.arange(1, num_modes, 2)
    cosine, sine, factor = waves(mode)
    sign = np.where(mode % 4 == 1, 1.0, -1.0)[None, :]
    odd_forward = padded(
        [[cosine.T, (-sign * sine).T], [-sine.T, (-sign * cosine).T]], 2 * MODE_TILE, LANES
    )
    odd_inverse = padded(
        [
            [cosine * factor, -sine * factor],
            [-sign * sine * factor, -sign * cosine * factor],
        ],
        LANES,
        2 * MODE_TILE,
    )
    return tuple(
        jnp.asarray(table)
        for table in (np.stack(forward), odd_forward, np.stack(inverse), odd_inverse)
    )


def exchange(blocks, axis):
    return lax.all_to_all(blocks, axis, split_axis=0, concat_axis=0, tiled=True)


def spread(block, axis):
    return exchange(jnp.broadcast_to(block[None], (lax.axis_size(axis),) + block.shape), axis)


def filter_share(spec_filter):
    rows = 2 * spec_filter.shape[1]
    flat = spec_filter.reshape(rows, spec_filter.shape[2])
    share = rows // lax.axis_size(PLANE)
    mine = lax.dynamic_slice_in_dim(flat, lax.axis_index(PLANE) * share, share, 0)
    return mine.astype(jnp.bfloat16)


def collect_filter(mine):
    count = lax.axis_size("col")
    me = lax.axis_index("col")
    wide = jnp.broadcast_to(mine[None], (count,) + mine.shape)
    for step in range(1, count):
        block = shift(mine, "col", -step)
        wide = lax.dynamic_update_slice_in_dim(wide, block[None], (me + step) % count, 0)
    wide = jnp.swapaxes(wide, 0, 1).reshape(mine.shape[0], -1)
    return spread(wide, PLANE).reshape(-1, wide.shape[1])


def gelu(x):
    slope = math.sqrt(2.0 / math.pi)
    half = 0.5 * x
    return half + half * jnp.tanh(x * (slope + (0.044715 * slope) * (x * x)))


def latitude_kernel(hours, turns, step, place_ref, *refs):
    piece_refs, refs = refs[:4], refs[4:]
    even_forward_ref, odd_forward_ref, even_inverse_ref, odd_inverse_ref = refs[:4]
    filter_ref, skip_ref, mix_ref, decode_ref = refs[4:8]
    out_refs, strip_ref = refs[8:12], refs[12]
    state_ref, spectral_ref, gain_ref, coarse_ref, near_ref, packed_ref = refs[13:]
    f32, bf16 = jnp.float32, jnp.bfloat16
    piece, channels = piece_refs[0].shape[1:]
    padded = state_ref.shape[0] // 4
    group = LANES // PACKED
    span = near_ref.shape[0]
    rows = span // group
    spare = jnp.zeros((padded - piece, channels), bf16)
    for index in range(4):
        for turn in range(turns):
            state_ref[
                index * padded : (index + 1) * padded, turn * channels : (turn + 1) * channels
            ] = jnp.concatenate([piece_refs[index][turn], spare], axis=0)

    modes = filter_ref.shape[0] // 2
    for index in range(channels // LANES):
        lanes = slice(index * LANES, (index + 1) * LANES)
        gain_ref[index, : 2 * modes, :] = filter_ref[:, lanes].astype(f32)
        gain_ref[index, 2 * modes :, :] = jnp.zeros((gain_ref.shape[1] - 2 * modes, LANES), f32)

    def gain_rows(low, count, stride):
        rows = pl.ds(low, count, stride=stride)
        tiles = [gain_ref[index, rows, :] for index in range(channels // LANES)]
        return jnp.concatenate(tiles * turns, axis=1)

    def gain(spectrum, low, stride):
        half = spectrum.shape[0] // 2
        real, imag = spectrum[:half], spectrum[half:]
        gain_real = gain_rows(low, half, stride)
        gain_imag = gain_rows(modes + low, half, stride)
        return jnp.concatenate(
            [
                (real * gain_real - imag * gain_imag).astype(bf16),
                (real * gain_imag + imag * gain_real).astype(bf16),
            ],
            axis=0,
        )

    def dot(left, right):
        return jnp.dot(left, right, preferred_element_type=f32)

    def advance(hour, carry):
        pieces = [
            state_ref[index * padded : (index + 1) * padded, :].astype(f32) for index in range(4)
        ]
        both, other = pieces[0] + pieces[2], pieces[1] + pieces[3]
        shares = []
        for index, mixed in enumerate((both + other, both - other)):
            spectrum = dot(even_forward_ref[index], mixed.astype(bf16))
            shares.append(dot(even_inverse_ref[index], gain(spectrum, 2 * index, 4)))
        mixed = jnp.concatenate([pieces[0] - pieces[2], pieces[1] - pieces[3]], axis=0)
        odd = gain(dot(odd_forward_ref[...], mixed.astype(bf16)), 1, 2)
        odd = dot(odd_inverse_ref[...], odd)
        for index in range(4):
            even = shares[0] + shares[1] if index % 2 == 0 else shares[0] - shares[1]
            part = odd[:padded] if index % 2 == 0 else odd[padded:]
            total = even + part if index < 2 else even - part
            spectral_ref[index * padded : (index + 1) * padded, :] = total.astype(bf16)

        def mix(index, carry):
            here = pl.ds(pl.multiple_of(index * padded, LANES), padded)
            for turn in range(turns):
                lanes = slice(turn * channels, (turn + 1) * channels)
                state = state_ref[here, lanes]
                summed = spectral_ref[here, lanes].astype(f32) + dot(state, skip_ref[...])
                activated = gelu(summed).astype(bf16)
                update = dot(activated, mix_ref[...])
                state_ref[here, lanes] = (state.astype(f32) + update).astype(bf16)
            return carry

        lax.fori_loop(0, 4, mix, 0)

        for index in range(2):
            here = pl.ds(pl.multiple_of(place_ref[index] * padded, LANES), padded)
            coarse = dot(state_ref[here, :], decode_ref[...])
            for turn in range(turns):
                coarse_ref[turn, index * piece : (index + 1) * piece, :] = coarse[
                    :piece, turn * LANES : (turn + 1) * LANES
                ]
        for turn in range(turns):
            near_ref[...] = coarse_ref[turn, pl.ds(place_ref[2], span), :]
            packed = near_ref[pl.ds(0, rows, stride=group), :]
            for sub in range(1, group):
                packed += pltpu.roll(near_ref[pl.ds(sub, rows, stride=group), :], sub * PACKED, 1)
            packed_ref[turn, pl.ds(pl.multiple_of(hour * rows, 8), rows), :] = packed
        return carry

    lax.fori_loop(0, hours, advance, 0)
    for index in range(4):
        for turn in range(turns):
            out_refs[index][turn] = state_ref[
                index * padded : index * padded + piece, turn * channels : (turn + 1) * channels
            ]
    for target in range(4):
        low = target * step // group
        for turn in range(turns):
            strip = [
                packed_ref[turn, hour * rows + low : hour * rows + low + STRIP, :]
                for hour in range(hours)
            ]
            strip_ref[target, turn * hours * STRIP : (turn + 1) * hours * STRIP, :] = jnp.concatenate(
                strip, axis=0
            ).astype(bf16)


def advance_latitudes(hours, step, place, pieces, tables, gains, w_skip, w_mix, w_decode):
    turns, piece, channels = pieces[0].shape
    padded = round_up(piece, LANES)
    group = LANES // PACKED
    span = round_up(3 * step + STRIP * group, 8 * group)
    decode = jnp.pad(w_decode, ((0, 0), (0, LANES - w_decode.shape[1])))
    decode = jnp.concatenate(
        [jnp.pad(decode, ((0, 0), (t * LANES, (turns - 1 - t) * LANES))) for t in range(turns)], axis=0
    )
    modes = gains.shape[0] // 2
    spare = max(4 * (tables[0].shape[1] // 2), 2 * (tables[1].shape[0] // 2)) - modes
    flops = hours * turns * 8 * padded * channels * (3 * modes // 4 + 2 * channels)
    results = pl.pallas_call(
        functools.partial(latitude_kernel, hours, turns, step),
        out_shape=tuple(
            jax.ShapeDtypeStruct((turns, piece, channels), jnp.bfloat16) for _ in pieces
        )
        + (jax.ShapeDtypeStruct((4, turns * hours * STRIP, LANES), jnp.bfloat16),),
        in_specs=[pl.BlockSpec(memory_space=pltpu.SMEM)]
        + [pl.BlockSpec(memory_space=pltpu.VMEM)] * 12,
        scratch_shapes=[
            pltpu.VMEM((4 * padded, turns * channels), jnp.bfloat16),
            pltpu.VMEM((4 * padded, turns * channels), jnp.bfloat16),
            pltpu.VMEM((channels // LANES, gains.shape[0] + spare, LANES), jnp.float32),
            pltpu.VMEM((turns, 2 * piece, LANES), jnp.float32),
            pltpu.VMEM((span, LANES), jnp.float32),
            pltpu.VMEM((turns, hours * span // group, LANES), jnp.float32),
        ],
        compiler_params=pltpu.CompilerParams(vmem_limit_bytes=48 * 2**20),
        cost_estimate=pl.CostEstimate(
            flops=flops,
            bytes_accessed=12 * 2**20,
            transcendentals=hours * turns * 4 * piece * channels,
        ),
        name="advance_latitudes",
    )(place, *pieces, *tables, gains, w_skip, w_mix, decode)
    return results[:4], results[4]


def collate_kernel(count, place_ref, *refs):
    pieces, out_ref, sems = refs[:count], refs[count], refs[count + 1]
    copies = [
        pltpu.make_async_copy(
            piece, out_ref.at[pl.ds(place_ref[index], piece.shape[0])], sems.at[index]
        )
        for index, piece in enumerate(pieces)
    ]
    for copy in copies:
        copy.start()
    for copy in copies:
        copy.wait()


def collate(place, pieces):
    count = len(pieces)
    turns, piece, channels = pieces[0].shape
    return pl.pallas_call(
        functools.partial(collate_kernel, count),
        out_shape=jax.ShapeDtypeStruct((count * turns, piece, channels), pieces[0].dtype),
        in_specs=[pl.BlockSpec(memory_space=pltpu.SMEM)]
        + [pl.BlockSpec(memory_space=pltpu.VMEM)] * count,
        out_specs=pl.BlockSpec(memory_space=pl.ANY),
        scratch_shapes=[pltpu.SemaphoreType.DMA((count,))],
        name="collate",
    )(place, *pieces)


def shift(block, axis, step):
    count = lax.axis_size(axis)
    return lax.ppermute(block, axis, [(source, (source + step) % count) for source in range(count)])


def global_hour(current, spec_filter, w_skip, w_mix, forward, inverse):
    longitude = lax.all_to_all(current, "col", split_axis=2, concat_axis=1, tiled=True)
    spectrum = jnp.einsum("alc,ml->amc", longitude, forward, preferred_element_type=jnp.float32)
    num_modes = spec_filter.shape[1]
    real_part = spectrum[:, :num_modes, :]
    imag_part = spectrum[:, num_modes:, :]
    filt_real = spec_filter[0][None]
    filt_imag = spec_filter[1][None]
    mixed = jnp.concatenate(
        [
            real_part * filt_real - imag_part * filt_imag,
            real_part * filt_imag + imag_part * filt_real,
        ],
        axis=1,
    ).astype(jnp.bfloat16)
    filtered = jnp.einsum("amc,lm->alc", mixed, inverse, preferred_element_type=jnp.float32).astype(
        jnp.bfloat16
    )
    spectral = lax.all_to_all(filtered, "col", split_axis=1, concat_axis=2, tiled=True)
    skipped = jnp.einsum("alc,cd->ald", current, w_skip, preferred_element_type=jnp.float32)
    activated = jax.nn.gelu(spectral.astype(jnp.float32) + skipped).astype(jnp.bfloat16)
    update = jnp.einsum("ald,de->ale", activated, w_mix, preferred_element_type=jnp.float32)
    return (current.astype(jnp.float32) + update).astype(jnp.bfloat16)


def window_extent(cells):
    return (cells + RIM - 1) // RATIO + 3 - (-RIM // RATIO)


def window_base():
    return -(-RIM // RATIO)


def global_by_latitude(
    hours, global_state, spec_filter, w_skip, w_mix, w_decode, box_lat0, box_lon0, rows_here,
    cols_here, prepare,
):
    count = lax.axis_size("col")
    me = lax.axis_index("col")
    lats_here, piece, _ = global_state.shape
    turns = lats_here // count
    tables = split_tables(piece * count, spec_filter.shape[1])
    places = [[turn * count + (me - step) % count for step in range(count)] for turn in range(turns)]
    mine = filter_share(spec_filter)
    after = mine
    received = []
    for turn in range(turns):
        global_state, _ = lax.optimization_barrier((global_state, after))
        blocks = []
        for step in range(count):
            own = lax.dynamic_slice_in_dim(global_state, places[turn][step], 1, 0)
            blocks.append(shift(own, "col", -step) if step else own)
        received.append(blocks)
        after = blocks[1]
    gains = collect_filter(mine)
    prepared = prepare(received[0][1])
    start = (box_lon0[0] - window_base() - me * piece) % (piece * count)
    place = jnp.stack([start // piece, (start // piece + 1) % count, start % piece]).astype(jnp.int32)
    outcome, strips = [], []
    for turn in range(turns):
        blocks = received[turn]
        if turn == turns - 1:
            blocks, prepared = lax.optimization_barrier((blocks, prepared))
        blocks, strip = advance_latitudes(
            hours, cols_here // RATIO, place, blocks, tables, gains, w_skip, w_mix, w_decode
        )
        outcome.append(blocks)
        strips.append(strip)
    plane = lax.axis_size(PLANE)
    strips = jnp.concatenate(strips, axis=1)
    sent = jnp.broadcast_to(strips[None], (plane,) + strips.shape)
    got = exchange(sent.reshape((plane * count,) + strips.shape[1:]), PLANE + ("col",))
    outcome[-1], got = lax.optimization_barrier((outcome[-1], got))
    got = got.reshape((plane * lats_here, -1, LANES))
    lat = box_lat0[0] - window_base() + lax.axis_index(PLANE) * (rows_here // RATIO)
    lat = jnp.clip(lat + jnp.arange(window_extent(rows_here), dtype=jnp.int32), 0, plane * lats_here - 1)
    band, lat = lat // lats_here, lat % lats_here
    pick = (band * count + lat % count) * turns + lat // count
    finals = [
        shift(block, "col", step) if step else block
        for blocks in outcome
        for step, block in enumerate(blocks)
    ]

    def finish(after):
        blocks, after = lax.optimization_barrier((finals, after))
        return collate(jnp.stack(sum(places, [])).astype(jnp.int32), blocks), after

    return finish, got, pick.astype(jnp.int32), prepared


def global_by_channel(
    hours, global_state, spec_filter, w_skip, w_mix, w_decode, box_lat0, box_lon0, rows_here,
    cols_here, prepare,
):
    count = lax.axis_size("col")
    prepared = prepare(global_state)
    forward, inverse = fourier_tables(global_state.shape[1] * count, spec_filter.shape[1])
    base = window_base()
    high, wide = window_extent(rows_here), window_extent(cols_here)
    span = (count - 1) * (cols_here // RATIO) + wide
    lat_start = box_lat0[0] + lax.axis_index(PLANE) * (rows_here // RATIO)
    lon_start = box_lon0[0] + lax.axis_index("col") * (cols_here // RATIO)
    windows = []
    for _ in range(hours):
        global_state = global_hour(global_state, spec_filter, w_skip, w_mix, forward, inverse)
        coarse = jnp.einsum(
            "alc,ck->alk", global_state, w_decode, preferred_element_type=jnp.float32
        ).astype(jnp.bfloat16)
        coarse = lax.all_gather(coarse, "col", axis=1, tiled=True)
        coarse = jnp.pad(coarse, ((0, 0), (base, span), (0, 0)))
        coarse = lax.dynamic_slice_in_dim(coarse, box_lon0[0], base + span, 1)
        coarse = lax.all_gather(coarse, PLANE, axis=0, tiled=True)
        coarse = lax.dynamic_slice_in_dim(coarse, lon_start - box_lon0[0], wide, 1)
        coarse = jnp.pad(coarse, ((base, high), (0, 0), (0, 0)))
        coarse = lax.dynamic_slice_in_dim(coarse, lat_start, high, 0)
        windows.append(coarse)
    group = LANES // PACKED
    windows = jnp.stack(windows, axis=1)
    windows = jnp.pad(
        windows, ((0, 0), (0, 0), (0, STRIP * group - wide), (0, PACKED - windows.shape[3]))
    )
    windows = windows.reshape(high, hours * STRIP, LANES)
    return lambda after: (global_state, after), windows, jnp.arange(high, dtype=jnp.int32), prepared


def next_to(low, high, axis):
    count = lax.axis_size(axis)
    forward = [(i, i + 1) for i in range(count - 1)]
    backward = [(target, source) for source, target in forward]
    return lax.ppermute(low, axis, forward), lax.ppermute(high, axis, backward)


def grid_place(start_ref, total, base, extent):
    place = start_ref + base + lax.broadcasted_iota(jnp.int32, (extent, 1), 0)
    return (place >= 0) & (place < total)


def assemble_kernel(
    rows, cols, totals, high, lanes, place_ref, mid0_ref, mid1_ref, above_ref, below_ref,
    left_ref, right_ref, noisy_ref, noise_ref, blend_ref,
):
    inner = RIM - RIM_USED
    pad = (noisy_ref.shape[1] - cols) // 2
    width = noisy_ref.shape[1]
    for ref, mid_ref, rim, part in ((noisy_ref, mid0_ref, RIM, 0), (noise_ref, mid1_ref, inner, RIM)):
        ref[0:rim, pad : pad + cols, :] = above_ref[part : part + rim]
        ref[rim : rim + rows, pad : pad + cols, :] = mid_ref[...]
        ref[rim + rows :, pad : pad + cols, :] = below_ref[part : part + rim]
        skip = RIM - rim
        for side_ref, low, to in (
            (left_ref, 0, pad - rim),
            (right_ref, pad + cols, 0),
        ):
            side = side_ref[skip : skip + rows + 2 * rim].astype(jnp.float32)
            side = pltpu.roll(side, (to - part) % pad, 1)
            ref[:, low : low + pad, :] = side.astype(jnp.bfloat16)

    base = window_base()
    col = lax.broadcasted_iota(jnp.int32, (width, 1), 0) - pad
    col_in = grid_place(place_ref[1], totals[1], -pad, width)
    frac_col = ((col % RATIO).astype(jnp.float32) + 0.5) / RATIO
    col_base = jnp.where(col_in, (col + pad) // RATIO - pad // RATIO + base, FAR)
    group = LANES // PACKED
    point = lax.broadcasted_iota(jnp.int32, (width, group * high * STRIP), 1)
    point_lat = (point // STRIP % high).astype(jnp.float32)
    point_lon = (point % STRIP * group + point // (STRIP * high)).astype(jnp.float32)

    def weigh(index, carry):
        row = index - RIM
        whole = (row + 2 * RATIO) // RATIO - 2
        frac_row = ((row - whole * RATIO).astype(jnp.float32) + 0.5) / RATIO
        there = place_ref[0] + row
        row_base = jnp.where((there >= 0) & (there < totals[0]), whole + base, FAR)
        shifts = noisy_ref[index, :, :].astype(jnp.float32)
        lat = row_base.astype(jnp.float32) + shifts[:, lanes : lanes + 1]
        lon = col_base.astype(jnp.float32) + shifts[:, lanes + 1 : lanes + 2]
        from_lat = point_lat - lat
        from_lon = point_lon - lon
        weight_lat = jnp.where(
            from_lat == 0.0, 1.0 - frac_row, jnp.where(from_lat == 1.0, frac_row, 0.0)
        )
        weight_lon = jnp.where(
            from_lon == 0.0, 1.0 - frac_col, jnp.where(from_lon == 1.0, frac_col, 0.0)
        )
        blend_ref[index, :, :] = (weight_lat * weight_lon).astype(jnp.bfloat16)
        return carry

    lax.fori_loop(0, rows + 2 * RIM, weigh, 0)


def assemble(rows, cols, totals, high, lanes, place, mid0, mid1, above, below, left, right):
    inner = RIM - RIM_USED
    width = cols + 2 * left.shape[1]
    channels = mid0.shape[2]
    return pl.pallas_call(
        functools.partial(assemble_kernel, rows, cols, totals, high, lanes),
        out_shape=(
            jax.ShapeDtypeStruct((rows + 2 * RIM, width, channels), jnp.bfloat16),
            jax.ShapeDtypeStruct((rows + 2 * inner, width, channels), jnp.bfloat16),
            jax.ShapeDtypeStruct(
                (rows + 2 * RIM, width, LANES // PACKED * high * STRIP), jnp.bfloat16
            ),
        ),
        in_specs=[pl.BlockSpec(memory_space=pltpu.SMEM)]
        + [pl.BlockSpec(memory_space=pltpu.VMEM)] * 6,
        compiler_params=pltpu.CompilerParams(vmem_limit_bytes=40 * 2**20),
        cost_estimate=pl.CostEstimate(flops=2 * 10**8, bytes_accessed=10**7, transcendentals=0),
        name="assemble",
    )(place, mid0, mid1, above, below, left, right)


def silu(x):
    half = 0.5 * x
    return half + half * jnp.tanh(half)


def denoise_kernel(
    rows, cols, totals, variables, conds, place_ref, pick_ref, noisy_ref, noise_ref, blend_ref,
    strip_ref, first_w_ref, down_w_ref, up_w_ref, bridge_w_ref, last_w_ref, out_ref, stack_ref, first_ref, pooled_ref,
    lifted_ref, third_ref, pair_ref, spread_ref, window_ref,
):
    width = noisy_ref.shape[1]
    half = width // 2
    pad = (width - cols) // 2
    channels = noisy_ref.shape[2]
    f32, bf16 = jnp.float32, jnp.bfloat16
    col_in = grid_place(place_ref[1], totals[1], -pad, width).astype(f32)
    lane = lax.broadcasted_iota(jnp.int32, (1, channels), 1)
    is_state = lane < variables
    is_cond = (lane >= variables) & (lane < variables + conds)
    high = pick_ref.shape[0]
    strips = [strip_ref[pick_ref[index]].astype(f32) for index in range(high)]
    for hour in range(2):
        near = jnp.concatenate([s[hour * STRIP : (hour + 1) * STRIP] for s in strips], axis=0)
        for turn in range(LANES // PACKED):
            moved = pltpu.roll(near, (variables - turn * PACKED) % LANES, 1)
            window_ref[hour, turn * high * STRIP : (turn + 1) * high * STRIP, :] = jnp.where(
                is_cond, moved, 0.0
            ).astype(bf16)

    def flat(start, count, unit):
        return pl.ds(pl.multiple_of(start * unit, 16), count * unit)

    def inside(row, count):
        marks = []
        for step in range(count):
            there = place_ref[0] + row + step
            marks.append(col_in * jnp.where((there >= 0) & (there < totals[0]), 1.0, 0.0))
        return jnp.concatenate(marks, axis=0)

    def conv(source_ref, row, count, unit, weight_ref):
        lhs = jnp.concatenate(
            [source_ref[flat(row + step, count, unit), :] for step in range(3)], axis=1
        )
        wide = jnp.dot(lhs, weight_ref[...], preferred_element_type=f32)
        size = weight_ref.shape[1] // 3
        span = count * unit
        return (
            pltpu.roll(wide[:, :size], 1, 0)
            + wide[:, size : 2 * size]
            + pltpu.roll(wide[:, 2 * size :], span - 1, 0)
        )

    for hour in range(2):
        rim = RIM - RIM_USED * hour
        tall = rows + 2 * rim

        def stack(index, carry, hour=hour, rim=rim):
            here = flat(index * 2, 2, width)
            weights = blend_ref[pl.ds(index * 2 + RIM - rim, 2)].reshape(2 * width, -1)
            cond = jnp.dot(weights, window_ref[hour], preferred_element_type=f32).astype(bf16)
            if hour == 0:
                own = noisy_ref[pl.ds(index * 2, 2)].reshape(2 * width, channels)
            else:
                own = stack_ref[here, :]
            stack_ref[here, :] = jnp.where(is_state, own, cond)
            return carry

        lax.fori_loop(0, tall // 2, stack, 0)

        def make_first(index, carry, rim=rim):
            row = index * 8
            value = silu(conv(stack_ref, row, 8, width, first_w_ref)) * inside(row - rim + 1, 8)
            value = value.astype(bf16)
            first_ref[flat(row, 8, width), :] = value
            value = value.astype(f32)
            for step in range(4):
                at = 2 * step * width
                pair_ref[step] = value[at : at + width] + value[at + width : at + 2 * width]
                even = pair_ref[step, pl.ds(0, half, stride=2), :]
                odd = pair_ref[step, pl.ds(1, half, stride=2), :]
                pooled_ref[flat(index * 4 + step, 1, half), :] = ((even + odd) * 0.25).astype(bf16)
            return carry

        lax.fori_loop(0, (tall - 2) // 8, make_first, 0)

        half_rows = (tall - 2) // 2 - 2

        def make_lifted(index, carry, part=half_rows // 2):
            value = silu(conv(pooled_ref, index * part, part, half, down_w_ref)).astype(bf16)
            lifted_ref[flat(index * part, part, half), :] = jnp.dot(
                value, up_w_ref[...], preferred_element_type=f32
            )
            return carry

        lax.fori_loop(0, 2, make_lifted, 0)

        def make_third(index, carry, rim=rim):
            row = index * 4
            spreads = []
            for step in range(2):
                lifted = lifted_ref[flat(index * 2 + step, 1, half), :]
                spread_ref[step, pl.ds(0, half, stride=2), :] = lifted
                spread_ref[step, pl.ds(1, half, stride=2), :] = lifted
                spreads += [spread_ref[step]] * 2
            bridged = jnp.dot(
                first_ref[flat(row + 2, 4, width), :], bridge_w_ref[...], preferred_element_type=f32
            )
            value = silu(bridged + jnp.concatenate(spreads, axis=0))
            value = value * inside(row - rim + 3, 4)
            third_ref[flat(row, 4, width), :] = value.astype(bf16)
            return carry

        lax.fori_loop(0, half_rows // 2, make_third, 0)

        part = (rows + 2 * (rim - RIM_USED)) // 2 if hour == 0 else rows // 2

        def finish(index, carry, hour=hour, rim=rim, part=part):
            row = index * part
            skip = 1 if hour == 1 else 0
            fresh = conv(third_ref, row + skip, part, width, last_w_ref)
            own = stack_ref[flat(row + RIM_USED + skip, part, width), :].astype(f32)
            fresh = (own + fresh).astype(bf16)
            if hour == 0:
                noise = noise_ref[pl.ds(row, part)].reshape(part * width, channels).astype(f32)
                fresh = (fresh.astype(f32) + noise_level * noise) * inside(row - rim + RIM_USED, part)
                stack_ref[flat(row, part, width), :] = fresh.astype(bf16)
            else:
                for step in range(part):
                    at = step * width + pad
                    out_ref[row + step] = fresh[at : at + cols]
            return carry

        lax.fori_loop(0, 2, finish, 0)


def denoise(rows, cols, totals, variables, conds, place, pick, noisy, noise, blend, strips, weights):
    width, channels = noisy.shape[1:]
    tall = rows + 2 * RIM
    bf16, f32 = jnp.bfloat16, jnp.float32
    return pl.pallas_call(
        functools.partial(denoise_kernel, rows, cols, totals, variables, conds),
        out_shape=jax.ShapeDtypeStruct((rows, cols, channels), bf16),
        in_specs=[pl.BlockSpec(memory_space=pltpu.SMEM)] * 2
        + [pl.BlockSpec(memory_space=pltpu.VMEM)] * 9,
        scratch_shapes=[
            pltpu.VMEM((tall * width, channels), bf16),
            pltpu.VMEM((tall * width, channels), bf16),
            pltpu.VMEM((tall // 2 * width // 2, channels), bf16),
            pltpu.VMEM((tall // 2 * width // 2, channels), f32),
            pltpu.VMEM((tall * width, channels), bf16),
            pltpu.VMEM((4, width, channels), f32),
            pltpu.VMEM((2, width, channels), f32),
            pltpu.VMEM((2, blend.shape[2], channels), bf16),
        ],
        compiler_params=pltpu.CompilerParams(vmem_limit_bytes=40 * 2**20),
        cost_estimate=pl.CostEstimate(
            flops=10**10, bytes_accessed=10**7, transcendentals=4 * 10**6
        ),
        name="denoise",
    )(place, pick, noisy, noise, blend, strips, *weights)


def conv_weight(weight, depth, width):
    out, _, given = weight.shape
    weight = weight.reshape(out, 3, 3, given)
    weight = jnp.pad(weight, ((0, width - out), (0, 0), (0, 0), (0, depth - given)))
    return jnp.transpose(weight, (1, 3, 2, 0)).reshape(3 * depth, 3 * width)


def shards(
    global_state,
    spec_filter,
    w_skip,
    w_mix,
    w_decode,
    regional_state,
    noise_draws,
    w_first,
    w_down,
    w_up,
    w_bridge,
    w_last,
    box_lat0,
    box_lon0,
    stencil_lat,
    stencil_lon,
):
    hours = noise_draws.shape[0]
    rows_here, cols_here = regional_state.shape[1:]
    row_start = lax.axis_index(PLANE) * rows_here
    col_start = lax.axis_index("col") * cols_here
    total_rows = rows_here * lax.axis_size(PLANE)
    total_cols = cols_here * lax.axis_size("col")
    assert hours == 2

    variables = regional_state.shape[0]
    conds = w_decode.shape[1]
    lanes = variables + conds
    noisy = (
        regional_state.astype(jnp.float32) + noise_level * noise_draws[0].astype(jnp.float32)
    ).astype(jnp.bfloat16)
    lat_shift = stencil_lat - (row_start + jnp.arange(rows_here, dtype=jnp.int32))[:, None] // RATIO
    lon_shift = stencil_lon - (col_start + jnp.arange(cols_here, dtype=jnp.int32))[None, :] // RATIO
    cells = (rows_here, cols_here)
    mids = jnp.concatenate(
        [
            noisy,
            jnp.zeros((conds,) + cells, jnp.bfloat16),
            lat_shift.astype(jnp.bfloat16)[None],
            lon_shift.astype(jnp.bfloat16)[None],
            jnp.zeros((LANES - lanes - 2,) + cells, jnp.bfloat16),
            noise_draws[1],
            jnp.zeros((LANES - variables,) + cells, jnp.bfloat16),
        ],
        axis=0,
    )
    mids = jnp.transpose(mids.reshape((2, LANES) + cells), (0, 2, 3, 1))
    mid0, mid1 = mids[0], mids[1]
    inner = RIM - RIM_USED
    high = window_extent(rows_here)
    place = jnp.stack([row_start, col_start]).astype(jnp.int32)
    totals = (total_rows, total_cols)

    def prepare(after):
        lows = jnp.concatenate([mid0[rows_here - RIM :], mid1[rows_here - inner :]], axis=0)
        highs = jnp.concatenate([mid0[:RIM], mid1[:inner]], axis=0)
        above, below = next_to(lows, highs, PLANE)

        def rim_cols(first, first_inner):
            wide, thin = slice(first, first + RIM), slice(first_inner, first_inner + inner)
            noise = jnp.concatenate([above[RIM:, thin], mid1[:, thin], below[RIM:, thin]], axis=0)
            noise = jnp.pad(
                noise, ((RIM_USED, RIM_USED), (0, RIM_COLS - RIM - inner), (0, 0))
            )
            return jnp.concatenate(
                [
                    jnp.concatenate([above[:RIM, wide], mid0[:, wide], below[:RIM, wide]], axis=0),
                    noise,
                ],
                axis=1,
            )

        left, right = next_to(
            rim_cols(cols_here - RIM, cols_here - inner), rim_cols(0, 0), "col"
        )
        weights = (
            conv_weight(w_first, LANES, w_first.shape[0]),
            conv_weight(w_down, w_down.shape[2], w_down.shape[0]),
            w_up.T,
            w_bridge.T,
            conv_weight(w_last, w_last.shape[2], LANES),
        )
        return (mid0, mid1, above, below, left, right), weights

    by_latitude = lax.axis_size("col") == 4 and global_state.shape[0] % 4 == 0
    global_steps = global_by_latitude if by_latitude else global_by_channel
    finish, strips, pick, (parts, weights) = global_steps(
        hours, global_state, spec_filter, w_skip, w_mix, w_decode, box_lat0, box_lon0,
        rows_here, cols_here, prepare,
    )
    noisy, noise, blend = assemble(rows_here, cols_here, totals, high, lanes, place, *parts)
    regional_final = denoise(
        rows_here, cols_here, totals, variables, conds, place, pick, noisy, noise, blend, strips, weights
    )
    regional_final = jnp.transpose(regional_final[:, :, :variables], (2, 0, 1))
    return finish(regional_final)


def solution(mesh):
    return jax.shard_map(
        shards,
        mesh=mesh,
        in_specs=(
            P(PLANE, "col", None),
            P(None, None, "col"),
            P(),
            P(),
            P(),
            P(None, PLANE, "col"),
            P(None, None, PLANE, "col"),
            P(),
            P(),
            P(),
            P(),
            P(),
            P(),
            P(),
            P(PLANE, "col"),
            P(PLANE, "col"),
        ),
        out_specs=(P(PLANE, "col", None), P(None, PLANE, "col")),
        check_vma=False,
    )
```

```python
import functools
import math

import jax
import jax.numpy as jnp
import ml_dtypes
import numpy as np
from jax import lax
from jax.experimental import pallas as pl
from jax.experimental.pallas import tpu as pltpu
from jax.sharding import PartitionSpec as P

RATIO = 8
noise_level = 0.5
PLANE = ("grp", "row")
RIM = 9
RIM_USED = 4
LANES = 128
PACKED = 32
MODE_TILE = 64
STRIP = 8
FAR = -4096
RIM_COLS = 16


def fourier_tables(length, num_modes):
    position = np.arange(length, dtype=np.int64)[:, None]
    frequency = np.arange(num_modes, dtype=np.int64)[None, :]
    angle = (position * frequency % length).astype(np.float64) * (2.0 * math.pi / length)
    cosine = np.cos(angle)
    sine = np.sin(angle)
    factor = np.where(frequency == 0, 1.0, 2.0) / length
    forward = np.concatenate([cosine, -sine], axis=1).T.astype(ml_dtypes.bfloat16)
    inverse = np.concatenate([cosine * factor, -sine * factor], axis=1).astype(ml_dtypes.bfloat16)
    return forward, inverse


def round_up(size, unit):
    return -(-size // unit) * unit


def split_tables(length, num_modes):
    piece = length // 4
    place = np.arange(piece, dtype=np.int64)[:, None]

    def waves(mode):
        angle = (place * mode[None, :] % length).astype(np.float64) * (2.0 * math.pi / length)
        return np.cos(angle), np.sin(angle), np.where(mode == 0, 1.0, 2.0)[None, :] / length

    def padded(blocks, unit_rows, unit_cols):
        rows = []
        for row in blocks:
            cols = []
            for block in row:
                spare = [(0, -block.shape[0] % unit_rows), (0, -block.shape[1] % unit_cols)]
                cols.append(np.pad(block, spare))
            rows.append(np.concatenate(cols, axis=1))
        return np.concatenate(rows, axis=0).astype(ml_dtypes.bfloat16)

    forward, inverse = [], []
    for residue in (0, 2):
        cosine, sine, factor = waves(np.arange(residue, num_modes, 4))
        forward.append(padded([[cosine.T], [-sine.T]], MODE_TILE, LANES))
        inverse.append(padded([[cosine * factor, -sine * factor]], LANES, MODE_TILE))
    mode = np.arange(1, num_modes, 2)
    cosine, sine, factor = waves(mode)
    sign = np.where(mode % 4 == 1, 1.0, -1.0)[None, :]
    odd_forward = padded(
        [[cosine.T, (-sign * sine).T], [-sine.T, (-sign * cosine).T]], 2 * MODE_TILE, LANES
    )
    odd_inverse = padded(
        [
            [cosine * factor, -sine * factor],
            [-sign * sine * factor, -sign * cosine * factor],
        ],
        LANES,
        2 * MODE_TILE,
    )
    return tuple(
        jnp.asarray(table)
        for table in (np.stack(forward), odd_forward, np.stack(inverse), odd_inverse)
    )


def exchange(blocks, axis):
    return lax.all_to_all(blocks, axis, split_axis=0, concat_axis=0, tiled=True)


def spread(block, axis):
    return exchange(jnp.broadcast_to(block[None], (lax.axis_size(axis),) + block.shape), axis)


def filter_share(spec_filter):
    rows = 2 * spec_filter.shape[1]
    flat = spec_filter.reshape(rows, spec_filter.shape[2])
    share = rows // lax.axis_size(PLANE)
    mine = lax.dynamic_slice_in_dim(flat, lax.axis_index(PLANE) * share, share, 0)
    return mine.astype(jnp.bfloat16)


def every_channel(mine):
    count = lax.axis_size("col")
    me = lax.axis_index("col")
    blocks = [shift(mine, "col", -step) if step else mine for step in range(count)]
    ring = jnp.concatenate(blocks + blocks[:-1], axis=1)
    width = mine.shape[1]
    return lax.dynamic_slice_in_dim(ring, (count - me) % count * width, count * width, 1)


def gelu(x):
    slope = math.sqrt(2.0 / math.pi)
    half = 0.5 * x
    return half + half * jnp.tanh(x * (slope + (0.044715 * slope) * (x * x)))


def latitude_kernel(hours, turns, step, place_ref, *refs):
    piece_refs, refs = refs[:4], refs[4:]
    even_forward_ref, odd_forward_ref, even_inverse_ref, odd_inverse_ref = refs[:4]
    filter_ref, skip_ref, mix_ref, decode_ref = refs[4:8]
    out_refs, strip_ref = refs[8:12], refs[12]
    state_ref, spectral_ref, gain_ref, coarse_ref, near_ref, packed_ref = refs[13:]
    f32, bf16 = jnp.float32, jnp.bfloat16
    piece, channels = piece_refs[0].shape[1:]
    padded = state_ref.shape[0] // 4
    group = LANES // PACKED
    span = near_ref.shape[0]
    rows = span // group
    spare = jnp.zeros((padded - piece, channels), bf16)
    for index in range(4):
        for turn in range(turns):
            state_ref[
                index * padded : (index + 1) * padded, turn * channels : (turn + 1) * channels
            ] = jnp.concatenate([piece_refs[index][turn], spare], axis=0)

    modes = filter_ref.shape[0] // 2
    for index in range(channels // LANES):
        lanes = slice(index * LANES, (index + 1) * LANES)
        gain_ref[index, : 2 * modes, :] = filter_ref[:, lanes].astype(f32)
        gain_ref[index, 2 * modes :, :] = jnp.zeros((gain_ref.shape[1] - 2 * modes, LANES), f32)

    def gain_rows(low, count, stride):
        rows = pl.ds(low, count, stride=stride)
        tiles = [gain_ref[index, rows, :] for index in range(channels // LANES)]
        return jnp.concatenate(tiles * turns, axis=1)

    def gain(spectrum, low, stride):
        half = spectrum.shape[0] // 2
        real, imag = spectrum[:half], spectrum[half:]
        gain_real = gain_rows(low, half, stride)
        gain_imag = gain_rows(modes + low, half, stride)
        return jnp.concatenate(
            [
                (real * gain_real - imag * gain_imag).astype(bf16),
                (real * gain_imag + imag * gain_real).astype(bf16),
            ],
            axis=0,
        )

    def dot(left, right):
        return jnp.dot(left, right, preferred_element_type=f32)

    def advance(hour, carry):
        pieces = [
            state_ref[index * padded : (index + 1) * padded, :].astype(f32) for index in range(4)
        ]
        both, other = pieces[0] + pieces[2], pieces[1] + pieces[3]
        shares = []
        for index, mixed in enumerate((both + other, both - other)):
            spectrum = dot(even_forward_ref[index], mixed.astype(bf16))
            shares.append(dot(even_inverse_ref[index], gain(spectrum, 2 * index, 4)))
        mixed = jnp.concatenate([pieces[0] - pieces[2], pieces[1] - pieces[3]], axis=0)
        odd = gain(dot(odd_forward_ref[...], mixed.astype(bf16)), 1, 2)
        odd = dot(odd_inverse_ref[...], odd)
        for index in range(4):
            even = shares[0] + shares[1] if index % 2 == 0 else shares[0] - shares[1]
            part = odd[:padded] if index % 2 == 0 else odd[padded:]
            total = even + part if index < 2 else even - part
            spectral_ref[index * padded : (index + 1) * padded, :] = total.astype(bf16)

        def mix(index, carry):
            here = pl.ds(pl.multiple_of(index * padded, LANES), padded)
            for turn in range(turns):
                lanes = slice(turn * channels, (turn + 1) * channels)
                state = state_ref[here, lanes]
                summed = spectral_ref[here, lanes].astype(f32) + dot(state, skip_ref[...])
                activated = gelu(summed).astype(bf16)
                update = dot(activated, mix_ref[...])
                state_ref[here, lanes] = (state.astype(f32) + update).astype(bf16)
            return carry

        lax.fori_loop(0, 4, mix, 0)

        for index in range(2):
            here = pl.ds(pl.multiple_of(place_ref[index] * padded, LANES), padded)
            coarse = dot(state_ref[here, :], decode_ref[...])
            for turn in range(turns):
                coarse_ref[turn, index * piece : (index + 1) * piece, :] = coarse[
                    :piece, turn * LANES : (turn + 1) * LANES
                ]
        for turn in range(turns):
            near_ref[...] = coarse_ref[turn, pl.ds(place_ref[2], span), :]
            packed = near_ref[pl.ds(0, rows, stride=group), :]
            for sub in range(1, group):
                packed += pltpu.roll(near_ref[pl.ds(sub, rows, stride=group), :], sub * PACKED, 1)
            packed_ref[turn, pl.ds(pl.multiple_of(hour * rows, 8), rows), :] = packed
        return carry

    lax.fori_loop(0, hours, advance, 0)
    for index in range(4):
        for turn in range(turns):
            out_refs[index][turn] = state_ref[
                index * padded : index * padded + piece, turn * channels : (turn + 1) * channels
            ]
    for target in range(4):
        low = target * step // group
        for turn in range(turns):
            strip = [
                packed_ref[turn, hour * rows + low : hour * rows + low + STRIP, :]
                for hour in range(hours)
            ]
            strip_ref[target, turn * hours * STRIP : (turn + 1) * hours * STRIP, :] = jnp.concatenate(
                strip, axis=0
            ).astype(bf16)


def advance_latitude(hours, turn, step, place, pieces, tables, gains, w_skip, w_mix, w_decode):
    _, piece, channels = pieces[0].shape
    padded = round_up(piece, LANES)
    group = LANES // PACKED
    span = round_up(3 * step + STRIP * group, 8 * group)
    decode = jnp.pad(w_decode, ((0, 0), (0, LANES - w_decode.shape[1])))
    modes = gains.shape[0] // 2
    spare = max(4 * (tables[0].shape[1] // 2), 2 * (tables[1].shape[0] // 2)) - modes
    results = pl.pallas_call(
        functools.partial(latitude_kernel, hours, 1, step),
        grid=(1,),
        out_shape=tuple(jax.ShapeDtypeStruct((1, piece, channels), jnp.bfloat16) for _ in pieces)
        + (jax.ShapeDtypeStruct((4, hours * STRIP, LANES), jnp.bfloat16),),
        in_specs=[pl.BlockSpec(memory_space=pltpu.SMEM)]
        + [pl.BlockSpec((1, piece, channels), lambda i: (turn, 0, 0))] * 4
        + [pl.BlockSpec(memory_space=pltpu.VMEM)] * 8,
        scratch_shapes=[
            pltpu.VMEM((4 * padded, channels), jnp.bfloat16),
            pltpu.VMEM((4 * padded, channels), jnp.bfloat16),
            pltpu.VMEM((channels // LANES, gains.shape[0] + spare, LANES), jnp.float32),
            pltpu.VMEM((1, 2 * piece, LANES), jnp.float32),
            pltpu.VMEM((span, LANES), jnp.float32),
            pltpu.VMEM((1, hours * span // group, LANES), jnp.float32),
        ],
        compiler_params=pltpu.CompilerParams(vmem_limit_bytes=48 * 2**20),
        cost_estimate=pl.CostEstimate(
            flops=16 * 10**9, bytes_accessed=8 * 2**20, transcendentals=hours * 4 * piece * channels
        ),
        name="advance_latitude",
    )(place, *pieces, *tables, gains, w_skip, w_mix, decode)
    return results[:4], results[4]


def collate_kernel(count, place_ref, *refs):
    pieces, out_ref, sems = refs[:count], refs[count], refs[count + 1]
    copies = [
        pltpu.make_async_copy(
            piece, out_ref.at[pl.ds(place_ref[index], piece.shape[0])], sems.at[index]
        )
        for index, piece in enumerate(pieces)
    ]
    for copy in copies:
        copy.start()
    for copy in copies:
        copy.wait()


def collate(place, pieces):
    count = len(pieces)
    turns, piece, channels = pieces[0].shape
    return pl.pallas_call(
        functools.partial(collate_kernel, count),
        out_shape=jax.ShapeDtypeStruct((count * turns, piece, channels), pieces[0].dtype),
        in_specs=[pl.BlockSpec(memory_space=pltpu.SMEM)]
        + [pl.BlockSpec(memory_space=pltpu.VMEM)] * count,
        out_specs=pl.BlockSpec(memory_space=pl.ANY),
        scratch_shapes=[pltpu.SemaphoreType.DMA((count,))],
        name="collate",
    )(place, *pieces)


def shift(block, axis, step):
    count = lax.axis_size(axis)
    return lax.ppermute(block, axis, [(source, (source + step) % count) for source in range(count)])


def global_hour(current, spec_filter, w_skip, w_mix, forward, inverse):
    longitude = lax.all_to_all(current, "col", split_axis=2, concat_axis=1, tiled=True)
    spectrum = jnp.einsum("alc,ml->amc", longitude, forward, preferred_element_type=jnp.float32)
    num_modes = spec_filter.shape[1]
    real_part = spectrum[:, :num_modes, :]
    imag_part = spectrum[:, num_modes:, :]
    filt_real = spec_filter[0][None]
    filt_imag = spec_filter[1][None]
    mixed = jnp.concatenate(
        [
            real_part * filt_real - imag_part * filt_imag,
            real_part * filt_imag + imag_part * filt_real,
        ],
        axis=1,
    ).astype(jnp.bfloat16)
    filtered = jnp.einsum("amc,lm->alc", mixed, inverse, preferred_element_type=jnp.float32).astype(
        jnp.bfloat16
    )
    spectral = lax.all_to_all(filtered, "col", split_axis=1, concat_axis=2, tiled=True)
    skipped = jnp.einsum("alc,cd->ald", current, w_skip, preferred_element_type=jnp.float32)
    activated = jax.nn.gelu(spectral.astype(jnp.float32) + skipped).astype(jnp.bfloat16)
    update = jnp.einsum("ald,de->ale", activated, w_mix, preferred_element_type=jnp.float32)
    return (current.astype(jnp.float32) + update).astype(jnp.bfloat16)


def window_extent(cells):
    return (cells + RIM - 1) // RATIO + 3 - (-RIM // RATIO)


def window_base():
    return -(-RIM // RATIO)


def global_by_latitude(
    hours, global_state, spec_filter, w_skip, w_mix, w_decode, box_lat0, box_lon0, rows_here,
    cols_here, prepare,
):
    count = lax.axis_size("col")
    me = lax.axis_index("col")
    lats_here, piece, _ = global_state.shape
    turns = lats_here // count
    tables = split_tables(piece * count, spec_filter.shape[1])
    owners = [(me - step) % count * turns for step in range(count)]
    mine = filter_share(spec_filter)
    global_state, mine = lax.optimization_barrier((global_state, mine))
    received = []
    for step, owner in enumerate(owners):
        own = lax.dynamic_slice_in_dim(global_state, owner, turns, 0)
        received.append(shift(own, "col", -step) if step else own)
    wide = every_channel(mine)
    gains = spread(wide, PLANE).reshape(-1, wide.shape[1])
    prepared = prepare(wide)
    start = (box_lon0[0] - window_base() - me * piece) % (piece * count)
    place = jnp.stack([start // piece, (start // piece + 1) % count, start % piece]).astype(jnp.int32)
    outcome, strips = [], []
    for turn in range(turns):
        if turn == turns - 1:
            received, prepared = lax.optimization_barrier((received, prepared))
        blocks, strip = advance_latitude(
            hours, turn, cols_here // RATIO, place, received, tables, gains, w_skip, w_mix, w_decode
        )
        outcome.append(blocks)
        strips.append(strip)
    plane = lax.axis_size(PLANE)
    strips = jnp.concatenate(strips, axis=1)
    sent = jnp.broadcast_to(strips[None], (plane,) + strips.shape)
    got = exchange(sent.reshape((plane * count,) + strips.shape[1:]), PLANE + ("col",))
    outcome[-1], got = lax.optimization_barrier((outcome[-1], got))
    got = got.reshape((plane * lats_here, -1, LANES))
    lat = box_lat0[0] - window_base() + lax.axis_index(PLANE) * (rows_here // RATIO)
    lat = jnp.clip(lat + jnp.arange(window_extent(rows_here), dtype=jnp.int32), 0, plane * lats_here - 1)
    places = [owner + turn for turn in range(turns) for owner in owners]
    finals = [
        shift(block, "col", step) if step else block
        for blocks in outcome
        for step, block in enumerate(blocks)
    ]

    def finish(after):
        blocks, after = lax.optimization_barrier((finals, after))
        return collate(jnp.stack(places).astype(jnp.int32), blocks), after

    return finish, got, lat.astype(jnp.int32), prepared


def global_by_channel(
    hours, global_state, spec_filter, w_skip, w_mix, w_decode, box_lat0, box_lon0, rows_here,
    cols_here, prepare,
):
    count = lax.axis_size("col")
    prepared = prepare(global_state)
    forward, inverse = fourier_tables(global_state.shape[1] * count, spec_filter.shape[1])
    base = window_base()
    high, wide = window_extent(rows_here), window_extent(cols_here)
    span = (count - 1) * (cols_here // RATIO) + wide
    lat_start = box_lat0[0] + lax.axis_index(PLANE) * (rows_here // RATIO)
    lon_start = box_lon0[0] + lax.axis_index("col") * (cols_here // RATIO)
    windows = []
    for _ in range(hours):
        global_state = global_hour(global_state, spec_filter, w_skip, w_mix, forward, inverse)
        coarse = jnp.einsum(
            "alc,ck->alk", global_state, w_decode, preferred_element_type=jnp.float32
        ).astype(jnp.bfloat16)
        coarse = lax.all_gather(coarse, "col", axis=1, tiled=True)
        coarse = jnp.pad(coarse, ((0, 0), (base, span), (0, 0)))
        coarse = lax.dynamic_slice_in_dim(coarse, box_lon0[0], base + span, 1)
        coarse = lax.all_gather(coarse, PLANE, axis=0, tiled=True)
        coarse = lax.dynamic_slice_in_dim(coarse, lon_start - box_lon0[0], wide, 1)
        coarse = jnp.pad(coarse, ((base, high), (0, 0), (0, 0)))
        coarse = lax.dynamic_slice_in_dim(coarse, lat_start, high, 0)
        windows.append(coarse)
    group = LANES // PACKED
    windows = jnp.stack(windows, axis=1)
    windows = jnp.pad(
        windows, ((0, 0), (0, 0), (0, STRIP * group - wide), (0, PACKED - windows.shape[3]))
    )
    windows = windows.reshape(high, hours * STRIP, LANES)
    return lambda after: (global_state, after), windows, jnp.arange(high, dtype=jnp.int32), prepared


def next_to(low, high, axis):
    count = lax.axis_size(axis)
    forward = [(i, i + 1) for i in range(count - 1)]
    backward = [(target, source) for source, target in forward]
    return lax.ppermute(low, axis, forward), lax.ppermute(high, axis, backward)


def grid_place(start_ref, total, base, extent):
    place = start_ref + base + lax.broadcasted_iota(jnp.int32, (extent, 1), 0)
    return (place >= 0) & (place < total)


def assemble_kernel(
    rows, cols, totals, high, lanes, place_ref, mid0_ref, mid1_ref, above_ref, below_ref,
    left_ref, right_ref, noisy_ref, noise_ref, blend_ref,
):
    inner = RIM - RIM_USED
    pad = (noisy_ref.shape[1] - cols) // 2
    width = noisy_ref.shape[1]
    for ref, mid_ref, rim, part in ((noisy_ref, mid0_ref, RIM, 0), (noise_ref, mid1_ref, inner, RIM)):
        ref[0:rim, pad : pad + cols, :] = above_ref[part : part + rim]
        ref[rim : rim + rows, pad : pad + cols, :] = mid_ref[...]
        ref[rim + rows :, pad : pad + cols, :] = below_ref[part : part + rim]
        skip = RIM - rim
        for side_ref, low, to in (
            (left_ref, 0, pad - rim),
            (right_ref, pad + cols, 0),
        ):
            side = side_ref[skip : skip + rows + 2 * rim].astype(jnp.float32)
            side = pltpu.roll(side, (to - part) % pad, 1)
            ref[:, low : low + pad, :] = side.astype(jnp.bfloat16)

    base = window_base()
    col = lax.broadcasted_iota(jnp.int32, (width, 1), 0) - pad
    col_in = grid_place(place_ref[1], totals[1], -pad, width)
    frac_col = ((col % RATIO).astype(jnp.float32) + 0.5) / RATIO
    col_base = jnp.where(col_in, (col + pad) // RATIO - pad // RATIO + base, FAR)
    group = LANES // PACKED
    point = lax.broadcasted_iota(jnp.int32, (width, group * high * STRIP), 1)
    point_lat = (point // STRIP % high).astype(jnp.float32)
    point_lon = (point % STRIP * group + point // (STRIP * high)).astype(jnp.float32)

    def weigh(index, carry):
        row = index - RIM
        whole = (row + 2 * RATIO) // RATIO - 2
        frac_row = ((row - whole * RATIO).astype(jnp.float32) + 0.5) / RATIO
        there = place_ref[0] + row
        row_base = jnp.where((there >= 0) & (there < totals[0]), whole + base, FAR)
        shifts = noisy_ref[index, :, :].astype(jnp.float32)
        lat = row_base.astype(jnp.float32) + shifts[:, lanes : lanes + 1]
        lon = col_base.astype(jnp.float32) + shifts[:, lanes + 1 : lanes + 2]
        from_lat = point_lat - lat
        from_lon = point_lon - lon
        weight_lat = jnp.where(
            from_lat == 0.0, 1.0 - frac_row, jnp.where(from_lat == 1.0, frac_row, 0.0)
        )
        weight_lon = jnp.where(
            from_lon == 0.0, 1.0 - frac_col, jnp.where(from_lon == 1.0, frac_col, 0.0)
        )
        blend_ref[index, :, :] = (weight_lat * weight_lon).astype(jnp.bfloat16)
        return carry

    lax.fori_loop(0, rows + 2 * RIM, weigh, 0)


def assemble(rows, cols, totals, high, lanes, place, mid0, mid1, above, below, left, right):
    inner = RIM - RIM_USED
    width = cols + 2 * left.shape[1]
    channels = mid0.shape[2]
    return pl.pallas_call(
        functools.partial(assemble_kernel, rows, cols, totals, high, lanes),
        out_shape=(
            jax.ShapeDtypeStruct((rows + 2 * RIM, width, channels), jnp.bfloat16),
            jax.ShapeDtypeStruct((rows + 2 * inner, width, channels), jnp.bfloat16),
            jax.ShapeDtypeStruct(
                (rows + 2 * RIM, width, LANES // PACKED * high * STRIP), jnp.bfloat16
            ),
        ),
        in_specs=[pl.BlockSpec(memory_space=pltpu.SMEM)]
        + [pl.BlockSpec(memory_space=pltpu.VMEM)] * 6,
        compiler_params=pltpu.CompilerParams(vmem_limit_bytes=40 * 2**20),
        cost_estimate=pl.CostEstimate(flops=10**6, bytes_accessed=10**5, transcendentals=0),
        name="assemble",
    )(place, mid0, mid1, above, below, left, right)


def silu(x):
    half = 0.5 * x
    return half + half * jnp.tanh(half)


def denoise_kernel(
    rows, cols, totals, variables, conds, place_ref, pick_ref, noisy_ref, noise_ref, blend_ref,
    strip_ref, first_w_ref, down_w_ref, up_w_ref, bridge_w_ref, last_w_ref, out_ref, stack_ref, first_ref, pooled_ref,
    lifted_ref, third_ref, pair_ref, spread_ref, window_ref,
):
    width = noisy_ref.shape[1]
    half = width // 2
    pad = (width - cols) // 2
    channels = noisy_ref.shape[2]
    f32, bf16 = jnp.float32, jnp.bfloat16
    col_in = grid_place(place_ref[1], totals[1], -pad, width).astype(f32)
    lane = lax.broadcasted_iota(jnp.int32, (1, channels), 1)
    is_state = lane < variables
    is_cond = (lane >= variables) & (lane < variables + conds)
    high = pick_ref.shape[0]
    strips = [strip_ref[pick_ref[index]].astype(f32) for index in range(high)]
    for hour in range(2):
        near = jnp.concatenate([s[hour * STRIP : (hour + 1) * STRIP] for s in strips], axis=0)
        for turn in range(LANES // PACKED):
            moved = pltpu.roll(near, (variables - turn * PACKED) % LANES, 1)
            window_ref[hour, turn * high * STRIP : (turn + 1) * high * STRIP, :] = jnp.where(
                is_cond, moved, 0.0
            ).astype(bf16)

    def flat(start, count, unit):
        return pl.ds(pl.multiple_of(start * unit, 16), count * unit)

    def inside(row, count):
        marks = []
        for step in range(count):
            there = place_ref[0] + row + step
            marks.append(col_in * jnp.where((there >= 0) & (there < totals[0]), 1.0, 0.0))
        return jnp.concatenate(marks, axis=0)

    def conv(source_ref, row, count, unit, weight_ref):
        lhs = jnp.concatenate(
            [source_ref[flat(row + step, count, unit), :] for step in range(3)], axis=1
        )
        wide = jnp.dot(lhs, weight_ref[...], preferred_element_type=f32)
        size = weight_ref.shape[1] // 3
        span = count * unit
        return (
            pltpu.roll(wide[:, :size], 1, 0)
            + wide[:, size : 2 * size]
            + pltpu.roll(wide[:, 2 * size :], span - 1, 0)
        )

    for hour in range(2):
        rim = RIM - RIM_USED * hour
        tall = rows + 2 * rim

        def stack(index, carry, hour=hour, rim=rim):
            here = flat(index * 2, 2, width)
            weights = blend_ref[pl.ds(index * 2 + RIM - rim, 2)].reshape(2 * width, -1)
            cond = jnp.dot(weights, window_ref[hour], preferred_element_type=f32).astype(bf16)
            if hour == 0:
                own = noisy_ref[pl.ds(index * 2, 2)].reshape(2 * width, channels)
            else:
                own = stack_ref[here, :]
            stack_ref[here, :] = jnp.where(is_state, own, cond)
            return carry

        lax.fori_loop(0, tall // 2, stack, 0)

        def make_first(index, carry, rim=rim):
            row = index * 8
            value = silu(conv(stack_ref, row, 8, width, first_w_ref)) * inside(row - rim + 1, 8)
            value = value.astype(bf16)
            first_ref[flat(row, 8, width), :] = value
            value = value.astype(f32)
            for step in range(4):
                at = 2 * step * width
                pair_ref[step] = value[at : at + width] + value[at + width : at + 2 * width]
                even = pair_ref[step, pl.ds(0, half, stride=2), :]
                odd = pair_ref[step, pl.ds(1, half, stride=2), :]
                pooled_ref[flat(index * 4 + step, 1, half), :] = ((even + odd) * 0.25).astype(bf16)
            return carry

        lax.fori_loop(0, (tall - 2) // 8, make_first, 0)

        half_rows = (tall - 2) // 2 - 2

        def make_lifted(index, carry, part=half_rows // 2):
            value = silu(conv(pooled_ref, index * part, part, half, down_w_ref)).astype(bf16)
            lifted_ref[flat(index * part, part, half), :] = jnp.dot(
                value, up_w_ref[...], preferred_element_type=f32
            )
            return carry

        lax.fori_loop(0, 2, make_lifted, 0)

        def make_third(index, carry, rim=rim):
            row = index * 4
            spreads = []
            for step in range(2):
                lifted = lifted_ref[flat(index * 2 + step, 1, half), :]
                spread_ref[step, pl.ds(0, half, stride=2), :] = lifted
                spread_ref[step, pl.ds(1, half, stride=2), :] = lifted
                spreads += [spread_ref[step]] * 2
            bridged = jnp.dot(
                first_ref[flat(row + 2, 4, width), :], bridge_w_ref[...], preferred_element_type=f32
            )
            value = silu(bridged + jnp.concatenate(spreads, axis=0))
            value = value * inside(row - rim + 3, 4)
            third_ref[flat(row, 4, width), :] = value.astype(bf16)
            return carry

        lax.fori_loop(0, half_rows // 2, make_third, 0)

        part = (rows + 2 * (rim - RIM_USED)) // 2 if hour == 0 else rows // 2

        def finish(index, carry, hour=hour, rim=rim, part=part):
            row = index * part
            skip = 1 if hour == 1 else 0
            fresh = conv(third_ref, row + skip, part, width, last_w_ref)
            own = stack_ref[flat(row + RIM_USED + skip, part, width), :].astype(f32)
            fresh = (own + fresh).astype(bf16)
            if hour == 0:
                noise = noise_ref[pl.ds(row, part)].reshape(part * width, channels).astype(f32)
                fresh = (fresh.astype(f32) + noise_level * noise) * inside(row - rim + RIM_USED, part)
                stack_ref[flat(row, part, width), :] = fresh.astype(bf16)
            else:
                for step in range(part):
                    at = step * width + pad
                    out_ref[row + step] = fresh[at : at + cols]
            return carry

        lax.fori_loop(0, 2, finish, 0)


def denoise(rows, cols, totals, variables, conds, place, pick, noisy, noise, blend, strips, weights):
    width, channels = noisy.shape[1:]
    tall = rows + 2 * RIM
    bf16, f32 = jnp.bfloat16, jnp.float32
    return pl.pallas_call(
        functools.partial(denoise_kernel, rows, cols, totals, variables, conds),
        out_shape=jax.ShapeDtypeStruct((rows, cols, channels), bf16),
        in_specs=[pl.BlockSpec(memory_space=pltpu.SMEM)] * 2
        + [pl.BlockSpec(memory_space=pltpu.VMEM)] * 9,
        scratch_shapes=[
            pltpu.VMEM((tall * width, channels), bf16),
            pltpu.VMEM((tall * width, channels), bf16),
            pltpu.VMEM((tall // 2 * width // 2, channels), bf16),
            pltpu.VMEM((tall // 2 * width // 2, channels), f32),
            pltpu.VMEM((tall * width, channels), bf16),
            pltpu.VMEM((4, width, channels), f32),
            pltpu.VMEM((2, width, channels), f32),
            pltpu.VMEM((2, blend.shape[2], channels), bf16),
        ],
        compiler_params=pltpu.CompilerParams(vmem_limit_bytes=40 * 2**20),
        cost_estimate=pl.CostEstimate(flops=10**6, bytes_accessed=10**5, transcendentals=0),
        name="denoise",
    )(place, pick, noisy, noise, blend, strips, *weights)


def conv_weight(weight, depth, width):
    out, _, given = weight.shape
    weight = weight.reshape(out, 3, 3, given)
    weight = jnp.pad(weight, ((0, width - out), (0, 0), (0, 0), (0, depth - given)))
    return jnp.transpose(weight, (1, 3, 2, 0)).reshape(3 * depth, 3 * width)


def shards(
    global_state,
    spec_filter,
    w_skip,
    w_mix,
    w_decode,
    regional_state,
    noise_draws,
    w_first,
    w_down,
    w_up,
    w_bridge,
    w_last,
    box_lat0,
    box_lon0,
    stencil_lat,
    stencil_lon,
):
    hours = noise_draws.shape[0]
    rows_here, cols_here = regional_state.shape[1:]
    row_start = lax.axis_index(PLANE) * rows_here
    col_start = lax.axis_index("col") * cols_here
    total_rows = rows_here * lax.axis_size(PLANE)
    total_cols = cols_here * lax.axis_size("col")
    assert hours == 2

    variables = regional_state.shape[0]
    conds = w_decode.shape[1]
    lanes = variables + conds
    noisy = (
        regional_state.astype(jnp.float32) + noise_level * noise_draws[0].astype(jnp.float32)
    ).astype(jnp.bfloat16)
    lat_shift = stencil_lat - (row_start + jnp.arange(rows_here, dtype=jnp.int32))[:, None] // RATIO
    lon_shift = stencil_lon - (col_start + jnp.arange(cols_here, dtype=jnp.int32))[None, :] // RATIO
    cells = (rows_here, cols_here)
    mids = jnp.concatenate(
        [
            noisy,
            jnp.zeros((conds,) + cells, jnp.bfloat16),
            lat_shift.astype(jnp.bfloat16)[None],
            lon_shift.astype(jnp.bfloat16)[None],
            jnp.zeros((LANES - lanes - 2,) + cells, jnp.bfloat16),
            noise_draws[1],
            jnp.zeros((LANES - variables,) + cells, jnp.bfloat16),
        ],
        axis=0,
    )
    mids = jnp.transpose(mids.reshape((2, LANES) + cells), (0, 2, 3, 1))
    mid0, mid1 = mids[0], mids[1]
    inner = RIM - RIM_USED
    high = window_extent(rows_here)
    place = jnp.stack([row_start, col_start]).astype(jnp.int32)
    totals = (total_rows, total_cols)

    def prepare(after):
        lows = jnp.concatenate([mid0[rows_here - RIM :], mid1[rows_here - inner :]], axis=0)
        highs = jnp.concatenate([mid0[:RIM], mid1[:inner]], axis=0)
        lows, highs, _ = lax.optimization_barrier((lows, highs, after))
        above, below = next_to(lows, highs, PLANE)

        def rim_cols(first, first_inner):
            wide, thin = slice(first, first + RIM), slice(first_inner, first_inner + inner)
            noise = jnp.concatenate([above[RIM:, thin], mid1[:, thin], below[RIM:, thin]], axis=0)
            noise = jnp.pad(
                noise, ((RIM_USED, RIM_USED), (0, RIM_COLS - RIM - inner), (0, 0))
            )
            return jnp.concatenate(
                [
                    jnp.concatenate([above[:RIM, wide], mid0[:, wide], below[:RIM, wide]], axis=0),
                    noise,
                ],
                axis=1,
            )

        left, right = next_to(
            rim_cols(cols_here - RIM, cols_here - inner), rim_cols(0, 0), "col"
        )
        weights = (
            conv_weight(w_first, LANES, w_first.shape[0]),
            conv_weight(w_down, w_down.shape[2], w_down.shape[0]),
            w_up.T,
            w_bridge.T,
            conv_weight(w_last, w_last.shape[2], LANES),
        )
        return (mid0, mid1, above, below, left, right), weights

    by_latitude = lax.axis_size("col") == 4 and global_state.shape[0] % 4 == 0
    global_steps = global_by_latitude if by_latitude else global_by_channel
    finish, strips, pick, (parts, weights) = global_steps(
        hours, global_state, spec_filter, w_skip, w_mix, w_decode, box_lat0, box_lon0,
        rows_here, cols_here, prepare,
    )
    noisy, noise, blend = assemble(rows_here, cols_here, totals, high, lanes, place, *parts)
    regional_final = denoise(
        rows_here, cols_here, totals, variables, conds, place, pick, noisy, noise, blend, strips, weights
    )
    regional_final = jnp.transpose(regional_final[:, :, :variables], (2, 0, 1))
    return finish(regional_final)


def solution(mesh):
    return jax.shard_map(
        shards,
        mesh=mesh,
        in_specs=(
            P(PLANE, "col", None),
            P(None, None, "col"),
            P(),
            P(),
            P(),
            P(None, PLANE, "col"),
            P(None, None, PLANE, "col"),
            P(),
            P(),
            P(),
            P(),
            P(),
            P(),
            P(),
            P(PLANE, "col"),
            P(PLANE, "col"),
        ),
        out_specs=(P(PLANE, "col", None), P(None, PLANE, "col")),
        check_vma=False,
    )
```

```python
import functools
import math

import jax
import jax.numpy as jnp
import ml_dtypes
import numpy as np
from jax import lax
from jax.experimental import pallas as pl
from jax.experimental.pallas import tpu as pltpu
from jax.sharding import PartitionSpec as P

RATIO = 8
noise_level = 0.5
PLANE = ("grp", "row")
RIM = 9
RIM_USED = 4
LANES = 128
VMEM = 60 * 2**20
PACKED = 32
MODE_TILE = 64
STRIP = 8
FAR = -4096
RIM_COLS = 16


def fourier_tables(length, num_modes):
    position = np.arange(length, dtype=np.int64)[:, None]
    frequency = np.arange(num_modes, dtype=np.int64)[None, :]
    angle = (position * frequency % length).astype(np.float64) * (2.0 * math.pi / length)
    cosine = np.cos(angle)
    sine = np.sin(angle)
    factor = np.where(frequency == 0, 1.0, 2.0) / length
    forward = np.concatenate([cosine, -sine], axis=1).T.astype(ml_dtypes.bfloat16)
    inverse = np.concatenate([cosine * factor, -sine * factor], axis=1).astype(ml_dtypes.bfloat16)
    return forward, inverse


def round_up(size, unit):
    return -(-size // unit) * unit


def split_tables(length, num_modes):
    piece = length // 4
    place = np.arange(piece, dtype=np.int64)[:, None]

    def waves(mode):
        angle = (place * mode[None, :] % length).astype(np.float64) * (2.0 * math.pi / length)
        return np.cos(angle), np.sin(angle), np.where(mode == 0, 1.0, 2.0)[None, :] / length

    def padded(blocks, unit_rows, unit_cols):
        rows = []
        for row in blocks:
            cols = []
            for block in row:
                spare = [(0, -block.shape[0] % unit_rows), (0, -block.shape[1] % unit_cols)]
                cols.append(np.pad(block, spare))
            rows.append(np.concatenate(cols, axis=1))
        return np.concatenate(rows, axis=0).astype(ml_dtypes.bfloat16)

    forward, inverse = [], []
    for residue in (0, 2):
        cosine, sine, factor = waves(np.arange(residue, num_modes, 4))
        forward.append(padded([[cosine.T], [-sine.T]], MODE_TILE, LANES))
        inverse.append(padded([[cosine * factor, -sine * factor]], LANES, MODE_TILE))
    mode = np.arange(1, num_modes, 2)
    cosine, sine, factor = waves(mode)
    sign = np.where(mode % 4 == 1, 1.0, -1.0)[None, :]
    odd_forward = padded(
        [[cosine.T, (-sign * sine).T], [-sine.T, (-sign * cosine).T]], 2 * MODE_TILE, LANES
    )
    odd_inverse = padded(
        [
            [cosine * factor, -sine * factor],
            [-sign * sine * factor, -sign * cosine * factor],
        ],
        LANES,
        2 * MODE_TILE,
    )
    return tuple(
        jnp.asarray(table)
        for table in (np.stack(forward), odd_forward, np.stack(inverse), odd_inverse)
    )


def exchange(blocks, axis):
    return lax.all_to_all(blocks, axis, split_axis=0, concat_axis=0, tiled=True)


def spread(block, axis):
    return exchange(jnp.broadcast_to(block[None], (lax.axis_size(axis),) + block.shape), axis)


def filter_share(spec_filter):
    rows = 2 * spec_filter.shape[1]
    flat = spec_filter.reshape(rows, spec_filter.shape[2])
    share = rows // lax.axis_size(PLANE)
    mine = lax.dynamic_slice_in_dim(flat, lax.axis_index(PLANE) * share, share, 0)
    return mine.astype(jnp.bfloat16)


def every_channel(mine):
    count = lax.axis_size("col")
    me = lax.axis_index("col")
    blocks = [shift(mine, "col", -step) if step else mine for step in range(count)]
    ring = jnp.concatenate(blocks + blocks[:-1], axis=1)
    width = mine.shape[1]
    return lax.dynamic_slice_in_dim(ring, (count - me) % count * width, count * width, 1)


def gelu(x):
    slope = math.sqrt(2.0 / math.pi)
    half = 0.5 * x
    return half + half * jnp.tanh(x * (slope + (0.044715 * slope) * (x * x)))


def latitude_kernel(hours, turns, step, place_ref, *refs):
    piece_refs, refs = refs[:4], refs[4:]
    even_forward_ref, odd_forward_ref, even_inverse_ref, odd_inverse_ref = refs[:4]
    filter_ref, skip_ref, mix_ref, decode_ref = refs[4:8]
    out_refs, strip_ref = refs[8:12], refs[12]
    state_ref, spectral_ref, gain_ref, coarse_ref, near_ref, packed_ref = refs[13:]
    f32, bf16 = jnp.float32, jnp.bfloat16
    piece, channels = piece_refs[0].shape[1:]
    padded = state_ref.shape[0] // 4
    group = LANES // PACKED
    span = near_ref.shape[0]
    rows = span // group
    spare = jnp.zeros((padded - piece, channels), bf16)
    for index in range(4):
        for turn in range(turns):
            state_ref[
                index * padded : (index + 1) * padded, turn * channels : (turn + 1) * channels
            ] = jnp.concatenate([piece_refs[index][turn], spare], axis=0)

    modes = filter_ref.shape[0] // 2
    for index in range(channels // LANES):
        lanes = slice(index * LANES, (index + 1) * LANES)
        gain_ref[index, : 2 * modes, :] = filter_ref[:, lanes].astype(f32)
        gain_ref[index, 2 * modes :, :] = jnp.zeros((gain_ref.shape[1] - 2 * modes, LANES), f32)

    def gain_rows(low, count, stride):
        rows = pl.ds(low, count, stride=stride)
        tiles = [gain_ref[index, rows, :] for index in range(channels // LANES)]
        return jnp.concatenate(tiles * turns, axis=1)

    def gain(spectrum, low, stride):
        half = spectrum.shape[0] // 2
        real, imag = spectrum[:half], spectrum[half:]
        gain_real = gain_rows(low, half, stride)
        gain_imag = gain_rows(modes + low, half, stride)
        return jnp.concatenate(
            [
                (real * gain_real - imag * gain_imag).astype(bf16),
                (real * gain_imag + imag * gain_real).astype(bf16),
            ],
            axis=0,
        )

    def dot(left, right):
        return jnp.dot(left, right, preferred_element_type=f32)

    def advance(hour, carry):
        pieces = [
            state_ref[index * padded : (index + 1) * padded, :].astype(f32) for index in range(4)
        ]
        both, other = pieces[0] + pieces[2], pieces[1] + pieces[3]
        shares = []
        for index, mixed in enumerate((both + other, both - other)):
            spectrum = dot(even_forward_ref[index], mixed.astype(bf16))
            shares.append(dot(even_inverse_ref[index], gain(spectrum, 2 * index, 4)))
        mixed = jnp.concatenate([pieces[0] - pieces[2], pieces[1] - pieces[3]], axis=0)
        odd = gain(dot(odd_forward_ref[...], mixed.astype(bf16)), 1, 2)
        odd = dot(odd_inverse_ref[...], odd)
        for index in range(4):
            even = shares[0] + shares[1] if index % 2 == 0 else shares[0] - shares[1]
            part = odd[:padded] if index % 2 == 0 else odd[padded:]
            total = even + part if index < 2 else even - part
            spectral_ref[index * padded : (index + 1) * padded, :] = total.astype(bf16)

        def mix(index, carry):
            here = pl.ds(pl.multiple_of(index * padded, LANES), padded)
            for turn in range(turns):
                lanes = slice(turn * channels, (turn + 1) * channels)
                state = state_ref[here, lanes]
                summed = spectral_ref[here, lanes].astype(f32) + dot(state, skip_ref[...])
                activated = gelu(summed).astype(bf16)
                update = dot(activated, mix_ref[...])
                state_ref[here, lanes] = (state.astype(f32) + update).astype(bf16)
            return carry

        lax.fori_loop(0, 4, mix, 0)

        for index in range(2):
            here = pl.ds(pl.multiple_of(place_ref[index] * padded, LANES), padded)
            coarse = dot(state_ref[here, :], decode_ref[...])
            for turn in range(turns):
                coarse_ref[turn, index * piece : (index + 1) * piece, :] = coarse[
                    :piece, turn * LANES : (turn + 1) * LANES
                ]
        for turn in range(turns):
            near_ref[...] = coarse_ref[turn, pl.ds(place_ref[2], span), :]
            packed = near_ref[pl.ds(0, rows, stride=group), :]
            for sub in range(1, group):
                packed += pltpu.roll(near_ref[pl.ds(sub, rows, stride=group), :], sub * PACKED, 1)
            packed_ref[turn, pl.ds(pl.multiple_of(hour * rows, 8), rows), :] = packed
        return carry

    lax.fori_loop(0, hours, advance, 0)
    for index in range(4):
        for turn in range(turns):
            out_refs[index][turn] = state_ref[
                index * padded : index * padded + piece, turn * channels : (turn + 1) * channels
            ]
    for target in range(4):
        low = target * step // group
        for turn in range(turns):
            strip = [
                packed_ref[turn, hour * rows + low : hour * rows + low + STRIP, :]
                for hour in range(hours)
            ]
            strip_ref[target, turn * hours * STRIP : (turn + 1) * hours * STRIP, :] = jnp.concatenate(
                strip, axis=0
            ).astype(bf16)


def advance_latitude(hours, turn, step, place, pieces, tables, gains, w_skip, w_mix, w_decode):
    _, piece, channels = pieces[0].shape
    padded = round_up(piece, LANES)
    group = LANES // PACKED
    span = round_up(3 * step + STRIP * group, 8 * group)
    decode = jnp.pad(w_decode, ((0, 0), (0, LANES - w_decode.shape[1])))
    modes = gains.shape[0] // 2
    spare = max(4 * (tables[0].shape[1] // 2), 2 * (tables[1].shape[0] // 2)) - modes
    results = pl.pallas_call(
        functools.partial(latitude_kernel, hours, 1, step),
        grid=(1,),
        out_shape=tuple(jax.ShapeDtypeStruct((1, piece, channels), jnp.bfloat16) for _ in pieces)
        + (jax.ShapeDtypeStruct((4, hours * STRIP, LANES), jnp.bfloat16),),
        in_specs=[pl.BlockSpec(memory_space=pltpu.SMEM)]
        + [pl.BlockSpec((1, piece, channels), lambda i: (turn, 0, 0))] * 4
        + [pl.BlockSpec(memory_space=pltpu.VMEM)] * 8,
        scratch_shapes=[
            pltpu.VMEM((4 * padded, channels), jnp.bfloat16),
            pltpu.VMEM((4 * padded, channels), jnp.bfloat16),
            pltpu.VMEM((channels // LANES, gains.shape[0] + spare, LANES), jnp.float32),
            pltpu.VMEM((1, 2 * piece, LANES), jnp.float32),
            pltpu.VMEM((span, LANES), jnp.float32),
            pltpu.VMEM((1, hours * span // group, LANES), jnp.float32),
        ],
        compiler_params=pltpu.CompilerParams(vmem_limit_bytes=VMEM),
        cost_estimate=pl.CostEstimate(
            flops=16 * 10**9, bytes_accessed=8 * 2**20, transcendentals=hours * 4 * piece * channels
        ),
        name="advance_latitude",
    )(place, *pieces, *tables, gains, w_skip, w_mix, decode)
    return results[:4], results[4]


def collate_kernel(count, place_ref, *refs):
    pieces, out_ref, sems = refs[:count], refs[count], refs[count + 1]
    copies = [
        pltpu.make_async_copy(
            piece, out_ref.at[pl.ds(place_ref[index], piece.shape[0])], sems.at[index]
        )
        for index, piece in enumerate(pieces)
    ]
    for copy in copies:
        copy.start()
    for copy in copies:
        copy.wait()


def collate(place, pieces):
    count = len(pieces)
    turns, piece, channels = pieces[0].shape
    return pl.pallas_call(
        functools.partial(collate_kernel, count),
        out_shape=jax.ShapeDtypeStruct((count * turns, piece, channels), pieces[0].dtype),
        in_specs=[pl.BlockSpec(memory_space=pltpu.SMEM)]
        + [pl.BlockSpec(memory_space=pltpu.VMEM)] * count,
        out_specs=pl.BlockSpec(memory_space=pl.ANY),
        scratch_shapes=[pltpu.SemaphoreType.DMA((count,))],
        name="collate",
    )(place, *pieces)


def shift(block, axis, step):
    count = lax.axis_size(axis)
    return lax.ppermute(block, axis, [(source, (source + step) % count) for source in range(count)])


def global_hour(current, spec_filter, w_skip, w_mix, forward, inverse):
    longitude = lax.all_to_all(current, "col", split_axis=2, concat_axis=1, tiled=True)
    spectrum = jnp.einsum("alc,ml->amc", longitude, forward, preferred_element_type=jnp.float32)
    num_modes = spec_filter.shape[1]
    real_part = spectrum[:, :num_modes, :]
    imag_part = spectrum[:, num_modes:, :]
    filt_real = spec_filter[0][None]
    filt_imag = spec_filter[1][None]
    mixed = jnp.concatenate(
        [
            real_part * filt_real - imag_part * filt_imag,
            real_part * filt_imag + imag_part * filt_real,
        ],
        axis=1,
    ).astype(jnp.bfloat16)
    filtered = jnp.einsum("amc,lm->alc", mixed, inverse, preferred_element_type=jnp.float32).astype(
        jnp.bfloat16
    )
    spectral = lax.all_to_all(filtered, "col", split_axis=1, concat_axis=2, tiled=True)
    skipped = jnp.einsum("alc,cd->ald", current, w_skip, preferred_element_type=jnp.float32)
    activated = jax.nn.gelu(spectral.astype(jnp.float32) + skipped).astype(jnp.bfloat16)
    update = jnp.einsum("ald,de->ale", activated, w_mix, preferred_element_type=jnp.float32)
    return (current.astype(jnp.float32) + update).astype(jnp.bfloat16)


def window_extent(cells):
    return (cells + RIM - 1) // RATIO + 3 - (-RIM // RATIO)


def window_base():
    return -(-RIM // RATIO)


def global_by_latitude(
    hours, global_state, spec_filter, w_skip, w_mix, w_decode, box_lat0, box_lon0, rows_here,
    cols_here, prepare,
):
    count = lax.axis_size("col")
    me = lax.axis_index("col")
    lats_here, piece, _ = global_state.shape
    turns = lats_here // count
    tables = split_tables(piece * count, spec_filter.shape[1])
    owners = [(me - step) % count * turns for step in range(count)]
    mine = filter_share(spec_filter)
    global_state, mine = lax.optimization_barrier((global_state, mine))
    received = []
    for step, owner in enumerate(owners):
        own = lax.dynamic_slice_in_dim(global_state, owner, turns, 0)
        received.append(shift(own, "col", -step) if step else own)
    wide = every_channel(mine)
    gains = spread(wide, PLANE).reshape(-1, wide.shape[1])
    prepared = prepare(wide)
    start = (box_lon0[0] - window_base() - me * piece) % (piece * count)
    place = jnp.stack([start // piece, (start // piece + 1) % count, start % piece]).astype(jnp.int32)
    received, prepared = lax.optimization_barrier((received, prepared))
    outcome, strips = [], []
    for turn in range(turns):
        blocks, strip = advance_latitude(
            hours, turn, cols_here // RATIO, place, received, tables, gains, w_skip, w_mix, w_decode
        )
        if turn < turns - 1:
            blocks = [shift(block, "col", step) if step else block for step, block in enumerate(blocks)]
        outcome.append(blocks)
        strips.append(strip)
    plane = lax.axis_size(PLANE)
    strips, outcome[:-1] = lax.optimization_barrier((jnp.concatenate(strips, axis=1), outcome[:-1]))
    sent = jnp.broadcast_to(strips[None], (plane,) + strips.shape)
    got = exchange(sent.reshape((plane * count,) + strips.shape[1:]), PLANE + ("col",))
    outcome[-1], got = lax.optimization_barrier((outcome[-1], got))
    got = got.reshape((plane * lats_here, -1, LANES))
    lat = box_lat0[0] - window_base() + lax.axis_index(PLANE) * (rows_here // RATIO)
    lat = jnp.clip(lat + jnp.arange(window_extent(rows_here), dtype=jnp.int32), 0, plane * lats_here - 1)
    places = [owner + turn for turn in range(turns) for owner in owners]
    outcome[-1] = [
        shift(block, "col", step) if step else block for step, block in enumerate(outcome[-1])
    ]
    finals = sum(outcome, [])

    def finish(after):
        blocks, after = lax.optimization_barrier((finals, after))
        return collate(jnp.stack(places).astype(jnp.int32), blocks), after

    return finish, got, lat.astype(jnp.int32), prepared


def global_by_channel(
    hours, global_state, spec_filter, w_skip, w_mix, w_decode, box_lat0, box_lon0, rows_here,
    cols_here, prepare,
):
    count = lax.axis_size("col")
    prepared = prepare(global_state)
    forward, inverse = fourier_tables(global_state.shape[1] * count, spec_filter.shape[1])
    base = window_base()
    high, wide = window_extent(rows_here), window_extent(cols_here)
    span = (count - 1) * (cols_here // RATIO) + wide
    lat_start = box_lat0[0] + lax.axis_index(PLANE) * (rows_here // RATIO)
    lon_start = box_lon0[0] + lax.axis_index("col") * (cols_here // RATIO)
    windows = []
    for _ in range(hours):
        global_state = global_hour(global_state, spec_filter, w_skip, w_mix, forward, inverse)
        coarse = jnp.einsum(
            "alc,ck->alk", global_state, w_decode, preferred_element_type=jnp.float32
        ).astype(jnp.bfloat16)
        coarse = lax.all_gather(coarse, "col", axis=1, tiled=True)
        coarse = jnp.pad(coarse, ((0, 0), (base, span), (0, 0)))
        coarse = lax.dynamic_slice_in_dim(coarse, box_lon0[0], base + span, 1)
        coarse = lax.all_gather(coarse, PLANE, axis=0, tiled=True)
        coarse = lax.dynamic_slice_in_dim(coarse, lon_start - box_lon0[0], wide, 1)
        coarse = jnp.pad(coarse, ((base, high), (0, 0), (0, 0)))
        coarse = lax.dynamic_slice_in_dim(coarse, lat_start, high, 0)
        windows.append(coarse)
    group = LANES // PACKED
    windows = jnp.stack(windows, axis=1)
    windows = jnp.pad(
        windows, ((0, 0), (0, 0), (0, STRIP * group - wide), (0, PACKED - windows.shape[3]))
    )
    windows = windows.reshape(high, hours * STRIP, LANES)
    return lambda after: (global_state, after), windows, jnp.arange(high, dtype=jnp.int32), prepared


def next_to(low, high, axis):
    count = lax.axis_size(axis)
    forward = [(i, i + 1) for i in range(count - 1)]
    backward = [(target, source) for source, target in forward]
    return lax.ppermute(low, axis, forward), lax.ppermute(high, axis, backward)


def grid_place(start_ref, total, base, extent):
    place = start_ref + base + lax.broadcasted_iota(jnp.int32, (extent, 1), 0)
    return (place >= 0) & (place < total)


def assemble_kernel(
    rows, cols, totals, high, lanes, place_ref, mid0_ref, mid1_ref, above_ref, below_ref,
    left_ref, right_ref, noisy_ref, noise_ref, blend_ref,
):
    inner = RIM - RIM_USED
    pad = (noisy_ref.shape[1] - cols) // 2
    width = noisy_ref.shape[1]
    for ref, mid_ref, rim, part in ((noisy_ref, mid0_ref, RIM, 0), (noise_ref, mid1_ref, inner, RIM)):
        ref[0:rim, pad : pad + cols, :] = above_ref[part : part + rim]
        ref[rim : rim + rows, pad : pad + cols, :] = mid_ref[...]
        ref[rim + rows :, pad : pad + cols, :] = below_ref[part : part + rim]
        skip = RIM - rim
        for side_ref, low, to in (
            (left_ref, 0, pad - rim),
            (right_ref, pad + cols, 0),
        ):
            side = side_ref[skip : skip + rows + 2 * rim].astype(jnp.float32)
            side = pltpu.roll(side, (to - part) % pad, 1)
            ref[:, low : low + pad, :] = side.astype(jnp.bfloat16)

    base = window_base()
    col = lax.broadcasted_iota(jnp.int32, (width, 1), 0) - pad
    col_in = grid_place(place_ref[1], totals[1], -pad, width)
    frac_col = ((col % RATIO).astype(jnp.float32) + 0.5) / RATIO
    col_base = jnp.where(col_in, (col + pad) // RATIO - pad // RATIO + base, FAR)
    group = LANES // PACKED
    point = lax.broadcasted_iota(jnp.int32, (width, group * high * STRIP), 1)
    point_lat = (point // STRIP % high).astype(jnp.float32)
    point_lon = (point % STRIP * group + point // (STRIP * high)).astype(jnp.float32)

    def weigh(index, carry):
        row = index - RIM
        whole = (row + 2 * RATIO) // RATIO - 2
        frac_row = ((row - whole * RATIO).astype(jnp.float32) + 0.5) / RATIO
        there = place_ref[0] + row
        row_base = jnp.where((there >= 0) & (there < totals[0]), whole + base, FAR)
        shifts = noisy_ref[index, :, :].astype(jnp.float32)
        lat = row_base.astype(jnp.float32) + shifts[:, lanes : lanes + 1]
        lon = col_base.astype(jnp.float32) + shifts[:, lanes + 1 : lanes + 2]
        from_lat = point_lat - lat
        from_lon = point_lon - lon
        weight_lat = jnp.where(
            from_lat == 0.0, 1.0 - frac_row, jnp.where(from_lat == 1.0, frac_row, 0.0)
        )
        weight_lon = jnp.where(
            from_lon == 0.0, 1.0 - frac_col, jnp.where(from_lon == 1.0, frac_col, 0.0)
        )
        blend_ref[index, :, :] = (weight_lat * weight_lon).astype(jnp.bfloat16)
        return carry

    lax.fori_loop(0, rows + 2 * RIM, weigh, 0)


def assemble(rows, cols, totals, high, lanes, place, mid0, mid1, above, below, left, right):
    inner = RIM - RIM_USED
    width = cols + 2 * left.shape[1]
    channels = mid0.shape[2]
    return pl.pallas_call(
        functools.partial(assemble_kernel, rows, cols, totals, high, lanes),
        out_shape=(
            jax.ShapeDtypeStruct((rows + 2 * RIM, width, channels), jnp.bfloat16),
            jax.ShapeDtypeStruct((rows + 2 * inner, width, channels), jnp.bfloat16),
            jax.ShapeDtypeStruct(
                (rows + 2 * RIM, width, LANES // PACKED * high * STRIP), jnp.bfloat16
            ),
        ),
        in_specs=[pl.BlockSpec(memory_space=pltpu.SMEM)]
        + [pl.BlockSpec(memory_space=pltpu.VMEM)] * 6,
        compiler_params=pltpu.CompilerParams(vmem_limit_bytes=VMEM),
        cost_estimate=pl.CostEstimate(flops=10**6, bytes_accessed=10**5, transcendentals=0),
        name="assemble",
    )(place, mid0, mid1, above, below, left, right)


def silu(x):
    half = 0.5 * x
    return half + half * jnp.tanh(half)


def denoise_kernel(
    rows, cols, totals, variables, conds, place_ref, pick_ref, noisy_ref, noise_ref, blend_ref,
    strip_ref, first_w_ref, down_w_ref, up_w_ref, bridge_w_ref, last_w_ref, out_ref, stack_ref, first_ref, pooled_ref,
    lifted_ref, third_ref, pair_ref, spread_ref, window_ref,
):
    width = noisy_ref.shape[1]
    half = width // 2
    pad = (width - cols) // 2
    channels = noisy_ref.shape[2]
    f32, bf16 = jnp.float32, jnp.bfloat16
    col_in = grid_place(place_ref[1], totals[1], -pad, width).astype(f32)
    lane = lax.broadcasted_iota(jnp.int32, (1, channels), 1)
    is_state = lane < variables
    is_cond = (lane >= variables) & (lane < variables + conds)
    high = pick_ref.shape[0]
    strips = [strip_ref[pick_ref[index]].astype(f32) for index in range(high)]
    for hour in range(2):
        near = jnp.concatenate([s[hour * STRIP : (hour + 1) * STRIP] for s in strips], axis=0)
        for turn in range(LANES // PACKED):
            moved = pltpu.roll(near, (variables - turn * PACKED) % LANES, 1)
            window_ref[hour, turn * high * STRIP : (turn + 1) * high * STRIP, :] = jnp.where(
                is_cond, moved, 0.0
            ).astype(bf16)

    def flat(start, count, unit):
        return pl.ds(pl.multiple_of(start * unit, 16), count * unit)

    def inside(row, count):
        marks = []
        for step in range(count):
            there = place_ref[0] + row + step
            marks.append(col_in * jnp.where((there >= 0) & (there < totals[0]), 1.0, 0.0))
        return jnp.concatenate(marks, axis=0)

    def conv(source_ref, row, count, unit, weight_ref):
        lhs = jnp.concatenate(
            [source_ref[flat(row + step, count, unit), :] for step in range(3)], axis=1
        )
        wide = jnp.dot(lhs, weight_ref[...], preferred_element_type=f32)
        size = weight_ref.shape[1] // 3
        span = count * unit
        return (
            pltpu.roll(wide[:, :size], 1, 0)
            + wide[:, size : 2 * size]
            + pltpu.roll(wide[:, 2 * size :], span - 1, 0)
        )

    for hour in range(2):
        rim = RIM - RIM_USED * hour
        tall = rows + 2 * rim

        def stack(index, carry, hour=hour, rim=rim):
            here = flat(index * 2, 2, width)
            weights = blend_ref[pl.ds(index * 2 + RIM - rim, 2)].reshape(2 * width, -1)
            cond = jnp.dot(weights, window_ref[hour], preferred_element_type=f32).astype(bf16)
            if hour == 0:
                own = noisy_ref[pl.ds(index * 2, 2)].reshape(2 * width, channels)
            else:
                own = stack_ref[here, :]
            stack_ref[here, :] = jnp.where(is_state, own, cond)
            return carry

        lax.fori_loop(0, tall // 2, stack, 0)

        def make_first(index, carry, rim=rim):
            row = index * 8
            value = silu(conv(stack_ref, row, 8, width, first_w_ref)) * inside(row - rim + 1, 8)
            value = value.astype(bf16)
            first_ref[flat(row, 8, width), :] = value
            value = value.astype(f32)
            for step in range(4):
                at = 2 * step * width
                pair_ref[step] = value[at : at + width] + value[at + width : at + 2 * width]
                even = pair_ref[step, pl.ds(0, half, stride=2), :]
                odd = pair_ref[step, pl.ds(1, half, stride=2), :]
                pooled_ref[flat(index * 4 + step, 1, half), :] = ((even + odd) * 0.25).astype(bf16)
            return carry

        lax.fori_loop(0, (tall - 2) // 8, make_first, 0)

        half_rows = (tall - 2) // 2 - 2

        def make_lifted(index, carry, part=half_rows // 2):
            value = silu(conv(pooled_ref, index * part, part, half, down_w_ref)).astype(bf16)
            lifted_ref[flat(index * part, part, half), :] = jnp.dot(
                value, up_w_ref[...], preferred_element_type=f32
            )
            return carry

        lax.fori_loop(0, 2, make_lifted, 0)

        def make_third(index, carry, rim=rim):
            row = index * 4
            spreads = []
            for step in range(2):
                lifted = lifted_ref[flat(index * 2 + step, 1, half), :]
                spread_ref[step, pl.ds(0, half, stride=2), :] = lifted
                spread_ref[step, pl.ds(1, half, stride=2), :] = lifted
                spreads += [spread_ref[step]] * 2
            bridged = jnp.dot(
                first_ref[flat(row + 2, 4, width), :], bridge_w_ref[...], preferred_element_type=f32
            )
            value = silu(bridged + jnp.concatenate(spreads, axis=0))
            value = value * inside(row - rim + 3, 4)
            third_ref[flat(row, 4, width), :] = value.astype(bf16)
            return carry

        lax.fori_loop(0, half_rows // 2, make_third, 0)

        part = (rows + 2 * (rim - RIM_USED)) // 2 if hour == 0 else rows // 2

        def finish(index, carry, hour=hour, rim=rim, part=part):
            row = index * part
            skip = 1 if hour == 1 else 0
            fresh = conv(third_ref, row + skip, part, width, last_w_ref)
            own = stack_ref[flat(row + RIM_USED + skip, part, width), :].astype(f32)
            fresh = (own + fresh).astype(bf16)
            if hour == 0:
                noise = noise_ref[pl.ds(row, part)].reshape(part * width, channels).astype(f32)
                fresh = (fresh.astype(f32) + noise_level * noise) * inside(row - rim + RIM_USED, part)
                stack_ref[flat(row, part, width), :] = fresh.astype(bf16)
            else:
                for step in range(part):
                    at = step * width + pad
                    out_ref[row + step] = fresh[at : at + cols]
            return carry

        lax.fori_loop(0, 2, finish, 0)


def denoise(rows, cols, totals, variables, conds, place, pick, noisy, noise, blend, strips, weights):
    width, channels = noisy.shape[1:]
    tall = rows + 2 * RIM
    bf16, f32 = jnp.bfloat16, jnp.float32
    return pl.pallas_call(
        functools.partial(denoise_kernel, rows, cols, totals, variables, conds),
        out_shape=jax.ShapeDtypeStruct((rows, cols, channels), bf16),
        in_specs=[pl.BlockSpec(memory_space=pltpu.SMEM)] * 2
        + [pl.BlockSpec(memory_space=pltpu.VMEM)] * 9,
        scratch_shapes=[
            pltpu.VMEM((tall * width, channels), bf16),
            pltpu.VMEM((tall * width, channels), bf16),
            pltpu.VMEM((tall // 2 * width // 2, channels), bf16),
            pltpu.VMEM((tall // 2 * width // 2, channels), f32),
            pltpu.VMEM((tall * width, channels), bf16),
            pltpu.VMEM((4, width, channels), f32),
            pltpu.VMEM((2, width, channels), f32),
            pltpu.VMEM((2, blend.shape[2], channels), bf16),
        ],
        compiler_params=pltpu.CompilerParams(vmem_limit_bytes=VMEM),
        cost_estimate=pl.CostEstimate(flops=10**6, bytes_accessed=10**5, transcendentals=0),
        name="denoise",
    )(place, pick, noisy, noise, blend, strips, *weights)


def conv_weight(weight, depth, width):
    out, _, given = weight.shape
    weight = weight.reshape(out, 3, 3, given)
    weight = jnp.pad(weight, ((0, width - out), (0, 0), (0, 0), (0, depth - given)))
    return jnp.transpose(weight, (1, 3, 2, 0)).reshape(3 * depth, 3 * width)


def shards(
    global_state,
    spec_filter,
    w_skip,
    w_mix,
    w_decode,
    regional_state,
    noise_draws,
    w_first,
    w_down,
    w_up,
    w_bridge,
    w_last,
    box_lat0,
    box_lon0,
    stencil_lat,
    stencil_lon,
):
    hours = noise_draws.shape[0]
    rows_here, cols_here = regional_state.shape[1:]
    row_start = lax.axis_index(PLANE) * rows_here
    col_start = lax.axis_index("col") * cols_here
    total_rows = rows_here * lax.axis_size(PLANE)
    total_cols = cols_here * lax.axis_size("col")
    assert hours == 2

    variables = regional_state.shape[0]
    conds = w_decode.shape[1]
    lanes = variables + conds
    noisy = (
        regional_state.astype(jnp.float32) + noise_level * noise_draws[0].astype(jnp.float32)
    ).astype(jnp.bfloat16)
    lat_shift = stencil_lat - (row_start + jnp.arange(rows_here, dtype=jnp.int32))[:, None] // RATIO
    lon_shift = stencil_lon - (col_start + jnp.arange(cols_here, dtype=jnp.int32))[None, :] // RATIO
    cells = (rows_here, cols_here)
    mids = jnp.concatenate(
        [
            noisy,
            jnp.zeros((conds,) + cells, jnp.bfloat16),
            lat_shift.astype(jnp.bfloat16)[None],
            lon_shift.astype(jnp.bfloat16)[None],
            jnp.zeros((LANES - lanes - 2,) + cells, jnp.bfloat16),
            noise_draws[1],
            jnp.zeros((LANES - variables,) + cells, jnp.bfloat16),
        ],
        axis=0,
    )
    mids = jnp.transpose(mids.reshape((2, LANES) + cells), (0, 2, 3, 1))
    mid0, mid1 = mids[0], mids[1]
    inner = RIM - RIM_USED
    high = window_extent(rows_here)
    place = jnp.stack([row_start, col_start]).astype(jnp.int32)
    totals = (total_rows, total_cols)

    def prepare(after):
        lows = jnp.concatenate([mid0[rows_here - RIM :], mid1[rows_here - inner :]], axis=0)
        highs = jnp.concatenate([mid0[:RIM], mid1[:inner]], axis=0)
        lows, highs, _ = lax.optimization_barrier((lows, highs, after))
        above, below = next_to(lows, highs, PLANE)

        def rim_cols(first, first_inner):
            wide, thin = slice(first, first + RIM), slice(first_inner, first_inner + inner)
            noise = jnp.concatenate([above[RIM:, thin], mid1[:, thin], below[RIM:, thin]], axis=0)
            noise = jnp.pad(
                noise, ((RIM_USED, RIM_USED), (0, RIM_COLS - RIM - inner), (0, 0))
            )
            return jnp.concatenate(
                [
                    jnp.concatenate([above[:RIM, wide], mid0[:, wide], below[:RIM, wide]], axis=0),
                    noise,
                ],
                axis=1,
            )

        left, right = next_to(
            rim_cols(cols_here - RIM, cols_here - inner), rim_cols(0, 0), "col"
        )
        weights = (
            conv_weight(w_first, LANES, w_first.shape[0]),
            conv_weight(w_down, w_down.shape[2], w_down.shape[0]),
            w_up.T,
            w_bridge.T,
            conv_weight(w_last, w_last.shape[2], LANES),
        )
        parts = (mid0, mid1, above, below, left, right)
        return assemble(rows_here, cols_here, totals, high, lanes, place, *parts), weights

    by_latitude = lax.axis_size("col") == 4 and global_state.shape[0] % 4 == 0
    global_steps = global_by_latitude if by_latitude else global_by_channel
    finish, strips, pick, (fields, weights) = global_steps(
        hours, global_state, spec_filter, w_skip, w_mix, w_decode, box_lat0, box_lon0,
        rows_here, cols_here, prepare,
    )
    regional_final = denoise(
        rows_here, cols_here, totals, variables, conds, place, pick, *fields, strips, weights
    )
    regional_final = jnp.transpose(regional_final[:, :, :variables], (2, 0, 1))
    return finish(regional_final)


def solution(mesh):
    return jax.shard_map(
        shards,
        mesh=mesh,
        in_specs=(
            P(PLANE, "col", None),
            P(None, None, "col"),
            P(),
            P(),
            P(),
            P(None, PLANE, "col"),
            P(None, None, PLANE, "col"),
            P(),
            P(),
            P(),
            P(),
            P(),
            P(),
            P(),
            P(PLANE, "col"),
            P(PLANE, "col"),
        ),
        out_specs=(P(PLANE, "col", None), P(None, PLANE, "col")),
        check_vma=False,
    )
```

```python
import functools
import math

import jax
import jax.numpy as jnp
import ml_dtypes
import numpy as np
from jax import lax
from jax.experimental import pallas as pl
from jax.experimental.pallas import tpu as pltpu
from jax.sharding import PartitionSpec as P

RATIO = 8
noise_level = 0.5
PLANE = ("grp", "row")
RIM = 9
RIM_USED = 4
LANES = 128
VMEM = 60 * 2**20
PACKED = 32
MODE_TILE = 64
STRIP = 8
FAR = -4096
RIM_COLS = 16


def fourier_tables(length, num_modes):
    position = np.arange(length, dtype=np.int64)[:, None]
    frequency = np.arange(num_modes, dtype=np.int64)[None, :]
    angle = (position * frequency % length).astype(np.float64) * (2.0 * math.pi / length)
    cosine = np.cos(angle)
    sine = np.sin(angle)
    factor = np.where(frequency == 0, 1.0, 2.0) / length
    forward = np.concatenate([cosine, -sine], axis=1).T.astype(ml_dtypes.bfloat16)
    inverse = np.concatenate([cosine * factor, -sine * factor], axis=1).astype(ml_dtypes.bfloat16)
    return forward, inverse


def round_up(size, unit):
    return -(-size // unit) * unit


def split_tables(length, num_modes):
    piece = length // 4
    place = np.arange(piece, dtype=np.int64)[:, None]

    def waves(mode):
        angle = (place * mode[None, :] % length).astype(np.float64) * (2.0 * math.pi / length)
        return np.cos(angle), np.sin(angle), np.where(mode == 0, 1.0, 2.0)[None, :] / length

    def padded(blocks, unit_rows, unit_cols):
        rows = []
        for row in blocks:
            cols = []
            for block in row:
                spare = [(0, -block.shape[0] % unit_rows), (0, -block.shape[1] % unit_cols)]
                cols.append(np.pad(block, spare))
            rows.append(np.concatenate(cols, axis=1))
        return np.concatenate(rows, axis=0).astype(ml_dtypes.bfloat16)

    forward, inverse = [], []
    for residue in (0, 2):
        cosine, sine, factor = waves(np.arange(residue, num_modes, 4))
        forward.append(padded([[cosine.T], [-sine.T]], MODE_TILE, LANES))
        inverse.append(padded([[cosine * factor, -sine * factor]], LANES, MODE_TILE))
    mode = np.arange(1, num_modes, 2)
    cosine, sine, factor = waves(mode)
    sign = np.where(mode % 4 == 1, 1.0, -1.0)[None, :]
    odd_forward = padded(
        [[cosine.T, (-sign * sine).T], [-sine.T, (-sign * cosine).T]], 2 * MODE_TILE, LANES
    )
    odd_inverse = padded(
        [
            [cosine * factor, -sine * factor],
            [-sign * sine * factor, -sign * cosine * factor],
        ],
        LANES,
        2 * MODE_TILE,
    )
    return tuple(
        jnp.asarray(table)
        for table in (np.stack(forward), odd_forward, np.stack(inverse), odd_inverse)
    )


def exchange(blocks, axis):
    return lax.all_to_all(blocks, axis, split_axis=0, concat_axis=0, tiled=True)


def spread(block, axis):
    return exchange(jnp.broadcast_to(block[None], (lax.axis_size(axis),) + block.shape), axis)


def filter_share(spec_filter):
    rows = 2 * spec_filter.shape[1]
    flat = spec_filter.reshape(rows, spec_filter.shape[2])
    share = rows // lax.axis_size(PLANE)
    mine = lax.dynamic_slice_in_dim(flat, lax.axis_index(PLANE) * share, share, 0)
    return mine.astype(jnp.bfloat16)


def every_channel(mine):
    count = lax.axis_size("col")
    me = lax.axis_index("col")
    blocks = [shift(mine, "col", -step) if step else mine for step in range(count)]
    ring = jnp.concatenate(blocks + blocks[:-1], axis=1)
    width = mine.shape[1]
    return lax.dynamic_slice_in_dim(ring, (count - me) % count * width, count * width, 1)


def gelu(x):
    slope = math.sqrt(2.0 / math.pi)
    half = 0.5 * x
    return half + half * jnp.tanh(x * (slope + (0.044715 * slope) * (x * x)))


def latitude_kernel(hours, turns, step, place_ref, *refs):
    piece_refs, refs = refs[:4], refs[4:]
    even_forward_ref, odd_forward_ref, even_inverse_ref, odd_inverse_ref = refs[:4]
    filter_ref, skip_ref, mix_ref, decode_ref = refs[4:8]
    out_refs, strip_ref = refs[8:12], refs[12]
    state_ref, spectral_ref, gain_ref, coarse_ref, near_ref, packed_ref = refs[13:]
    f32, bf16 = jnp.float32, jnp.bfloat16
    piece, channels = piece_refs[0].shape[1:]
    padded = state_ref.shape[0] // 4
    group = LANES // PACKED
    span = near_ref.shape[0]
    rows = span // group
    spare = jnp.zeros((padded - piece, channels), bf16)
    for index in range(4):
        for turn in range(turns):
            state_ref[
                index * padded : (index + 1) * padded, turn * channels : (turn + 1) * channels
            ] = jnp.concatenate([piece_refs[index][turn], spare], axis=0)

    modes = filter_ref.shape[0] // 2
    for index in range(channels // LANES):
        lanes = slice(index * LANES, (index + 1) * LANES)
        gain_ref[index, : 2 * modes, :] = filter_ref[:, lanes].astype(f32)
        gain_ref[index, 2 * modes :, :] = jnp.zeros((gain_ref.shape[1] - 2 * modes, LANES), f32)

    def gain_rows(low, count, stride):
        rows = pl.ds(low, count, stride=stride)
        tiles = [gain_ref[index, rows, :] for index in range(channels // LANES)]
        return jnp.concatenate(tiles * turns, axis=1)

    def gain(spectrum, low, stride):
        half = spectrum.shape[0] // 2
        real, imag = spectrum[:half], spectrum[half:]
        gain_real = gain_rows(low, half, stride)
        gain_imag = gain_rows(modes + low, half, stride)
        return jnp.concatenate(
            [
                (real * gain_real - imag * gain_imag).astype(bf16),
                (real * gain_imag + imag * gain_real).astype(bf16),
            ],
            axis=0,
        )

    def dot(left, right):
        return jnp.dot(left, right, preferred_element_type=f32)

    def advance(hour, carry):
        pieces = [
            state_ref[index * padded : (index + 1) * padded, :].astype(f32) for index in range(4)
        ]
        both, other = pieces[0] + pieces[2], pieces[1] + pieces[3]
        shares = []
        for index, mixed in enumerate((both + other, both - other)):
            spectrum = dot(even_forward_ref[index], mixed.astype(bf16))
            shares.append(dot(even_inverse_ref[index], gain(spectrum, 2 * index, 4)))
        mixed = jnp.concatenate([pieces[0] - pieces[2], pieces[1] - pieces[3]], axis=0)
        odd = gain(dot(odd_forward_ref[...], mixed.astype(bf16)), 1, 2)
        odd = dot(odd_inverse_ref[...], odd)
        for index in range(4):
            even = shares[0] + shares[1] if index % 2 == 0 else shares[0] - shares[1]
            part = odd[:padded] if index % 2 == 0 else odd[padded:]
            total = even + part if index < 2 else even - part
            spectral_ref[index * padded : (index + 1) * padded, :] = total.astype(bf16)

        def mix(index, carry):
            here = pl.ds(pl.multiple_of(index * padded, LANES), padded)
            for turn in range(turns):
                lanes = slice(turn * channels, (turn + 1) * channels)
                state = state_ref[here, lanes]
                summed = spectral_ref[here, lanes].astype(f32) + dot(state, skip_ref[...])
                activated = gelu(summed).astype(bf16)
                update = dot(activated, mix_ref[...])
                state_ref[here, lanes] = (state.astype(f32) + update).astype(bf16)
            return carry

        lax.fori_loop(0, 4, mix, 0)

        for index in range(2):
            here = pl.ds(pl.multiple_of(place_ref[index] * padded, LANES), padded)
            coarse = dot(state_ref[here, :], decode_ref[...])
            for turn in range(turns):
                coarse_ref[turn, index * piece : (index + 1) * piece, :] = coarse[
                    :piece, turn * LANES : (turn + 1) * LANES
                ]
        for turn in range(turns):
            near_ref[...] = coarse_ref[turn, pl.ds(place_ref[2], span), :]
            packed = near_ref[pl.ds(0, rows, stride=group), :]
            for sub in range(1, group):
                packed += pltpu.roll(near_ref[pl.ds(sub, rows, stride=group), :], sub * PACKED, 1)
            packed_ref[turn, pl.ds(pl.multiple_of(hour * rows, 8), rows), :] = packed
        return carry

    lax.fori_loop(0, hours, advance, 0)
    for index in range(4):
        for turn in range(turns):
            out_refs[index][turn] = state_ref[
                index * padded : index * padded + piece, turn * channels : (turn + 1) * channels
            ]
    for target in range(4):
        low = target * step // group
        for turn in range(turns):
            strip = [
                packed_ref[turn, hour * rows + low : hour * rows + low + STRIP, :]
                for hour in range(hours)
            ]
            strip_ref[target, turn * hours * STRIP : (turn + 1) * hours * STRIP, :] = jnp.concatenate(
                strip, axis=0
            ).astype(bf16)


def advance_latitude(hours, turn, step, place, pieces, tables, gains, w_skip, w_mix, w_decode):
    _, piece, channels = pieces[0].shape
    padded = round_up(piece, LANES)
    group = LANES // PACKED
    span = round_up(3 * step + STRIP * group, 8 * group)
    decode = jnp.pad(w_decode, ((0, 0), (0, LANES - w_decode.shape[1])))
    modes = gains.shape[0] // 2
    spare = max(4 * (tables[0].shape[1] // 2), 2 * (tables[1].shape[0] // 2)) - modes
    results = pl.pallas_call(
        functools.partial(latitude_kernel, hours, 1, step),
        grid=(1,),
        out_shape=tuple(jax.ShapeDtypeStruct((1, piece, channels), jnp.bfloat16) for _ in pieces)
        + (jax.ShapeDtypeStruct((4, hours * STRIP, LANES), jnp.bfloat16),),
        in_specs=[pl.BlockSpec(memory_space=pltpu.SMEM)]
        + [pl.BlockSpec((1, piece, channels), lambda i: (turn, 0, 0))] * 4
        + [pl.BlockSpec(memory_space=pltpu.VMEM)] * 8,
        scratch_shapes=[
            pltpu.VMEM((4 * padded, channels), jnp.bfloat16),
            pltpu.VMEM((4 * padded, channels), jnp.bfloat16),
            pltpu.VMEM((channels // LANES, gains.shape[0] + spare, LANES), jnp.float32),
            pltpu.VMEM((1, 2 * piece, LANES), jnp.float32),
            pltpu.VMEM((span, LANES), jnp.float32),
            pltpu.VMEM((1, hours * span // group, LANES), jnp.float32),
        ],
        compiler_params=pltpu.CompilerParams(vmem_limit_bytes=VMEM),
        cost_estimate=pl.CostEstimate(
            flops=16 * 10**9, bytes_accessed=8 * 2**20, transcendentals=hours * 4 * piece * channels
        ),
        name="advance_latitude",
    )(place, *pieces, *tables, gains, w_skip, w_mix, decode)
    return results[:4], results[4]


def collate_kernel(count, place_ref, *refs):
    pieces, out_ref, sems = refs[:count], refs[count], refs[count + 1]
    copies = [
        pltpu.make_async_copy(
            piece, out_ref.at[pl.ds(place_ref[index], piece.shape[0])], sems.at[index]
        )
        for index, piece in enumerate(pieces)
    ]
    for copy in copies:
        copy.start()
    for copy in copies:
        copy.wait()


def collate(place, pieces):
    count = len(pieces)
    turns, piece, channels = pieces[0].shape
    return pl.pallas_call(
        functools.partial(collate_kernel, count),
        out_shape=jax.ShapeDtypeStruct((count * turns, piece, channels), pieces[0].dtype),
        in_specs=[pl.BlockSpec(memory_space=pltpu.SMEM)]
        + [pl.BlockSpec(memory_space=pltpu.VMEM)] * count,
        out_specs=pl.BlockSpec(memory_space=pl.ANY),
        scratch_shapes=[pltpu.SemaphoreType.DMA((count,))],
        name="collate",
    )(place, *pieces)


def shift(block, axis, step):
    count = lax.axis_size(axis)
    return lax.ppermute(block, axis, [(source, (source + step) % count) for source in range(count)])


def global_hour(current, spec_filter, w_skip, w_mix, forward, inverse):
    longitude = lax.all_to_all(current, "col", split_axis=2, concat_axis=1, tiled=True)
    spectrum = jnp.einsum("alc,ml->amc", longitude, forward, preferred_element_type=jnp.float32)
    num_modes = spec_filter.shape[1]
    real_part = spectrum[:, :num_modes, :]
    imag_part = spectrum[:, num_modes:, :]
    filt_real = spec_filter[0][None]
    filt_imag = spec_filter[1][None]
    mixed = jnp.concatenate(
        [
            real_part * filt_real - imag_part * filt_imag,
            real_part * filt_imag + imag_part * filt_real,
        ],
        axis=1,
    ).astype(jnp.bfloat16)
    filtered = jnp.einsum("amc,lm->alc", mixed, inverse, preferred_element_type=jnp.float32).astype(
        jnp.bfloat16
    )
    spectral = lax.all_to_all(filtered, "col", split_axis=1, concat_axis=2, tiled=True)
    skipped = jnp.einsum("alc,cd->ald", current, w_skip, preferred_element_type=jnp.float32)
    activated = jax.nn.gelu(spectral.astype(jnp.float32) + skipped).astype(jnp.bfloat16)
    update = jnp.einsum("ald,de->ale", activated, w_mix, preferred_element_type=jnp.float32)
    return (current.astype(jnp.float32) + update).astype(jnp.bfloat16)


def window_extent(cells):
    return (cells + RIM - 1) // RATIO + 3 - (-RIM // RATIO)


def window_base():
    return -(-RIM // RATIO)


def global_by_latitude(
    hours, global_state, spec_filter, w_skip, w_mix, w_decode, box_lat0, box_lon0, rows_here,
    cols_here, prepare,
):
    count = lax.axis_size("col")
    me = lax.axis_index("col")
    lats_here, piece, _ = global_state.shape
    turns = lats_here // count
    tables = split_tables(piece * count, spec_filter.shape[1])
    owners = [(me - step) % count * turns for step in range(count)]
    mine = filter_share(spec_filter)
    bands = [lax.dynamic_slice_in_dim(global_state, owner, turns, 0) for owner in owners]
    bands, mine = lax.optimization_barrier((bands, mine))
    received = [shift(band, "col", -step) if step else band for step, band in enumerate(bands)]
    wide = every_channel(mine)
    gains = spread(wide, PLANE).reshape(-1, wide.shape[1])
    prepared = prepare(wide)
    start = (box_lon0[0] - window_base() - me * piece) % (piece * count)
    place = jnp.stack([start // piece, (start // piece + 1) % count, start % piece]).astype(jnp.int32)
    received, prepared = lax.optimization_barrier((received, prepared))
    outcome, strips = [], []
    for turn in range(turns):
        blocks, strip = advance_latitude(
            hours, turn, cols_here // RATIO, place, received, tables, gains, w_skip, w_mix, w_decode
        )
        if turn < turns - 1:
            blocks = [shift(block, "col", step) if step else block for step, block in enumerate(blocks)]
        outcome.append(blocks)
        strips.append(strip)
    strips, outcome[:-1] = lax.optimization_barrier((jnp.concatenate(strips, axis=1), outcome[:-1]))
    near = []
    for step in range(count):
        strip = lax.dynamic_index_in_dim(strips, (me - step) % count, 0, keepdims=False)
        near.append(shift(strip, "col", -step) if step else strip)
    got = spread(jnp.stack(near), PLANE)
    plane = lax.axis_size(PLANE)
    got = got.reshape((plane * lats_here, -1, LANES))
    lat = box_lat0[0] - window_base() + lax.axis_index(PLANE) * (rows_here // RATIO)
    lat = jnp.clip(lat + jnp.arange(window_extent(rows_here), dtype=jnp.int32), 0, plane * lats_here - 1)
    places = [owner + turn for turn in range(turns) for owner in owners]
    band, lat = lat // lats_here, lat % lats_here
    pick = (band * count + (lat // turns - me) % count) * turns + lat % turns
    outcome[-1] = [
        shift(block, "col", step) if step else block for step, block in enumerate(outcome[-1])
    ]
    finals = sum(outcome, [])

    def finish(after):
        blocks, after = lax.optimization_barrier((finals, after))
        return collate(jnp.stack(places).astype(jnp.int32), blocks), after

    return finish, got, pick.astype(jnp.int32), prepared


def global_by_channel(
    hours, global_state, spec_filter, w_skip, w_mix, w_decode, box_lat0, box_lon0, rows_here,
    cols_here, prepare,
):
    count = lax.axis_size("col")
    prepared = prepare(global_state)
    forward, inverse = fourier_tables(global_state.shape[1] * count, spec_filter.shape[1])
    base = window_base()
    high, wide = window_extent(rows_here), window_extent(cols_here)
    span = (count - 1) * (cols_here // RATIO) + wide
    lat_start = box_lat0[0] + lax.axis_index(PLANE) * (rows_here // RATIO)
    lon_start = box_lon0[0] + lax.axis_index("col") * (cols_here // RATIO)
    windows = []
    for _ in range(hours):
        global_state = global_hour(global_state, spec_filter, w_skip, w_mix, forward, inverse)
        coarse = jnp.einsum(
            "alc,ck->alk", global_state, w_decode, preferred_element_type=jnp.float32
        ).astype(jnp.bfloat16)
        coarse = lax.all_gather(coarse, "col", axis=1, tiled=True)
        coarse = jnp.pad(coarse, ((0, 0), (base, span), (0, 0)))
        coarse = lax.dynamic_slice_in_dim(coarse, box_lon0[0], base + span, 1)
        coarse = lax.all_gather(coarse, PLANE, axis=0, tiled=True)
        coarse = lax.dynamic_slice_in_dim(coarse, lon_start - box_lon0[0], wide, 1)
        coarse = jnp.pad(coarse, ((base, high), (0, 0), (0, 0)))
        coarse = lax.dynamic_slice_in_dim(coarse, lat_start, high, 0)
        windows.append(coarse)
    group = LANES // PACKED
    windows = jnp.stack(windows, axis=1)
    windows = jnp.pad(
        windows, ((0, 0), (0, 0), (0, STRIP * group - wide), (0, PACKED - windows.shape[3]))
    )
    windows = windows.reshape(high, hours * STRIP, LANES)
    return lambda after: (global_state, after), windows, jnp.arange(high, dtype=jnp.int32), prepared


def next_to(low, high, axis):
    count = lax.axis_size(axis)
    forward = [(i, i + 1) for i in range(count - 1)]
    backward = [(target, source) for source, target in forward]
    return lax.ppermute(low, axis, forward), lax.ppermute(high, axis, backward)


def grid_place(start_ref, total, base, extent):
    place = start_ref + base + lax.broadcasted_iota(jnp.int32, (extent, 1), 0)
    return (place >= 0) & (place < total)


def assemble_kernel(
    rows, cols, totals, high, lanes, place_ref, mid0_ref, mid1_ref, above_ref, below_ref,
    left_ref, right_ref, noisy_ref, noise_ref, blend_ref,
):
    inner = RIM - RIM_USED
    pad = (noisy_ref.shape[1] - cols) // 2
    width = noisy_ref.shape[1]
    for ref, mid_ref, rim, part in ((noisy_ref, mid0_ref, RIM, 0), (noise_ref, mid1_ref, inner, RIM)):
        ref[0:rim, pad : pad + cols, :] = above_ref[part : part + rim]
        ref[rim : rim + rows, pad : pad + cols, :] = mid_ref[...]
        ref[rim + rows :, pad : pad + cols, :] = below_ref[part : part + rim]
        skip = RIM - rim
        for side_ref, low, to in (
            (left_ref, 0, pad - rim),
            (right_ref, pad + cols, 0),
        ):
            side = side_ref[skip : skip + rows + 2 * rim].astype(jnp.float32)
            side = pltpu.roll(side, (to - part) % pad, 1)
            ref[:, low : low + pad, :] = side.astype(jnp.bfloat16)

    base = window_base()
    col = lax.broadcasted_iota(jnp.int32, (width, 1), 0) - pad
    col_in = grid_place(place_ref[1], totals[1], -pad, width)
    frac_col = ((col % RATIO).astype(jnp.float32) + 0.5) / RATIO
    col_base = jnp.where(col_in, (col + pad) // RATIO - pad // RATIO + base, FAR)
    group = LANES // PACKED
    point = lax.broadcasted_iota(jnp.int32, (width, group * high * STRIP), 1)
    point_lat = (point // STRIP % high).astype(jnp.float32)
    point_lon = (point % STRIP * group + point // (STRIP * high)).astype(jnp.float32)

    def weigh(index, carry):
        row = index - RIM
        whole = (row + 2 * RATIO) // RATIO - 2
        frac_row = ((row - whole * RATIO).astype(jnp.float32) + 0.5) / RATIO
        there = place_ref[0] + row
        row_base = jnp.where((there >= 0) & (there < totals[0]), whole + base, FAR)
        shifts = noisy_ref[index, :, :].astype(jnp.float32)
        lat = row_base.astype(jnp.float32) + shifts[:, lanes : lanes + 1]
        lon = col_base.astype(jnp.float32) + shifts[:, lanes + 1 : lanes + 2]
        from_lat = point_lat - lat
        from_lon = point_lon - lon
        weight_lat = jnp.where(
            from_lat == 0.0, 1.0 - frac_row, jnp.where(from_lat == 1.0, frac_row, 0.0)
        )
        weight_lon = jnp.where(
            from_lon == 0.0, 1.0 - frac_col, jnp.where(from_lon == 1.0, frac_col, 0.0)
        )
        blend_ref[index, :, :] = (weight_lat * weight_lon).astype(jnp.bfloat16)
        return carry

    lax.fori_loop(0, rows + 2 * RIM, weigh, 0)


def assemble(rows, cols, totals, high, lanes, place, mid0, mid1, above, below, left, right):
    inner = RIM - RIM_USED
    width = cols + 2 * left.shape[1]
    channels = mid0.shape[2]
    return pl.pallas_call(
        functools.partial(assemble_kernel, rows, cols, totals, high, lanes),
        out_shape=(
            jax.ShapeDtypeStruct((rows + 2 * RIM, width, channels), jnp.bfloat16),
            jax.ShapeDtypeStruct((rows + 2 * inner, width, channels), jnp.bfloat16),
            jax.ShapeDtypeStruct(
                (rows + 2 * RIM, width, LANES // PACKED * high * STRIP), jnp.bfloat16
            ),
        ),
        in_specs=[pl.BlockSpec(memory_space=pltpu.SMEM)]
        + [pl.BlockSpec(memory_space=pltpu.VMEM)] * 6,
        compiler_params=pltpu.CompilerParams(vmem_limit_bytes=VMEM),
        cost_estimate=pl.CostEstimate(flops=10**6, bytes_accessed=10**5, transcendentals=0),
        name="assemble",
    )(place, mid0, mid1, above, below, left, right)


def silu(x):
    half = 0.5 * x
    return half + half * jnp.tanh(half)


def denoise_kernel(
    rows, cols, totals, variables, conds, place_ref, pick_ref, noisy_ref, noise_ref, blend_ref,
    strip_ref, first_w_ref, down_w_ref, up_w_ref, bridge_w_ref, last_w_ref, out_ref, own_ref,
    stack_ref, first_ref, pooled_ref, lifted_ref, third_ref, pair_ref, spread_ref, window_ref,
):
    width = noisy_ref.shape[1]
    half = width // 2
    pad = (width - cols) // 2
    channels = noisy_ref.shape[2]
    f32, bf16 = jnp.float32, jnp.bfloat16
    col_in = grid_place(place_ref[1], totals[1], -pad, width).astype(f32)
    lane = lax.broadcasted_iota(jnp.int32, (1, channels), 1)
    is_state = lane < variables
    is_cond = (lane >= variables) & (lane < variables + conds)
    high = pick_ref.shape[0]
    strips = [strip_ref[pick_ref[index]].astype(f32) for index in range(high)]
    for hour in range(2):
        near = jnp.concatenate([s[hour * STRIP : (hour + 1) * STRIP] for s in strips], axis=0)
        for turn in range(LANES // PACKED):
            moved = pltpu.roll(near, (variables - turn * PACKED) % LANES, 1)
            window_ref[hour, turn * high * STRIP : (turn + 1) * high * STRIP, :] = jnp.where(
                is_cond, moved, 0.0
            ).astype(bf16)

    def flat(start, count, unit):
        return pl.ds(pl.multiple_of(start * unit, 16), count * unit)

    def inside(row):
        marks = []
        for step in range(2):
            there = place_ref[0] + row + step
            mark = col_in * jnp.where((there >= 0) & (there < totals[0]), 1.0, 0.0)
            marks.append(jnp.broadcast_to(mark, (width, channels)))
        return jnp.concatenate(marks, axis=1)

    def keep(ref, where, value):
        size = value.shape[0]
        ref[0, where, :] = pltpu.roll(value, 1, 0).astype(bf16)
        ref[1, where, :] = value.astype(bf16)
        ref[2, where, :] = pltpu.roll(value, size - 1, 0).astype(bf16)

    def pairs(ref, row, count):
        blocks = []
        for pair in range(count):
            taps = [
                ref[shift, flat(row + 2 * pair + step, 1, width), :]
                for step in range(4)
                for shift in range(3)
            ]
            blocks.append(jnp.concatenate(taps, axis=1))
        return jnp.concatenate(blocks, axis=0)

    for hour in range(2):
        rim = RIM - RIM_USED * hour
        tall = rows + 2 * rim

        def stack(index, carry, hour=hour, rim=rim):
            here = flat(index * 2, 2, width)
            weights = blend_ref[pl.ds(index * 2 + RIM - rim, 2)].reshape(2 * width, -1)
            cond = jnp.dot(weights, window_ref[hour], preferred_element_type=f32)
            if hour == 0:
                own = noisy_ref[pl.ds(index * 2, 2)].reshape(2 * width, channels).astype(f32)
                own_ref[here, :] = own
            else:
                own = own_ref[here, :]
            keep(stack_ref, here, jnp.where(is_state, own, cond))
            return carry

        lax.fori_loop(0, tall // 2, stack, 0)

        def make_first(index, carry, rim=rim):
            row = index * 8
            value = jnp.dot(
                pairs(stack_ref, row, 4), first_w_ref[...], preferred_element_type=f32
            )
            for pair in range(4):
                top = row + 2 * pair
                part = silu(value[pair * width : (pair + 1) * width]) * inside(top - rim + 1)
                part = part.astype(bf16)
                first_ref[flat(index * 4 + pair, 1, width), :] = part
                part = part.astype(f32)
                pair_ref[pair] = part[:, :channels] + part[:, channels:]
                even = pair_ref[pair, pl.ds(0, half, stride=2), :]
                odd = pair_ref[pair, pl.ds(1, half, stride=2), :]
                keep(pooled_ref, flat(index * 4 + pair, 1, half), (even + odd) * 0.25)
            return carry

        lax.fori_loop(0, (tall - 2) // 8, make_first, 0)

        half_rows = (tall - 2) // 2 - 2

        def make_third(index, carry, part=half_rows // 2, rim=rim):
            row = index * part
            taps = [
                pooled_ref[shift, flat(row + step, part, half), :]
                for step in range(3)
                for shift in range(3)
            ]
            second = jnp.dot(
                jnp.concatenate(taps, axis=1), down_w_ref[...], preferred_element_type=f32
            )
            lifted_ref[: part * half, :] = jnp.dot(
                silu(second).astype(bf16), up_w_ref[...], preferred_element_type=f32
            )
            bridged = jnp.dot(
                first_ref[flat(row + 1, part, width), :], bridge_w_ref[...], preferred_element_type=f32
            )
            for step in range(part):
                lifted = lifted_ref[step * half : (step + 1) * half, :]
                spread_ref[step, pl.ds(0, half, stride=2), :] = lifted
                spread_ref[step, pl.ds(1, half, stride=2), :] = lifted
                spread = spread_ref[step]
                value = bridged[step * width : (step + 1) * width]
                value = silu(value + jnp.concatenate([spread, spread], axis=1))
                top = 2 * (row + step)
                value = value * inside(top - rim + 3)
                keep(third_ref, flat(top, 1, width), value[:, :channels])
                keep(third_ref, flat(top + 1, 1, width), value[:, channels:])
            return carry

        lax.fori_loop(0, 2, make_third, 0)

        part = (rows + 2 * (rim - RIM_USED)) // 2 if hour == 0 else rows // 4
        skip = 1 if hour == 1 else 0

        def finish(index, carry, hour=hour, rim=rim, part=part, skip=skip):
            start = index * 2 * part
            value = jnp.dot(
                pairs(third_ref, start + skip, part), last_w_ref[...], preferred_element_type=f32
            )
            for pair in range(part):
                for step in range(2):
                    row = start + 2 * pair + step
                    fresh = value[
                        pair * width : (pair + 1) * width, step * channels : (step + 1) * channels
                    ]
                    own = own_ref[flat(row + RIM_USED + skip, 1, width), :]
                    fresh = (own + fresh).astype(bf16)
                    if hour == 0:
                        there = place_ref[0] + row - rim + RIM_USED
                        mark = col_in * jnp.where((there >= 0) & (there < totals[0]), 1.0, 0.0)
                        noise = noise_ref[row].astype(f32)
                        fresh = (fresh.astype(f32) + noise_level * noise) * mark
                        own_ref[flat(row, 1, width), :] = fresh.astype(bf16).astype(f32)
                    else:
                        out_ref[row] = fresh[pad : pad + cols]
            return carry

        lax.fori_loop(0, 1 if hour == 0 else 2, finish, 0)


def denoise(rows, cols, totals, variables, conds, place, pick, noisy, noise, blend, strips, weights):
    width, channels = noisy.shape[1:]
    tall = rows + 2 * RIM
    most = (tall - 2) // 4 - 1
    bf16, f32 = jnp.bfloat16, jnp.float32
    return pl.pallas_call(
        functools.partial(denoise_kernel, rows, cols, totals, variables, conds),
        out_shape=jax.ShapeDtypeStruct((rows, cols, channels), bf16),
        in_specs=[pl.BlockSpec(memory_space=pltpu.SMEM)] * 2
        + [pl.BlockSpec(memory_space=pltpu.VMEM)] * 9,
        scratch_shapes=[
            pltpu.VMEM((tall * width, channels), f32),
            pltpu.VMEM((3, tall * width, channels), bf16),
            pltpu.VMEM((tall // 2 * width, 2 * channels), bf16),
            pltpu.VMEM((3, tall // 2 * width // 2, channels), bf16),
            pltpu.VMEM((most * width // 2, channels), f32),
            pltpu.VMEM((3, tall * width, channels), bf16),
            pltpu.VMEM((4, width, channels), f32),
            pltpu.VMEM((most, width, channels), f32),
            pltpu.VMEM((2, blend.shape[2], channels), bf16),
        ],
        compiler_params=pltpu.CompilerParams(vmem_limit_bytes=VMEM),
        cost_estimate=pl.CostEstimate(flops=10**6, bytes_accessed=10**5, transcendentals=0),
        name="denoise",
    )(place, pick, noisy, noise, blend, strips, *weights)


def conv_weight(weight, depth, width):
    out, _, given = weight.shape
    weight = jnp.pad(weight, ((0, width - out), (0, 0), (0, depth - given)))
    return jnp.transpose(weight, (1, 2, 0)).reshape(9 * depth, width)


def pair_weight(weight):
    row = weight.shape[0] // 3
    return jnp.concatenate(
        [jnp.pad(weight, ((0, row), (0, 0))), jnp.pad(weight, ((row, 0), (0, 0)))], axis=1
    )


def shards(
    global_state,
    spec_filter,
    w_skip,
    w_mix,
    w_decode,
    regional_state,
    noise_draws,
    w_first,
    w_down,
    w_up,
    w_bridge,
    w_last,
    box_lat0,
    box_lon0,
    stencil_lat,
    stencil_lon,
):
    hours = noise_draws.shape[0]
    rows_here, cols_here = regional_state.shape[1:]
    row_start = lax.axis_index(PLANE) * rows_here
    col_start = lax.axis_index("col") * cols_here
    total_rows = rows_here * lax.axis_size(PLANE)
    total_cols = cols_here * lax.axis_size("col")
    assert hours == 2

    variables = regional_state.shape[0]
    conds = w_decode.shape[1]
    lanes = variables + conds
    noisy = (
        regional_state.astype(jnp.float32) + noise_level * noise_draws[0].astype(jnp.float32)
    ).astype(jnp.bfloat16)
    lat_shift = stencil_lat - (row_start + jnp.arange(rows_here, dtype=jnp.int32))[:, None] // RATIO
    lon_shift = stencil_lon - (col_start + jnp.arange(cols_here, dtype=jnp.int32))[None, :] // RATIO
    cells = (rows_here, cols_here)
    mids = jnp.concatenate(
        [
            noisy,
            jnp.zeros((conds,) + cells, jnp.bfloat16),
            lat_shift.astype(jnp.bfloat16)[None],
            lon_shift.astype(jnp.bfloat16)[None],
            jnp.zeros((LANES - lanes - 2,) + cells, jnp.bfloat16),
            noise_draws[1],
            jnp.zeros((LANES - variables,) + cells, jnp.bfloat16),
        ],
        axis=0,
    )
    mids = jnp.transpose(mids.reshape((2, LANES) + cells), (0, 2, 3, 1))
    mid0, mid1 = mids[0], mids[1]
    inner = RIM - RIM_USED
    high = window_extent(rows_here)
    place = jnp.stack([row_start, col_start]).astype(jnp.int32)
    totals = (total_rows, total_cols)

    def prepare(after):
        lows = jnp.concatenate([mid0[rows_here - RIM :], mid1[rows_here - inner :]], axis=0)
        highs = jnp.concatenate([mid0[:RIM], mid1[:inner]], axis=0)
        lows, highs, _ = lax.optimization_barrier((lows, highs, after))
        above, below = next_to(lows, highs, PLANE)

        def rim_cols(first, first_inner):
            wide, thin = slice(first, first + RIM), slice(first_inner, first_inner + inner)
            noise = jnp.concatenate([above[RIM:, thin], mid1[:, thin], below[RIM:, thin]], axis=0)
            noise = jnp.pad(
                noise, ((RIM_USED, RIM_USED), (0, RIM_COLS - RIM - inner), (0, 0))
            )
            return jnp.concatenate(
                [
                    jnp.concatenate([above[:RIM, wide], mid0[:, wide], below[:RIM, wide]], axis=0),
                    noise,
                ],
                axis=1,
            )

        left, right = next_to(
            rim_cols(cols_here - RIM, cols_here - inner), rim_cols(0, 0), "col"
        )
        weights = (
            pair_weight(conv_weight(w_first, LANES, w_first.shape[0])),
            conv_weight(w_down, w_down.shape[2], w_down.shape[0]),
            w_up.T,
            jnp.concatenate(
                [jnp.pad(w_bridge.T, ((0, 0), (0, LANES))), jnp.pad(w_bridge.T, ((0, 0), (LANES, 0)))],
                axis=0,
            ),
            pair_weight(conv_weight(w_last, w_last.shape[2], LANES)),
        )
        parts = (mid0, mid1, above, below, left, right)
        return assemble(rows_here, cols_here, totals, high, lanes, place, *parts), weights

    by_latitude = lax.axis_size("col") == 4 and global_state.shape[0] % 4 == 0
    global_steps = global_by_latitude if by_latitude else global_by_channel
    finish, strips, pick, (fields, weights) = global_steps(
        hours, global_state, spec_filter, w_skip, w_mix, w_decode, box_lat0, box_lon0,
        rows_here, cols_here, prepare,
    )
    regional_final = denoise(
        rows_here, cols_here, totals, variables, conds, place, pick, *fields, strips, weights
    )
    regional_final = jnp.transpose(regional_final[:, :, :variables], (2, 0, 1))
    return finish(regional_final)


def solution(mesh):
    return jax.shard_map(
        shards,
        mesh=mesh,
        in_specs=(
            P(PLANE, "col", None),
            P(None, None, "col"),
            P(),
            P(),
            P(),
            P(None, PLANE, "col"),
            P(None, None, PLANE, "col"),
            P(),
            P(),
            P(),
            P(),
            P(),
            P(),
            P(),
            P(PLANE, "col"),
            P(PLANE, "col"),
        ),
        out_specs=(P(PLANE, "col", None), P(None, PLANE, "col")),
        check_vma=False,
    )
```

```python
import functools
import math

import jax
import jax.numpy as jnp
import ml_dtypes
import numpy as np
from jax import lax
from jax.experimental import pallas as pl
from jax.experimental.pallas import tpu as pltpu
from jax.sharding import PartitionSpec as P

RATIO = 8
noise_level = 0.5
PLANE = ("grp", "row")
RIM = 9
RIM_USED = 4
LANES = 128
VMEM = 60 * 2**20
PACKED = 32
MODE_TILE = 64
STRIP = 8
FAR = -4096
RIM_COLS = 16


def fourier_tables(length, num_modes):
    position = np.arange(length, dtype=np.int64)[:, None]
    frequency = np.arange(num_modes, dtype=np.int64)[None, :]
    angle = (position * frequency % length).astype(np.float64) * (2.0 * math.pi / length)
    cosine = np.cos(angle)
    sine = np.sin(angle)
    factor = np.where(frequency == 0, 1.0, 2.0) / length
    forward = np.concatenate([cosine, -sine], axis=1).T.astype(ml_dtypes.bfloat16)
    inverse = np.concatenate([cosine * factor, -sine * factor], axis=1).astype(ml_dtypes.bfloat16)
    return forward, inverse


def round_up(size, unit):
    return -(-size // unit) * unit


def split_tables(length, num_modes):
    piece = length // 4
    place = np.arange(piece, dtype=np.int64)[:, None]

    def waves(mode):
        angle = (place * mode[None, :] % length).astype(np.float64) * (2.0 * math.pi / length)
        return np.cos(angle), np.sin(angle), np.where(mode == 0, 1.0, 2.0)[None, :] / length

    def padded(blocks, unit_rows, unit_cols):
        rows = []
        for row in blocks:
            cols = []
            for block in row:
                spare = [(0, -block.shape[0] % unit_rows), (0, -block.shape[1] % unit_cols)]
                cols.append(np.pad(block, spare))
            rows.append(np.concatenate(cols, axis=1))
        return np.concatenate(rows, axis=0).astype(ml_dtypes.bfloat16)

    forward, inverse = [], []
    for residue in (0, 2):
        cosine, sine, factor = waves(np.arange(residue, num_modes, 4))
        forward.append(padded([[cosine.T], [-sine.T]], MODE_TILE, LANES))
        inverse.append(padded([[cosine * factor, -sine * factor]], LANES, MODE_TILE))
    mode = np.arange(1, num_modes, 2)
    cosine, sine, factor = waves(mode)
    sign = np.where(mode % 4 == 1, 1.0, -1.0)[None, :]
    odd_forward = padded(
        [[cosine.T, (-sign * sine).T], [-sine.T, (-sign * cosine).T]], 2 * MODE_TILE, LANES
    )
    odd_inverse = padded(
        [
            [cosine * factor, -sine * factor],
            [-sign * sine * factor, -sign * cosine * factor],
        ],
        LANES,
        2 * MODE_TILE,
    )
    return tuple(
        jnp.asarray(table)
        for table in (np.stack(forward), odd_forward, np.stack(inverse), odd_inverse)
    )


def exchange(blocks, axis):
    return lax.all_to_all(blocks, axis, split_axis=0, concat_axis=0, tiled=True)


def spread(block, axis):
    return exchange(jnp.broadcast_to(block[None], (lax.axis_size(axis),) + block.shape), axis)


def filter_share(spec_filter):
    rows = 2 * spec_filter.shape[1]
    flat = spec_filter.reshape(rows, spec_filter.shape[2])
    share = rows // lax.axis_size(PLANE)
    mine = lax.dynamic_slice_in_dim(flat, lax.axis_index(PLANE) * share, share, 0)
    return mine.astype(jnp.bfloat16)


def every_channel(mine):
    count = lax.axis_size("col")
    me = lax.axis_index("col")
    blocks = [shift(mine, "col", -step) if step else mine for step in range(count)]
    ring = jnp.concatenate(blocks + blocks[:-1], axis=1)
    width = mine.shape[1]
    return lax.dynamic_slice_in_dim(ring, (count - me) % count * width, count * width, 1)


def gelu(x):
    slope = math.sqrt(2.0 / math.pi)
    half = 0.5 * x
    return half + half * jnp.tanh(x * (slope + (0.044715 * slope) * (x * x)))


def latitude_kernel(hours, turns, step, place_ref, *refs):
    piece_refs, refs = refs[:4], refs[4:]
    even_forward_ref, odd_forward_ref = refs[:2]
    far_refs, out_refs, strip_ref, refs = refs[2:8], refs[8:12], refs[12], refs[13:]
    near_refs, sems, refs = refs[:6], refs[6], refs[7:]
    filter_ref, even_inverse_ref, odd_inverse_ref, skip_ref, mix_ref, decode_ref = near_refs
    state_ref, gain_ref, coarse_ref, near_ref, packed_ref = refs
    copies = [
        pltpu.make_async_copy(far, near, sems.at[index])
        for index, (far, near) in enumerate(zip(far_refs, near_refs))
    ]
    for copy in copies:
        copy.start()
    f32, bf16 = jnp.float32, jnp.bfloat16
    piece, channels = piece_refs[0].shape[1:]
    padded = state_ref.shape[0] // 4
    group = LANES // PACKED
    span = near_ref.shape[0]
    rows = span // group
    spare = jnp.zeros((padded - piece, channels), bf16)
    for index in range(4):
        for turn in range(turns):
            state_ref[
                index * padded : (index + 1) * padded, turn * channels : (turn + 1) * channels
            ] = jnp.concatenate([piece_refs[index][turn], spare], axis=0)

    modes = filter_ref.shape[0] // 2

    def spread_gains():
        for index in range(channels // LANES):
            lanes = slice(index * LANES, (index + 1) * LANES)
            gain_ref[index, : 2 * modes, :] = filter_ref[:, lanes].astype(f32)
            gain_ref[index, 2 * modes :, :] = jnp.zeros((gain_ref.shape[1] - 2 * modes, LANES), f32)

    def gain_rows(low, count, stride):
        rows = pl.ds(low, count, stride=stride)
        tiles = [gain_ref[index, rows, :] for index in range(channels // LANES)]
        return jnp.concatenate(tiles * turns, axis=1)

    def gain(spectrum, low, stride):
        half = spectrum.shape[0] // 2
        real, imag = spectrum[:half], spectrum[half:]
        gain_real = gain_rows(low, half, stride)
        gain_imag = gain_rows(modes + low, half, stride)
        return jnp.concatenate(
            [
                (real * gain_real - imag * gain_imag).astype(bf16),
                (real * gain_imag + imag * gain_real).astype(bf16),
            ],
            axis=0,
        )

    def dot(left, right):
        return jnp.dot(left, right, preferred_element_type=f32)

    for hour in range(hours):
        pieces = [
            state_ref[index * padded : (index + 1) * padded, :].astype(f32) for index in range(4)
        ]
        both, other = pieces[0] + pieces[2], pieces[1] + pieces[3]
        spectra = [
            dot(even_forward_ref[index], mixed.astype(bf16))
            for index, mixed in enumerate((both + other, both - other))
        ]
        mixed = jnp.concatenate([pieces[0] - pieces[2], pieces[1] - pieces[3]], axis=0)
        spectra.append(dot(odd_forward_ref[...], mixed.astype(bf16)))
        if hour == 0:
            copies[0].wait()
            spread_gains()
            for copy in copies[1:]:
                copy.wait()
        shares = [
            dot(even_inverse_ref[index], gain(spectra[index], 2 * index, 4)) for index in range(2)
        ]
        odd = dot(odd_inverse_ref[...], gain(spectra[2], 1, 2))
        for index in range(4):
            here = slice(index * padded, (index + 1) * padded)
            even = shares[0] + shares[1] if index % 2 == 0 else shares[0] - shares[1]
            part = odd[:padded] if index % 2 == 0 else odd[padded:]
            spectral = even + part if index < 2 else even - part
            for turn in range(turns):
                lanes = slice(turn * channels, (turn + 1) * channels)
                state = state_ref[here, lanes]
                activated = gelu(spectral[:, lanes] + dot(state, skip_ref[...])).astype(bf16)
                update = dot(activated, mix_ref[...])
                state_ref[here, lanes] = (state.astype(f32) + update).astype(bf16)

        for index in range(2):
            here = pl.ds(pl.multiple_of(place_ref[index] * padded, LANES), padded)
            coarse = dot(state_ref[here, :], decode_ref[...])
            for turn in range(turns):
                coarse_ref[turn, index * piece : (index + 1) * piece, :] = coarse[
                    :piece, turn * LANES : (turn + 1) * LANES
                ]
        for turn in range(turns):
            near_ref[...] = coarse_ref[turn, pl.ds(place_ref[2], span), :]
            packed = near_ref[pl.ds(0, rows, stride=group), :]
            for sub in range(1, group):
                packed += pltpu.roll(near_ref[pl.ds(sub, rows, stride=group), :], sub * PACKED, 1)
            packed_ref[turn, hour * rows : (hour + 1) * rows, :] = packed

    for index in range(4):
        for turn in range(turns):
            out_refs[index][turn] = state_ref[
                index * padded : index * padded + piece, turn * channels : (turn + 1) * channels
            ]
    for target in range(4):
        low = target * step // group
        for turn in range(turns):
            strip = [
                packed_ref[turn, hour * rows + low : hour * rows + low + STRIP, :]
                for hour in range(hours)
            ]
            strip_ref[target, turn * hours * STRIP : (turn + 1) * hours * STRIP, :] = jnp.concatenate(
                strip, axis=0
            ).astype(bf16)


def advance_latitude(hours, turn, step, place, pieces, tables, gains, w_skip, w_mix, w_decode):
    _, piece, channels = pieces[0].shape
    padded = round_up(piece, LANES)
    group = LANES // PACKED
    span = round_up(3 * step + STRIP * group, 8 * group)
    decode = jnp.pad(w_decode, ((0, 0), (0, LANES - w_decode.shape[1])))
    modes = gains.shape[0] // 2
    late = (gains,) + tables[2:] + (w_skip, w_mix, decode)
    spare = max(4 * (tables[0].shape[1] // 2), 2 * (tables[1].shape[0] // 2)) - modes
    results = pl.pallas_call(
        functools.partial(latitude_kernel, hours, 1, step),
        grid=(1,),
        out_shape=tuple(jax.ShapeDtypeStruct((1, piece, channels), jnp.bfloat16) for _ in pieces)
        + (jax.ShapeDtypeStruct((4, hours * STRIP, LANES), jnp.bfloat16),),
        in_specs=[pl.BlockSpec(memory_space=pltpu.SMEM)]
        + [pl.BlockSpec((1, piece, channels), lambda i: (turn, 0, 0))] * 4
        + [pl.BlockSpec(memory_space=pltpu.VMEM)] * 2
        + [pl.BlockSpec(memory_space=pl.ANY)] * len(late),
        scratch_shapes=[pltpu.VMEM(array.shape, array.dtype) for array in late]
        + [
            pltpu.SemaphoreType.DMA((len(late),)),
            pltpu.VMEM((4 * padded, channels), jnp.bfloat16),
            pltpu.VMEM((channels // LANES, gains.shape[0] + spare, LANES), jnp.float32),
            pltpu.VMEM((1, 2 * piece, LANES), jnp.float32),
            pltpu.VMEM((span, LANES), jnp.float32),
            pltpu.VMEM((1, hours * span // group, LANES), jnp.float32),
        ],
        compiler_params=pltpu.CompilerParams(vmem_limit_bytes=VMEM),
        cost_estimate=pl.CostEstimate(
            flops=16 * 10**9, bytes_accessed=8 * 2**20, transcendentals=hours * 4 * piece * channels
        ),
        name="advance_latitude",
    )(place, *pieces, *tables[:2], *late)
    return results[:4], results[4]


def collate_kernel(count, place_ref, *refs):
    pieces, out_ref, sems = refs[:count], refs[count], refs[count + 1]
    copies = [
        pltpu.make_async_copy(
            piece, out_ref.at[pl.ds(place_ref[index], piece.shape[0])], sems.at[index]
        )
        for index, piece in enumerate(pieces)
    ]
    for copy in copies:
        copy.start()
    for copy in copies:
        copy.wait()


def collate(place, pieces):
    count = len(pieces)
    turns, piece, channels = pieces[0].shape
    return pl.pallas_call(
        functools.partial(collate_kernel, count),
        out_shape=jax.ShapeDtypeStruct((count * turns, piece, channels), pieces[0].dtype),
        in_specs=[pl.BlockSpec(memory_space=pltpu.SMEM)]
        + [pl.BlockSpec(memory_space=pltpu.VMEM)] * count,
        out_specs=pl.BlockSpec(memory_space=pl.ANY),
        scratch_shapes=[pltpu.SemaphoreType.DMA((count,))],
        name="collate",
    )(place, *pieces)


def shift(block, axis, step):
    count = lax.axis_size(axis)
    return lax.ppermute(block, axis, [(source, (source + step) % count) for source in range(count)])


def global_hour(current, spec_filter, w_skip, w_mix, forward, inverse):
    longitude = lax.all_to_all(current, "col", split_axis=2, concat_axis=1, tiled=True)
    spectrum = jnp.einsum("alc,ml->amc", longitude, forward, preferred_element_type=jnp.float32)
    num_modes = spec_filter.shape[1]
    real_part = spectrum[:, :num_modes, :]
    imag_part = spectrum[:, num_modes:, :]
    filt_real = spec_filter[0][None]
    filt_imag = spec_filter[1][None]
    mixed = jnp.concatenate(
        [
            real_part * filt_real - imag_part * filt_imag,
            real_part * filt_imag + imag_part * filt_real,
        ],
        axis=1,
    ).astype(jnp.bfloat16)
    filtered = jnp.einsum("amc,lm->alc", mixed, inverse, preferred_element_type=jnp.float32).astype(
        jnp.bfloat16
    )
    spectral = lax.all_to_all(filtered, "col", split_axis=1, concat_axis=2, tiled=True)
    skipped = jnp.einsum("alc,cd->ald", current, w_skip, preferred_element_type=jnp.float32)
    activated = jax.nn.gelu(spectral.astype(jnp.float32) + skipped).astype(jnp.bfloat16)
    update = jnp.einsum("ald,de->ale", activated, w_mix, preferred_element_type=jnp.float32)
    return (current.astype(jnp.float32) + update).astype(jnp.bfloat16)


def window_extent(cells):
    return (cells + RIM - 1) // RATIO + 3 - (-RIM // RATIO)


def window_base():
    return -(-RIM // RATIO)


def global_by_latitude(
    hours, global_state, spec_filter, w_skip, w_mix, w_decode, box_lat0, box_lon0, rows_here,
    cols_here, first, prepare,
):
    count = lax.axis_size("col")
    me = lax.axis_index("col")
    lats_here, piece, _ = global_state.shape
    turns = lats_here // count
    tables = split_tables(piece * count, spec_filter.shape[1])
    owners = [(me - step) % count * turns for step in range(count)]
    mine = filter_share(spec_filter)
    bands = [lax.dynamic_slice_in_dim(global_state, owner, turns, 0) for owner in owners]
    mine, _ = lax.optimization_barrier((mine, (bands, first)))
    received = [shift(band, "col", -step) if step else band for step, band in enumerate(bands)]
    wide = every_channel(mine)
    parts, weights = prepare()
    gains = spread(wide, PLANE).reshape(-1, wide.shape[1])
    start = (box_lon0[0] - window_base() - me * piece) % (piece * count)
    place = jnp.stack([start // piece, (start // piece + 1) % count, start % piece]).astype(jnp.int32)
    received, weights = lax.optimization_barrier((received, weights))
    outcome, strips = [], []
    for turn in range(turns):
        blocks, strip = advance_latitude(
            hours, turn, cols_here // RATIO, place, received, tables, gains, w_skip, w_mix, w_decode
        )
        outcome.append(blocks)
        strips.append(strip)
    outcome = [list(blocks) for blocks in outcome]
    early = [shift(outcome[0][step], "col", step) for step in (1, 3)]
    strips, early = lax.optimization_barrier((jnp.concatenate(strips, axis=1), early))
    near = []
    for step in range(count):
        strip = lax.dynamic_index_in_dim(strips, (me - step) % count, 0, keepdims=False)
        near.append(shift(strip, "col", -step) if step else strip)
    near, outcome, parts = lax.optimization_barrier((jnp.stack(near), outcome, parts))
    got = spread(near, PLANE)
    plane = lax.axis_size(PLANE)
    got = got.reshape((plane * lats_here, -1, LANES))
    lat = box_lat0[0] - window_base() + lax.axis_index(PLANE) * (rows_here // RATIO)
    lat = jnp.clip(lat + jnp.arange(window_extent(rows_here), dtype=jnp.int32), 0, plane * lats_here - 1)
    places = [owner + turn for turn in range(turns) for owner in owners]
    band, lat = lat // lats_here, lat % lats_here
    pick = (band * count + (lat // turns - me) % count) * turns + lat % turns
    finals = []
    for turn, blocks in enumerate(outcome):
        for step, block in enumerate(blocks):
            if turn == 0 and step % 2 == 1:
                block = early[step // 2]
            elif step:
                block = shift(block, "col", step)
            finals.append(block)

    def finish(after):
        blocks, after = lax.optimization_barrier((finals, after))
        return collate(jnp.stack(places).astype(jnp.int32), blocks), after

    return finish, got, pick.astype(jnp.int32), (parts, weights)


def global_by_channel(
    hours, global_state, spec_filter, w_skip, w_mix, w_decode, box_lat0, box_lon0, rows_here,
    cols_here, first, prepare,
):
    count = lax.axis_size("col")
    prepared = prepare()
    forward, inverse = fourier_tables(global_state.shape[1] * count, spec_filter.shape[1])
    base = window_base()
    high, wide = window_extent(rows_here), window_extent(cols_here)
    span = (count - 1) * (cols_here // RATIO) + wide
    lat_start = box_lat0[0] + lax.axis_index(PLANE) * (rows_here // RATIO)
    lon_start = box_lon0[0] + lax.axis_index("col") * (cols_here // RATIO)
    windows = []
    for _ in range(hours):
        global_state = global_hour(global_state, spec_filter, w_skip, w_mix, forward, inverse)
        coarse = jnp.einsum(
            "alc,ck->alk", global_state, w_decode, preferred_element_type=jnp.float32
        ).astype(jnp.bfloat16)
        coarse = lax.all_gather(coarse, "col", axis=1, tiled=True)
        coarse = jnp.pad(coarse, ((0, 0), (base, span), (0, 0)))
        coarse = lax.dynamic_slice_in_dim(coarse, box_lon0[0], base + span, 1)
        coarse = lax.all_gather(coarse, PLANE, axis=0, tiled=True)
        coarse = lax.dynamic_slice_in_dim(coarse, lon_start - box_lon0[0], wide, 1)
        coarse = jnp.pad(coarse, ((base, high), (0, 0), (0, 0)))
        coarse = lax.dynamic_slice_in_dim(coarse, lat_start, high, 0)
        windows.append(coarse)
    group = LANES // PACKED
    windows = jnp.stack(windows, axis=1)
    windows = jnp.pad(
        windows, ((0, 0), (0, 0), (0, STRIP * group - wide), (0, PACKED - windows.shape[3]))
    )
    windows = windows.reshape(high, hours * STRIP, LANES)
    return lambda after: (global_state, after), windows, jnp.arange(high, dtype=jnp.int32), prepared


def next_to(low, high, axis):
    count = lax.axis_size(axis)
    forward = [(i, i + 1) for i in range(count - 1)]
    backward = [(target, source) for source, target in forward]
    return lax.ppermute(low, axis, forward), lax.ppermute(high, axis, backward)


def grid_place(start_ref, total, base, extent):
    place = start_ref + base + lax.broadcasted_iota(jnp.int32, (extent, 1), 0)
    return (place >= 0) & (place < total)


def assemble_kernel(
    rows, cols, totals, high, lanes, place_ref, mid0_ref, mid1_ref, above_ref, below_ref,
    left_ref, right_ref, noisy_ref, noise_ref, blend_ref,
):
    inner = RIM - RIM_USED
    pad = (noisy_ref.shape[1] - cols) // 2
    width = noisy_ref.shape[1]
    for ref, mid_ref, rim, part in ((noisy_ref, mid0_ref, RIM, 0), (noise_ref, mid1_ref, inner, RIM)):
        ref[0:rim, pad : pad + cols, :] = above_ref[part : part + rim]
        ref[rim : rim + rows, pad : pad + cols, :] = mid_ref[...]
        ref[rim + rows :, pad : pad + cols, :] = below_ref[part : part + rim]
        skip = RIM - rim
        for side_ref, low, to in (
            (left_ref, 0, pad - rim),
            (right_ref, pad + cols, 0),
        ):
            side = side_ref[skip : skip + rows + 2 * rim].astype(jnp.float32)
            side = pltpu.roll(side, (to - part) % pad, 1)
            ref[:, low : low + pad, :] = side.astype(jnp.bfloat16)

    base = window_base()
    col = lax.broadcasted_iota(jnp.int32, (width, 1), 0) - pad
    col_in = grid_place(place_ref[1], totals[1], -pad, width)
    frac_col = ((col % RATIO).astype(jnp.float32) + 0.5) / RATIO
    col_base = jnp.where(col_in, (col + pad) // RATIO - pad // RATIO + base, FAR)
    group = LANES // PACKED
    point = lax.broadcasted_iota(jnp.int32, (width, group * high * STRIP), 1)
    point_lat = (point // STRIP % high).astype(jnp.float32)
    point_lon = (point % STRIP * group + point // (STRIP * high)).astype(jnp.float32)

    def weigh(index, carry):
        row = index - RIM
        whole = (row + 2 * RATIO) // RATIO - 2
        frac_row = ((row - whole * RATIO).astype(jnp.float32) + 0.5) / RATIO
        there = place_ref[0] + row
        row_base = jnp.where((there >= 0) & (there < totals[0]), whole + base, FAR)
        shifts = noisy_ref[index, :, :].astype(jnp.float32)
        lat = row_base.astype(jnp.float32) + frac_row + shifts[:, lanes : lanes + 1]
        lon = col_base.astype(jnp.float32) + frac_col + shifts[:, lanes + 1 : lanes + 2]
        weight_lat = jnp.maximum(1.0 - jnp.abs(point_lat - lat), 0.0)
        weight_lon = jnp.maximum(1.0 - jnp.abs(point_lon - lon), 0.0)
        blend_ref[index, :, :] = (weight_lat * weight_lon).astype(jnp.bfloat16)
        return carry

    lax.fori_loop(0, rows + 2 * RIM, weigh, 0)


def assemble(rows, cols, totals, high, lanes, place, mid0, mid1, above, below, left, right):
    inner = RIM - RIM_USED
    width = cols + 2 * left.shape[1]
    channels = mid0.shape[2]
    return pl.pallas_call(
        functools.partial(assemble_kernel, rows, cols, totals, high, lanes),
        out_shape=(
            jax.ShapeDtypeStruct((rows + 2 * RIM, width, channels), jnp.bfloat16),
            jax.ShapeDtypeStruct((rows + 2 * inner, width, channels), jnp.bfloat16),
            jax.ShapeDtypeStruct(
                (rows + 2 * RIM, width, LANES // PACKED * high * STRIP), jnp.bfloat16
            ),
        ),
        in_specs=[pl.BlockSpec(memory_space=pltpu.SMEM)]
        + [pl.BlockSpec(memory_space=pltpu.VMEM)] * 6,
        compiler_params=pltpu.CompilerParams(vmem_limit_bytes=VMEM),
        cost_estimate=pl.CostEstimate(flops=10**10, bytes_accessed=10**7, transcendentals=0),
        name="assemble",
    )(place, mid0, mid1, above, below, left, right)


def denoise_kernel(
    rows, cols, totals, variables, conds, place_ref, pick_ref, noisy_ref, blend_ref, strip_ref, *refs
):
    far_refs, out_ref, refs = refs[:6], refs[6], refs[7:]
    near_refs, sems, refs = refs[:6], refs[6], refs[7:]
    noise_ref, first_w_ref, down_w_ref, up_w_ref, bridge_w_ref, last_w_ref = near_refs
    own_ref, stack_ref, first_ref, pooled_ref, third_ref, pair_ref, spread_ref, window_ref = refs
    copies = [
        pltpu.make_async_copy(far, near, sems.at[index])
        for index, (far, near) in enumerate(zip(far_refs, near_refs))
    ]
    for copy in copies:
        copy.start()
    width = noisy_ref.shape[1]
    half = width // 2
    pad = (width - cols) // 2
    channels = noisy_ref.shape[2]
    f32, bf16 = jnp.float32, jnp.bfloat16
    col_in = grid_place(place_ref[1], totals[1], -pad, width).astype(f32)
    edges = [jnp.broadcast_to(col_in[low : low + pad], (pad, channels)) for low in (0, pad + cols)]
    lane = lax.broadcasted_iota(jnp.int32, (1, channels), 1)
    is_state = lane < variables
    is_cond = (lane >= variables) & (lane < variables + conds)
    high = pick_ref.shape[0]
    strips = [strip_ref[pick_ref[index]].astype(f32) for index in range(high)]
    for hour in range(2):
        near = jnp.concatenate([s[hour * STRIP : (hour + 1) * STRIP] for s in strips], axis=0)
        for turn in range(LANES // PACKED):
            moved = pltpu.roll(near, (variables - turn * PACKED) % LANES, 1)
            window_ref[hour, turn * high * STRIP : (turn + 1) * high * STRIP, :] = jnp.where(
                is_cond, moved, 0.0
            ).astype(bf16)

    def flat(start, count, unit):
        return slice(start * unit, (start + count) * unit)

    def mask(value, row):
        low, mid, high = value[:pad], value[pad : pad + cols], value[pad + cols :]
        value = jnp.concatenate([low * edges[0], mid, high * edges[1]], axis=0)
        if 0 <= row < rows:
            return value
        there = place_ref[0] + row
        return value * jnp.where((there >= 0) & (there < totals[0]), 1.0, 0.0)

    def keep(ref, where, value):
        size = value.shape[0]
        ref[0, where, :] = pltpu.roll(value, 1, 0).astype(bf16)
        ref[1, where, :] = value.astype(bf16)
        ref[2, where, :] = pltpu.roll(value, size - 1, 0).astype(bf16)

    def pairs(ref, row, count):
        blocks = []
        for pair in range(count):
            taps = [
                ref[shift, flat(row + 2 * pair + step, 1, width), :]
                for step in range(4)
                for shift in range(3)
            ]
            blocks.append(jnp.concatenate(taps, axis=1))
        return jnp.concatenate(blocks, axis=0)

    def silu_of_half(half_value):
        return half_value + half_value * jnp.tanh(half_value)

    for hour in range(2):
        rim = RIM - RIM_USED * hour
        tall = rows + 2 * rim

        for row in range(0, tall, 2):
            here = flat(row, 2, width)
            weights = blend_ref[row + RIM - rim : row + RIM - rim + 2].reshape(2 * width, -1)
            cond = jnp.dot(weights, window_ref[hour], preferred_element_type=f32)
            if hour == 0:
                own = noisy_ref[row : row + 2].reshape(2 * width, channels).astype(f32)
                own_ref[here, :] = own
            else:
                own = own_ref[here, :]
            keep(stack_ref, here, jnp.where(is_state, own, cond))

        if hour == 0:
            copies[1].wait()
        for row in range(0, tall - 2, 8):
            value = jnp.dot(
                pairs(stack_ref, row, 4), first_w_ref[...], preferred_element_type=f32
            )
            for pair in range(4):
                top = row + 2 * pair
                here = flat(top // 2, 1, width)
                part = silu_of_half(value[pair * width : (pair + 1) * width])
                upper = mask(part[:, :channels], top - rim + 1)
                lower = mask(part[:, channels:], top - rim + 2)
                first_ref[here, :channels] = upper.astype(bf16)
                first_ref[here, channels:] = lower.astype(bf16)
                pair_ref[top // 2] = upper + lower
                even = pair_ref[top // 2, pl.ds(0, half, stride=2), :]
                odd = pair_ref[top // 2, pl.ds(1, half, stride=2), :]
                keep(pooled_ref, flat(top // 2, 1, half), even + odd)

        if hour == 0:
            for copy in copies[2:5]:
                copy.wait()
        half_rows = (tall - 2) // 2 - 2
        part = half_rows // 2
        for row in (0, part):
            taps = [
                pooled_ref[shift, flat(row + step, part, half), :]
                for step in range(3)
                for shift in range(3)
            ]
            second = jnp.dot(
                jnp.concatenate(taps, axis=1), down_w_ref[...], preferred_element_type=f32
            )
            lifted = jnp.dot(
                silu_of_half(second).astype(bf16), up_w_ref[...], preferred_element_type=f32
            )
            bridged = jnp.dot(
                first_ref[flat(row + 1, part, width), :], bridge_w_ref[...], preferred_element_type=f32
            )
            for step in range(part):
                own = lifted[step * half : (step + 1) * half]
                spread_ref[row + step, pl.ds(0, half, stride=2), :] = own
                spread_ref[row + step, pl.ds(1, half, stride=2), :] = own
                own = spread_ref[row + step]
                top = 2 * (row + step)
                for side in range(2):
                    value = bridged[
                        step * width : (step + 1) * width, side * channels : (side + 1) * channels
                    ]
                    value = mask(silu_of_half(value + own), top + side - rim + 3)
                    keep(third_ref, flat(top + side, 1, width), value)

        if hour == 0:
            copies[5].wait()
            copies[0].wait()
        skip = 1 if hour == 1 else 0
        count = (rows + 2 * (rim - RIM_USED)) // 2 if hour == 0 else rows // 2
        for first in range(0, count, 4):
            size = min(4, count - first)
            values = jnp.dot(
                pairs(third_ref, 2 * first + skip, size), last_w_ref[...], preferred_element_type=f32
            )
            for index in range(2 * size):
                pair, side = divmod(index, 2)
                row = 2 * first + index
                fresh = values[
                    pair * width : (pair + 1) * width, side * channels : (side + 1) * channels
                ]
                fresh = own_ref[flat(row + RIM_USED + skip, 1, width), :] + fresh
                if hour == 0:
                    fresh = fresh + noise_level * noise_ref[row].astype(f32)
                    own_ref[flat(row, 1, width), :] = mask(fresh, row - rim + RIM_USED)
                else:
                    out_ref[row] = fresh[pad : pad + cols].astype(bf16)


def denoise(rows, cols, totals, variables, conds, place, pick, noisy, noise, blend, strips, weights):
    width, channels = noisy.shape[1:]
    tall = rows + 2 * RIM
    most = (tall - 2) // 2
    bf16, f32 = jnp.bfloat16, jnp.float32
    late = (noise,) + weights
    return pl.pallas_call(
        functools.partial(denoise_kernel, rows, cols, totals, variables, conds),
        out_shape=jax.ShapeDtypeStruct((rows, cols, channels), bf16),
        in_specs=[pl.BlockSpec(memory_space=pltpu.SMEM)] * 2
        + [pl.BlockSpec(memory_space=pltpu.VMEM)] * 3
        + [pl.BlockSpec(memory_space=pl.ANY)] * len(late),
        scratch_shapes=[pltpu.VMEM(array.shape, array.dtype) for array in late]
        + [
            pltpu.SemaphoreType.DMA((len(late),)),
            pltpu.VMEM((tall * width, channels), f32),
            pltpu.VMEM((3, tall * width, channels), bf16),
            pltpu.VMEM((most * width, 2 * channels), bf16),
            pltpu.VMEM((3, most * width // 2, channels), bf16),
            pltpu.VMEM((3, tall * width, channels), bf16),
            pltpu.VMEM((most, width, channels), f32),
            pltpu.VMEM((most, width, channels), f32),
            pltpu.VMEM((2, blend.shape[2], channels), bf16),
        ],
        compiler_params=pltpu.CompilerParams(vmem_limit_bytes=VMEM),
        cost_estimate=pl.CostEstimate(flops=10**6, bytes_accessed=10**5, transcendentals=0),
        name="denoise",
    )(place, pick, noisy, blend, strips, *late)


def conv_weight(weight, depth, width):
    out, _, given = weight.shape
    weight = jnp.pad(weight, ((0, width - out), (0, 0), (0, depth - given)))
    return jnp.transpose(weight, (1, 2, 0)).reshape(9 * depth, width)


def pair_weight(weight):
    row = weight.shape[0] // 3
    return jnp.concatenate(
        [jnp.pad(weight, ((0, row), (0, 0))), jnp.pad(weight, ((row, 0), (0, 0)))], axis=1
    )


def shards(
    global_state,
    spec_filter,
    w_skip,
    w_mix,
    w_decode,
    regional_state,
    noise_draws,
    w_first,
    w_down,
    w_up,
    w_bridge,
    w_last,
    box_lat0,
    box_lon0,
    stencil_lat,
    stencil_lon,
):
    hours = noise_draws.shape[0]
    rows_here, cols_here = regional_state.shape[1:]
    row_start = lax.axis_index(PLANE) * rows_here
    col_start = lax.axis_index("col") * cols_here
    total_rows = rows_here * lax.axis_size(PLANE)
    total_cols = cols_here * lax.axis_size("col")
    assert hours == 2

    variables = regional_state.shape[0]
    conds = w_decode.shape[1]
    lanes = variables + conds
    noisy = (
        regional_state.astype(jnp.float32) + noise_level * noise_draws[0].astype(jnp.float32)
    ).astype(jnp.bfloat16)
    lat_shift = stencil_lat - (row_start + jnp.arange(rows_here, dtype=jnp.int32))[:, None] // RATIO
    lon_shift = stencil_lon - (col_start + jnp.arange(cols_here, dtype=jnp.int32))[None, :] // RATIO
    cells = (rows_here, cols_here)
    mids = jnp.concatenate(
        [
            noisy,
            jnp.zeros((conds,) + cells, jnp.bfloat16),
            lat_shift.astype(jnp.bfloat16)[None],
            lon_shift.astype(jnp.bfloat16)[None],
            jnp.zeros((LANES - lanes - 2,) + cells, jnp.bfloat16),
            noise_draws[1],
            jnp.zeros((LANES - variables,) + cells, jnp.bfloat16),
        ],
        axis=0,
    )
    mids = jnp.transpose(mids.reshape((2, LANES) + cells), (0, 2, 3, 1))
    mid0, mid1 = mids[0], mids[1]
    inner = RIM - RIM_USED
    high = window_extent(rows_here)
    place = jnp.stack([row_start, col_start]).astype(jnp.int32)
    totals = (total_rows, total_cols)

    def prepare():
        lows = jnp.concatenate([mid0[rows_here - RIM :], mid1[rows_here - inner :]], axis=0)
        highs = jnp.concatenate([mid0[:RIM], mid1[:inner]], axis=0)
        above, below = next_to(lows, highs, PLANE)

        def rim_cols(first, first_inner):
            wide, thin = slice(first, first + RIM), slice(first_inner, first_inner + inner)
            noise = jnp.concatenate([above[RIM:, thin], mid1[:, thin], below[RIM:, thin]], axis=0)
            noise = jnp.pad(
                noise, ((RIM_USED, RIM_USED), (0, RIM_COLS - RIM - inner), (0, 0))
            )
            return jnp.concatenate(
                [
                    jnp.concatenate([above[:RIM, wide], mid0[:, wide], below[:RIM, wide]], axis=0),
                    noise,
                ],
                axis=1,
            )

        left, right = next_to(
            rim_cols(cols_here - RIM, cols_here - inner), rim_cols(0, 0), "col"
        )
        weights = (
            pair_weight(conv_weight(0.5 * w_first, LANES, w_first.shape[0])),
            conv_weight(0.125 * w_down, w_down.shape[2], w_down.shape[0]),
            0.5 * w_up.T,
            0.5
            * jnp.concatenate(
                [jnp.pad(w_bridge.T, ((0, 0), (0, LANES))), jnp.pad(w_bridge.T, ((0, 0), (LANES, 0)))],
                axis=0,
            ),
            pair_weight(conv_weight(w_last, w_last.shape[2], LANES)),
        )
        return (mid0, mid1, above, below, left, right), weights

    by_latitude = lax.axis_size("col") == 4 and global_state.shape[0] % 4 == 0
    global_steps = global_by_latitude if by_latitude else global_by_channel
    finish, strips, pick, (parts, weights) = global_steps(
        hours, global_state, spec_filter, w_skip, w_mix, w_decode, box_lat0, box_lon0,
        rows_here, cols_here, mids, prepare,
    )
    fields = assemble(rows_here, cols_here, totals, high, lanes, place, *parts)
    regional_final = denoise(
        rows_here, cols_here, totals, variables, conds, place, pick, *fields, strips, weights
    )
    regional_final = jnp.transpose(regional_final[:, :, :variables], (2, 0, 1))
    return finish(regional_final)


def solution(mesh):
    return jax.shard_map(
        shards,
        mesh=mesh,
        in_specs=(
            P(PLANE, "col", None),
            P(None, None, "col"),
            P(),
            P(),
            P(),
            P(None, PLANE, "col"),
            P(None, None, PLANE, "col"),
            P(),
            P(),
            P(),
            P(),
            P(),
            P(),
            P(),
            P(PLANE, "col"),
            P(PLANE, "col"),
        ),
        out_specs=(P(PLANE, "col", None), P(None, PLANE, "col")),
        check_vma=False,
    )
```

```python
import functools
import math

import jax
import jax.numpy as jnp
import ml_dtypes
import numpy as np
from jax import lax
from jax.experimental import pallas as pl
from jax.experimental.pallas import tpu as pltpu
from jax.sharding import PartitionSpec as P

RATIO = 8
noise_level = 0.5
PLANE = ("grp", "row")
RIM = 9
RIM_USED = 4
LANES = 128
VMEM = 60 * 2**20
PACKED = 32
MODE_TILE = 64
STRIP = 8
FAR = -4096
RIM_COLS = 16


def fourier_tables(length, num_modes):
    position = np.arange(length, dtype=np.int64)[:, None]
    frequency = np.arange(num_modes, dtype=np.int64)[None, :]
    angle = (position * frequency % length).astype(np.float64) * (2.0 * math.pi / length)
    cosine = np.cos(angle)
    sine = np.sin(angle)
    factor = np.where(frequency == 0, 1.0, 2.0) / length
    forward = np.concatenate([cosine, -sine], axis=1).T.astype(ml_dtypes.bfloat16)
    inverse = np.concatenate([cosine * factor, -sine * factor], axis=1).astype(ml_dtypes.bfloat16)
    return forward, inverse


def round_up(size, unit):
    return -(-size // unit) * unit


def split_tables(length, num_modes):
    piece = length // 4
    place = np.arange(piece, dtype=np.int64)[:, None]

    def waves(mode):
        angle = (place * mode[None, :] % length).astype(np.float64) * (2.0 * math.pi / length)
        return np.cos(angle), np.sin(angle), np.where(mode == 0, 1.0, 2.0)[None, :] / length

    def padded(blocks, unit_rows, unit_cols):
        rows = []
        for row in blocks:
            cols = []
            for block in row:
                spare = [(0, -block.shape[0] % unit_rows), (0, -block.shape[1] % unit_cols)]
                cols.append(np.pad(block, spare))
            rows.append(np.concatenate(cols, axis=1))
        return np.concatenate(rows, axis=0).astype(ml_dtypes.bfloat16)

    forward, inverse = [], []
    for residue in (0, 2):
        cosine, sine, factor = waves(np.arange(residue, num_modes, 4))
        forward.append(padded([[cosine.T], [-sine.T]], MODE_TILE, LANES))
        inverse.append(padded([[cosine * factor, -sine * factor]], LANES, MODE_TILE))
    mode = np.arange(1, num_modes, 2)
    cosine, sine, factor = waves(mode)
    sign = np.where(mode % 4 == 1, 1.0, -1.0)[None, :]
    odd_forward = padded(
        [[cosine.T, (-sign * sine).T], [-sine.T, (-sign * cosine).T]], 2 * MODE_TILE, LANES
    )
    odd_inverse = padded(
        [
            [cosine * factor, -sine * factor],
            [-sign * sine * factor, -sign * cosine * factor],
        ],
        LANES,
        2 * MODE_TILE,
    )
    return tuple(
        jnp.asarray(table)
        for table in (np.stack(forward), odd_forward, np.stack(inverse), odd_inverse)
    )


def exchange(blocks, axis):
    return lax.all_to_all(blocks, axis, split_axis=0, concat_axis=0, tiled=True)


def spread(block, axis):
    return exchange(jnp.broadcast_to(block[None], (lax.axis_size(axis),) + block.shape), axis)


def filter_share(spec_filter):
    rows = 2 * spec_filter.shape[1]
    flat = spec_filter.reshape(rows, spec_filter.shape[2])
    share = rows // lax.axis_size(PLANE)
    mine = lax.dynamic_slice_in_dim(flat, lax.axis_index(PLANE) * share, share, 0)
    return mine.astype(jnp.bfloat16)


def every_channel(mine):
    count = lax.axis_size("col")
    me = lax.axis_index("col")
    blocks = [shift(mine, "col", -step) if step else mine for step in range(count)]
    ring = jnp.concatenate(blocks + blocks[:-1], axis=1)
    width = mine.shape[1]
    return lax.dynamic_slice_in_dim(ring, (count - me) % count * width, count * width, 1)


def gelu(x):
    slope = math.sqrt(2.0 / math.pi)
    half = 0.5 * x
    return half + half * jnp.tanh(x * (slope + (0.044715 * slope) * (x * x)))


def latitude_kernel(hours, turns, step, place_ref, *refs):
    piece_refs, refs = refs[:4], refs[4:]
    even_forward_ref, odd_forward_ref = refs[:2]
    far_refs, out_refs, strip_ref, refs = refs[2:8], refs[8:12], refs[12], refs[13:]
    near_refs, sems, refs = refs[:6], refs[6], refs[7:]
    filter_ref, even_inverse_ref, odd_inverse_ref, skip_ref, mix_ref, decode_ref = near_refs
    state_ref, gain_ref, coarse_ref, near_ref, packed_ref = refs
    copies = [
        pltpu.make_async_copy(far, near, sems.at[index])
        for index, (far, near) in enumerate(zip(far_refs, near_refs))
    ]
    for copy in copies:
        copy.start()
    f32, bf16 = jnp.float32, jnp.bfloat16
    piece, channels = piece_refs[0].shape[1:]
    padded = state_ref.shape[0] // 4
    group = LANES // PACKED
    span = near_ref.shape[0]
    rows = span // group
    spare = jnp.zeros((padded - piece, channels), bf16)
    for index in range(4):
        for turn in range(turns):
            state_ref[
                index * padded : (index + 1) * padded, turn * channels : (turn + 1) * channels
            ] = jnp.concatenate([piece_refs[index][turn], spare], axis=0)

    modes = filter_ref.shape[0] // 2

    def spread_gains():
        for index in range(channels // LANES):
            lanes = slice(index * LANES, (index + 1) * LANES)
            gain_ref[index, : 2 * modes, :] = filter_ref[:, lanes].astype(f32)
            gain_ref[index, 2 * modes :, :] = jnp.zeros((gain_ref.shape[1] - 2 * modes, LANES), f32)

    def gain_rows(low, count, stride):
        rows = pl.ds(low, count, stride=stride)
        tiles = [gain_ref[index, rows, :] for index in range(channels // LANES)]
        return jnp.concatenate(tiles * turns, axis=1)

    def gain(spectrum, low, stride):
        half = spectrum.shape[0] // 2
        real, imag = spectrum[:half], spectrum[half:]
        gain_real = gain_rows(low, half, stride)
        gain_imag = gain_rows(modes + low, half, stride)
        return jnp.concatenate(
            [
                (real * gain_real - imag * gain_imag).astype(bf16),
                (real * gain_imag + imag * gain_real).astype(bf16),
            ],
            axis=0,
        )

    def dot(left, right):
        return jnp.dot(left, right, preferred_element_type=f32)

    for hour in range(hours):
        pieces = [
            state_ref[index * padded : (index + 1) * padded, :].astype(f32) for index in range(4)
        ]
        both, other = pieces[0] + pieces[2], pieces[1] + pieces[3]
        spectra = [
            dot(even_forward_ref[index], mixed.astype(bf16))
            for index, mixed in enumerate((both + other, both - other))
        ]
        mixed = jnp.concatenate([pieces[0] - pieces[2], pieces[1] - pieces[3]], axis=0)
        spectra.append(dot(odd_forward_ref[...], mixed.astype(bf16)))
        if hour == 0:
            copies[0].wait()
            spread_gains()
            for copy in copies[1:]:
                copy.wait()
        shares = [
            dot(even_inverse_ref[index], gain(spectra[index], 2 * index, 4)) for index in range(2)
        ]
        odd = dot(odd_inverse_ref[...], gain(spectra[2], 1, 2))
        for index in range(4):
            here = slice(index * padded, (index + 1) * padded)
            even = shares[0] + shares[1] if index % 2 == 0 else shares[0] - shares[1]
            part = odd[:padded] if index % 2 == 0 else odd[padded:]
            spectral = even + part if index < 2 else even - part
            for turn in range(turns):
                lanes = slice(turn * channels, (turn + 1) * channels)
                state = state_ref[here, lanes]
                activated = gelu(spectral[:, lanes] + dot(state, skip_ref[...])).astype(bf16)
                update = dot(activated, mix_ref[...])
                state_ref[here, lanes] = (state.astype(f32) + update).astype(bf16)

        for index in range(2):
            here = pl.ds(pl.multiple_of(place_ref[index] * padded, LANES), padded)
            coarse = dot(state_ref[here, :], decode_ref[...])
            for turn in range(turns):
                coarse_ref[turn, index * piece : (index + 1) * piece, :] = coarse[
                    :piece, turn * LANES : (turn + 1) * LANES
                ]
        for turn in range(turns):
            near_ref[...] = coarse_ref[turn, pl.ds(place_ref[2], span), :]
            packed = near_ref[pl.ds(0, rows, stride=group), :]
            for sub in range(1, group):
                packed += pltpu.roll(near_ref[pl.ds(sub, rows, stride=group), :], sub * PACKED, 1)
            packed_ref[turn, hour * rows : (hour + 1) * rows, :] = packed

    for index in range(4):
        for turn in range(turns):
            out_refs[index][turn] = state_ref[
                index * padded : index * padded + piece, turn * channels : (turn + 1) * channels
            ]
    for target in range(4):
        low = target * step // group
        for turn in range(turns):
            strip = [
                packed_ref[turn, hour * rows + low : hour * rows + low + STRIP, :]
                for hour in range(hours)
            ]
            strip_ref[target, turn * hours * STRIP : (turn + 1) * hours * STRIP, :] = jnp.concatenate(
                strip, axis=0
            ).astype(bf16)


def advance_latitude(hours, turn, step, place, pieces, tables, gains, w_skip, w_mix, w_decode):
    _, piece, channels = pieces[0].shape
    padded = round_up(piece, LANES)
    group = LANES // PACKED
    span = round_up(3 * step + STRIP * group, 8 * group)
    decode = jnp.pad(w_decode, ((0, 0), (0, LANES - w_decode.shape[1])))
    modes = gains.shape[0] // 2
    late = (gains,) + tables[2:] + (w_skip, w_mix, decode)
    spare = max(4 * (tables[0].shape[1] // 2), 2 * (tables[1].shape[0] // 2)) - modes
    results = pl.pallas_call(
        functools.partial(latitude_kernel, hours, 1, step),
        grid=(1,),
        out_shape=tuple(jax.ShapeDtypeStruct((1, piece, channels), jnp.bfloat16) for _ in pieces)
        + (jax.ShapeDtypeStruct((4, hours * STRIP, LANES), jnp.bfloat16),),
        in_specs=[pl.BlockSpec(memory_space=pltpu.SMEM)]
        + [pl.BlockSpec((1, piece, channels), lambda i: (turn, 0, 0))] * 4
        + [pl.BlockSpec(memory_space=pltpu.VMEM)] * 2
        + [pl.BlockSpec(memory_space=pl.ANY)] * len(late),
        scratch_shapes=[pltpu.VMEM(array.shape, array.dtype) for array in late]
        + [
            pltpu.SemaphoreType.DMA((len(late),)),
            pltpu.VMEM((4 * padded, channels), jnp.bfloat16),
            pltpu.VMEM((channels // LANES, gains.shape[0] + spare, LANES), jnp.float32),
            pltpu.VMEM((1, 2 * piece, LANES), jnp.float32),
            pltpu.VMEM((span, LANES), jnp.float32),
            pltpu.VMEM((1, hours * span // group, LANES), jnp.float32),
        ],
        compiler_params=pltpu.CompilerParams(vmem_limit_bytes=VMEM),
        cost_estimate=pl.CostEstimate(
            flops=16 * 10**9, bytes_accessed=8 * 2**20, transcendentals=hours * 4 * piece * channels
        ),
        name="advance_latitude",
    )(place, *pieces, *tables[:2], *late)
    return results[:4], results[4]


def collate_kernel(count, place_ref, *refs):
    pieces, out_ref, sems = refs[:count], refs[count], refs[count + 1]
    copies = [
        pltpu.make_async_copy(
            piece, out_ref.at[pl.ds(place_ref[index], piece.shape[0])], sems.at[index]
        )
        for index, piece in enumerate(pieces)
    ]
    for copy in copies:
        copy.start()
    for copy in copies:
        copy.wait()


def collate(place, pieces):
    count = len(pieces)
    turns, piece, channels = pieces[0].shape
    return pl.pallas_call(
        functools.partial(collate_kernel, count),
        out_shape=jax.ShapeDtypeStruct((count * turns, piece, channels), pieces[0].dtype),
        in_specs=[pl.BlockSpec(memory_space=pltpu.SMEM)]
        + [pl.BlockSpec(memory_space=pltpu.VMEM)] * count,
        out_specs=pl.BlockSpec(memory_space=pl.ANY),
        scratch_shapes=[pltpu.SemaphoreType.DMA((count,))],
        name="collate",
    )(place, *pieces)


def shift(block, axis, step):
    count = lax.axis_size(axis)
    return lax.ppermute(block, axis, [(source, (source + step) % count) for source in range(count)])


def global_hour(current, spec_filter, w_skip, w_mix, forward, inverse):
    longitude = lax.all_to_all(current, "col", split_axis=2, concat_axis=1, tiled=True)
    spectrum = jnp.einsum("alc,ml->amc", longitude, forward, preferred_element_type=jnp.float32)
    num_modes = spec_filter.shape[1]
    real_part = spectrum[:, :num_modes, :]
    imag_part = spectrum[:, num_modes:, :]
    filt_real = spec_filter[0][None]
    filt_imag = spec_filter[1][None]
    mixed = jnp.concatenate(
        [
            real_part * filt_real - imag_part * filt_imag,
            real_part * filt_imag + imag_part * filt_real,
        ],
        axis=1,
    ).astype(jnp.bfloat16)
    filtered = jnp.einsum("amc,lm->alc", mixed, inverse, preferred_element_type=jnp.float32).astype(
        jnp.bfloat16
    )
    spectral = lax.all_to_all(filtered, "col", split_axis=1, concat_axis=2, tiled=True)
    skipped = jnp.einsum("alc,cd->ald", current, w_skip, preferred_element_type=jnp.float32)
    activated = jax.nn.gelu(spectral.astype(jnp.float32) + skipped).astype(jnp.bfloat16)
    update = jnp.einsum("ald,de->ale", activated, w_mix, preferred_element_type=jnp.float32)
    return (current.astype(jnp.float32) + update).astype(jnp.bfloat16)


def window_extent(cells):
    return (cells + RIM - 1) // RATIO + 3 - (-RIM // RATIO)


def window_base():
    return -(-RIM // RATIO)


def global_by_latitude(
    hours, global_state, spec_filter, w_skip, w_mix, w_decode, box_lat0, box_lon0, rows_here,
    cols_here, prepare,
):
    count = lax.axis_size("col")
    me = lax.axis_index("col")
    lats_here, piece, _ = global_state.shape
    turns = lats_here // count
    tables = split_tables(piece * count, spec_filter.shape[1])
    owners = [(me - step) % count * turns for step in range(count)]
    bands = [lax.dynamic_slice_in_dim(global_state, owner, turns, 0) for owner in owners[:2]]
    spec_filter, _ = lax.optimization_barrier((spec_filter, bands))
    mine = filter_share(spec_filter)
    global_state, mine = lax.optimization_barrier((global_state, mine))
    bands += [lax.dynamic_slice_in_dim(global_state, owner, turns, 0) for owner in owners[2:]]
    received = [shift(band, "col", -step) if step else band for step, band in enumerate(bands)]
    wide = every_channel(mine)
    parts, weights = prepare()
    gains = spread(wide, PLANE).reshape(-1, wide.shape[1])
    start = (box_lon0[0] - window_base() - me * piece) % (piece * count)
    place = jnp.stack([start // piece, (start // piece + 1) % count, start % piece]).astype(jnp.int32)
    received, weights = lax.optimization_barrier((received, weights))
    outcome, strips = [], []
    for turn in range(turns):
        blocks, strip = advance_latitude(
            hours, turn, cols_here // RATIO, place, received, tables, gains, w_skip, w_mix, w_decode
        )
        outcome.append(blocks)
        strips.append(strip)
    early = [
        [shift(block, "col", step) if step else block for step, block in enumerate(blocks)]
        for blocks in outcome[:-1]
    ]
    strips, early, parts = lax.optimization_barrier((jnp.concatenate(strips, axis=1), early, parts))
    near = []
    for step in range(count):
        strip = lax.dynamic_index_in_dim(strips, (me - step) % count, 0, keepdims=False)
        near.append(shift(strip, "col", -step) if step else strip)
    got = spread(jnp.stack(near), PLANE)
    plane = lax.axis_size(PLANE)
    got = got.reshape((plane * lats_here, -1, LANES))
    lat = box_lat0[0] - window_base() + lax.axis_index(PLANE) * (rows_here // RATIO)
    lat = jnp.clip(lat + jnp.arange(window_extent(rows_here), dtype=jnp.int32), 0, plane * lats_here - 1)
    places = [owner + turn for turn in range(turns) for owner in owners]
    band, lat = lat // lats_here, lat % lats_here
    pick = (band * count + (lat // turns - me) % count) * turns + lat % turns
    finals = sum(early, []) + [
        shift(block, "col", step) if step else block for step, block in enumerate(outcome[-1])
    ]

    def finish(after):
        blocks, after = lax.optimization_barrier((finals, after))
        return collate(jnp.stack(places).astype(jnp.int32), blocks), after

    return finish, got, pick.astype(jnp.int32), (parts, weights)


def global_by_channel(
    hours, global_state, spec_filter, w_skip, w_mix, w_decode, box_lat0, box_lon0, rows_here,
    cols_here, prepare,
):
    count = lax.axis_size("col")
    prepared = prepare()
    forward, inverse = fourier_tables(global_state.shape[1] * count, spec_filter.shape[1])
    base = window_base()
    high, wide = window_extent(rows_here), window_extent(cols_here)
    span = (count - 1) * (cols_here // RATIO) + wide
    lat_start = box_lat0[0] + lax.axis_index(PLANE) * (rows_here // RATIO)
    lon_start = box_lon0[0] + lax.axis_index("col") * (cols_here // RATIO)
    windows = []
    for _ in range(hours):
        global_state = global_hour(global_state, spec_filter, w_skip, w_mix, forward, inverse)
        coarse = jnp.einsum(
            "alc,ck->alk", global_state, w_decode, preferred_element_type=jnp.float32
        ).astype(jnp.bfloat16)
        coarse = lax.all_gather(coarse, "col", axis=1, tiled=True)
        coarse = jnp.pad(coarse, ((0, 0), (base, span), (0, 0)))
        coarse = lax.dynamic_slice_in_dim(coarse, box_lon0[0], base + span, 1)
        coarse = lax.all_gather(coarse, PLANE, axis=0, tiled=True)
        coarse = lax.dynamic_slice_in_dim(coarse, lon_start - box_lon0[0], wide, 1)
        coarse = jnp.pad(coarse, ((base, high), (0, 0), (0, 0)))
        coarse = lax.dynamic_slice_in_dim(coarse, lat_start, high, 0)
        windows.append(coarse)
    group = LANES // PACKED
    windows = jnp.stack(windows, axis=1)
    windows = jnp.pad(
        windows, ((0, 0), (0, 0), (0, STRIP * group - wide), (0, PACKED - windows.shape[3]))
    )
    windows = windows.reshape(high, hours * STRIP, LANES)
    return lambda after: (global_state, after), windows, jnp.arange(high, dtype=jnp.int32), prepared


def next_to(low, high, axis):
    count = lax.axis_size(axis)
    forward = [(i, i + 1) for i in range(count - 1)]
    backward = [(target, source) for source, target in forward]
    return lax.ppermute(low, axis, forward), lax.ppermute(high, axis, backward)


def grid_place(start_ref, total, base, extent):
    place = start_ref + base + lax.broadcasted_iota(jnp.int32, (extent, 1), 0)
    return (place >= 0) & (place < total)


def denoise_kernel(
    rows, cols, totals, variables, conds, width, place_ref, pick_ref, mid0_ref, mid1_ref, above_ref,
    below_ref, left_ref, right_ref, strip_ref, *refs
):
    far_refs, out_ref, refs = refs[:5], refs[5], refs[6:]
    near_refs, sems, refs = refs[:5], refs[5], refs[6:]
    first_w_ref, down_w_ref, up_w_ref, bridge_w_ref, last_w_ref = near_refs
    noisy_ref, noise_ref, blend_ref, own_ref, stack_ref, first_ref, pooled_ref, third_ref, pair_ref, spread_ref, window_ref = refs
    copies = [
        pltpu.make_async_copy(far, near, sems.at[index])
        for index, (far, near) in enumerate(zip(far_refs, near_refs))
    ]
    for copy in copies:
        copy.start()
    half = width // 2
    pad = (width - cols) // 2
    channels = mid0_ref.shape[2]
    f32, bf16 = jnp.float32, jnp.bfloat16

    inner = RIM - RIM_USED
    for ref, mid_ref, rim, part in ((noisy_ref, mid0_ref, RIM, 0), (noise_ref, mid1_ref, inner, RIM)):
        ref[0:rim, pad : pad + cols, :] = above_ref[part : part + rim]
        ref[rim : rim + rows, pad : pad + cols, :] = mid_ref[...]
        ref[rim + rows :, pad : pad + cols, :] = below_ref[part : part + rim]
        skip = RIM - rim
        for side_ref, low, to in ((left_ref, 0, pad - rim), (right_ref, pad + cols, 0)):
            side = side_ref[skip : skip + rows + 2 * rim].astype(f32)
            side = pltpu.roll(side, (to - part) % pad, 1)
            ref[:, low : low + pad, :] = side.astype(bf16)

    is_in = grid_place(place_ref[1], totals[1], -pad, width)
    col_in = is_in.astype(f32)
    base = window_base()
    col = lax.broadcasted_iota(jnp.int32, (width, 1), 0) - pad
    frac_col = ((col % RATIO).astype(f32) + 0.5) / RATIO
    col_base = jnp.where(is_in, (col + pad) // RATIO - pad // RATIO + base, FAR).astype(f32) + frac_col
    group = LANES // PACKED
    high = pick_ref.shape[0]
    point = lax.broadcasted_iota(jnp.int32, (1, group * high * STRIP), 1)
    point_lat = (point // STRIP % high).astype(f32)
    point_lon = (point % STRIP * group + point // (STRIP * high)).astype(f32)

    def blend(row):
        whole = row // RATIO
        frac_row = (row - whole * RATIO + 0.5) / RATIO
        there = place_ref[0] + row
        row_base = jnp.where((there >= 0) & (there < totals[0]), whole + base + frac_row, float(FAR))
        shifts = noisy_ref[row + RIM].astype(f32)
        lat = row_base + shifts[:, variables + conds : variables + conds + 1]
        lon = col_base + shifts[:, variables + conds + 1 : variables + conds + 2]
        weight_lat = jnp.maximum(1.0 - jnp.abs(point_lat - lat), 0.0)
        weight_lon = jnp.maximum(1.0 - jnp.abs(point_lon - lon), 0.0)
        return (weight_lat * weight_lon).astype(bf16)

    edges = [jnp.broadcast_to(col_in[low : low + pad], (pad, channels)) for low in (0, pad + cols)]
    lane = lax.broadcasted_iota(jnp.int32, (1, channels), 1)
    is_state = lane < variables
    is_cond = (lane >= variables) & (lane < variables + conds)
    strips = [strip_ref[pick_ref[index]].astype(f32) for index in range(high)]
    for hour in range(2):
        near = jnp.concatenate([s[hour * STRIP : (hour + 1) * STRIP] for s in strips], axis=0)
        for turn in range(LANES // PACKED):
            moved = pltpu.roll(near, (variables - turn * PACKED) % LANES, 1)
            window_ref[hour, turn * high * STRIP : (turn + 1) * high * STRIP, :] = jnp.where(
                is_cond, moved, 0.0
            ).astype(bf16)

    def flat(start, count, unit):
        return slice(start * unit, (start + count) * unit)

    def mask(value, row):
        low, mid, high = value[:pad], value[pad : pad + cols], value[pad + cols :]
        value = jnp.concatenate([low * edges[0], mid, high * edges[1]], axis=0)
        if 0 <= row < rows:
            return value
        there = place_ref[0] + row
        return value * jnp.where((there >= 0) & (there < totals[0]), 1.0, 0.0)

    def keep(ref, where, value):
        size = value.shape[0]
        ref[0, where, :] = pltpu.roll(value, 1, 0).astype(bf16)
        ref[1, where, :] = value.astype(bf16)
        ref[2, where, :] = pltpu.roll(value, size - 1, 0).astype(bf16)

    def pairs(ref, row, count):
        blocks = []
        for pair in range(count):
            taps = [
                ref[shift, flat(row + 2 * pair + step, 1, width), :]
                for step in range(4)
                for shift in range(3)
            ]
            blocks.append(jnp.concatenate(taps, axis=1))
        return jnp.concatenate(blocks, axis=0)

    def silu_of_half(half_value):
        return half_value + half_value * jnp.tanh(half_value)

    for hour in range(2):
        rim = RIM - RIM_USED * hour
        tall = rows + 2 * rim

        for row in range(0, tall, 2):
            here = flat(row, 2, width)
            if hour == 0:
                weights = jnp.concatenate([blend(row - RIM), blend(row + 1 - RIM)], axis=0)
                blend_ref[here, :] = weights
            else:
                weights = blend_ref[flat(row + RIM - rim, 2, width), :]
            cond = jnp.dot(weights, window_ref[hour], preferred_element_type=f32)
            if hour == 0:
                own = noisy_ref[row : row + 2].reshape(2 * width, channels).astype(f32)
                own_ref[here, :] = own
            else:
                own = own_ref[here, :]
            keep(stack_ref, here, jnp.where(is_state, own, cond))

        if hour == 0:
            copies[0].wait()
        for row in range(0, tall - 2, 8):
            value = jnp.dot(
                pairs(stack_ref, row, 4), first_w_ref[...], preferred_element_type=f32
            )
            for pair in range(4):
                top = row + 2 * pair
                here = flat(top // 2, 1, width)
                part = silu_of_half(value[pair * width : (pair + 1) * width])
                upper = mask(part[:, :channels], top - rim + 1)
                lower = mask(part[:, channels:], top - rim + 2)
                first_ref[here, :channels] = upper.astype(bf16)
                first_ref[here, channels:] = lower.astype(bf16)
                pair_ref[top // 2] = upper + lower
                even = pair_ref[top // 2, pl.ds(0, half, stride=2), :]
                odd = pair_ref[top // 2, pl.ds(1, half, stride=2), :]
                keep(pooled_ref, flat(top // 2, 1, half), even + odd)

        if hour == 0:
            for copy in copies[1:4]:
                copy.wait()
        half_rows = (tall - 2) // 2 - 2
        part = half_rows // 2
        for row in (0, part):
            taps = [
                pooled_ref[shift, flat(row + step, part, half), :]
                for step in range(3)
                for shift in range(3)
            ]
            second = jnp.dot(
                jnp.concatenate(taps, axis=1), down_w_ref[...], preferred_element_type=f32
            )
            lifted = jnp.dot(
                silu_of_half(second).astype(bf16), up_w_ref[...], preferred_element_type=f32
            )
            bridged = jnp.dot(
                first_ref[flat(row + 1, part, width), :], bridge_w_ref[...], preferred_element_type=f32
            )
            for step in range(part):
                own = lifted[step * half : (step + 1) * half]
                spread_ref[row + step, pl.ds(0, half, stride=2), :] = own
                spread_ref[row + step, pl.ds(1, half, stride=2), :] = own
                own = spread_ref[row + step]
                top = 2 * (row + step)
                for side in range(2):
                    value = bridged[
                        step * width : (step + 1) * width, side * channels : (side + 1) * channels
                    ]
                    value = mask(silu_of_half(value + own), top + side - rim + 3)
                    keep(third_ref, flat(top + side, 1, width), value)

        if hour == 0:
            copies[4].wait()
        skip = 1 if hour == 1 else 0
        count = (rows + 2 * (rim - RIM_USED)) // 2 if hour == 0 else rows // 2
        for first in range(0, count, 4):
            size = min(4, count - first)
            values = jnp.dot(
                pairs(third_ref, 2 * first + skip, size), last_w_ref[...], preferred_element_type=f32
            )
            for index in range(2 * size):
                pair, side = divmod(index, 2)
                row = 2 * first + index
                fresh = values[
                    pair * width : (pair + 1) * width, side * channels : (side + 1) * channels
                ]
                fresh = own_ref[flat(row + RIM_USED + skip, 1, width), :] + fresh
                if hour == 0:
                    fresh = fresh + noise_level * noise_ref[row].astype(f32)
                    own_ref[flat(row, 1, width), :] = mask(fresh, row - rim + RIM_USED)
                else:
                    out_ref[:, row * cols : (row + 1) * cols] = fresh[pad : pad + cols].T.astype(bf16)


def denoise(rows, cols, totals, variables, conds, place, pick, parts, strips, weights):
    mid0, _, _, _, left, _ = parts
    width, channels = cols + 2 * left.shape[1], mid0.shape[2]
    tall = rows + 2 * RIM
    most = (tall - 2) // 2
    points = LANES // PACKED * pick.shape[0] * STRIP
    bf16, f32 = jnp.bfloat16, jnp.float32
    return pl.pallas_call(
        functools.partial(denoise_kernel, rows, cols, totals, variables, conds, width),
        out_shape=jax.ShapeDtypeStruct((channels, rows * cols), bf16),
        in_specs=[pl.BlockSpec(memory_space=pltpu.SMEM)] * 2
        + [pl.BlockSpec(memory_space=pltpu.VMEM)] * 7
        + [pl.BlockSpec(memory_space=pl.ANY)] * len(weights),
        scratch_shapes=[pltpu.VMEM(array.shape, array.dtype) for array in weights]
        + [
            pltpu.SemaphoreType.DMA((len(weights),)),
            pltpu.VMEM((tall, width, channels), bf16),
            pltpu.VMEM((tall - 2 * RIM_USED, width, channels), bf16),
            pltpu.VMEM((tall * width, points), bf16),
            pltpu.VMEM((tall * width, channels), f32),
            pltpu.VMEM((3, tall * width, channels), bf16),
            pltpu.VMEM((most * width, 2 * channels), bf16),
            pltpu.VMEM((3, most * width // 2, channels), bf16),
            pltpu.VMEM((3, tall * width, channels), bf16),
            pltpu.VMEM((most, width, channels), f32),
            pltpu.VMEM((most, width, channels), f32),
            pltpu.VMEM((2, points, channels), bf16),
        ],
        compiler_params=pltpu.CompilerParams(vmem_limit_bytes=VMEM),
        cost_estimate=pl.CostEstimate(flops=10**6, bytes_accessed=10**5, transcendentals=0),
        name="denoise",
    )(place, pick, *parts, strips, *weights)


def conv_weight(weight, depth, width):
    out, _, given = weight.shape
    weight = jnp.pad(weight, ((0, width - out), (0, 0), (0, depth - given)))
    return jnp.transpose(weight, (1, 2, 0)).reshape(9 * depth, width)


def pair_weight(weight):
    row = weight.shape[0] // 3
    return jnp.concatenate(
        [jnp.pad(weight, ((0, row), (0, 0))), jnp.pad(weight, ((row, 0), (0, 0)))], axis=1
    )


def shards(
    global_state,
    spec_filter,
    w_skip,
    w_mix,
    w_decode,
    regional_state,
    noise_draws,
    w_first,
    w_down,
    w_up,
    w_bridge,
    w_last,
    box_lat0,
    box_lon0,
    stencil_lat,
    stencil_lon,
):
    hours = noise_draws.shape[0]
    rows_here, cols_here = regional_state.shape[1:]
    row_start = lax.axis_index(PLANE) * rows_here
    col_start = lax.axis_index("col") * cols_here
    total_rows = rows_here * lax.axis_size(PLANE)
    total_cols = cols_here * lax.axis_size("col")
    assert hours == 2

    variables = regional_state.shape[0]
    conds = w_decode.shape[1]
    lanes = variables + conds
    noisy = (
        regional_state.astype(jnp.float32) + noise_level * noise_draws[0].astype(jnp.float32)
    ).astype(jnp.bfloat16)
    lat_shift = stencil_lat - (row_start + jnp.arange(rows_here, dtype=jnp.int32))[:, None] // RATIO
    lon_shift = stencil_lon - (col_start + jnp.arange(cols_here, dtype=jnp.int32))[None, :] // RATIO
    cells = (rows_here, cols_here)
    mids = jnp.concatenate(
        [
            noisy,
            jnp.zeros((conds,) + cells, jnp.bfloat16),
            lat_shift.astype(jnp.bfloat16)[None],
            lon_shift.astype(jnp.bfloat16)[None],
            jnp.zeros((LANES - lanes - 2,) + cells, jnp.bfloat16),
            noise_draws[1],
            jnp.zeros((LANES - variables,) + cells, jnp.bfloat16),
        ],
        axis=0,
    )
    mids = jnp.transpose(mids.reshape((2, LANES) + cells), (0, 2, 3, 1))
    mid0, mid1 = mids[0], mids[1]
    inner = RIM - RIM_USED
    high = window_extent(rows_here)
    place = jnp.stack([row_start, col_start]).astype(jnp.int32)
    totals = (total_rows, total_cols)

    def prepare():
        lows = jnp.concatenate([mid0[rows_here - RIM :], mid1[rows_here - inner :]], axis=0)
        highs = jnp.concatenate([mid0[:RIM], mid1[:inner]], axis=0)
        above, below = next_to(lows, highs, PLANE)

        def rim_cols(first, first_inner):
            wide, thin = slice(first, first + RIM), slice(first_inner, first_inner + inner)
            noise = jnp.concatenate([above[RIM:, thin], mid1[:, thin], below[RIM:, thin]], axis=0)
            noise = jnp.pad(
                noise, ((RIM_USED, RIM_USED), (0, RIM_COLS - RIM - inner), (0, 0))
            )
            return jnp.concatenate(
                [
                    jnp.concatenate([above[:RIM, wide], mid0[:, wide], below[:RIM, wide]], axis=0),
                    noise,
                ],
                axis=1,
            )

        left, right = next_to(
            rim_cols(cols_here - RIM, cols_here - inner), rim_cols(0, 0), "col"
        )
        weights = (
            pair_weight(conv_weight(0.5 * w_first, LANES, w_first.shape[0])),
            conv_weight(0.125 * w_down, w_down.shape[2], w_down.shape[0]),
            0.5 * w_up.T,
            0.5
            * jnp.concatenate(
                [jnp.pad(w_bridge.T, ((0, 0), (0, LANES))), jnp.pad(w_bridge.T, ((0, 0), (LANES, 0)))],
                axis=0,
            ),
            pair_weight(conv_weight(w_last, w_last.shape[2], LANES)),
        )
        return (mid0, mid1, above, below, left, right), weights

    by_latitude = lax.axis_size("col") == 4 and global_state.shape[0] % 4 == 0
    global_steps = global_by_latitude if by_latitude else global_by_channel
    finish, strips, pick, (parts, weights) = global_steps(
        hours, global_state, spec_filter, w_skip, w_mix, w_decode, box_lat0, box_lon0,
        rows_here, cols_here, prepare,
    )
    regional_final = denoise(
        rows_here, cols_here, totals, variables, conds, place, pick, parts, strips, weights
    )
    regional_final = regional_final[:variables].reshape((variables, rows_here, cols_here))
    return finish(regional_final)


def solution(mesh):
    return jax.shard_map(
        shards,
        mesh=mesh,
        in_specs=(
            P(PLANE, "col", None),
            P(None, None, "col"),
            P(),
            P(),
            P(),
            P(None, PLANE, "col"),
            P(None, None, PLANE, "col"),
            P(),
            P(),
            P(),
            P(),
            P(),
            P(),
            P(),
            P(PLANE, "col"),
            P(PLANE, "col"),
        ),
        out_specs=(P(PLANE, "col", None), P(None, PLANE, "col")),
        check_vma=False,
    )
```

```python
import functools
import math

import jax
import jax.numpy as jnp
import ml_dtypes
import numpy as np
from jax import lax
from jax.experimental import pallas as pl
from jax.experimental.pallas import tpu as pltpu
from jax.sharding import PartitionSpec as P

RATIO = 8
noise_level = 0.5
PLANE = ("grp", "row")
RIM = 9
RIM_USED = 4
LANES = 128
VMEM = 60 * 2**20
PACKED = 32
MODE_TILE = 64
STRIP = 8
FAR = -4096
RIM_COLS = 16


def fourier_tables(length, num_modes):
    position = np.arange(length, dtype=np.int64)[:, None]
    frequency = np.arange(num_modes, dtype=np.int64)[None, :]
    angle = (position * frequency % length).astype(np.float64) * (2.0 * math.pi / length)
    cosine = np.cos(angle)
    sine = np.sin(angle)
    factor = np.where(frequency == 0, 1.0, 2.0) / length
    forward = np.concatenate([cosine, -sine], axis=1).T.astype(ml_dtypes.bfloat16)
    inverse = np.concatenate([cosine * factor, -sine * factor], axis=1).astype(ml_dtypes.bfloat16)
    return forward, inverse


def round_up(size, unit):
    return -(-size // unit) * unit


def split_tables(length, num_modes):
    piece = length // 4
    place = np.arange(piece, dtype=np.int64)[:, None]

    def waves(mode):
        angle = (place * mode[None, :] % length).astype(np.float64) * (2.0 * math.pi / length)
        return np.cos(angle), np.sin(angle), np.where(mode == 0, 1.0, 2.0)[None, :] / length

    def padded(blocks, unit_rows, unit_cols):
        rows = []
        for row in blocks:
            cols = []
            for block in row:
                spare = [(0, -block.shape[0] % unit_rows), (0, -block.shape[1] % unit_cols)]
                cols.append(np.pad(block, spare))
            rows.append(np.concatenate(cols, axis=1))
        return np.concatenate(rows, axis=0).astype(ml_dtypes.bfloat16)

    forward, inverse = [], []
    for residue in (0, 2):
        cosine, sine, factor = waves(np.arange(residue, num_modes, 4))
        forward.append(padded([[cosine.T], [-sine.T]], MODE_TILE, LANES))
        inverse.append(padded([[cosine * factor, -sine * factor]], LANES, MODE_TILE))
    mode = np.arange(1, num_modes, 2)
    cosine, sine, factor = waves(mode)
    sign = np.where(mode % 4 == 1, 1.0, -1.0)[None, :]
    odd_forward = padded(
        [[cosine.T, (-sign * sine).T], [-sine.T, (-sign * cosine).T]], 2 * MODE_TILE, LANES
    )
    odd_inverse = padded(
        [
            [cosine * factor, -sine * factor],
            [-sign * sine * factor, -sign * cosine * factor],
        ],
        LANES,
        2 * MODE_TILE,
    )
    return tuple(
        jnp.asarray(table)
        for table in (np.stack(forward), odd_forward, np.stack(inverse), odd_inverse)
    )


def exchange(blocks, axis):
    return lax.all_to_all(blocks, axis, split_axis=0, concat_axis=0, tiled=True)


def spread(block, axis):
    return exchange(jnp.broadcast_to(block[None], (lax.axis_size(axis),) + block.shape), axis)


def filter_share(spec_filter):
    rows = 2 * spec_filter.shape[1]
    flat = spec_filter.reshape(rows, spec_filter.shape[2])
    share = rows // lax.axis_size(PLANE)
    mine = lax.dynamic_slice_in_dim(flat, lax.axis_index(PLANE) * share, share, 0)
    return mine.astype(jnp.bfloat16)


def every_channel(mine):
    count = lax.axis_size("col")
    me = lax.axis_index("col")
    blocks = [shift(mine, "col", -step) if step else mine for step in range(count)]
    ring = jnp.concatenate(blocks + blocks[:-1], axis=1)
    width = mine.shape[1]
    return lax.dynamic_slice_in_dim(ring, (count - me) % count * width, count * width, 1)


def gelu(x):
    slope = math.sqrt(2.0 / math.pi)
    half = 0.5 * x
    return half + half * jnp.tanh(x * (slope + (0.044715 * slope) * (x * x)))


def latitude_kernel(hours, turns, step, place_ref, *refs):
    piece_refs, refs = refs[:4], refs[4:]
    even_forward_ref, odd_forward_ref = refs[:2]
    far_refs, out_refs, strip_ref, refs = refs[2:8], refs[8:12], refs[12], refs[13:]
    near_refs, sems, refs = refs[:6], refs[6], refs[7:]
    filter_ref, even_inverse_ref, odd_inverse_ref, skip_ref, mix_ref, decode_ref = near_refs
    state_ref, gain_ref, coarse_ref, near_ref, packed_ref = refs
    copies = [
        pltpu.make_async_copy(far, near, sems.at[index])
        for index, (far, near) in enumerate(zip(far_refs, near_refs))
    ]
    for copy in copies:
        copy.start()
    f32, bf16 = jnp.float32, jnp.bfloat16
    piece, channels = piece_refs[0].shape[1:]
    padded = state_ref.shape[0] // 4
    group = LANES // PACKED
    span = near_ref.shape[0]
    rows = span // group
    spare = jnp.zeros((padded - piece, channels), bf16)
    for index in range(4):
        for turn in range(turns):
            state_ref[
                index * padded : (index + 1) * padded, turn * channels : (turn + 1) * channels
            ] = jnp.concatenate([piece_refs[index][turn], spare], axis=0)

    modes = filter_ref.shape[0] // 2

    def spread_gains():
        for index in range(channels // LANES):
            lanes = slice(index * LANES, (index + 1) * LANES)
            gain_ref[index, : 2 * modes, :] = filter_ref[:, lanes].astype(f32)
            gain_ref[index, 2 * modes :, :] = jnp.zeros((gain_ref.shape[1] - 2 * modes, LANES), f32)

    def gain_rows(low, count, stride):
        rows = pl.ds(low, count, stride=stride)
        tiles = [gain_ref[index, rows, :] for index in range(channels // LANES)]
        return jnp.concatenate(tiles * turns, axis=1)

    def gain(spectrum, low, stride):
        half = spectrum.shape[0] // 2
        real, imag = spectrum[:half], spectrum[half:]
        gain_real = gain_rows(low, half, stride)
        gain_imag = gain_rows(modes + low, half, stride)
        return jnp.concatenate(
            [
                (real * gain_real - imag * gain_imag).astype(bf16),
                (real * gain_imag + imag * gain_real).astype(bf16),
            ],
            axis=0,
        )

    def dot(left, right):
        return jnp.dot(left, right, preferred_element_type=f32)

    for hour in range(hours):
        pieces = [
            state_ref[index * padded : (index + 1) * padded, :].astype(f32) for index in range(4)
        ]
        both, other = pieces[0] + pieces[2], pieces[1] + pieces[3]
        spectra = [
            dot(even_forward_ref[index], mixed.astype(bf16))
            for index, mixed in enumerate((both + other, both - other))
        ]
        mixed = jnp.concatenate([pieces[0] - pieces[2], pieces[1] - pieces[3]], axis=0)
        spectra.append(dot(odd_forward_ref[...], mixed.astype(bf16)))
        if hour == 0:
            copies[0].wait()
            spread_gains()
            for copy in copies[1:]:
                copy.wait()
        shares = [
            dot(even_inverse_ref[index], gain(spectra[index], 2 * index, 4)) for index in range(2)
        ]
        odd = dot(odd_inverse_ref[...], gain(spectra[2], 1, 2))
        for index in range(4):
            here = slice(index * padded, (index + 1) * padded)
            even = shares[0] + shares[1] if index % 2 == 0 else shares[0] - shares[1]
            part = odd[:padded] if index % 2 == 0 else odd[padded:]
            spectral = even + part if index < 2 else even - part
            for turn in range(turns):
                lanes = slice(turn * channels, (turn + 1) * channels)
                state = state_ref[here, lanes]
                activated = gelu(spectral[:, lanes] + dot(state, skip_ref[...])).astype(bf16)
                update = dot(activated, mix_ref[...])
                state_ref[here, lanes] = (state.astype(f32) + update).astype(bf16)

        for index in range(2):
            here = pl.ds(pl.multiple_of(place_ref[index] * padded, LANES), padded)
            for turn in range(turns):
                lanes = slice(turn * channels, (turn + 1) * channels)
                coarse = dot(state_ref[here, lanes], decode_ref[...])
                coarse_ref[turn, index * piece : (index + 1) * piece, :] = coarse[:piece]
        for turn in range(turns):
            near_ref[...] = coarse_ref[turn, pl.ds(place_ref[2], span), :]
            packed = near_ref[pl.ds(0, rows, stride=group), :]
            for sub in range(1, group):
                packed += pltpu.roll(near_ref[pl.ds(sub, rows, stride=group), :], sub * PACKED, 1)
            packed_ref[turn, hour * rows : (hour + 1) * rows, :] = packed

    for index in range(4):
        for turn in range(turns):
            out_refs[index][turn] = state_ref[
                index * padded : index * padded + piece, turn * channels : (turn + 1) * channels
            ]
    for target in range(4):
        low = target * step // group
        for turn in range(turns):
            strip = [
                packed_ref[turn, hour * rows + low : hour * rows + low + STRIP, :]
                for hour in range(hours)
            ]
            strip_ref[target, turn * hours * STRIP : (turn + 1) * hours * STRIP, :] = jnp.concatenate(
                strip, axis=0
            ).astype(bf16)


def advance_latitudes(hours, step, place, pieces, tables, gains, w_skip, w_mix, w_decode):
    turns, piece, channels = pieces[0].shape
    padded = round_up(piece, LANES)
    group = LANES // PACKED
    span = round_up(3 * step + STRIP * group, 8 * group)
    decode = jnp.pad(w_decode, ((0, 0), (0, LANES - w_decode.shape[1])))
    modes = gains.shape[0] // 2
    late = (gains,) + tables[2:] + (w_skip, w_mix, decode)
    spare = max(4 * (tables[0].shape[1] // 2), 2 * (tables[1].shape[0] // 2)) - modes
    results = pl.pallas_call(
        functools.partial(latitude_kernel, hours, turns, step),
        out_shape=tuple(
            jax.ShapeDtypeStruct((turns, piece, channels), jnp.bfloat16) for _ in pieces
        )
        + (jax.ShapeDtypeStruct((4, turns * hours * STRIP, LANES), jnp.bfloat16),),
        in_specs=[pl.BlockSpec(memory_space=pltpu.SMEM)]
        + [pl.BlockSpec(memory_space=pltpu.VMEM)] * 6
        + [pl.BlockSpec(memory_space=pl.ANY)] * len(late),
        scratch_shapes=[pltpu.VMEM(array.shape, array.dtype) for array in late]
        + [
            pltpu.SemaphoreType.DMA((len(late),)),
            pltpu.VMEM((4 * padded, turns * channels), jnp.bfloat16),
            pltpu.VMEM((channels // LANES, gains.shape[0] + spare, LANES), jnp.float32),
            pltpu.VMEM((turns, 2 * piece, LANES), jnp.float32),
            pltpu.VMEM((span, LANES), jnp.float32),
            pltpu.VMEM((turns, hours * span // group, LANES), jnp.float32),
        ],
        compiler_params=pltpu.CompilerParams(vmem_limit_bytes=VMEM),
        cost_estimate=pl.CostEstimate(
            flops=turns * 16 * 10**9,
            bytes_accessed=turns * 6 * 2**20,
            transcendentals=hours * turns * 4 * piece * channels,
        ),
        name="advance_latitudes",
    )(place, *pieces, *tables[:2], *late)
    return results[:4], results[4]


def collate_kernel(count, place_ref, *refs):
    pieces, out_ref, sems = refs[:count], refs[count], refs[count + 1]
    copies = [
        pltpu.make_async_copy(
            piece, out_ref.at[pl.ds(place_ref[index], piece.shape[0])], sems.at[index]
        )
        for index, piece in enumerate(pieces)
    ]
    for copy in copies:
        copy.start()
    for copy in copies:
        copy.wait()


def collate(place, pieces):
    count = len(pieces)
    turns, piece, channels = pieces[0].shape
    return pl.pallas_call(
        functools.partial(collate_kernel, count),
        out_shape=jax.ShapeDtypeStruct((count * turns, piece, channels), pieces[0].dtype),
        in_specs=[pl.BlockSpec(memory_space=pltpu.SMEM)]
        + [pl.BlockSpec(memory_space=pltpu.VMEM)] * count,
        out_specs=pl.BlockSpec(memory_space=pl.ANY),
        scratch_shapes=[pltpu.SemaphoreType.DMA((count,))],
        name="collate",
    )(place, *pieces)


def shift(block, axis, step):
    count = lax.axis_size(axis)
    return lax.ppermute(block, axis, [(source, (source + step) % count) for source in range(count)])


def global_hour(current, spec_filter, w_skip, w_mix, forward, inverse):
    longitude = lax.all_to_all(current, "col", split_axis=2, concat_axis=1, tiled=True)
    spectrum = jnp.einsum("alc,ml->amc", longitude, forward, preferred_element_type=jnp.float32)
    num_modes = spec_filter.shape[1]
    real_part = spectrum[:, :num_modes, :]
    imag_part = spectrum[:, num_modes:, :]
    filt_real = spec_filter[0][None]
    filt_imag = spec_filter[1][None]
    mixed = jnp.concatenate(
        [
            real_part * filt_real - imag_part * filt_imag,
            real_part * filt_imag + imag_part * filt_real,
        ],
        axis=1,
    ).astype(jnp.bfloat16)
    filtered = jnp.einsum("amc,lm->alc", mixed, inverse, preferred_element_type=jnp.float32).astype(
        jnp.bfloat16
    )
    spectral = lax.all_to_all(filtered, "col", split_axis=1, concat_axis=2, tiled=True)
    skipped = jnp.einsum("alc,cd->ald", current, w_skip, preferred_element_type=jnp.float32)
    activated = jax.nn.gelu(spectral.astype(jnp.float32) + skipped).astype(jnp.bfloat16)
    update = jnp.einsum("ald,de->ale", activated, w_mix, preferred_element_type=jnp.float32)
    return (current.astype(jnp.float32) + update).astype(jnp.bfloat16)


def window_extent(cells):
    return (cells + RIM - 1) // RATIO + 3 - (-RIM // RATIO)


def window_base():
    return -(-RIM // RATIO)


def global_by_latitude(
    hours, global_state, spec_filter, w_skip, w_mix, w_decode, box_lat0, box_lon0, rows_here,
    cols_here, prepare,
):
    count = lax.axis_size("col")
    me = lax.axis_index("col")
    lats_here, piece, _ = global_state.shape
    turns = lats_here // count
    tables = split_tables(piece * count, spec_filter.shape[1])
    owners = [(me - step) % count * turns for step in range(count)]
    mine = filter_share(spec_filter)
    bands = [lax.dynamic_slice_in_dim(global_state, owner, turns, 0) for owner in owners]
    bands, mine = lax.optimization_barrier((bands, mine))
    received = [shift(band, "col", -step) if step else band for step, band in enumerate(bands)]
    wide = every_channel(mine)
    parts, weights = prepare()
    gains = spread(wide, PLANE).reshape(-1, wide.shape[1])
    start = (box_lon0[0] - window_base() - me * piece) % (piece * count)
    place = jnp.stack([start // piece, (start // piece + 1) % count, start % piece]).astype(jnp.int32)
    received, weights = lax.optimization_barrier((received, weights))
    outcome, strips = advance_latitudes(
        hours, cols_here // RATIO, place, received, tables, gains, w_skip, w_mix, w_decode
    )
    strips, parts = lax.optimization_barrier((strips, parts))
    near = []
    for step in range(count):
        strip = lax.dynamic_index_in_dim(strips, (me - step) % count, 0, keepdims=False)
        near.append(shift(strip, "col", -step) if step else strip)
    near, outcome = lax.optimization_barrier((jnp.stack(near), outcome))
    got = spread(near, PLANE)
    plane = lax.axis_size(PLANE)
    got = got.reshape((plane * lats_here, -1, LANES))
    lat = box_lat0[0] - window_base() + lax.axis_index(PLANE) * (rows_here // RATIO)
    lat = jnp.clip(lat + jnp.arange(window_extent(rows_here), dtype=jnp.int32), 0, plane * lats_here - 1)
    band, lat = lat // lats_here, lat % lats_here
    pick = (band * count + (lat // turns - me) % count) * turns + lat % turns
    finals = [shift(block, "col", step) if step else block for step, block in enumerate(outcome)]

    def finish(after):
        blocks, after = lax.optimization_barrier((finals, after))
        return collate(jnp.stack(owners).astype(jnp.int32), blocks), after

    return finish, got, pick.astype(jnp.int32), (parts, weights)


def global_by_channel(
    hours, global_state, spec_filter, w_skip, w_mix, w_decode, box_lat0, box_lon0, rows_here,
    cols_here, prepare,
):
    count = lax.axis_size("col")
    prepared = prepare()
    forward, inverse = fourier_tables(global_state.shape[1] * count, spec_filter.shape[1])
    base = window_base()
    high, wide = window_extent(rows_here), window_extent(cols_here)
    span = (count - 1) * (cols_here // RATIO) + wide
    lat_start = box_lat0[0] + lax.axis_index(PLANE) * (rows_here // RATIO)
    lon_start = box_lon0[0] + lax.axis_index("col") * (cols_here // RATIO)
    windows = []
    for _ in range(hours):
        global_state = global_hour(global_state, spec_filter, w_skip, w_mix, forward, inverse)
        coarse = jnp.einsum(
            "alc,ck->alk", global_state, w_decode, preferred_element_type=jnp.float32
        ).astype(jnp.bfloat16)
        coarse = lax.all_gather(coarse, "col", axis=1, tiled=True)
        coarse = jnp.pad(coarse, ((0, 0), (base, span), (0, 0)))
        coarse = lax.dynamic_slice_in_dim(coarse, box_lon0[0], base + span, 1)
        coarse = lax.all_gather(coarse, PLANE, axis=0, tiled=True)
        coarse = lax.dynamic_slice_in_dim(coarse, lon_start - box_lon0[0], wide, 1)
        coarse = jnp.pad(coarse, ((base, high), (0, 0), (0, 0)))
        coarse = lax.dynamic_slice_in_dim(coarse, lat_start, high, 0)
        windows.append(coarse)
    group = LANES // PACKED
    windows = jnp.stack(windows, axis=1)
    windows = jnp.pad(
        windows, ((0, 0), (0, 0), (0, STRIP * group - wide), (0, PACKED - windows.shape[3]))
    )
    windows = windows.reshape(high, hours * STRIP, LANES)
    return lambda after: (global_state, after), windows, jnp.arange(high, dtype=jnp.int32), prepared


def next_to(low, high, axis):
    count = lax.axis_size(axis)
    forward = [(i, i + 1) for i in range(count - 1)]
    backward = [(target, source) for source, target in forward]
    return lax.ppermute(low, axis, forward), lax.ppermute(high, axis, backward)


def grid_place(start_ref, total, base, extent):
    place = start_ref + base + lax.broadcasted_iota(jnp.int32, (extent, 1), 0)
    return (place >= 0) & (place < total)


def denoise_kernel(
    rows, cols, totals, variables, conds, width, place_ref, pick_ref, mid0_ref, mid1_ref, above_ref,
    below_ref, left_ref, right_ref, strip_ref, *refs
):
    far_refs, out_ref, refs = refs[:5], refs[5], refs[6:]
    near_refs, sems, refs = refs[:5], refs[5], refs[6:]
    first_w_ref, down_w_ref, up_w_ref, bridge_w_ref, last_w_ref = near_refs
    noisy_ref, noise_ref, blend_ref, own_ref, stack_ref, first_ref, pooled_ref, third_ref, pair_ref, spread_ref, window_ref = refs
    copies = [
        pltpu.make_async_copy(far, near, sems.at[index])
        for index, (far, near) in enumerate(zip(far_refs, near_refs))
    ]
    for copy in copies:
        copy.start()
    half = width // 2
    pad = (width - cols) // 2
    channels = mid0_ref.shape[2]
    f32, bf16 = jnp.float32, jnp.bfloat16

    inner = RIM - RIM_USED
    for ref, mid_ref, rim, part in ((noisy_ref, mid0_ref, RIM, 0), (noise_ref, mid1_ref, inner, RIM)):
        ref[0:rim, pad : pad + cols, :] = above_ref[part : part + rim]
        ref[rim : rim + rows, pad : pad + cols, :] = mid_ref[...]
        ref[rim + rows :, pad : pad + cols, :] = below_ref[part : part + rim]
        skip = RIM - rim
        for side_ref, low, to in ((left_ref, 0, pad - rim), (right_ref, pad + cols, 0)):
            side = side_ref[skip : skip + rows + 2 * rim].astype(f32)
            side = pltpu.roll(side, (to - part) % pad, 1)
            ref[:, low : low + pad, :] = side.astype(bf16)

    is_in = grid_place(place_ref[1], totals[1], -pad, width)
    col_in = is_in.astype(f32)
    base = window_base()
    col = lax.broadcasted_iota(jnp.int32, (width, 1), 0) - pad
    frac_col = ((col % RATIO).astype(f32) + 0.5) / RATIO
    col_base = jnp.where(is_in, (col + pad) // RATIO - pad // RATIO + base, FAR).astype(f32) + frac_col
    group = LANES // PACKED
    high = pick_ref.shape[0]
    point = lax.broadcasted_iota(jnp.int32, (1, group * high * STRIP), 1)
    point_lat = (point // STRIP % high).astype(f32)
    point_lon = (point % STRIP * group + point // (STRIP * high)).astype(f32)

    def blend(row):
        whole = row // RATIO
        frac_row = (row - whole * RATIO + 0.5) / RATIO
        there = place_ref[0] + row
        row_base = jnp.where((there >= 0) & (there < totals[0]), whole + base + frac_row, float(FAR))
        shifts = noisy_ref[row + RIM].astype(f32)
        lat = row_base + shifts[:, variables + conds : variables + conds + 1]
        lon = col_base + shifts[:, variables + conds + 1 : variables + conds + 2]
        weight_lat = jnp.maximum(1.0 - jnp.abs(point_lat - lat), 0.0)
        weight_lon = jnp.maximum(1.0 - jnp.abs(point_lon - lon), 0.0)
        return (weight_lat * weight_lon).astype(bf16)

    edges = [jnp.broadcast_to(col_in[low : low + pad], (pad, channels)) for low in (0, pad + cols)]
    lane = lax.broadcasted_iota(jnp.int32, (1, channels), 1)
    is_state = lane < variables
    is_cond = (lane >= variables) & (lane < variables + conds)
    strips = [strip_ref[pick_ref[index]].astype(f32) for index in range(high)]
    for hour in range(2):
        near = jnp.concatenate([s[hour * STRIP : (hour + 1) * STRIP] for s in strips], axis=0)
        for turn in range(LANES // PACKED):
            moved = pltpu.roll(near, (variables - turn * PACKED) % LANES, 1)
            window_ref[hour, turn * high * STRIP : (turn + 1) * high * STRIP, :] = jnp.where(
                is_cond, moved, 0.0
            ).astype(bf16)

    def flat(start, count, unit):
        return slice(start * unit, (start + count) * unit)

    def mask(value, row):
        low, mid, high = value[:pad], value[pad : pad + cols], value[pad + cols :]
        value = jnp.concatenate([low * edges[0], mid, high * edges[1]], axis=0)
        if 0 <= row < rows:
            return value
        there = place_ref[0] + row
        return value * jnp.where((there >= 0) & (there < totals[0]), 1.0, 0.0)

    def keep(ref, where, value):
        size = value.shape[0]
        ref[0, where, :] = pltpu.roll(value, 1, 0).astype(bf16)
        ref[1, where, :] = value.astype(bf16)
        ref[2, where, :] = pltpu.roll(value, size - 1, 0).astype(bf16)

    def pairs(ref, row, count):
        blocks = []
        for pair in range(count):
            taps = [
                ref[shift, flat(row + 2 * pair + step, 1, width), :]
                for step in range(4)
                for shift in range(3)
            ]
            blocks.append(jnp.concatenate(taps, axis=1))
        return jnp.concatenate(blocks, axis=0)

    def silu_of_half(half_value):
        return half_value + half_value * jnp.tanh(half_value)

    for hour in range(2):
        rim = RIM - RIM_USED * hour
        tall = rows + 2 * rim

        for row in range(0, tall, 2):
            here = flat(row, 2, width)
            if hour == 0:
                weights = jnp.concatenate([blend(row - RIM), blend(row + 1 - RIM)], axis=0)
                blend_ref[here, :] = weights
            else:
                weights = blend_ref[flat(row + RIM - rim, 2, width), :]
            cond = jnp.dot(weights, window_ref[hour], preferred_element_type=f32)
            if hour == 0:
                own = noisy_ref[row : row + 2].reshape(2 * width, channels).astype(f32)
                own_ref[here, :] = own
            else:
                own = own_ref[here, :]
            keep(stack_ref, here, jnp.where(is_state, own, cond))

        if hour == 0:
            copies[0].wait()
        for row in range(0, tall - 2, 8):
            value = jnp.dot(
                pairs(stack_ref, row, 4), first_w_ref[...], preferred_element_type=f32
            )
            for pair in range(4):
                top = row + 2 * pair
                here = flat(top // 2, 1, width)
                part = silu_of_half(value[pair * width : (pair + 1) * width])
                upper = mask(part[:, :channels], top - rim + 1)
                lower = mask(part[:, channels:], top - rim + 2)
                first_ref[here, :channels] = upper.astype(bf16)
                first_ref[here, channels:] = lower.astype(bf16)
                pair_ref[top // 2] = upper + lower
                even = pair_ref[top // 2, pl.ds(0, half, stride=2), :]
                odd = pair_ref[top // 2, pl.ds(1, half, stride=2), :]
                keep(pooled_ref, flat(top // 2, 1, half), even + odd)

        if hour == 0:
            for copy in copies[1:4]:
                copy.wait()
        half_rows = (tall - 2) // 2 - 2
        part = half_rows // 2
        for row in (0, part):
            taps = [
                pooled_ref[shift, flat(row + step, part, half), :]
                for step in range(3)
                for shift in range(3)
            ]
            second = jnp.dot(
                jnp.concatenate(taps, axis=1), down_w_ref[...], preferred_element_type=f32
            )
            lifted = jnp.dot(
                silu_of_half(second).astype(bf16), up_w_ref[...], preferred_element_type=f32
            )
            bridged = jnp.dot(
                first_ref[flat(row + 1, part, width), :], bridge_w_ref[...], preferred_element_type=f32
            )
            for step in range(part):
                own = lifted[step * half : (step + 1) * half]
                spread_ref[row + step, pl.ds(0, half, stride=2), :] = own
                spread_ref[row + step, pl.ds(1, half, stride=2), :] = own
                own = spread_ref[row + step]
                top = 2 * (row + step)
                for side in range(2):
                    value = bridged[
                        step * width : (step + 1) * width, side * channels : (side + 1) * channels
                    ]
                    value = mask(silu_of_half(value + own), top + side - rim + 3)
                    keep(third_ref, flat(top + side, 1, width), value)

        if hour == 0:
            copies[4].wait()
        skip = 1 if hour == 1 else 0
        count = (rows + 2 * (rim - RIM_USED)) // 2 if hour == 0 else rows // 2
        for first in range(0, count, 4):
            size = min(4, count - first)
            values = jnp.dot(
                pairs(third_ref, 2 * first + skip, size), last_w_ref[...], preferred_element_type=f32
            )
            for index in range(2 * size):
                pair, side = divmod(index, 2)
                row = 2 * first + index
                fresh = values[
                    pair * width : (pair + 1) * width, side * channels : (side + 1) * channels
                ]
                fresh = own_ref[flat(row + RIM_USED + skip, 1, width), :] + fresh
                if hour == 0:
                    fresh = fresh + noise_level * noise_ref[row].astype(f32)
                    own_ref[flat(row, 1, width), :] = mask(fresh, row - rim + RIM_USED)
                else:
                    out_ref[:, row * cols : (row + 1) * cols] = fresh[pad : pad + cols].T.astype(bf16)


def denoise(rows, cols, totals, variables, conds, place, pick, parts, strips, weights):
    mid0, _, _, _, left, _ = parts
    width, channels = cols + 2 * left.shape[1], mid0.shape[2]
    tall = rows + 2 * RIM
    most = (tall - 2) // 2
    points = LANES // PACKED * pick.shape[0] * STRIP
    bf16, f32 = jnp.bfloat16, jnp.float32
    return pl.pallas_call(
        functools.partial(denoise_kernel, rows, cols, totals, variables, conds, width),
        out_shape=jax.ShapeDtypeStruct((channels, rows * cols), bf16),
        in_specs=[pl.BlockSpec(memory_space=pltpu.SMEM)] * 2
        + [pl.BlockSpec(memory_space=pltpu.VMEM)] * 7
        + [pl.BlockSpec(memory_space=pl.ANY)] * len(weights),
        scratch_shapes=[pltpu.VMEM(array.shape, array.dtype) for array in weights]
        + [
            pltpu.SemaphoreType.DMA((len(weights),)),
            pltpu.VMEM((tall, width, channels), bf16),
            pltpu.VMEM((tall - 2 * RIM_USED, width, channels), bf16),
            pltpu.VMEM((tall * width, points), bf16),
            pltpu.VMEM((tall * width, channels), f32),
            pltpu.VMEM((3, tall * width, channels), bf16),
            pltpu.VMEM((most * width, 2 * channels), bf16),
            pltpu.VMEM((3, most * width // 2, channels), bf16),
            pltpu.VMEM((3, tall * width, channels), bf16),
            pltpu.VMEM((most, width, channels), f32),
            pltpu.VMEM((most, width, channels), f32),
            pltpu.VMEM((2, points, channels), bf16),
        ],
        compiler_params=pltpu.CompilerParams(vmem_limit_bytes=VMEM),
        cost_estimate=pl.CostEstimate(flops=10**6, bytes_accessed=10**5, transcendentals=0),
        name="denoise",
    )(place, pick, *parts, strips, *weights)


def conv_weight(weight, depth, width):
    out, _, given = weight.shape
    weight = jnp.pad(weight, ((0, width - out), (0, 0), (0, depth - given)))
    return jnp.transpose(weight, (1, 2, 0)).reshape(9 * depth, width)


def pair_weight(weight):
    row = weight.shape[0] // 3
    return jnp.concatenate(
        [jnp.pad(weight, ((0, row), (0, 0))), jnp.pad(weight, ((row, 0), (0, 0)))], axis=1
    )


def shards(
    global_state,
    spec_filter,
    w_skip,
    w_mix,
    w_decode,
    regional_state,
    noise_draws,
    w_first,
    w_down,
    w_up,
    w_bridge,
    w_last,
    box_lat0,
    box_lon0,
    stencil_lat,
    stencil_lon,
):
    hours = noise_draws.shape[0]
    rows_here, cols_here = regional_state.shape[1:]
    row_start = lax.axis_index(PLANE) * rows_here
    col_start = lax.axis_index("col") * cols_here
    total_rows = rows_here * lax.axis_size(PLANE)
    total_cols = cols_here * lax.axis_size("col")
    assert hours == 2

    variables = regional_state.shape[0]
    conds = w_decode.shape[1]
    lanes = variables + conds
    noisy = (
        regional_state.astype(jnp.float32) + noise_level * noise_draws[0].astype(jnp.float32)
    ).astype(jnp.bfloat16)
    lat_shift = stencil_lat - (row_start + jnp.arange(rows_here, dtype=jnp.int32))[:, None] // RATIO
    lon_shift = stencil_lon - (col_start + jnp.arange(cols_here, dtype=jnp.int32))[None, :] // RATIO
    cells = (rows_here, cols_here)
    mids = jnp.concatenate(
        [
            noisy,
            jnp.zeros((conds,) + cells, jnp.bfloat16),
            lat_shift.astype(jnp.bfloat16)[None],
            lon_shift.astype(jnp.bfloat16)[None],
            jnp.zeros((LANES - lanes - 2,) + cells, jnp.bfloat16),
            noise_draws[1],
            jnp.zeros((LANES - variables,) + cells, jnp.bfloat16),
        ],
        axis=0,
    )
    mids = jnp.transpose(mids.reshape((2, LANES) + cells), (0, 2, 3, 1))
    mid0, mid1 = mids[0], mids[1]
    inner = RIM - RIM_USED
    high = window_extent(rows_here)
    place = jnp.stack([row_start, col_start]).astype(jnp.int32)
    totals = (total_rows, total_cols)

    def prepare():
        lows = jnp.concatenate([mid0[rows_here - RIM :], mid1[rows_here - inner :]], axis=0)
        highs = jnp.concatenate([mid0[:RIM], mid1[:inner]], axis=0)
        above, below = next_to(lows, highs, PLANE)

        def rim_cols(first, first_inner):
            wide, thin = slice(first, first + RIM), slice(first_inner, first_inner + inner)
            noise = jnp.concatenate([above[RIM:, thin], mid1[:, thin], below[RIM:, thin]], axis=0)
            noise = jnp.pad(
                noise, ((RIM_USED, RIM_USED), (0, RIM_COLS - RIM - inner), (0, 0))
            )
            return jnp.concatenate(
                [
                    jnp.concatenate([above[:RIM, wide], mid0[:, wide], below[:RIM, wide]], axis=0),
                    noise,
                ],
                axis=1,
            )

        left, right = next_to(
            rim_cols(cols_here - RIM, cols_here - inner), rim_cols(0, 0), "col"
        )
        weights = (
            pair_weight(conv_weight(0.5 * w_first, LANES, w_first.shape[0])),
            conv_weight(0.125 * w_down, w_down.shape[2], w_down.shape[0]),
            0.5 * w_up.T,
            0.5
            * jnp.concatenate(
                [jnp.pad(w_bridge.T, ((0, 0), (0, LANES))), jnp.pad(w_bridge.T, ((0, 0), (LANES, 0)))],
                axis=0,
            ),
            pair_weight(conv_weight(w_last, w_last.shape[2], LANES)),
        )
        return (mid0, mid1, above, below, left, right), weights

    by_latitude = lax.axis_size("col") == 4 and global_state.shape[0] % 4 == 0
    global_steps = global_by_latitude if by_latitude else global_by_channel
    finish, strips, pick, (parts, weights) = global_steps(
        hours, global_state, spec_filter, w_skip, w_mix, w_decode, box_lat0, box_lon0,
        rows_here, cols_here, prepare,
    )
    regional_final = denoise(
        rows_here, cols_here, totals, variables, conds, place, pick, parts, strips, weights
    )
    regional_final = regional_final[:variables].reshape((variables, rows_here, cols_here))
    return finish(regional_final)


def solution(mesh):
    return jax.shard_map(
        shards,
        mesh=mesh,
        in_specs=(
            P(PLANE, "col", None),
            P(None, None, "col"),
            P(),
            P(),
            P(),
            P(None, PLANE, "col"),
            P(None, None, PLANE, "col"),
            P(),
            P(),
            P(),
            P(),
            P(),
            P(),
            P(),
            P(PLANE, "col"),
            P(PLANE, "col"),
        ),
        out_specs=(P(PLANE, "col", None), P(None, PLANE, "col")),
        check_vma=False,
    )
```

```python
import functools
import math

import jax
import jax.numpy as jnp
import ml_dtypes
import numpy as np
from jax import lax
from jax.experimental import pallas as pl
from jax.experimental.pallas import tpu as pltpu
from jax.sharding import PartitionSpec as P

RATIO = 8
noise_level = 0.5
PLANE = ("grp", "row")
RIM = 9
RIM_USED = 4
LANES = 128
VMEM = 60 * 2**20
PACKED = 32
MODE_TILE = 64
STRIP = 8
FAR = -4096
RIM_COLS = 16


def fourier_tables(length, num_modes):
    position = np.arange(length, dtype=np.int64)[:, None]
    frequency = np.arange(num_modes, dtype=np.int64)[None, :]
    angle = (position * frequency % length).astype(np.float64) * (2.0 * math.pi / length)
    cosine = np.cos(angle)
    sine = np.sin(angle)
    factor = np.where(frequency == 0, 1.0, 2.0) / length
    forward = np.concatenate([cosine, -sine], axis=1).T.astype(ml_dtypes.bfloat16)
    inverse = np.concatenate([cosine * factor, -sine * factor], axis=1).astype(ml_dtypes.bfloat16)
    return forward, inverse


def round_up(size, unit):
    return -(-size // unit) * unit


def split_tables(length, num_modes):
    piece = length // 4
    place = np.arange(piece, dtype=np.int64)[:, None]

    def waves(mode):
        angle = (place * mode[None, :] % length).astype(np.float64) * (2.0 * math.pi / length)
        return np.cos(angle), np.sin(angle), np.where(mode == 0, 1.0, 2.0)[None, :] / length

    def padded(blocks, unit_rows, unit_cols):
        rows = []
        for row in blocks:
            cols = []
            for block in row:
                spare = [(0, -block.shape[0] % unit_rows), (0, -block.shape[1] % unit_cols)]
                cols.append(np.pad(block, spare))
            rows.append(np.concatenate(cols, axis=1))
        return np.concatenate(rows, axis=0).astype(ml_dtypes.bfloat16)

    forward, inverse = [], []
    for residue in (0, 2):
        cosine, sine, factor = waves(np.arange(residue, num_modes, 4))
        forward.append(padded([[cosine.T], [-sine.T]], MODE_TILE, LANES))
        inverse.append(padded([[cosine * factor, -sine * factor]], LANES, MODE_TILE))
    mode = np.arange(1, num_modes, 2)
    cosine, sine, factor = waves(mode)
    sign = np.where(mode % 4 == 1, 1.0, -1.0)[None, :]
    odd_forward = padded(
        [[cosine.T, (-sign * sine).T], [-sine.T, (-sign * cosine).T]], 2 * MODE_TILE, LANES
    )
    odd_inverse = padded(
        [
            [cosine * factor, -sine * factor],
            [-sign * sine * factor, -sign * cosine * factor],
        ],
        LANES,
        2 * MODE_TILE,
    )
    return tuple(
        jnp.asarray(table)
        for table in (np.stack(forward), odd_forward, np.stack(inverse), odd_inverse)
    )


def exchange(blocks, axis):
    return lax.all_to_all(blocks, axis, split_axis=0, concat_axis=0, tiled=True)


def spread(block, axis):
    return exchange(jnp.broadcast_to(block[None], (lax.axis_size(axis),) + block.shape), axis)


def filter_share(spec_filter):
    rows = 2 * spec_filter.shape[1]
    flat = spec_filter.reshape(rows, spec_filter.shape[2])
    share = rows // lax.axis_size(PLANE)
    mine = lax.dynamic_slice_in_dim(flat, lax.axis_index(PLANE) * share, share, 0)
    return mine.astype(jnp.bfloat16)


def every_channel(mine):
    count = lax.axis_size("col")
    me = lax.axis_index("col")
    blocks = [shift(mine, "col", -step) if step else mine for step in range(count)]
    ring = jnp.concatenate(blocks + blocks[:-1], axis=1)
    width = mine.shape[1]
    return lax.dynamic_slice_in_dim(ring, (count - me) % count * width, count * width, 1)


def gelu(x):
    slope = math.sqrt(2.0 / math.pi)
    half = 0.5 * x
    return half + half * jnp.tanh(x * (slope + (0.044715 * slope) * (x * x)))


def latitude_kernel(hours, turns, step, place_ref, *refs):
    piece_refs, refs = refs[:4], refs[4:]
    even_forward_ref, odd_forward_ref = refs[:2]
    far_refs, out_refs, strip_ref, refs = refs[2:8], refs[8:12], refs[12], refs[13:]
    near_refs, sems, refs = refs[:6], refs[6], refs[7:]
    filter_ref, even_inverse_ref, odd_inverse_ref, skip_ref, mix_ref, decode_ref = near_refs
    state_ref, gain_ref, coarse_ref, near_ref, packed_ref = refs
    copies = [
        pltpu.make_async_copy(far, near, sems.at[index])
        for index, (far, near) in enumerate(zip(far_refs, near_refs))
    ]
    for copy in copies:
        copy.start()
    f32, bf16 = jnp.float32, jnp.bfloat16
    piece, channels = piece_refs[0].shape[1:]
    padded = state_ref.shape[0] // 4
    group = LANES // PACKED
    span = near_ref.shape[0]
    rows = span // group
    spare = jnp.zeros((padded - piece, channels), bf16)
    for index in range(4):
        for turn in range(turns):
            state_ref[
                index * padded : (index + 1) * padded, turn * channels : (turn + 1) * channels
            ] = jnp.concatenate([piece_refs[index][turn], spare], axis=0)

    modes = filter_ref.shape[0] // 2

    def spread_gains():
        for index in range(channels // LANES):
            lanes = slice(index * LANES, (index + 1) * LANES)
            gain_ref[index, : 2 * modes, :] = filter_ref[:, lanes].astype(f32)
            gain_ref[index, 2 * modes :, :] = jnp.zeros((gain_ref.shape[1] - 2 * modes, LANES), f32)

    def gain_rows(low, count, stride):
        rows = pl.ds(low, count, stride=stride)
        tiles = [gain_ref[index, rows, :] for index in range(channels // LANES)]
        return jnp.concatenate(tiles * turns, axis=1)

    def gain(real, imag, low, stride):
        gain_real = gain_rows(low, real.shape[0], stride)
        gain_imag = gain_rows(modes + low, real.shape[0], stride)
        return (
            (real * gain_real - imag * gain_imag).astype(bf16),
            (real * gain_imag + imag * gain_real).astype(bf16),
        )

    def dot(left, right):
        return jnp.dot(left, right, preferred_element_type=f32)

    for hour in range(hours):
        pieces = [
            state_ref[index * padded : (index + 1) * padded, :].astype(f32) for index in range(4)
        ]
        mixed = jnp.concatenate([pieces[0] - pieces[2], pieces[1] - pieces[3]], axis=0).astype(bf16)
        span_odd = odd_forward_ref.shape[0] // 2
        thirds = span_odd // 3
        spectra = []
        for index in range(3):
            low = index * thirds
            spectra.append(
                (
                    dot(odd_forward_ref[low : low + thirds, :], mixed),
                    dot(odd_forward_ref[span_odd + low : span_odd + low + thirds, :], mixed),
                )
            )
            if index == 0:
                both, other = pieces[0] + pieces[2], pieces[1] + pieces[3]
                mixes = [(both + other).astype(bf16), (both - other).astype(bf16)]
        evens = [dot(even_forward_ref[index], mixes[index]) for index in range(2)]
        if hour == 0:
            copies[0].wait()
            spread_gains()
            for copy in copies[1:]:
                copy.wait()
        odd = [gain(*spectra[index], 1 + 2 * index * thirds, 2) for index in range(3)]
        odd = jnp.concatenate([part[0] for part in odd] + [part[1] for part in odd], axis=0)
        odd_shares = [dot(odd_inverse_ref[:padded, :], odd)]
        shares = []
        for index in range(2):
            half = evens[index].shape[0] // 2
            even = gain(evens[index][:half], evens[index][half:], 2 * index, 4)
            shares.append(dot(even_inverse_ref[index], jnp.concatenate(even, axis=0)))
        odd_shares.append(dot(odd_inverse_ref[padded:, :], odd))

        def block_of(ref, index, turn):
            return ref[
                index * padded : (index + 1) * padded, turn * channels : (turn + 1) * channels
            ]

        order = [(index, turn) for index in (0, 2, 1, 3) for turn in range(turns)]
        skipped = dot(block_of(state_ref, *order[0]), skip_ref[...])
        for place, (index, turn) in enumerate(order):
            if place + 1 < len(order):
                following = dot(block_of(state_ref, *order[place + 1]), skip_ref[...])
            if turn == 0:
                even = shares[0] + shares[1] if index % 2 == 0 else shares[0] - shares[1]
                spectral = even + odd_shares[index % 2] if index < 2 else even - odd_shares[index % 2]
            own = spectral[:, turn * channels : (turn + 1) * channels]
            activated = gelu(own + skipped).astype(bf16)
            fresh = block_of(state_ref, index, turn).astype(f32) + dot(activated, mix_ref[...])
            state_ref[
                index * padded : (index + 1) * padded, turn * channels : (turn + 1) * channels
            ] = fresh.astype(bf16)
            skipped = following

        for index in range(2):
            here = pl.ds(pl.multiple_of(place_ref[index] * padded, LANES), padded)
            for turn in range(turns):
                lanes = slice(turn * channels, (turn + 1) * channels)
                coarse = dot(state_ref[here, lanes], decode_ref[...])
                coarse_ref[turn, index * piece : (index + 1) * piece, :] = coarse[:piece]
        for turn in range(turns):
            near_ref[...] = coarse_ref[turn, pl.ds(place_ref[2], span), :]
            packed = near_ref[pl.ds(0, rows, stride=group), :]
            for sub in range(1, group):
                packed += pltpu.roll(near_ref[pl.ds(sub, rows, stride=group), :], sub * PACKED, 1)
            packed_ref[turn, hour * rows : (hour + 1) * rows, :] = packed

    for index in range(4):
        for turn in range(turns):
            out_refs[index][turn] = state_ref[
                index * padded : index * padded + piece, turn * channels : (turn + 1) * channels
            ]
    for target in range(4):
        low = target * step // group
        for turn in range(turns):
            strip = [
                packed_ref[turn, hour * rows + low : hour * rows + low + STRIP, :]
                for hour in range(hours)
            ]
            strip_ref[target, turn * hours * STRIP : (turn + 1) * hours * STRIP, :] = jnp.concatenate(
                strip, axis=0
            ).astype(bf16)


def advance_latitudes(hours, step, place, pieces, tables, gains, w_skip, w_mix, w_decode):
    turns, piece, channels = pieces[0].shape
    padded = round_up(piece, LANES)
    group = LANES // PACKED
    span = round_up(3 * step + STRIP * group, 8 * group)
    decode = jnp.pad(w_decode, ((0, 0), (0, LANES - w_decode.shape[1])))
    modes = gains.shape[0] // 2
    late = (gains,) + tables[2:] + (w_skip, w_mix, decode)
    spare = max(4 * (tables[0].shape[1] // 2), 2 * (tables[1].shape[0] // 2)) - modes
    results = pl.pallas_call(
        functools.partial(latitude_kernel, hours, turns, step),
        out_shape=tuple(
            jax.ShapeDtypeStruct((turns, piece, channels), jnp.bfloat16) for _ in pieces
        )
        + (jax.ShapeDtypeStruct((4, turns * hours * STRIP, LANES), jnp.bfloat16),),
        in_specs=[pl.BlockSpec(memory_space=pltpu.SMEM)]
        + [pl.BlockSpec(memory_space=pltpu.VMEM)] * 6
        + [pl.BlockSpec(memory_space=pl.ANY)] * len(late),
        scratch_shapes=[pltpu.VMEM(array.shape, array.dtype) for array in late]
        + [
            pltpu.SemaphoreType.DMA((len(late),)),
            pltpu.VMEM((4 * padded, turns * channels), jnp.bfloat16),
            pltpu.VMEM((channels // LANES, gains.shape[0] + spare, LANES), jnp.float32),
            pltpu.VMEM((turns, 2 * piece, LANES), jnp.float32),
            pltpu.VMEM((span, LANES), jnp.float32),
            pltpu.VMEM((turns, hours * span // group, LANES), jnp.float32),
        ],
        compiler_params=pltpu.CompilerParams(vmem_limit_bytes=VMEM),
        cost_estimate=pl.CostEstimate(
            flops=turns * 16 * 10**9,
            bytes_accessed=turns * 6 * 2**20,
            transcendentals=hours * turns * 4 * piece * channels,
        ),
        name="advance_latitudes",
    )(place, *pieces, *tables[:2], *late)
    return results[:4], results[4]


def collate_kernel(count, place_ref, *refs):
    far, out_ref, near, sems = refs[:count], refs[count], refs[count + 1 : -1], refs[-1]
    loads = [
        pltpu.make_async_copy(far[index], near[index], sems.at[0, index]) for index in range(count)
    ]
    stores = [
        pltpu.make_async_copy(
            near[index], out_ref.at[pl.ds(place_ref[index], near[index].shape[0])], sems.at[1, index]
        )
        for index in range(count)
    ]
    for load in loads:
        load.start()
    for load, store in zip(loads, stores):
        load.wait()
        store.start()
    for store in stores:
        store.wait()


def collate(place, pieces):
    count = len(pieces)
    turns, piece, channels = pieces[0].shape
    return pl.pallas_call(
        functools.partial(collate_kernel, count),
        out_shape=jax.ShapeDtypeStruct((count * turns, piece, channels), pieces[0].dtype),
        in_specs=[pl.BlockSpec(memory_space=pltpu.SMEM)]
        + [pl.BlockSpec(memory_space=pl.ANY)] * count,
        out_specs=pl.BlockSpec(memory_space=pl.ANY),
        scratch_shapes=[pltpu.VMEM(block.shape, block.dtype) for block in pieces]
        + [pltpu.SemaphoreType.DMA((2, count))],
        compiler_params=pltpu.CompilerParams(vmem_limit_bytes=VMEM),
        name="collate",
    )(place, *pieces)


def shift(block, axis, step):
    count = lax.axis_size(axis)
    return lax.ppermute(block, axis, [(source, (source + step) % count) for source in range(count)])


def global_hour(current, spec_filter, w_skip, w_mix, forward, inverse):
    longitude = lax.all_to_all(current, "col", split_axis=2, concat_axis=1, tiled=True)
    spectrum = jnp.einsum("alc,ml->amc", longitude, forward, preferred_element_type=jnp.float32)
    num_modes = spec_filter.shape[1]
    real_part = spectrum[:, :num_modes, :]
    imag_part = spectrum[:, num_modes:, :]
    filt_real = spec_filter[0][None]
    filt_imag = spec_filter[1][None]
    mixed = jnp.concatenate(
        [
            real_part * filt_real - imag_part * filt_imag,
            real_part * filt_imag + imag_part * filt_real,
        ],
        axis=1,
    ).astype(jnp.bfloat16)
    filtered = jnp.einsum("amc,lm->alc", mixed, inverse, preferred_element_type=jnp.float32).astype(
        jnp.bfloat16
    )
    spectral = lax.all_to_all(filtered, "col", split_axis=1, concat_axis=2, tiled=True)
    skipped = jnp.einsum("alc,cd->ald", current, w_skip, preferred_element_type=jnp.float32)
    activated = jax.nn.gelu(spectral.astype(jnp.float32) + skipped).astype(jnp.bfloat16)
    update = jnp.einsum("ald,de->ale", activated, w_mix, preferred_element_type=jnp.float32)
    return (current.astype(jnp.float32) + update).astype(jnp.bfloat16)


def window_extent(cells):
    return (cells + RIM - 1) // RATIO + 3 - (-RIM // RATIO)


def window_base():
    return -(-RIM // RATIO)


def global_by_latitude(
    hours, global_state, spec_filter, w_skip, w_mix, w_decode, box_lat0, box_lon0, rows_here,
    cols_here, prepare,
):
    count = lax.axis_size("col")
    me = lax.axis_index("col")
    lats_here, piece, _ = global_state.shape
    turns = lats_here // count
    tables = split_tables(piece * count, spec_filter.shape[1])
    owners = [(me - step) % count * turns for step in range(count)]
    mine = filter_share(spec_filter)
    bands = [lax.dynamic_slice_in_dim(global_state, owner, turns, 0) for owner in owners]
    bands, mine = lax.optimization_barrier((bands, mine))
    received = [shift(band, "col", -step) if step else band for step, band in enumerate(bands)]
    wide = every_channel(mine)
    parts, weights = prepare()
    gains = spread(wide, PLANE).reshape(-1, wide.shape[1])
    start = (box_lon0[0] - window_base() - me * piece) % (piece * count)
    place = jnp.stack([start // piece, (start // piece + 1) % count, start % piece]).astype(jnp.int32)
    received, weights = lax.optimization_barrier((received, weights))
    outcome, strips = advance_latitudes(
        hours, cols_here // RATIO, place, received, tables, gains, w_skip, w_mix, w_decode
    )
    near = [
        lax.dynamic_index_in_dim(strips, (me - step) % count, 0, keepdims=False)
        for step in range(count)
    ]
    near, parts = lax.optimization_barrier((near, parts))
    near = [shift(strip, "col", -step) if step else strip for step, strip in enumerate(near)]
    near, outcome = lax.optimization_barrier((near, outcome))
    got = spread(jnp.stack(near), PLANE)
    plane = lax.axis_size(PLANE)
    got = got.reshape((plane * lats_here, -1, LANES))
    lat = box_lat0[0] - window_base() + lax.axis_index(PLANE) * (rows_here // RATIO)
    lat = jnp.clip(lat + jnp.arange(window_extent(rows_here), dtype=jnp.int32), 0, plane * lats_here - 1)
    band, lat = lat // lats_here, lat % lats_here
    pick = (band * count + (lat // turns - me) % count) * turns + lat % turns
    finals = [shift(block, "col", step) if step else block for step, block in enumerate(outcome)]

    def finish(after):
        blocks, after = lax.optimization_barrier((finals, after))
        return collate(jnp.stack(owners).astype(jnp.int32), blocks), after

    return finish, got, pick.astype(jnp.int32), (parts, weights)


def global_by_channel(
    hours, global_state, spec_filter, w_skip, w_mix, w_decode, box_lat0, box_lon0, rows_here,
    cols_here, prepare,
):
    count = lax.axis_size("col")
    prepared = prepare()
    forward, inverse = fourier_tables(global_state.shape[1] * count, spec_filter.shape[1])
    base = window_base()
    high, wide = window_extent(rows_here), window_extent(cols_here)
    span = (count - 1) * (cols_here // RATIO) + wide
    lat_start = box_lat0[0] + lax.axis_index(PLANE) * (rows_here // RATIO)
    lon_start = box_lon0[0] + lax.axis_index("col") * (cols_here // RATIO)
    windows = []
    for _ in range(hours):
        global_state = global_hour(global_state, spec_filter, w_skip, w_mix, forward, inverse)
        coarse = jnp.einsum(
            "alc,ck->alk", global_state, w_decode, preferred_element_type=jnp.float32
        ).astype(jnp.bfloat16)
        coarse = lax.all_gather(coarse, "col", axis=1, tiled=True)
        coarse = jnp.pad(coarse, ((0, 0), (base, span), (0, 0)))
        coarse = lax.dynamic_slice_in_dim(coarse, box_lon0[0], base + span, 1)
        coarse = lax.all_gather(coarse, PLANE, axis=0, tiled=True)
        coarse = lax.dynamic_slice_in_dim(coarse, lon_start - box_lon0[0], wide, 1)
        coarse = jnp.pad(coarse, ((base, high), (0, 0), (0, 0)))
        coarse = lax.dynamic_slice_in_dim(coarse, lat_start, high, 0)
        windows.append(coarse)
    group = LANES // PACKED
    windows = jnp.stack(windows, axis=1)
    windows = jnp.pad(
        windows, ((0, 0), (0, 0), (0, STRIP * group - wide), (0, PACKED - windows.shape[3]))
    )
    windows = windows.reshape(high, hours * STRIP, LANES)
    return lambda after: (global_state, after), windows, jnp.arange(high, dtype=jnp.int32), prepared


def next_to(low, high, axis):
    count = lax.axis_size(axis)
    forward = [(i, i + 1) for i in range(count - 1)]
    backward = [(target, source) for source, target in forward]
    return lax.ppermute(low, axis, forward), lax.ppermute(high, axis, backward)


def grid_place(start_ref, total, base, extent):
    place = start_ref + base + lax.broadcasted_iota(jnp.int32, (extent, 1), 0)
    return (place >= 0) & (place < total)


def denoise_kernel(
    rows, cols, totals, variables, conds, width, place_ref, pick_ref, mid0_ref, mid1_ref, above_ref,
    below_ref, left_ref, right_ref, strip_ref, *refs
):
    far_refs, out_ref, refs = refs[:5], refs[5], refs[6:]
    near_refs, sems, refs = refs[:5], refs[5], refs[6:]
    first_w_ref, down_w_ref, up_w_ref, bridge_w_ref, last_w_ref = near_refs
    noisy_ref, noise_ref, blend_ref, own_ref, stack_ref, first_ref, pooled_ref, third_ref, pair_ref, spread_ref, window_ref = refs
    copies = [
        pltpu.make_async_copy(far, near, sems.at[index])
        for index, (far, near) in enumerate(zip(far_refs, near_refs))
    ]
    for copy in copies:
        copy.start()
    half = width // 2
    pad = (width - cols) // 2
    channels = mid0_ref.shape[2]
    f32, bf16 = jnp.float32, jnp.bfloat16

    inner = RIM - RIM_USED
    for ref, mid_ref, rim, part in ((noisy_ref, mid0_ref, RIM, 0), (noise_ref, mid1_ref, inner, RIM)):
        ref[0:rim, pad : pad + cols, :] = above_ref[part : part + rim]
        ref[rim : rim + rows, pad : pad + cols, :] = mid_ref[...]
        ref[rim + rows :, pad : pad + cols, :] = below_ref[part : part + rim]
        skip = RIM - rim
        for side_ref, low, to in ((left_ref, 0, pad - rim), (right_ref, pad + cols, 0)):
            side = side_ref[skip : skip + rows + 2 * rim].astype(f32)
            side = pltpu.roll(side, (to - part) % pad, 1)
            ref[:, low : low + pad, :] = side.astype(bf16)

    is_in = grid_place(place_ref[1], totals[1], -pad, width)
    col_in = is_in.astype(f32)
    base = window_base()
    col = lax.broadcasted_iota(jnp.int32, (width, 1), 0) - pad
    frac_col = ((col % RATIO).astype(f32) + 0.5) / RATIO
    col_base = jnp.where(is_in, (col + pad) // RATIO - pad // RATIO + base, FAR).astype(f32) + frac_col
    group = LANES // PACKED
    high = pick_ref.shape[0]
    point = lax.broadcasted_iota(jnp.int32, (1, group * high * STRIP), 1)
    point_lat = (point // STRIP % high).astype(f32)
    point_lon = (point % STRIP * group + point // (STRIP * high)).astype(f32)

    def blend(row):
        whole = row // RATIO
        frac_row = (row - whole * RATIO + 0.5) / RATIO
        there = place_ref[0] + row
        row_base = jnp.where((there >= 0) & (there < totals[0]), whole + base + frac_row, float(FAR))
        shifts = noisy_ref[row + RIM].astype(f32)
        lat = row_base + shifts[:, variables + conds : variables + conds + 1]
        lon = col_base + shifts[:, variables + conds + 1 : variables + conds + 2]
        weight_lat = jnp.maximum(1.0 - jnp.abs(point_lat - lat), 0.0)
        weight_lon = jnp.maximum(1.0 - jnp.abs(point_lon - lon), 0.0)
        return (weight_lat * weight_lon).astype(bf16)

    edges = [jnp.broadcast_to(col_in[low : low + pad], (pad, channels)) for low in (0, pad + cols)]
    lane = lax.broadcasted_iota(jnp.int32, (1, channels), 1)
    is_state = lane < variables
    is_cond = (lane >= variables) & (lane < variables + conds)
    strips = [strip_ref[pick_ref[index]].astype(f32) for index in range(high)]
    for hour in range(2):
        near = jnp.concatenate([s[hour * STRIP : (hour + 1) * STRIP] for s in strips], axis=0)
        for turn in range(LANES // PACKED):
            moved = pltpu.roll(near, (variables - turn * PACKED) % LANES, 1)
            window_ref[hour, turn * high * STRIP : (turn + 1) * high * STRIP, :] = jnp.where(
                is_cond, moved, 0.0
            ).astype(bf16)

    def flat(start, count, unit):
        return slice(start * unit, (start + count) * unit)

    def mask(value, row):
        low, mid, high = value[:pad], value[pad : pad + cols], value[pad + cols :]
        value = jnp.concatenate([low * edges[0], mid, high * edges[1]], axis=0)
        if 0 <= row < rows:
            return value
        there = place_ref[0] + row
        return value * jnp.where((there >= 0) & (there < totals[0]), 1.0, 0.0)

    def keep(ref, where, value):
        size = value.shape[0]
        ref[0, where, :] = pltpu.roll(value, 1, 0).astype(bf16)
        ref[1, where, :] = value.astype(bf16)
        ref[2, where, :] = pltpu.roll(value, size - 1, 0).astype(bf16)

    def pairs(ref, row, count):
        blocks = []
        for pair in range(count):
            taps = [
                ref[shift, flat(row + 2 * pair + step, 1, width), :]
                for step in range(4)
                for shift in range(3)
            ]
            blocks.append(jnp.concatenate(taps, axis=1))
        return jnp.concatenate(blocks, axis=0)

    def silu_of_half(half_value):
        return half_value + half_value * jnp.tanh(half_value)

    for hour in range(2):
        rim = RIM - RIM_USED * hour
        tall = rows + 2 * rim

        for row in range(0, tall, 2):
            here = flat(row, 2, width)
            if hour == 0:
                weights = jnp.concatenate([blend(row - RIM), blend(row + 1 - RIM)], axis=0)
                blend_ref[here, :] = weights
            else:
                weights = blend_ref[flat(row + RIM - rim, 2, width), :]
            cond = jnp.dot(weights, window_ref[hour], preferred_element_type=f32)
            if hour == 0:
                own = noisy_ref[row : row + 2].reshape(2 * width, channels).astype(f32)
                own_ref[here, :] = own
            else:
                own = own_ref[here, :]
            keep(stack_ref, here, jnp.where(is_state, own, cond))

        if hour == 0:
            copies[0].wait()
        for row in range(0, tall - 2, 8):
            value = jnp.dot(
                pairs(stack_ref, row, 4), first_w_ref[...], preferred_element_type=f32
            )
            for pair in range(4):
                top = row + 2 * pair
                here = flat(top // 2, 1, width)
                part = silu_of_half(value[pair * width : (pair + 1) * width])
                upper = mask(part[:, :channels], top - rim + 1)
                lower = mask(part[:, channels:], top - rim + 2)
                first_ref[here, :channels] = upper.astype(bf16)
                first_ref[here, channels:] = lower.astype(bf16)
                pair_ref[top // 2] = upper + lower
                even = pair_ref[top // 2, pl.ds(0, half, stride=2), :]
                odd = pair_ref[top // 2, pl.ds(1, half, stride=2), :]
                keep(pooled_ref, flat(top // 2, 1, half), even + odd)

        if hour == 0:
            for copy in copies[1:4]:
                copy.wait()
        half_rows = (tall - 2) // 2 - 2
        part = half_rows // 2
        for row in (0, part):
            taps = [
                pooled_ref[shift, flat(row + step, part, half), :]
                for step in range(3)
                for shift in range(3)
            ]
            second = jnp.dot(
                jnp.concatenate(taps, axis=1), down_w_ref[...], preferred_element_type=f32
            )
            lifted = jnp.dot(
                silu_of_half(second).astype(bf16), up_w_ref[...], preferred_element_type=f32
            )
            bridged = jnp.dot(
                first_ref[flat(row + 1, part, width), :], bridge_w_ref[...], preferred_element_type=f32
            )
            for step in range(part):
                own = lifted[step * half : (step + 1) * half]
                spread_ref[row + step, pl.ds(0, half, stride=2), :] = own
                spread_ref[row + step, pl.ds(1, half, stride=2), :] = own
                own = spread_ref[row + step]
                top = 2 * (row + step)
                for side in range(2):
                    value = bridged[
                        step * width : (step + 1) * width, side * channels : (side + 1) * channels
                    ]
                    value = mask(silu_of_half(value + own), top + side - rim + 3)
                    keep(third_ref, flat(top + side, 1, width), value)

        if hour == 0:
            copies[4].wait()
        skip = 1 if hour == 1 else 0
        count = (rows + 2 * (rim - RIM_USED)) // 2 if hour == 0 else rows // 2
        for first in range(0, count, 4):
            size = min(4, count - first)
            values = jnp.dot(
                pairs(third_ref, 2 * first + skip, size), last_w_ref[...], preferred_element_type=f32
            )
            for index in range(2 * size):
                pair, side = divmod(index, 2)
                row = 2 * first + index
                fresh = values[
                    pair * width : (pair + 1) * width, side * channels : (side + 1) * channels
                ]
                fresh = own_ref[flat(row + RIM_USED + skip, 1, width), :] + fresh
                if hour == 0:
                    fresh = fresh + noise_level * noise_ref[row].astype(f32)
                    own_ref[flat(row, 1, width), :] = mask(fresh, row - rim + RIM_USED)
                else:
                    out_ref[:, row * cols : (row + 1) * cols] = fresh[pad : pad + cols].T.astype(bf16)


def denoise(rows, cols, totals, variables, conds, place, pick, parts, strips, weights):
    mid0, _, _, _, left, _ = parts
    width, channels = cols + 2 * left.shape[1], mid0.shape[2]
    tall = rows + 2 * RIM
    most = (tall - 2) // 2
    points = LANES // PACKED * pick.shape[0] * STRIP
    bf16, f32 = jnp.bfloat16, jnp.float32
    return pl.pallas_call(
        functools.partial(denoise_kernel, rows, cols, totals, variables, conds, width),
        out_shape=jax.ShapeDtypeStruct((channels, rows * cols), bf16),
        in_specs=[pl.BlockSpec(memory_space=pltpu.SMEM)] * 2
        + [pl.BlockSpec(memory_space=pltpu.VMEM)] * 7
        + [pl.BlockSpec(memory_space=pl.ANY)] * len(weights),
        scratch_shapes=[pltpu.VMEM(array.shape, array.dtype) for array in weights]
        + [
            pltpu.SemaphoreType.DMA((len(weights),)),
            pltpu.VMEM((tall, width, channels), bf16),
            pltpu.VMEM((tall - 2 * RIM_USED, width, channels), bf16),
            pltpu.VMEM((tall * width, points), bf16),
            pltpu.VMEM((tall * width, channels), f32),
            pltpu.VMEM((3, tall * width, channels), bf16),
            pltpu.VMEM((most * width, 2 * channels), bf16),
            pltpu.VMEM((3, most * width // 2, channels), bf16),
            pltpu.VMEM((3, tall * width, channels), bf16),
            pltpu.VMEM((most, width, channels), f32),
            pltpu.VMEM((most, width, channels), f32),
            pltpu.VMEM((2, points, channels), bf16),
        ],
        compiler_params=pltpu.CompilerParams(vmem_limit_bytes=VMEM),
        cost_estimate=pl.CostEstimate(flops=10**6, bytes_accessed=10**5, transcendentals=0),
        name="denoise",
    )(place, pick, *parts, strips, *weights)


def conv_weight(weight, depth, width):
    out, _, given = weight.shape
    weight = jnp.pad(weight, ((0, width - out), (0, 0), (0, depth - given)))
    return jnp.transpose(weight, (1, 2, 0)).reshape(9 * depth, width)


def pair_weight(weight):
    row = weight.shape[0] // 3
    return jnp.concatenate(
        [jnp.pad(weight, ((0, row), (0, 0))), jnp.pad(weight, ((row, 0), (0, 0)))], axis=1
    )


def shards(
    global_state,
    spec_filter,
    w_skip,
    w_mix,
    w_decode,
    regional_state,
    noise_draws,
    w_first,
    w_down,
    w_up,
    w_bridge,
    w_last,
    box_lat0,
    box_lon0,
    stencil_lat,
    stencil_lon,
):
    hours = noise_draws.shape[0]
    rows_here, cols_here = regional_state.shape[1:]
    row_start = lax.axis_index(PLANE) * rows_here
    col_start = lax.axis_index("col") * cols_here
    total_rows = rows_here * lax.axis_size(PLANE)
    total_cols = cols_here * lax.axis_size("col")
    assert hours == 2

    variables = regional_state.shape[0]
    conds = w_decode.shape[1]
    lanes = variables + conds
    noisy = (
        regional_state.astype(jnp.float32) + noise_level * noise_draws[0].astype(jnp.float32)
    ).astype(jnp.bfloat16)
    lat_shift = stencil_lat - (row_start + jnp.arange(rows_here, dtype=jnp.int32))[:, None] // RATIO
    lon_shift = stencil_lon - (col_start + jnp.arange(cols_here, dtype=jnp.int32))[None, :] // RATIO
    cells = (rows_here, cols_here)
    mids = jnp.concatenate(
        [
            noisy,
            jnp.zeros((conds,) + cells, jnp.bfloat16),
            lat_shift.astype(jnp.bfloat16)[None],
            lon_shift.astype(jnp.bfloat16)[None],
            jnp.zeros((LANES - lanes - 2,) + cells, jnp.bfloat16),
            noise_draws[1],
            jnp.zeros((LANES - variables,) + cells, jnp.bfloat16),
        ],
        axis=0,
    )
    mids = jnp.transpose(mids.reshape((2, LANES) + cells), (0, 2, 3, 1))
    mid0, mid1 = mids[0], mids[1]
    inner = RIM - RIM_USED
    high = window_extent(rows_here)
    place = jnp.stack([row_start, col_start]).astype(jnp.int32)
    totals = (total_rows, total_cols)

    def prepare():
        lows = jnp.concatenate([mid0[rows_here - RIM :], mid1[rows_here - inner :]], axis=0)
        highs = jnp.concatenate([mid0[:RIM], mid1[:inner]], axis=0)
        above, below = next_to(lows, highs, PLANE)

        def rim_cols(first, first_inner):
            wide, thin = slice(first, first + RIM), slice(first_inner, first_inner + inner)
            noise = jnp.concatenate([above[RIM:, thin], mid1[:, thin], below[RIM:, thin]], axis=0)
            noise = jnp.pad(
                noise, ((RIM_USED, RIM_USED), (0, RIM_COLS - RIM - inner), (0, 0))
            )
            return jnp.concatenate(
                [
                    jnp.concatenate([above[:RIM, wide], mid0[:, wide], below[:RIM, wide]], axis=0),
                    noise,
                ],
                axis=1,
            )

        left, right = next_to(
            rim_cols(cols_here - RIM, cols_here - inner), rim_cols(0, 0), "col"
        )
        weights = (
            pair_weight(conv_weight(0.5 * w_first, LANES, w_first.shape[0])),
            conv_weight(0.125 * w_down, w_down.shape[2], w_down.shape[0]),
            0.5 * w_up.T,
            0.5
            * jnp.concatenate(
                [jnp.pad(w_bridge.T, ((0, 0), (0, LANES))), jnp.pad(w_bridge.T, ((0, 0), (LANES, 0)))],
                axis=0,
            ),
            pair_weight(conv_weight(w_last, w_last.shape[2], LANES)),
        )
        return (mid0, mid1, above, below, left, right), weights

    by_latitude = lax.axis_size("col") == 4 and global_state.shape[0] % 4 == 0
    global_steps = global_by_latitude if by_latitude else global_by_channel
    finish, strips, pick, (parts, weights) = global_steps(
        hours, global_state, spec_filter, w_skip, w_mix, w_decode, box_lat0, box_lon0,
        rows_here, cols_here, prepare,
    )
    regional_final = denoise(
        rows_here, cols_here, totals, variables, conds, place, pick, parts, strips, weights
    )
    regional_final = regional_final[:variables].reshape((variables, rows_here, cols_here))
    return finish(regional_final)


def solution(mesh):
    return jax.shard_map(
        shards,
        mesh=mesh,
        in_specs=(
            P(PLANE, "col", None),
            P(None, None, "col"),
            P(),
            P(),
            P(),
            P(None, PLANE, "col"),
            P(None, None, PLANE, "col"),
            P(),
            P(),
            P(),
            P(),
            P(),
            P(),
            P(),
            P(PLANE, "col"),
            P(PLANE, "col"),
        ),
        out_specs=(P(PLANE, "col", None), P(None, PLANE, "col")),
        check_vma=False,
    )
```

```python
import functools
import math

import jax
import jax.numpy as jnp
import ml_dtypes
import numpy as np
from jax import lax
from jax.experimental import pallas as pl
from jax.experimental.pallas import tpu as pltpu
from jax.sharding import PartitionSpec as P

RATIO = 8
noise_level = 0.5
PLANE = ("grp", "row")
RIM = 9
RIM_USED = 4
LANES = 128
VMEM = 60 * 2**20
PACKED = 32
MODE_TILE = 64
STRIP = 8
FAR = -4096
RIM_COLS = 16


def fourier_tables(length, num_modes):
    position = np.arange(length, dtype=np.int64)[:, None]
    frequency = np.arange(num_modes, dtype=np.int64)[None, :]
    angle = (position * frequency % length).astype(np.float64) * (2.0 * math.pi / length)
    cosine = np.cos(angle)
    sine = np.sin(angle)
    factor = np.where(frequency == 0, 1.0, 2.0) / length
    forward = np.concatenate([cosine, -sine], axis=1).T.astype(ml_dtypes.bfloat16)
    inverse = np.concatenate([cosine * factor, -sine * factor], axis=1).astype(ml_dtypes.bfloat16)
    return forward, inverse


def round_up(size, unit):
    return -(-size // unit) * unit


def split_tables(length, num_modes):
    piece = length // 4
    place = np.arange(piece, dtype=np.int64)[:, None]

    def waves(mode):
        angle = (place * mode[None, :] % length).astype(np.float64) * (2.0 * math.pi / length)
        return np.cos(angle), np.sin(angle), np.where(mode == 0, 1.0, 2.0)[None, :] / length

    def padded(blocks, unit_rows, unit_cols):
        rows = []
        for row in blocks:
            cols = []
            for block in row:
                spare = [(0, -block.shape[0] % unit_rows), (0, -block.shape[1] % unit_cols)]
                cols.append(np.pad(block, spare))
            rows.append(np.concatenate(cols, axis=1))
        return np.concatenate(rows, axis=0).astype(ml_dtypes.bfloat16)

    forward, inverse = [], []
    for residue in (0, 2):
        cosine, sine, factor = waves(np.arange(residue, num_modes, 4))
        forward.append(padded([[cosine.T], [-sine.T]], MODE_TILE, LANES))
        inverse.append(padded([[cosine * factor, -sine * factor]], LANES, MODE_TILE))
    mode = np.arange(1, num_modes, 2)
    cosine, sine, factor = waves(mode)
    sign = np.where(mode % 4 == 1, 1.0, -1.0)[None, :]
    odd_forward = padded(
        [[cosine.T, (-sign * sine).T], [-sine.T, (-sign * cosine).T]], 2 * MODE_TILE, LANES
    )
    odd_inverse = padded(
        [
            [cosine * factor, -sine * factor],
            [-sign * sine * factor, -sign * cosine * factor],
        ],
        LANES,
        2 * MODE_TILE,
    )
    return tuple(
        jnp.asarray(table)
        for table in (np.stack(forward), odd_forward, np.stack(inverse), odd_inverse)
    )


def exchange(blocks, axis):
    return lax.all_to_all(blocks, axis, split_axis=0, concat_axis=0, tiled=True)


def spread(block, axis):
    return exchange(jnp.broadcast_to(block[None], (lax.axis_size(axis),) + block.shape), axis)


def filter_share(spec_filter):
    rows = 2 * spec_filter.shape[1]
    flat = spec_filter.reshape(rows, spec_filter.shape[2])
    share = rows // lax.axis_size(PLANE)
    mine = lax.dynamic_slice_in_dim(flat, lax.axis_index(PLANE) * share, share, 0)
    return mine.astype(jnp.bfloat16)


def every_channel(mine):
    count = lax.axis_size("col")
    me = lax.axis_index("col")
    blocks = [shift(mine, "col", -step) if step else mine for step in range(count)]
    ring = jnp.concatenate(blocks + blocks[:-1], axis=1)
    width = mine.shape[1]
    return lax.dynamic_slice_in_dim(ring, (count - me) % count * width, count * width, 1)


def gelu(x):
    slope = math.sqrt(2.0 / math.pi)
    half = 0.5 * x
    return half + half * jnp.tanh(x * (slope + (0.044715 * slope) * (x * x)))


def latitude_kernel(hours, turns, step, place_ref, *refs):
    piece_refs, refs = refs[:4], refs[4:]
    even_forward_ref, odd_forward_ref = refs[:2]
    far_refs, out_refs, strip_ref, refs = refs[2:8], refs[8:12], refs[12], refs[13:]
    near_refs, sems, refs = refs[:6], refs[6], refs[7:]
    filter_ref, even_inverse_ref, odd_inverse_ref, skip_ref, mix_ref, decode_ref = near_refs
    state_ref, gain_ref, coarse_ref, near_ref, packed_ref = refs
    copies = [
        pltpu.make_async_copy(far, near, sems.at[index])
        for index, (far, near) in enumerate(zip(far_refs, near_refs))
    ]
    for copy in copies:
        copy.start()
    f32, bf16 = jnp.float32, jnp.bfloat16
    piece, channels = piece_refs[0].shape[1:]
    padded = state_ref.shape[0] // 4
    group = LANES // PACKED
    span = near_ref.shape[0]
    rows = span // group
    spare = jnp.zeros((padded - piece, channels), bf16)
    for index in range(4):
        for turn in range(turns):
            state_ref[
                index * padded : (index + 1) * padded, turn * channels : (turn + 1) * channels
            ] = jnp.concatenate([piece_refs[index][turn], spare], axis=0)

    modes = filter_ref.shape[0] // 2

    def spread_gains():
        for index in range(channels // LANES):
            lanes = slice(index * LANES, (index + 1) * LANES)
            gain_ref[index, : 2 * modes, :] = filter_ref[:, lanes].astype(f32)
            gain_ref[index, 2 * modes :, :] = jnp.zeros((gain_ref.shape[1] - 2 * modes, LANES), f32)

    def gain_rows(low, count, stride):
        rows = pl.ds(low, count, stride=stride)
        tiles = [gain_ref[index, rows, :] for index in range(channels // LANES)]
        return jnp.concatenate(tiles * turns, axis=1)

    def gain(real, imag, low, stride):
        gain_real = gain_rows(low, real.shape[0], stride)
        gain_imag = gain_rows(modes + low, real.shape[0], stride)
        return (
            (real * gain_real - imag * gain_imag).astype(bf16),
            (real * gain_imag + imag * gain_real).astype(bf16),
        )

    def dot(left, right):
        return jnp.dot(left, right, preferred_element_type=f32)

    for hour in range(hours):
        pieces = [
            state_ref[index * padded : (index + 1) * padded, :].astype(f32) for index in range(4)
        ]
        mixed = jnp.concatenate([pieces[0] - pieces[2], pieces[1] - pieces[3]], axis=0).astype(bf16)
        span_odd = odd_forward_ref.shape[0] // 2
        thirds = span_odd // 3
        spectra = []
        for index in range(3):
            low = index * thirds
            spectra.append(
                (
                    dot(odd_forward_ref[low : low + thirds, :], mixed),
                    dot(odd_forward_ref[span_odd + low : span_odd + low + thirds, :], mixed),
                )
            )
            if index == 0:
                both, other = pieces[0] + pieces[2], pieces[1] + pieces[3]
                mixes = [(both + other).astype(bf16), (both - other).astype(bf16)]
        evens = [dot(even_forward_ref[index], mixes[index]) for index in range(2)]
        if hour == 0:
            copies[0].wait()
            spread_gains()
            for copy in copies[1:]:
                copy.wait()
        odd = [gain(*spectra[index], 1 + 2 * index * thirds, 2) for index in range(3)]
        odd = jnp.concatenate([part[0] for part in odd] + [part[1] for part in odd], axis=0)
        odd_shares = [dot(odd_inverse_ref[:padded, :], odd)]
        shares = []
        for index in range(2):
            half = evens[index].shape[0] // 2
            even = gain(evens[index][:half], evens[index][half:], 2 * index, 4)
            shares.append(dot(even_inverse_ref[index], jnp.concatenate(even, axis=0)))
        odd_shares.append(dot(odd_inverse_ref[padded:, :], odd))

        def block_of(ref, index, turn):
            return ref[
                index * padded : (index + 1) * padded, turn * channels : (turn + 1) * channels
            ]

        order = [(index, turn) for index in (0, 2, 1, 3) for turn in range(turns)]
        skipped = dot(block_of(state_ref, *order[0]), skip_ref[...])
        for place, (index, turn) in enumerate(order):
            if place + 1 < len(order):
                following = dot(block_of(state_ref, *order[place + 1]), skip_ref[...])
            if turn == 0:
                even = shares[0] + shares[1] if index % 2 == 0 else shares[0] - shares[1]
                spectral = even + odd_shares[index % 2] if index < 2 else even - odd_shares[index % 2]
            own = spectral[:, turn * channels : (turn + 1) * channels]
            activated = gelu(own + skipped).astype(bf16)
            fresh = block_of(state_ref, index, turn).astype(f32) + dot(activated, mix_ref[...])
            state_ref[
                index * padded : (index + 1) * padded, turn * channels : (turn + 1) * channels
            ] = fresh.astype(bf16)
            skipped = following

        for index in range(2):
            here = pl.ds(pl.multiple_of(place_ref[index] * padded, LANES), padded)
            for turn in range(turns):
                lanes = slice(turn * channels, (turn + 1) * channels)
                coarse = dot(state_ref[here, lanes], decode_ref[...])
                coarse_ref[turn, index * piece : (index + 1) * piece, :] = coarse[:piece]
        for turn in range(turns):
            near_ref[...] = coarse_ref[turn, pl.ds(place_ref[2], span), :]
            packed = near_ref[pl.ds(0, rows, stride=group), :]
            for sub in range(1, group):
                packed += pltpu.roll(near_ref[pl.ds(sub, rows, stride=group), :], sub * PACKED, 1)
            packed_ref[turn, hour * rows : (hour + 1) * rows, :] = packed

    for index in range(4):
        for turn in range(turns):
            out_refs[index][turn] = state_ref[
                index * padded : index * padded + piece, turn * channels : (turn + 1) * channels
            ]
    for target in range(4):
        low = target * step // group
        for turn in range(turns):
            strip = [
                packed_ref[turn, hour * rows + low : hour * rows + low + STRIP, :]
                for hour in range(hours)
            ]
            strip_ref[target, turn * hours * STRIP : (turn + 1) * hours * STRIP, :] = jnp.concatenate(
                strip, axis=0
            ).astype(bf16)


def advance_latitudes(hours, step, place, pieces, tables, gains, w_skip, w_mix, w_decode):
    turns, piece, channels = pieces[0].shape
    padded = round_up(piece, LANES)
    group = LANES // PACKED
    span = round_up(3 * step + STRIP * group, 8 * group)
    decode = jnp.pad(w_decode, ((0, 0), (0, LANES - w_decode.shape[1])))
    modes = gains.shape[0] // 2
    late = (gains,) + tables[2:] + (w_skip, w_mix, decode)
    spare = max(4 * (tables[0].shape[1] // 2), 2 * (tables[1].shape[0] // 2)) - modes
    results = pl.pallas_call(
        functools.partial(latitude_kernel, hours, turns, step),
        out_shape=tuple(
            jax.ShapeDtypeStruct((turns, piece, channels), jnp.bfloat16) for _ in pieces
        )
        + (jax.ShapeDtypeStruct((4, turns * hours * STRIP, LANES), jnp.bfloat16),),
        in_specs=[pl.BlockSpec(memory_space=pltpu.SMEM)]
        + [pl.BlockSpec(memory_space=pltpu.VMEM)] * 6
        + [pl.BlockSpec(memory_space=pl.ANY)] * len(late),
        scratch_shapes=[pltpu.VMEM(array.shape, array.dtype) for array in late]
        + [
            pltpu.SemaphoreType.DMA((len(late),)),
            pltpu.VMEM((4 * padded, turns * channels), jnp.bfloat16),
            pltpu.VMEM((channels // LANES, gains.shape[0] + spare, LANES), jnp.float32),
            pltpu.VMEM((turns, 2 * piece, LANES), jnp.float32),
            pltpu.VMEM((span, LANES), jnp.float32),
            pltpu.VMEM((turns, hours * span // group, LANES), jnp.float32),
        ],
        compiler_params=pltpu.CompilerParams(vmem_limit_bytes=VMEM),
        cost_estimate=pl.CostEstimate(
            flops=turns * 16 * 10**9,
            bytes_accessed=turns * 6 * 2**20,
            transcendentals=hours * turns * 4 * piece * channels,
        ),
        name="advance_latitudes",
    )(place, *pieces, *tables[:2], *late)
    return results[:4], results[4]


def collate_kernel(count, place_ref, *refs):
    far, out_ref, near, sems = refs[:count], refs[count], refs[count + 1 : -1], refs[-1]
    loads = [
        pltpu.make_async_copy(far[index], near[index], sems.at[0, index]) for index in range(count)
    ]
    stores = [
        pltpu.make_async_copy(
            near[index], out_ref.at[pl.ds(place_ref[index], near[index].shape[0])], sems.at[1, index]
        )
        for index in range(count)
    ]
    for load in loads:
        load.start()
    for load, store in zip(loads, stores):
        load.wait()
        store.start()
    for store in stores:
        store.wait()


def collate(place, pieces):
    count = len(pieces)
    turns, piece, channels = pieces[0].shape
    return pl.pallas_call(
        functools.partial(collate_kernel, count),
        out_shape=jax.ShapeDtypeStruct((count * turns, piece, channels), pieces[0].dtype),
        in_specs=[pl.BlockSpec(memory_space=pltpu.SMEM)]
        + [pl.BlockSpec(memory_space=pl.ANY)] * count,
        out_specs=pl.BlockSpec(memory_space=pl.ANY),
        scratch_shapes=[pltpu.VMEM(block.shape, block.dtype) for block in pieces]
        + [pltpu.SemaphoreType.DMA((2, count))],
        compiler_params=pltpu.CompilerParams(vmem_limit_bytes=VMEM),
        name="collate",
    )(place, *pieces)


def shift(block, axis, step):
    count = lax.axis_size(axis)
    return lax.ppermute(block, axis, [(source, (source + step) % count) for source in range(count)])


def global_hour(current, spec_filter, w_skip, w_mix, forward, inverse):
    longitude = lax.all_to_all(current, "col", split_axis=2, concat_axis=1, tiled=True)
    spectrum = jnp.einsum("alc,ml->amc", longitude, forward, preferred_element_type=jnp.float32)
    num_modes = spec_filter.shape[1]
    real_part = spectrum[:, :num_modes, :]
    imag_part = spectrum[:, num_modes:, :]
    filt_real = spec_filter[0][None]
    filt_imag = spec_filter[1][None]
    mixed = jnp.concatenate(
        [
            real_part * filt_real - imag_part * filt_imag,
            real_part * filt_imag + imag_part * filt_real,
        ],
        axis=1,
    ).astype(jnp.bfloat16)
    filtered = jnp.einsum("amc,lm->alc", mixed, inverse, preferred_element_type=jnp.float32).astype(
        jnp.bfloat16
    )
    spectral = lax.all_to_all(filtered, "col", split_axis=1, concat_axis=2, tiled=True)
    skipped = jnp.einsum("alc,cd->ald", current, w_skip, preferred_element_type=jnp.float32)
    activated = jax.nn.gelu(spectral.astype(jnp.float32) + skipped).astype(jnp.bfloat16)
    update = jnp.einsum("ald,de->ale", activated, w_mix, preferred_element_type=jnp.float32)
    return (current.astype(jnp.float32) + update).astype(jnp.bfloat16)


def window_extent(cells):
    return (cells + RIM - 1) // RATIO + 3 - (-RIM // RATIO)


def window_base():
    return -(-RIM // RATIO)


def global_by_latitude(
    hours, global_state, spec_filter, w_skip, w_mix, w_decode, box_lat0, box_lon0, rows_here,
    cols_here, prepare,
):
    count = lax.axis_size("col")
    me = lax.axis_index("col")
    lats_here, piece, _ = global_state.shape
    turns = lats_here // count
    tables = split_tables(piece * count, spec_filter.shape[1])
    owners = [(me - step) % count * turns for step in range(count)]
    def bands_of(turn):
        return [lax.dynamic_slice_in_dim(global_state, owner + turn, 1, 0) for owner in owners]

    bands, mine = lax.optimization_barrier((bands_of(0), filter_share(spec_filter)))
    received = [[shift(band, "col", -step) if step else band for step, band in enumerate(bands)]]
    wide = every_channel(mine)
    gains = spread(wide, PLANE).reshape(-1, wide.shape[1])
    parts, weights = prepare(wide, gains)
    for turn in range(1, turns):
        bands, received[-1] = lax.optimization_barrier((bands_of(turn), received[-1]))
        received.append([shift(band, "col", -step) if step else band for step, band in enumerate(bands)])
    start = (box_lon0[0] - window_base() - me * piece) % (piece * count)
    place = jnp.stack([start // piece, (start // piece + 1) % count, start % piece]).astype(jnp.int32)
    outcome, strips, early = [], [], []
    for turn in range(turns):
        if turn > 0:
            received[turn], _ = lax.optimization_barrier((received[turn], (strips, parts[2:4])))
        blocks, strip = advance_latitudes(
            hours, cols_here // RATIO, place, received[turn], tables, gains, w_skip, w_mix, w_decode
        )
        if turn < turns - 1:
            early += [shift(blocks[step], "col", step) for step in (1, 3)]
        outcome.append(list(blocks))
        strips.append(strip)
    strips = jnp.concatenate(strips, axis=1)
    near = [
        lax.dynamic_index_in_dim(strips, (me - step) % count, 0, keepdims=False)
        for step in range(count)
    ]
    near, early = lax.optimization_barrier((near, early))
    near = [shift(strip, "col", -step) if step else strip for step, strip in enumerate(near)]
    near, outcome, parts = lax.optimization_barrier((near, outcome, parts))
    got = spread(jnp.stack(near), PLANE)
    plane = lax.axis_size(PLANE)
    got = got.reshape((plane * lats_here, -1, LANES))
    lat = box_lat0[0] - window_base() + lax.axis_index(PLANE) * (rows_here // RATIO)
    lat = jnp.clip(lat + jnp.arange(window_extent(rows_here), dtype=jnp.int32), 0, plane * lats_here - 1)
    band, lat = lat // lats_here, lat % lats_here
    pick = (band * count + (lat // turns - me) % count) * turns + lat % turns
    places, finals = [], []
    for turn, blocks in enumerate(outcome):
        for step, block in enumerate(blocks):
            if turn < turns - 1 and step % 2 == 1:
                block = early[2 * turn + step // 2]
            elif step:
                block = shift(block, "col", step)
            places.append(owners[step] + turn)
            finals.append(block)

    def finish(after):
        blocks, after = lax.optimization_barrier((finals, after))
        return collate(jnp.stack(places).astype(jnp.int32), blocks), after

    return finish, got, pick.astype(jnp.int32), (parts, weights)


def global_by_channel(
    hours, global_state, spec_filter, w_skip, w_mix, w_decode, box_lat0, box_lon0, rows_here,
    cols_here, prepare,
):
    count = lax.axis_size("col")
    prepared = prepare(w_decode, w_decode)
    forward, inverse = fourier_tables(global_state.shape[1] * count, spec_filter.shape[1])
    base = window_base()
    high, wide = window_extent(rows_here), window_extent(cols_here)
    span = (count - 1) * (cols_here // RATIO) + wide
    lat_start = box_lat0[0] + lax.axis_index(PLANE) * (rows_here // RATIO)
    lon_start = box_lon0[0] + lax.axis_index("col") * (cols_here // RATIO)
    windows = []
    for _ in range(hours):
        global_state = global_hour(global_state, spec_filter, w_skip, w_mix, forward, inverse)
        coarse = jnp.einsum(
            "alc,ck->alk", global_state, w_decode, preferred_element_type=jnp.float32
        ).astype(jnp.bfloat16)
        coarse = lax.all_gather(coarse, "col", axis=1, tiled=True)
        coarse = jnp.pad(coarse, ((0, 0), (base, span), (0, 0)))
        coarse = lax.dynamic_slice_in_dim(coarse, box_lon0[0], base + span, 1)
        coarse = lax.all_gather(coarse, PLANE, axis=0, tiled=True)
        coarse = lax.dynamic_slice_in_dim(coarse, lon_start - box_lon0[0], wide, 1)
        coarse = jnp.pad(coarse, ((base, high), (0, 0), (0, 0)))
        coarse = lax.dynamic_slice_in_dim(coarse, lat_start, high, 0)
        windows.append(coarse)
    group = LANES // PACKED
    windows = jnp.stack(windows, axis=1)
    windows = jnp.pad(
        windows, ((0, 0), (0, 0), (0, STRIP * group - wide), (0, PACKED - windows.shape[3]))
    )
    windows = windows.reshape(high, hours * STRIP, LANES)
    return lambda after: (global_state, after), windows, jnp.arange(high, dtype=jnp.int32), prepared


def next_to(low, high, axis):
    count = lax.axis_size(axis)
    forward = [(i, i + 1) for i in range(count - 1)]
    backward = [(target, source) for source, target in forward]
    return lax.ppermute(low, axis, forward), lax.ppermute(high, axis, backward)


def grid_place(start_ref, total, base, extent):
    place = start_ref + base + lax.broadcasted_iota(jnp.int32, (extent, 1), 0)
    return (place >= 0) & (place < total)


def denoise_kernel(
    rows, cols, totals, variables, conds, width, place_ref, pick_ref, mid0_ref, mid1_ref, above_ref,
    below_ref, left_ref, right_ref, strip_ref, *refs
):
    far_refs, out_ref, refs = refs[:5], refs[5], refs[6:]
    near_refs, sems, refs = refs[:5], refs[5], refs[6:]
    first_w_ref, down_w_ref, up_w_ref, bridge_w_ref, last_w_ref = near_refs
    noisy_ref, noise_ref, blend_ref, own_ref, stack_ref, first_ref, pooled_ref, third_ref, pair_ref, spread_ref, window_ref = refs
    copies = [
        pltpu.make_async_copy(far, near, sems.at[index])
        for index, (far, near) in enumerate(zip(far_refs, near_refs))
    ]
    for copy in copies:
        copy.start()
    half = width // 2
    pad = (width - cols) // 2
    channels = mid0_ref.shape[2]
    f32, bf16 = jnp.float32, jnp.bfloat16

    inner = RIM - RIM_USED
    for ref, mid_ref, rim, part in ((noisy_ref, mid0_ref, RIM, 0), (noise_ref, mid1_ref, inner, RIM)):
        ref[0:rim, pad : pad + cols, :] = above_ref[part : part + rim]
        ref[rim : rim + rows, pad : pad + cols, :] = mid_ref[...]
        ref[rim + rows :, pad : pad + cols, :] = below_ref[part : part + rim]
        skip = RIM - rim
        for side_ref, low, to in ((left_ref, 0, pad - rim), (right_ref, pad + cols, 0)):
            side = side_ref[skip : skip + rows + 2 * rim].astype(f32)
            side = pltpu.roll(side, (to - part) % pad, 1)
            ref[:, low : low + pad, :] = side.astype(bf16)

    is_in = grid_place(place_ref[1], totals[1], -pad, width)
    col_in = is_in.astype(f32)
    base = window_base()
    col = lax.broadcasted_iota(jnp.int32, (width, 1), 0) - pad
    frac_col = ((col % RATIO).astype(f32) + 0.5) / RATIO
    col_base = jnp.where(is_in, (col + pad) // RATIO - pad // RATIO + base, FAR).astype(f32) + frac_col
    group = LANES // PACKED
    high = pick_ref.shape[0]
    point = lax.broadcasted_iota(jnp.int32, (1, group * high * STRIP), 1)
    point_lat = (point // STRIP % high).astype(f32)
    point_lon = (point % STRIP * group + point // (STRIP * high)).astype(f32)

    def blend(row):
        whole = row // RATIO
        frac_row = (row - whole * RATIO + 0.5) / RATIO
        there = place_ref[0] + row
        row_base = jnp.where((there >= 0) & (there < totals[0]), whole + base + frac_row, float(FAR))
        shifts = noisy_ref[row + RIM].astype(f32)
        lat = row_base + shifts[:, variables + conds : variables + conds + 1]
        lon = col_base + shifts[:, variables + conds + 1 : variables + conds + 2]
        weight_lat = jnp.maximum(1.0 - jnp.abs(point_lat - lat), 0.0)
        weight_lon = jnp.maximum(1.0 - jnp.abs(point_lon - lon), 0.0)
        return (weight_lat * weight_lon).astype(bf16)

    edges = [jnp.broadcast_to(col_in[low : low + pad], (pad, channels)) for low in (0, pad + cols)]
    lane = lax.broadcasted_iota(jnp.int32, (1, channels), 1)
    is_state = lane < variables
    is_cond = (lane >= variables) & (lane < variables + conds)
    strips = [strip_ref[pick_ref[index]].astype(f32) for index in range(high)]
    for hour in range(2):
        near = jnp.concatenate([s[hour * STRIP : (hour + 1) * STRIP] for s in strips], axis=0)
        for turn in range(LANES // PACKED):
            moved = pltpu.roll(near, (variables - turn * PACKED) % LANES, 1)
            window_ref[hour, turn * high * STRIP : (turn + 1) * high * STRIP, :] = jnp.where(
                is_cond, moved, 0.0
            ).astype(bf16)

    def flat(start, count, unit):
        return slice(start * unit, (start + count) * unit)

    def mask(value, row):
        low, mid, high = value[:pad], value[pad : pad + cols], value[pad + cols :]
        value = jnp.concatenate([low * edges[0], mid, high * edges[1]], axis=0)
        if 0 <= row < rows:
            return value
        there = place_ref[0] + row
        return value * jnp.where((there >= 0) & (there < totals[0]), 1.0, 0.0)

    def keep(ref, where, value):
        size = value.shape[0]
        ref[0, where, :] = pltpu.roll(value, 1, 0).astype(bf16)
        ref[1, where, :] = value.astype(bf16)
        ref[2, where, :] = pltpu.roll(value, size - 1, 0).astype(bf16)

    def pairs(ref, row, count):
        blocks = []
        for pair in range(count):
            taps = [
                ref[shift, flat(row + 2 * pair + step, 1, width), :]
                for step in range(4)
                for shift in range(3)
            ]
            blocks.append(jnp.concatenate(taps, axis=1))
        return jnp.concatenate(blocks, axis=0)

    def silu_of_half(half_value):
        return half_value + half_value * jnp.tanh(half_value)

    for hour in range(2):
        rim = RIM - RIM_USED * hour
        tall = rows + 2 * rim

        for row in range(0, tall, 2):
            here = flat(row, 2, width)
            if hour == 0:
                weights = jnp.concatenate([blend(row - RIM), blend(row + 1 - RIM)], axis=0)
                blend_ref[here, :] = weights
            else:
                weights = blend_ref[flat(row + RIM - rim, 2, width), :]
            cond = jnp.dot(weights, window_ref[hour], preferred_element_type=f32)
            if hour == 0:
                own = noisy_ref[row : row + 2].reshape(2 * width, channels).astype(f32)
                own_ref[here, :] = own
            else:
                own = own_ref[here, :]
            keep(stack_ref, here, jnp.where(is_state, own, cond))

        if hour == 0:
            copies[0].wait()
        for row in range(0, tall - 2, 8):
            value = jnp.dot(
                pairs(stack_ref, row, 4), first_w_ref[...], preferred_element_type=f32
            )
            for pair in range(4):
                top = row + 2 * pair
                here = flat(top // 2, 1, width)
                part = silu_of_half(value[pair * width : (pair + 1) * width])
                upper = mask(part[:, :channels], top - rim + 1)
                lower = mask(part[:, channels:], top - rim + 2)
                first_ref[here, :channels] = upper.astype(bf16)
                first_ref[here, channels:] = lower.astype(bf16)
                pair_ref[top // 2] = upper + lower
                even = pair_ref[top // 2, pl.ds(0, half, stride=2), :]
                odd = pair_ref[top // 2, pl.ds(1, half, stride=2), :]
                keep(pooled_ref, flat(top // 2, 1, half), even + odd)

        if hour == 0:
            for copy in copies[1:4]:
                copy.wait()
        half_rows = (tall - 2) // 2 - 2
        part = half_rows // 2
        for row in (0, part):
            taps = [
                pooled_ref[shift, flat(row + step, part, half), :]
                for step in range(3)
                for shift in range(3)
            ]
            second = jnp.dot(
                jnp.concatenate(taps, axis=1), down_w_ref[...], preferred_element_type=f32
            )
            lifted = jnp.dot(
                silu_of_half(second).astype(bf16), up_w_ref[...], preferred_element_type=f32
            )
            bridged = jnp.dot(
                first_ref[flat(row + 1, part, width), :], bridge_w_ref[...], preferred_element_type=f32
            )
            for step in range(part):
                own = lifted[step * half : (step + 1) * half]
                spread_ref[row + step, pl.ds(0, half, stride=2), :] = own
                spread_ref[row + step, pl.ds(1, half, stride=2), :] = own
                own = spread_ref[row + step]
                top = 2 * (row + step)
                for side in range(2):
                    value = bridged[
                        step * width : (step + 1) * width, side * channels : (side + 1) * channels
                    ]
                    value = mask(silu_of_half(value + own), top + side - rim + 3)
                    keep(third_ref, flat(top + side, 1, width), value)

        if hour == 0:
            copies[4].wait()
        skip = 1 if hour == 1 else 0
        count = (rows + 2 * (rim - RIM_USED)) // 2 if hour == 0 else rows // 2
        for first in range(0, count, 4):
            size = min(4, count - first)
            values = jnp.dot(
                pairs(third_ref, 2 * first + skip, size), last_w_ref[...], preferred_element_type=f32
            )
            for index in range(2 * size):
                pair, side = divmod(index, 2)
                row = 2 * first + index
                fresh = values[
                    pair * width : (pair + 1) * width, side * channels : (side + 1) * channels
                ]
                fresh = own_ref[flat(row + RIM_USED + skip, 1, width), :] + fresh
                if hour == 0:
                    fresh = fresh + noise_level * noise_ref[row].astype(f32)
                    own_ref[flat(row, 1, width), :] = mask(fresh, row - rim + RIM_USED)
                else:
                    out_ref[:, row * cols : (row + 1) * cols] = fresh[pad : pad + cols].T.astype(bf16)


def denoise(rows, cols, totals, variables, conds, place, pick, parts, strips, weights):
    mid0, _, _, _, left, _ = parts
    width, channels = cols + 2 * left.shape[1], mid0.shape[2]
    tall = rows + 2 * RIM
    most = (tall - 2) // 2
    points = LANES // PACKED * pick.shape[0] * STRIP
    bf16, f32 = jnp.bfloat16, jnp.float32
    return pl.pallas_call(
        functools.partial(denoise_kernel, rows, cols, totals, variables, conds, width),
        out_shape=jax.ShapeDtypeStruct((channels, rows * cols), bf16),
        in_specs=[pl.BlockSpec(memory_space=pltpu.SMEM)] * 2
        + [pl.BlockSpec(memory_space=pltpu.VMEM)] * 7
        + [pl.BlockSpec(memory_space=pl.ANY)] * len(weights),
        scratch_shapes=[pltpu.VMEM(array.shape, array.dtype) for array in weights]
        + [
            pltpu.SemaphoreType.DMA((len(weights),)),
            pltpu.VMEM((tall, width, channels), bf16),
            pltpu.VMEM((tall - 2 * RIM_USED, width, channels), bf16),
            pltpu.VMEM((tall * width, points), bf16),
            pltpu.VMEM((tall * width, channels), f32),
            pltpu.VMEM((3, tall * width, channels), bf16),
            pltpu.VMEM((most * width, 2 * channels), bf16),
            pltpu.VMEM((3, most * width // 2, channels), bf16),
            pltpu.VMEM((3, tall * width, channels), bf16),
            pltpu.VMEM((most, width, channels), f32),
            pltpu.VMEM((most, width, channels), f32),
            pltpu.VMEM((2, points, channels), bf16),
        ],
        compiler_params=pltpu.CompilerParams(vmem_limit_bytes=VMEM),
        cost_estimate=pl.CostEstimate(flops=10**6, bytes_accessed=10**5, transcendentals=0),
        name="denoise",
    )(place, pick, *parts, strips, *weights)


def conv_weight(weight, depth, width):
    out, _, given = weight.shape
    weight = jnp.pad(weight, ((0, width - out), (0, 0), (0, depth - given)))
    return jnp.transpose(weight, (1, 2, 0)).reshape(9 * depth, width)


def pair_weight(weight):
    row = weight.shape[0] // 3
    return jnp.concatenate(
        [jnp.pad(weight, ((0, row), (0, 0))), jnp.pad(weight, ((row, 0), (0, 0)))], axis=1
    )


def shards(
    global_state,
    spec_filter,
    w_skip,
    w_mix,
    w_decode,
    regional_state,
    noise_draws,
    w_first,
    w_down,
    w_up,
    w_bridge,
    w_last,
    box_lat0,
    box_lon0,
    stencil_lat,
    stencil_lon,
):
    hours = noise_draws.shape[0]
    rows_here, cols_here = regional_state.shape[1:]
    row_start = lax.axis_index(PLANE) * rows_here
    col_start = lax.axis_index("col") * cols_here
    total_rows = rows_here * lax.axis_size(PLANE)
    total_cols = cols_here * lax.axis_size("col")
    assert hours == 2

    variables = regional_state.shape[0]
    conds = w_decode.shape[1]
    lanes = variables + conds
    inner = RIM - RIM_USED
    high = window_extent(rows_here)
    place = jnp.stack([row_start, col_start]).astype(jnp.int32)
    totals = (total_rows, total_cols)

    def prepare(after, later):
        state, noise, _ = lax.optimization_barrier((regional_state, noise_draws, after))
        noisy = (
            state.astype(jnp.float32) + noise_level * noise[0].astype(jnp.float32)
        ).astype(jnp.bfloat16)
        lat_shift = stencil_lat - (row_start + jnp.arange(rows_here, dtype=jnp.int32))[:, None] // RATIO
        lon_shift = stencil_lon - (col_start + jnp.arange(cols_here, dtype=jnp.int32))[None, :] // RATIO
        cells = (rows_here, cols_here)
        mids = jnp.concatenate(
            [
                noisy,
                jnp.zeros((conds,) + cells, jnp.bfloat16),
                lat_shift.astype(jnp.bfloat16)[None],
                lon_shift.astype(jnp.bfloat16)[None],
                jnp.zeros((LANES - lanes - 2,) + cells, jnp.bfloat16),
                noise[1],
                jnp.zeros((LANES - variables,) + cells, jnp.bfloat16),
            ],
            axis=0,
        )
        mids = jnp.transpose(mids.reshape((2, LANES) + cells), (0, 2, 3, 1))
        mid0, mid1 = mids[0], mids[1]
        lows = jnp.concatenate([mid0[rows_here - RIM :], mid1[rows_here - inner :]], axis=0)
        highs = jnp.concatenate([mid0[:RIM], mid1[:inner]], axis=0)
        lows, highs, _ = lax.optimization_barrier((lows, highs, later))
        above, below = next_to(lows, highs, PLANE)

        def rim_cols(first, first_inner):
            wide, thin = slice(first, first + RIM), slice(first_inner, first_inner + inner)
            noise = jnp.concatenate([above[RIM:, thin], mid1[:, thin], below[RIM:, thin]], axis=0)
            noise = jnp.pad(
                noise, ((RIM_USED, RIM_USED), (0, RIM_COLS - RIM - inner), (0, 0))
            )
            return jnp.concatenate(
                [
                    jnp.concatenate([above[:RIM, wide], mid0[:, wide], below[:RIM, wide]], axis=0),
                    noise,
                ],
                axis=1,
            )

        left, right = next_to(
            rim_cols(cols_here - RIM, cols_here - inner), rim_cols(0, 0), "col"
        )
        weights = (
            pair_weight(conv_weight(0.5 * w_first, LANES, w_first.shape[0])),
            conv_weight(0.125 * w_down, w_down.shape[2], w_down.shape[0]),
            0.5 * w_up.T,
            0.5
            * jnp.concatenate(
                [jnp.pad(w_bridge.T, ((0, 0), (0, LANES))), jnp.pad(w_bridge.T, ((0, 0), (LANES, 0)))],
                axis=0,
            ),
            pair_weight(conv_weight(w_last, w_last.shape[2], LANES)),
        )
        return (mid0, mid1, above, below, left, right), weights

    by_latitude = lax.axis_size("col") == 4 and global_state.shape[0] % 4 == 0
    global_steps = global_by_latitude if by_latitude else global_by_channel
    finish, strips, pick, (parts, weights) = global_steps(
        hours, global_state, spec_filter, w_skip, w_mix, w_decode, box_lat0, box_lon0,
        rows_here, cols_here, prepare,
    )
    regional_final = denoise(
        rows_here, cols_here, totals, variables, conds, place, pick, parts, strips, weights
    )
    regional_final = regional_final[:variables].reshape((variables, rows_here, cols_here))
    return finish(regional_final)


def solution(mesh):
    return jax.shard_map(
        shards,
        mesh=mesh,
        in_specs=(
            P(PLANE, "col", None),
            P(None, None, "col"),
            P(),
            P(),
            P(),
            P(None, PLANE, "col"),
            P(None, None, PLANE, "col"),
            P(),
            P(),
            P(),
            P(),
            P(),
            P(),
            P(),
            P(PLANE, "col"),
            P(PLANE, "col"),
        ),
        out_specs=(P(PLANE, "col", None), P(None, PLANE, "col")),
        check_vma=False,
    )
```

```python
import functools
import math

import jax
import jax.numpy as jnp
import ml_dtypes
import numpy as np
from jax import lax
from jax.experimental import pallas as pl
from jax.experimental.pallas import tpu as pltpu
from jax.sharding import PartitionSpec as P

RATIO = 8
noise_level = 0.5
PLANE = ("grp", "row")
RIM = 9
RIM_USED = 4
LANES = 128
VMEM = 60 * 2**20
PACKED = 32
MODE_TILE = 64
STRIP = 8
FAR = -4096
RIM_COLS = 16


def fourier_tables(length, num_modes):
    position = np.arange(length, dtype=np.int64)[:, None]
    frequency = np.arange(num_modes, dtype=np.int64)[None, :]
    angle = (position * frequency % length).astype(np.float64) * (2.0 * math.pi / length)
    cosine = np.cos(angle)
    sine = np.sin(angle)
    factor = np.where(frequency == 0, 1.0, 2.0) / length
    forward = np.concatenate([cosine, -sine], axis=1).T.astype(ml_dtypes.bfloat16)
    inverse = np.concatenate([cosine * factor, -sine * factor], axis=1).astype(ml_dtypes.bfloat16)
    return forward, inverse


def round_up(size, unit):
    return -(-size // unit) * unit


def split_tables(length, num_modes):
    piece = length // 4
    place = np.arange(piece, dtype=np.int64)[:, None]

    def waves(mode):
        angle = (place * mode[None, :] % length).astype(np.float64) * (2.0 * math.pi / length)
        return np.cos(angle), np.sin(angle), np.where(mode == 0, 1.0, 2.0)[None, :] / length

    def padded(blocks, unit_rows, unit_cols):
        rows = []
        for row in blocks:
            cols = []
            for block in row:
                spare = [(0, -block.shape[0] % unit_rows), (0, -block.shape[1] % unit_cols)]
                cols.append(np.pad(block, spare))
            rows.append(np.concatenate(cols, axis=1))
        return np.concatenate(rows, axis=0).astype(ml_dtypes.bfloat16)

    forward, inverse = [], []
    for residue in (0, 2):
        cosine, sine, factor = waves(np.arange(residue, num_modes, 4))
        forward.append(padded([[cosine.T], [-sine.T]], MODE_TILE, LANES))
        inverse.append(padded([[cosine * factor, -sine * factor]], LANES, MODE_TILE))
    mode = np.arange(1, num_modes, 2)
    cosine, sine, factor = waves(mode)
    sign = np.where(mode % 4 == 1, 1.0, -1.0)[None, :]
    odd_forward = padded(
        [[cosine.T, (-sign * sine).T], [-sine.T, (-sign * cosine).T]], 2 * MODE_TILE, LANES
    )
    odd_inverse = padded(
        [
            [cosine * factor, -sine * factor],
            [-sign * sine * factor, -sign * cosine * factor],
        ],
        LANES,
        2 * MODE_TILE,
    )
    return tuple(
        jnp.asarray(table)
        for table in (np.stack(forward), odd_forward, np.stack(inverse), odd_inverse)
    )


def exchange(blocks, axis):
    return lax.all_to_all(blocks, axis, split_axis=0, concat_axis=0, tiled=True)


def spread(block, axis):
    return exchange(jnp.broadcast_to(block[None], (lax.axis_size(axis),) + block.shape), axis)


def filter_share(spec_filter):
    rows = 2 * spec_filter.shape[1]
    flat = spec_filter.reshape(rows, spec_filter.shape[2])
    share = rows // lax.axis_size(PLANE)
    mine = lax.dynamic_slice_in_dim(flat, lax.axis_index(PLANE) * share, share, 0)
    return mine.astype(jnp.bfloat16)


def every_channel(mine):
    count = lax.axis_size("col")
    me = lax.axis_index("col")
    blocks = [shift(mine, "col", -step) if step else mine for step in range(count)]
    ring = jnp.concatenate(blocks + blocks[:-1], axis=1)
    width = mine.shape[1]
    return lax.dynamic_slice_in_dim(ring, (count - me) % count * width, count * width, 1)


def gelu(x):
    slope = math.sqrt(2.0 / math.pi)
    half = 0.5 * x
    return half + half * jnp.tanh(x * (slope + (0.044715 * slope) * (x * x)))


def latitude_kernel(hours, turns, step, place_ref, *refs):
    piece_refs, refs = refs[:4], refs[4:]
    even_forward_ref, odd_forward_ref = refs[:2]
    far_refs, out_refs, strip_ref, refs = refs[2:8], refs[8:12], refs[12], refs[13:]
    near_refs, sems, refs = refs[:6], refs[6], refs[7:]
    filter_ref, even_inverse_ref, odd_inverse_ref, skip_ref, mix_ref, decode_ref = near_refs
    state_ref, gain_ref, coarse_ref, near_ref, packed_ref = refs
    copies = [
        pltpu.make_async_copy(far, near, sems.at[index])
        for index, (far, near) in enumerate(zip(far_refs, near_refs))
    ]
    for copy in copies:
        copy.start()
    f32, bf16 = jnp.float32, jnp.bfloat16
    piece, channels = piece_refs[0].shape[1:]
    padded = state_ref.shape[0] // 4
    group = LANES // PACKED
    span = near_ref.shape[0]
    rows = span // group
    spare = jnp.zeros((padded - piece, channels), bf16)
    for index in range(4):
        for turn in range(turns):
            state_ref[
                index * padded : (index + 1) * padded, turn * channels : (turn + 1) * channels
            ] = jnp.concatenate([piece_refs[index][turn], spare], axis=0)

    modes = filter_ref.shape[0] // 2

    def spread_gains():
        for index in range(channels // LANES):
            lanes = slice(index * LANES, (index + 1) * LANES)
            gain_ref[index, : 2 * modes, :] = filter_ref[:, lanes].astype(f32)
            gain_ref[index, 2 * modes :, :] = jnp.zeros((gain_ref.shape[1] - 2 * modes, LANES), f32)

    def gain_rows(low, count, stride):
        rows = pl.ds(low, count, stride=stride)
        tiles = [gain_ref[index, rows, :] for index in range(channels // LANES)]
        return jnp.concatenate(tiles * turns, axis=1)

    def gain(real, imag, low, stride):
        gain_real = gain_rows(low, real.shape[0], stride)
        gain_imag = gain_rows(modes + low, real.shape[0], stride)
        return (
            (real * gain_real - imag * gain_imag).astype(bf16),
            (real * gain_imag + imag * gain_real).astype(bf16),
        )

    def dot(left, right):
        return jnp.dot(left, right, preferred_element_type=f32)

    for hour in range(hours):
        pieces = [
            state_ref[index * padded : (index + 1) * padded, :].astype(f32) for index in range(4)
        ]
        mixed = jnp.concatenate([pieces[0] - pieces[2], pieces[1] - pieces[3]], axis=0).astype(bf16)
        span_odd = odd_forward_ref.shape[0] // 2
        thirds = span_odd // 3
        spectra = []
        for index in range(3):
            low = index * thirds
            spectra.append(
                (
                    dot(odd_forward_ref[low : low + thirds, :], mixed),
                    dot(odd_forward_ref[span_odd + low : span_odd + low + thirds, :], mixed),
                )
            )
            if index == 0:
                both, other = pieces[0] + pieces[2], pieces[1] + pieces[3]
                mixes = [(both + other).astype(bf16), (both - other).astype(bf16)]
        evens = [dot(even_forward_ref[index], mixes[index]) for index in range(2)]
        if hour == 0:
            copies[0].wait()
            spread_gains()
            for copy in copies[1:]:
                copy.wait()
        odd = [gain(*spectra[index], 1 + 2 * index * thirds, 2) for index in range(3)]
        odd = jnp.concatenate([part[0] for part in odd] + [part[1] for part in odd], axis=0)
        odd_shares = [dot(odd_inverse_ref[:padded, :], odd)]
        shares = []
        for index in range(2):
            half = evens[index].shape[0] // 2
            even = gain(evens[index][:half], evens[index][half:], 2 * index, 4)
            shares.append(dot(even_inverse_ref[index], jnp.concatenate(even, axis=0)))
        odd_shares.append(dot(odd_inverse_ref[padded:, :], odd))

        def block_of(ref, index, turn):
            return ref[
                index * padded : (index + 1) * padded, turn * channels : (turn + 1) * channels
            ]

        order = [(index, turn) for index in (0, 2, 1, 3) for turn in range(turns)]
        skipped = dot(block_of(state_ref, *order[0]), skip_ref[...])
        for place, (index, turn) in enumerate(order):
            if place + 1 < len(order):
                following = dot(block_of(state_ref, *order[place + 1]), skip_ref[...])
            if turn == 0:
                even = shares[0] + shares[1] if index % 2 == 0 else shares[0] - shares[1]
                spectral = even + odd_shares[index % 2] if index < 2 else even - odd_shares[index % 2]
            own = spectral[:, turn * channels : (turn + 1) * channels]
            activated = gelu(own + skipped).astype(bf16)
            fresh = block_of(state_ref, index, turn).astype(f32) + dot(activated, mix_ref[...])
            state_ref[
                index * padded : (index + 1) * padded, turn * channels : (turn + 1) * channels
            ] = fresh.astype(bf16)
            skipped = following

        for index in range(2):
            here = pl.ds(pl.multiple_of(place_ref[index] * padded, LANES), padded)
            for turn in range(turns):
                lanes = slice(turn * channels, (turn + 1) * channels)
                coarse = dot(state_ref[here, lanes], decode_ref[...])
                coarse_ref[turn, index * piece : (index + 1) * piece, :] = coarse[:piece]
        for turn in range(turns):
            near_ref[...] = coarse_ref[turn, pl.ds(place_ref[2], span), :]
            packed = near_ref[pl.ds(0, rows, stride=group), :]
            for sub in range(1, group):
                packed += pltpu.roll(near_ref[pl.ds(sub, rows, stride=group), :], sub * PACKED, 1)
            packed_ref[turn, hour * rows : (hour + 1) * rows, :] = packed

    for index in range(4):
        for turn in range(turns):
            out_refs[index][turn] = state_ref[
                index * padded : index * padded + piece, turn * channels : (turn + 1) * channels
            ]
    for target in range(4):
        low = target * step // group
        for turn in range(turns):
            strip = [
                packed_ref[turn, hour * rows + low : hour * rows + low + STRIP, :]
                for hour in range(hours)
            ]
            strip_ref[target, turn * hours * STRIP : (turn + 1) * hours * STRIP, :] = jnp.concatenate(
                strip, axis=0
            ).astype(bf16)


def advance_latitudes(hours, step, place, pieces, tables, gains, w_skip, w_mix, w_decode):
    turns, piece, channels = pieces[0].shape
    padded = round_up(piece, LANES)
    group = LANES // PACKED
    span = round_up(3 * step + STRIP * group, 8 * group)
    decode = jnp.pad(w_decode, ((0, 0), (0, LANES - w_decode.shape[1])))
    modes = gains.shape[0] // 2
    late = (gains,) + tables[2:] + (w_skip, w_mix, decode)
    spare = max(4 * (tables[0].shape[1] // 2), 2 * (tables[1].shape[0] // 2)) - modes
    results = pl.pallas_call(
        functools.partial(latitude_kernel, hours, turns, step),
        out_shape=tuple(
            jax.ShapeDtypeStruct((turns, piece, channels), jnp.bfloat16) for _ in pieces
        )
        + (jax.ShapeDtypeStruct((4, turns * hours * STRIP, LANES), jnp.bfloat16),),
        in_specs=[pl.BlockSpec(memory_space=pltpu.SMEM)]
        + [pl.BlockSpec(memory_space=pltpu.VMEM)] * 6
        + [pl.BlockSpec(memory_space=pl.ANY)] * len(late),
        scratch_shapes=[pltpu.VMEM(array.shape, array.dtype) for array in late]
        + [
            pltpu.SemaphoreType.DMA((len(late),)),
            pltpu.VMEM((4 * padded, turns * channels), jnp.bfloat16),
            pltpu.VMEM((channels // LANES, gains.shape[0] + spare, LANES), jnp.float32),
            pltpu.VMEM((turns, 2 * piece, LANES), jnp.float32),
            pltpu.VMEM((span, LANES), jnp.float32),
            pltpu.VMEM((turns, hours * span // group, LANES), jnp.float32),
        ],
        compiler_params=pltpu.CompilerParams(vmem_limit_bytes=VMEM),
        cost_estimate=pl.CostEstimate(
            flops=turns * 16 * 10**9,
            bytes_accessed=turns * 6 * 2**20,
            transcendentals=hours * turns * 4 * piece * channels,
        ),
        name="advance_latitudes",
    )(place, *pieces, *tables[:2], *late)
    return results[:4], results[4]


def collate_kernel(count, place_ref, *refs):
    far, out_ref, near, sems = refs[:count], refs[count], refs[count + 1 : -1], refs[-1]
    loads = [
        pltpu.make_async_copy(far[index], near[index], sems.at[0, index]) for index in range(count)
    ]
    stores = [
        pltpu.make_async_copy(
            near[index], out_ref.at[pl.ds(place_ref[index], near[index].shape[0])], sems.at[1, index]
        )
        for index in range(count)
    ]
    for load in loads:
        load.start()
    for load, store in zip(loads, stores):
        load.wait()
        store.start()
    for store in stores:
        store.wait()


def collate(place, pieces):
    count = len(pieces)
    turns, piece, channels = pieces[0].shape
    return pl.pallas_call(
        functools.partial(collate_kernel, count),
        out_shape=jax.ShapeDtypeStruct((count * turns, piece, channels), pieces[0].dtype),
        in_specs=[pl.BlockSpec(memory_space=pltpu.SMEM)]
        + [pl.BlockSpec(memory_space=pl.ANY)] * count,
        out_specs=pl.BlockSpec(memory_space=pl.ANY),
        scratch_shapes=[pltpu.VMEM(block.shape, block.dtype) for block in pieces]
        + [pltpu.SemaphoreType.DMA((2, count))],
        compiler_params=pltpu.CompilerParams(vmem_limit_bytes=VMEM),
        name="collate",
    )(place, *pieces)


def shift(block, axis, step):
    count = lax.axis_size(axis)
    return lax.ppermute(block, axis, [(source, (source + step) % count) for source in range(count)])


def global_hour(current, spec_filter, w_skip, w_mix, forward, inverse):
    longitude = lax.all_to_all(current, "col", split_axis=2, concat_axis=1, tiled=True)
    spectrum = jnp.einsum("alc,ml->amc", longitude, forward, preferred_element_type=jnp.float32)
    num_modes = spec_filter.shape[1]
    real_part = spectrum[:, :num_modes, :]
    imag_part = spectrum[:, num_modes:, :]
    filt_real = spec_filter[0][None]
    filt_imag = spec_filter[1][None]
    mixed = jnp.concatenate(
        [
            real_part * filt_real - imag_part * filt_imag,
            real_part * filt_imag + imag_part * filt_real,
        ],
        axis=1,
    ).astype(jnp.bfloat16)
    filtered = jnp.einsum("amc,lm->alc", mixed, inverse, preferred_element_type=jnp.float32).astype(
        jnp.bfloat16
    )
    spectral = lax.all_to_all(filtered, "col", split_axis=1, concat_axis=2, tiled=True)
    skipped = jnp.einsum("alc,cd->ald", current, w_skip, preferred_element_type=jnp.float32)
    activated = jax.nn.gelu(spectral.astype(jnp.float32) + skipped).astype(jnp.bfloat16)
    update = jnp.einsum("ald,de->ale", activated, w_mix, preferred_element_type=jnp.float32)
    return (current.astype(jnp.float32) + update).astype(jnp.bfloat16)


def window_extent(cells):
    return (cells + RIM - 1) // RATIO + 3 - (-RIM // RATIO)


def window_base():
    return -(-RIM // RATIO)


def global_by_latitude(
    hours, global_state, spec_filter, w_skip, w_mix, w_decode, box_lat0, box_lon0, rows_here,
    cols_here, prepare,
):
    count = lax.axis_size("col")
    me = lax.axis_index("col")
    lats_here, piece, _ = global_state.shape
    turns = lats_here // count
    tables = split_tables(piece * count, spec_filter.shape[1])
    owners = [(me - step) % count * turns for step in range(count)]
    def bands_of(turn):
        return [lax.dynamic_slice_in_dim(global_state, owner + turn, 1, 0) for owner in owners]

    bands, mine = lax.optimization_barrier((bands_of(0), filter_share(spec_filter)))
    received = [[shift(band, "col", -step) if step else band for step, band in enumerate(bands)]]
    wide = every_channel(mine)
    gains = spread(wide, PLANE).reshape(-1, wide.shape[1])
    parts, weights = prepare(wide, wide, gains)
    for turn in range(1, turns):
        bands, received[-1] = lax.optimization_barrier((bands_of(turn), received[-1]))
        received.append([shift(band, "col", -step) if step else band for step, band in enumerate(bands)])
    start = (box_lon0[0] - window_base() - me * piece) % (piece * count)
    place = jnp.stack([start // piece, (start // piece + 1) % count, start % piece]).astype(jnp.int32)
    outcome, strips, early = [], [], []
    for turn in range(turns):
        if turn > 0:
            received[turn], _ = lax.optimization_barrier((received[turn], (strips, parts)))
        blocks, strip = advance_latitudes(
            hours, cols_here // RATIO, place, received[turn], tables, gains, w_skip, w_mix, w_decode
        )
        if turn < turns - 1:
            early += [shift(blocks[step], "col", step) for step in (1, 3)]
        outcome.append(list(blocks))
        strips.append(strip)
    strips = jnp.concatenate(strips, axis=1)
    near = [
        lax.dynamic_index_in_dim(strips, (me - step) % count, 0, keepdims=False)
        for step in range(count)
    ]
    near, early = lax.optimization_barrier((near, early))
    near = [shift(strip, "col", -step) if step else strip for step, strip in enumerate(near)]
    plane = lax.axis_size(PLANE)
    near = jnp.stack(near)
    sent = jnp.broadcast_to(near[None], (plane,) + near.shape)
    sent, outcome = lax.optimization_barrier((sent, outcome))
    got = exchange(sent, PLANE)
    got = got.reshape((plane * lats_here, -1, LANES))
    lat = box_lat0[0] - window_base() + lax.axis_index(PLANE) * (rows_here // RATIO)
    lat = jnp.clip(lat + jnp.arange(window_extent(rows_here), dtype=jnp.int32), 0, plane * lats_here - 1)
    band, lat = lat // lats_here, lat % lats_here
    pick = (band * count + (lat // turns - me) % count) * turns + lat % turns
    places, finals = [], []
    for turn, blocks in enumerate(outcome):
        for step, block in enumerate(blocks):
            if turn < turns - 1 and step % 2 == 1:
                block = early[2 * turn + step // 2]
            elif step:
                block = shift(block, "col", step)
            places.append(owners[step] + turn)
            finals.append(block)

    def finish(after):
        blocks, after = lax.optimization_barrier((finals, after))
        return collate(jnp.stack(places).astype(jnp.int32), blocks), after

    return finish, got, pick.astype(jnp.int32), (parts, weights)


def global_by_channel(
    hours, global_state, spec_filter, w_skip, w_mix, w_decode, box_lat0, box_lon0, rows_here,
    cols_here, prepare,
):
    count = lax.axis_size("col")
    prepared = prepare(w_decode, w_decode, w_decode)
    forward, inverse = fourier_tables(global_state.shape[1] * count, spec_filter.shape[1])
    base = window_base()
    high, wide = window_extent(rows_here), window_extent(cols_here)
    span = (count - 1) * (cols_here // RATIO) + wide
    lat_start = box_lat0[0] + lax.axis_index(PLANE) * (rows_here // RATIO)
    lon_start = box_lon0[0] + lax.axis_index("col") * (cols_here // RATIO)
    windows = []
    for _ in range(hours):
        global_state = global_hour(global_state, spec_filter, w_skip, w_mix, forward, inverse)
        coarse = jnp.einsum(
            "alc,ck->alk", global_state, w_decode, preferred_element_type=jnp.float32
        ).astype(jnp.bfloat16)
        coarse = lax.all_gather(coarse, "col", axis=1, tiled=True)
        coarse = jnp.pad(coarse, ((0, 0), (base, span), (0, 0)))
        coarse = lax.dynamic_slice_in_dim(coarse, box_lon0[0], base + span, 1)
        coarse = lax.all_gather(coarse, PLANE, axis=0, tiled=True)
        coarse = lax.dynamic_slice_in_dim(coarse, lon_start - box_lon0[0], wide, 1)
        coarse = jnp.pad(coarse, ((base, high), (0, 0), (0, 0)))
        coarse = lax.dynamic_slice_in_dim(coarse, lat_start, high, 0)
        windows.append(coarse)
    group = LANES // PACKED
    windows = jnp.stack(windows, axis=1)
    windows = jnp.pad(
        windows, ((0, 0), (0, 0), (0, STRIP * group - wide), (0, PACKED - windows.shape[3]))
    )
    windows = windows.reshape(high, hours * STRIP, LANES)
    return lambda after: (global_state, after), windows, jnp.arange(high, dtype=jnp.int32), prepared


def next_to(low, high, axis):
    count = lax.axis_size(axis)
    forward = [(i, i + 1) for i in range(count - 1)]
    backward = [(target, source) for source, target in forward]
    return lax.ppermute(low, axis, forward), lax.ppermute(high, axis, backward)


def grid_place(start_ref, total, base, extent):
    place = start_ref + base + lax.broadcasted_iota(jnp.int32, (extent, 1), 0)
    return (place >= 0) & (place < total)


def denoise_kernel(
    rows, cols, totals, variables, conds, width, place_ref, pick_ref, mid0_ref, mid1_ref, above_ref,
    below_ref, left_ref, right_ref, strip_ref, *refs
):
    far_refs, out_ref, refs = refs[:5], refs[5], refs[6:]
    near_refs, sems, refs = refs[:5], refs[5], refs[6:]
    first_w_ref, down_w_ref, up_w_ref, bridge_w_ref, last_w_ref = near_refs
    noisy_ref, noise_ref, blend_ref, own_ref, stack_ref, first_ref, pooled_ref, third_ref, pair_ref, spread_ref, window_ref = refs
    copies = [
        pltpu.make_async_copy(far, near, sems.at[index])
        for index, (far, near) in enumerate(zip(far_refs, near_refs))
    ]
    for copy in copies:
        copy.start()
    half = width // 2
    pad = (width - cols) // 2
    channels = mid0_ref.shape[2]
    f32, bf16 = jnp.float32, jnp.bfloat16

    inner = RIM - RIM_USED
    for ref, mid_ref, rim, part in ((noisy_ref, mid0_ref, RIM, 0), (noise_ref, mid1_ref, inner, RIM)):
        ref[0:rim, pad : pad + cols, :] = above_ref[part : part + rim]
        ref[rim : rim + rows, pad : pad + cols, :] = mid_ref[...]
        ref[rim + rows :, pad : pad + cols, :] = below_ref[part : part + rim]
        skip = RIM - rim
        for side_ref, low, to in ((left_ref, 0, pad - rim), (right_ref, pad + cols, 0)):
            side = side_ref[skip : skip + rows + 2 * rim].astype(f32)
            side = pltpu.roll(side, (to - part) % pad, 1)
            ref[:, low : low + pad, :] = side.astype(bf16)

    is_in = grid_place(place_ref[1], totals[1], -pad, width)
    col_in = is_in.astype(f32)
    base = window_base()
    col = lax.broadcasted_iota(jnp.int32, (width, 1), 0) - pad
    frac_col = ((col % RATIO).astype(f32) + 0.5) / RATIO
    col_base = jnp.where(is_in, (col + pad) // RATIO - pad // RATIO + base, FAR).astype(f32) + frac_col
    group = LANES // PACKED
    high = pick_ref.shape[0]
    point = lax.broadcasted_iota(jnp.int32, (1, group * high * STRIP), 1)
    point_lat = (point // STRIP % high).astype(f32)
    point_lon = (point % STRIP * group + point // (STRIP * high)).astype(f32)

    def blend(row):
        whole = row // RATIO
        frac_row = (row - whole * RATIO + 0.5) / RATIO
        there = place_ref[0] + row
        row_base = jnp.where((there >= 0) & (there < totals[0]), whole + base + frac_row, float(FAR))
        shifts = noisy_ref[row + RIM].astype(f32)
        lat = row_base + shifts[:, variables + conds : variables + conds + 1]
        lon = col_base + shifts[:, variables + conds + 1 : variables + conds + 2]
        weight_lat = jnp.maximum(1.0 - jnp.abs(point_lat - lat), 0.0)
        weight_lon = jnp.maximum(1.0 - jnp.abs(point_lon - lon), 0.0)
        return (weight_lat * weight_lon).astype(bf16)

    edges = [jnp.broadcast_to(col_in[low : low + pad], (pad, channels)) for low in (0, pad + cols)]
    lane = lax.broadcasted_iota(jnp.int32, (1, channels), 1)
    is_state = lane < variables
    is_cond = (lane >= variables) & (lane < variables + conds)
    strips = [strip_ref[pick_ref[index]].astype(f32) for index in range(high)]
    for hour in range(2):
        near = jnp.concatenate([s[hour * STRIP : (hour + 1) * STRIP] for s in strips], axis=0)
        for turn in range(LANES // PACKED):
            moved = pltpu.roll(near, (variables - turn * PACKED) % LANES, 1)
            window_ref[hour, turn * high * STRIP : (turn + 1) * high * STRIP, :] = jnp.where(
                is_cond, moved, 0.0
            ).astype(bf16)

    def flat(start, count, unit):
        return slice(start * unit, (start + count) * unit)

    def mask(value, row):
        low, mid, high = value[:pad], value[pad : pad + cols], value[pad + cols :]
        value = jnp.concatenate([low * edges[0], mid, high * edges[1]], axis=0)
        if 0 <= row < rows:
            return value
        there = place_ref[0] + row
        return value * jnp.where((there >= 0) & (there < totals[0]), 1.0, 0.0)

    def keep(ref, where, value):
        size = value.shape[0]
        ref[0, where, :] = pltpu.roll(value, 1, 0).astype(bf16)
        ref[1, where, :] = value.astype(bf16)
        ref[2, where, :] = pltpu.roll(value, size - 1, 0).astype(bf16)

    def pairs(ref, row, count):
        blocks = []
        for pair in range(count):
            taps = [
                ref[shift, flat(row + 2 * pair + step, 1, width), :]
                for step in range(4)
                for shift in range(3)
            ]
            blocks.append(jnp.concatenate(taps, axis=1))
        return jnp.concatenate(blocks, axis=0)

    def silu_of_half(half_value):
        return half_value + half_value * jnp.tanh(half_value)

    for hour in range(2):
        rim = RIM - RIM_USED * hour
        tall = rows + 2 * rim

        for row in range(0, tall, 2):
            here = flat(row, 2, width)
            if hour == 0:
                weights = jnp.concatenate([blend(row - RIM), blend(row + 1 - RIM)], axis=0)
                blend_ref[here, :] = weights
            else:
                weights = blend_ref[flat(row + RIM - rim, 2, width), :]
            cond = jnp.dot(weights, window_ref[hour], preferred_element_type=f32)
            if hour == 0:
                own = noisy_ref[row : row + 2].reshape(2 * width, channels).astype(f32)
                own_ref[here, :] = own
            else:
                own = own_ref[here, :]
            keep(stack_ref, here, jnp.where(is_state, own, cond))

        if hour == 0:
            copies[0].wait()
        for row in range(0, tall - 2, 8):
            value = jnp.dot(
                pairs(stack_ref, row, 4), first_w_ref[...], preferred_element_type=f32
            )
            for pair in range(4):
                top = row + 2 * pair
                here = flat(top // 2, 1, width)
                part = silu_of_half(value[pair * width : (pair + 1) * width])
                upper = mask(part[:, :channels], top - rim + 1)
                lower = mask(part[:, channels:], top - rim + 2)
                first_ref[here, :channels] = upper.astype(bf16)
                first_ref[here, channels:] = lower.astype(bf16)
                pair_ref[top // 2] = upper + lower
                even = pair_ref[top // 2, pl.ds(0, half, stride=2), :]
                odd = pair_ref[top // 2, pl.ds(1, half, stride=2), :]
                keep(pooled_ref, flat(top // 2, 1, half), even + odd)

        if hour == 0:
            for copy in copies[1:4]:
                copy.wait()
        half_rows = (tall - 2) // 2 - 2
        part = half_rows // 2
        for row in (0, part):
            taps = [
                pooled_ref[shift, flat(row + step, part, half), :]
                for step in range(3)
                for shift in range(3)
            ]
            second = jnp.dot(
                jnp.concatenate(taps, axis=1), down_w_ref[...], preferred_element_type=f32
            )
            lifted = jnp.dot(
                silu_of_half(second).astype(bf16), up_w_ref[...], preferred_element_type=f32
            )
            bridged = jnp.dot(
                first_ref[flat(row + 1, part, width), :], bridge_w_ref[...], preferred_element_type=f32
            )
            for step in range(part):
                own = lifted[step * half : (step + 1) * half]
                spread_ref[row + step, pl.ds(0, half, stride=2), :] = own
                spread_ref[row + step, pl.ds(1, half, stride=2), :] = own
                own = spread_ref[row + step]
                top = 2 * (row + step)
                for side in range(2):
                    value = bridged[
                        step * width : (step + 1) * width, side * channels : (side + 1) * channels
                    ]
                    value = mask(silu_of_half(value + own), top + side - rim + 3)
                    keep(third_ref, flat(top + side, 1, width), value)

        if hour == 0:
            copies[4].wait()
        skip = 1 if hour == 1 else 0
        count = (rows + 2 * (rim - RIM_USED)) // 2 if hour == 0 else rows // 2
        for first in range(0, count, 4):
            size = min(4, count - first)
            values = jnp.dot(
                pairs(third_ref, 2 * first + skip, size), last_w_ref[...], preferred_element_type=f32
            )
            for index in range(2 * size):
                pair, side = divmod(index, 2)
                row = 2 * first + index
                fresh = values[
                    pair * width : (pair + 1) * width, side * channels : (side + 1) * channels
                ]
                fresh = own_ref[flat(row + RIM_USED + skip, 1, width), :] + fresh
                if hour == 0:
                    fresh = fresh + noise_level * noise_ref[row].astype(f32)
                    own_ref[flat(row, 1, width), :] = mask(fresh, row - rim + RIM_USED)
                else:
                    out_ref[:, row * cols : (row + 1) * cols] = fresh[pad : pad + cols].T[:variables].astype(bf16)


def denoise(rows, cols, totals, variables, conds, place, pick, parts, strips, weights):
    mid0, _, _, _, left, _ = parts
    width, channels = cols + 2 * left.shape[1], mid0.shape[2]
    tall = rows + 2 * RIM
    most = (tall - 2) // 2
    points = LANES // PACKED * pick.shape[0] * STRIP
    bf16, f32 = jnp.bfloat16, jnp.float32
    return pl.pallas_call(
        functools.partial(denoise_kernel, rows, cols, totals, variables, conds, width),
        out_shape=jax.ShapeDtypeStruct((variables, rows * cols), bf16),
        in_specs=[pl.BlockSpec(memory_space=pltpu.SMEM)] * 2
        + [pl.BlockSpec(memory_space=pltpu.VMEM)] * 7
        + [pl.BlockSpec(memory_space=pl.ANY)] * len(weights),
        scratch_shapes=[pltpu.VMEM(array.shape, array.dtype) for array in weights]
        + [
            pltpu.SemaphoreType.DMA((len(weights),)),
            pltpu.VMEM((tall, width, channels), bf16),
            pltpu.VMEM((tall - 2 * RIM_USED, width, channels), bf16),
            pltpu.VMEM((tall * width, points), bf16),
            pltpu.VMEM((tall * width, channels), f32),
            pltpu.VMEM((3, tall * width, channels), bf16),
            pltpu.VMEM((most * width, 2 * channels), bf16),
            pltpu.VMEM((3, most * width // 2, channels), bf16),
            pltpu.VMEM((3, tall * width, channels), bf16),
            pltpu.VMEM((most, width, channels), f32),
            pltpu.VMEM((most, width, channels), f32),
            pltpu.VMEM((2, points, channels), bf16),
        ],
        compiler_params=pltpu.CompilerParams(vmem_limit_bytes=VMEM),
        cost_estimate=pl.CostEstimate(flops=10**6, bytes_accessed=10**5, transcendentals=0),
        name="denoise",
    )(place, pick, *parts, strips, *weights)


def conv_weight(weight, depth, width):
    out, _, given = weight.shape
    weight = jnp.pad(weight, ((0, width - out), (0, 0), (0, depth - given)))
    return jnp.transpose(weight, (1, 2, 0)).reshape(9 * depth, width)


def pair_weight(weight):
    row = weight.shape[0] // 3
    return jnp.concatenate(
        [jnp.pad(weight, ((0, row), (0, 0))), jnp.pad(weight, ((row, 0), (0, 0)))], axis=1
    )


def shards(
    global_state,
    spec_filter,
    w_skip,
    w_mix,
    w_decode,
    regional_state,
    noise_draws,
    w_first,
    w_down,
    w_up,
    w_bridge,
    w_last,
    box_lat0,
    box_lon0,
    stencil_lat,
    stencil_lon,
):
    hours = noise_draws.shape[0]
    rows_here, cols_here = regional_state.shape[1:]
    row_start = lax.axis_index(PLANE) * rows_here
    col_start = lax.axis_index("col") * cols_here
    total_rows = rows_here * lax.axis_size(PLANE)
    total_cols = cols_here * lax.axis_size("col")
    assert hours == 2

    variables = regional_state.shape[0]
    conds = w_decode.shape[1]
    lanes = variables + conds
    inner = RIM - RIM_USED
    high = window_extent(rows_here)
    place = jnp.stack([row_start, col_start]).astype(jnp.int32)
    totals = (total_rows, total_cols)

    def prepare(after, after_rows, after_cols):
        state, noise, _ = lax.optimization_barrier((regional_state, noise_draws, after))
        noisy = (
            state.astype(jnp.float32) + noise_level * noise[0].astype(jnp.float32)
        ).astype(jnp.bfloat16)
        lat_shift = stencil_lat - (row_start + jnp.arange(rows_here, dtype=jnp.int32))[:, None] // RATIO
        lon_shift = stencil_lon - (col_start + jnp.arange(cols_here, dtype=jnp.int32))[None, :] // RATIO
        cells = (rows_here, cols_here)
        mids = jnp.concatenate(
            [
                noisy,
                jnp.zeros((conds,) + cells, jnp.bfloat16),
                lat_shift.astype(jnp.bfloat16)[None],
                lon_shift.astype(jnp.bfloat16)[None],
                jnp.zeros((LANES - lanes - 2,) + cells, jnp.bfloat16),
                noise[1],
                jnp.zeros((LANES - variables,) + cells, jnp.bfloat16),
            ],
            axis=0,
        )
        mids = jnp.transpose(mids.reshape((2, LANES) + cells), (0, 2, 3, 1))
        mid0, mid1 = mids[0], mids[1]
        lows = jnp.concatenate([mid0[rows_here - RIM :], mid1[rows_here - inner :]], axis=0)
        highs = jnp.concatenate([mid0[:RIM], mid1[:inner]], axis=0)
        lows, highs, _ = lax.optimization_barrier((lows, highs, after_rows))
        above, below = next_to(lows, highs, PLANE)

        def rim_cols(first, first_inner):
            wide, thin = slice(first, first + RIM), slice(first_inner, first_inner + inner)
            noise = jnp.concatenate([above[RIM:, thin], mid1[:, thin], below[RIM:, thin]], axis=0)
            noise = jnp.pad(
                noise, ((RIM_USED, RIM_USED), (0, RIM_COLS - RIM - inner), (0, 0))
            )
            return jnp.concatenate(
                [
                    jnp.concatenate([above[:RIM, wide], mid0[:, wide], below[:RIM, wide]], axis=0),
                    noise,
                ],
                axis=1,
            )

        lows, highs, _ = lax.optimization_barrier(
            (rim_cols(cols_here - RIM, cols_here - inner), rim_cols(0, 0), after_cols)
        )
        left, right = next_to(lows, highs, "col")
        weights = (
            pair_weight(conv_weight(0.5 * w_first, LANES, w_first.shape[0])),
            conv_weight(0.125 * w_down, w_down.shape[2], w_down.shape[0]),
            0.5 * w_up.T,
            0.5
            * jnp.concatenate(
                [jnp.pad(w_bridge.T, ((0, 0), (0, LANES))), jnp.pad(w_bridge.T, ((0, 0), (LANES, 0)))],
                axis=0,
            ),
            pair_weight(conv_weight(w_last, w_last.shape[2], LANES)),
        )
        return (mid0, mid1, above, below, left, right), weights

    by_latitude = lax.axis_size("col") == 4 and global_state.shape[0] % 4 == 0
    global_steps = global_by_latitude if by_latitude else global_by_channel
    finish, strips, pick, (parts, weights) = global_steps(
        hours, global_state, spec_filter, w_skip, w_mix, w_decode, box_lat0, box_lon0,
        rows_here, cols_here, prepare,
    )
    regional_final = denoise(
        rows_here, cols_here, totals, variables, conds, place, pick, parts, strips, weights
    )
    regional_final = regional_final.reshape((variables, rows_here, cols_here))
    return finish(regional_final)


def solution(mesh):
    return jax.shard_map(
        shards,
        mesh=mesh,
        in_specs=(
            P(PLANE, "col", None),
            P(None, None, "col"),
            P(),
            P(),
            P(),
            P(None, PLANE, "col"),
            P(None, None, PLANE, "col"),
            P(),
            P(),
            P(),
            P(),
            P(),
            P(),
            P(),
            P(PLANE, "col"),
            P(PLANE, "col"),
        ),
        out_specs=(P(PLANE, "col", None), P(None, PLANE, "col")),
        check_vma=False,
    )
```

```python
import functools
import math

import jax
import jax.numpy as jnp
import ml_dtypes
import numpy as np
from jax import lax
from jax.experimental import pallas as pl
from jax.experimental.pallas import tpu as pltpu
from jax.sharding import PartitionSpec as P

RATIO = 8
noise_level = 0.5
PLANE = ("grp", "row")
RIM = 9
RIM_USED = 4
LANES = 128
VMEM = 60 * 2**20
PACKED = 32
MODE_TILE = 64
STRIP = 8
FAR = -4096
RIM_COLS = 16


def fourier_tables(length, num_modes):
    position = np.arange(length, dtype=np.int64)[:, None]
    frequency = np.arange(num_modes, dtype=np.int64)[None, :]
    angle = (position * frequency % length).astype(np.float64) * (2.0 * math.pi / length)
    cosine = np.cos(angle)
    sine = np.sin(angle)
    factor = np.where(frequency == 0, 1.0, 2.0) / length
    forward = np.concatenate([cosine, -sine], axis=1).T.astype(ml_dtypes.bfloat16)
    inverse = np.concatenate([cosine * factor, -sine * factor], axis=1).astype(ml_dtypes.bfloat16)
    return forward, inverse


def round_up(size, unit):
    return -(-size // unit) * unit


def split_tables(length, num_modes):
    piece = length // 4
    place = np.arange(piece, dtype=np.int64)[:, None]

    def waves(mode):
        angle = (place * mode[None, :] % length).astype(np.float64) * (2.0 * math.pi / length)
        return np.cos(angle), np.sin(angle), np.where(mode == 0, 1.0, 2.0)[None, :] / length

    def padded(blocks, unit_rows, unit_cols):
        rows = []
        for row in blocks:
            cols = []
            for block in row:
                spare = [(0, -block.shape[0] % unit_rows), (0, -block.shape[1] % unit_cols)]
                cols.append(np.pad(block, spare))
            rows.append(np.concatenate(cols, axis=1))
        return np.concatenate(rows, axis=0).astype(ml_dtypes.bfloat16)

    forward, inverse = [], []
    for residue in (0, 2):
        cosine, sine, factor = waves(np.arange(residue, num_modes, 4))
        forward.append(padded([[cosine.T], [-sine.T]], MODE_TILE, LANES))
        inverse.append(padded([[cosine * factor, -sine * factor]], LANES, MODE_TILE))
    mode = np.arange(1, num_modes, 2)
    cosine, sine, factor = waves(mode)
    sign = np.where(mode % 4 == 1, 1.0, -1.0)[None, :]
    odd_forward = padded(
        [[cosine.T, (-sign * sine).T], [-sine.T, (-sign * cosine).T]], 2 * MODE_TILE, LANES
    )
    odd_inverse = padded(
        [
            [cosine * factor, -sine * factor],
            [-sign * sine * factor, -sign * cosine * factor],
        ],
        LANES,
        2 * MODE_TILE,
    )
    return tuple(
        jnp.asarray(table)
        for table in (np.stack(forward), odd_forward, np.stack(inverse), odd_inverse)
    )


def exchange(blocks, axis):
    return lax.all_to_all(blocks, axis, split_axis=0, concat_axis=0, tiled=True)


def spread(block, axis):
    return exchange(jnp.broadcast_to(block[None], (lax.axis_size(axis),) + block.shape), axis)


def filter_share(spec_filter):
    rows = 2 * spec_filter.shape[1]
    flat = spec_filter.reshape(rows, spec_filter.shape[2])
    share = rows // lax.axis_size(PLANE)
    mine = lax.dynamic_slice_in_dim(flat, lax.axis_index(PLANE) * share, share, 0)
    return mine.astype(jnp.bfloat16)


def every_channel(mine):
    count = lax.axis_size("col")
    me = lax.axis_index("col")
    blocks = [shift(mine, "col", -step) if step else mine for step in range(count)]
    ring = jnp.concatenate(blocks + blocks[:-1], axis=1)
    width = mine.shape[1]
    return lax.dynamic_slice_in_dim(ring, (count - me) % count * width, count * width, 1)


def gelu(x):
    slope = math.sqrt(2.0 / math.pi)
    half = 0.5 * x
    return half + half * jnp.tanh(x * (slope + (0.044715 * slope) * (x * x)))


def latitude_kernel(hours, turns, step, place_ref, *refs):
    piece_refs, refs = refs[:4], refs[4:]
    even_forward_ref, odd_forward_ref = refs[:2]
    far_refs, out_refs, strip_ref, refs = refs[2:8], refs[8:12], refs[12], refs[13:]
    near_refs, sems, refs = refs[:6], refs[6], refs[7:]
    filter_ref, even_inverse_ref, odd_inverse_ref, skip_ref, mix_ref, decode_ref = near_refs
    state_ref, gain_ref, coarse_ref, near_ref, packed_ref = refs
    copies = [
        pltpu.make_async_copy(far, near, sems.at[index])
        for index, (far, near) in enumerate(zip(far_refs, near_refs))
    ]
    for copy in copies:
        copy.start()
    f32, bf16 = jnp.float32, jnp.bfloat16
    piece, channels = piece_refs[0].shape[1:]
    padded = state_ref.shape[0] // 4
    group = LANES // PACKED
    span = near_ref.shape[0]
    rows = span // group
    spare = jnp.zeros((padded - piece, channels), bf16)
    for index in range(4):
        for turn in range(turns):
            state_ref[
                index * padded : (index + 1) * padded, turn * channels : (turn + 1) * channels
            ] = jnp.concatenate([piece_refs[index][turn], spare], axis=0)

    modes = filter_ref.shape[0] // 2

    def spread_gains():
        for index in range(channels // LANES):
            lanes = slice(index * LANES, (index + 1) * LANES)
            gain_ref[index, : 2 * modes, :] = filter_ref[:, lanes].astype(f32)
            gain_ref[index, 2 * modes :, :] = jnp.zeros((gain_ref.shape[1] - 2 * modes, LANES), f32)

    def gain_rows(low, count, stride):
        rows = pl.ds(low, count, stride=stride)
        tiles = [gain_ref[index, rows, :] for index in range(channels // LANES)]
        return jnp.concatenate(tiles * turns, axis=1)

    def gain(real, imag, low, stride):
        gain_real = gain_rows(low, real.shape[0], stride)
        gain_imag = gain_rows(modes + low, real.shape[0], stride)
        return (
            (real * gain_real - imag * gain_imag).astype(bf16),
            (real * gain_imag + imag * gain_real).astype(bf16),
        )

    def dot(left, right):
        return jnp.dot(left, right, preferred_element_type=f32)

    for hour in range(hours):
        pieces = [
            state_ref[index * padded : (index + 1) * padded, :].astype(f32) for index in range(4)
        ]
        mixed = jnp.concatenate([pieces[0] - pieces[2], pieces[1] - pieces[3]], axis=0).astype(bf16)
        span_odd = odd_forward_ref.shape[0] // 2
        thirds = span_odd // 3
        spectra = []
        for index in range(3):
            low = index * thirds
            spectra.append(
                (
                    dot(odd_forward_ref[low : low + thirds, :], mixed),
                    dot(odd_forward_ref[span_odd + low : span_odd + low + thirds, :], mixed),
                )
            )
            if index == 0:
                both, other = pieces[0] + pieces[2], pieces[1] + pieces[3]
                mixes = [(both + other).astype(bf16), (both - other).astype(bf16)]
        evens = [dot(even_forward_ref[index], mixes[index]) for index in range(2)]
        if hour == 0:
            copies[0].wait()
            spread_gains()
            for copy in copies[1:]:
                copy.wait()
        odd = [gain(*spectra[index], 1 + 2 * index * thirds, 2) for index in range(3)]
        odd = jnp.concatenate([part[0] for part in odd] + [part[1] for part in odd], axis=0)
        odd_shares = [dot(odd_inverse_ref[:padded, :], odd)]
        shares = []
        for index in range(2):
            half = evens[index].shape[0] // 2
            even = gain(evens[index][:half], evens[index][half:], 2 * index, 4)
            shares.append(dot(even_inverse_ref[index], jnp.concatenate(even, axis=0)))
        odd_shares.append(dot(odd_inverse_ref[padded:, :], odd))

        def block_of(ref, index, turn):
            return ref[
                index * padded : (index + 1) * padded, turn * channels : (turn + 1) * channels
            ]

        order = [(index, turn) for index in (0, 2, 1, 3) for turn in range(turns)]
        skipped = dot(block_of(state_ref, *order[0]), skip_ref[...])
        for place, (index, turn) in enumerate(order):
            if place + 1 < len(order):
                following = dot(block_of(state_ref, *order[place + 1]), skip_ref[...])
            if turn == 0:
                even = shares[0] + shares[1] if index % 2 == 0 else shares[0] - shares[1]
                spectral = even + odd_shares[index % 2] if index < 2 else even - odd_shares[index % 2]
            own = spectral[:, turn * channels : (turn + 1) * channels]
            activated = gelu(own + skipped).astype(bf16)
            fresh = block_of(state_ref, index, turn).astype(f32) + dot(activated, mix_ref[...])
            state_ref[
                index * padded : (index + 1) * padded, turn * channels : (turn + 1) * channels
            ] = fresh.astype(bf16)
            skipped = following

        for index in range(2):
            here = pl.ds(pl.multiple_of(place_ref[index] * padded, LANES), padded)
            for turn in range(turns):
                lanes = slice(turn * channels, (turn + 1) * channels)
                coarse = dot(state_ref[here, lanes], decode_ref[...])
                coarse_ref[turn, index * piece : (index + 1) * piece, :] = coarse[:piece]
        for turn in range(turns):
            near_ref[...] = coarse_ref[turn, pl.ds(place_ref[2], span), :]
            packed = near_ref[pl.ds(0, rows, stride=group), :]
            for sub in range(1, group):
                packed += pltpu.roll(near_ref[pl.ds(sub, rows, stride=group), :], sub * PACKED, 1)
            packed_ref[turn, hour * rows : (hour + 1) * rows, :] = packed

    for index in range(4):
        for turn in range(turns):
            out_refs[index][turn] = state_ref[
                index * padded : index * padded + piece, turn * channels : (turn + 1) * channels
            ]
    for target in range(4):
        low = target * step // group
        for turn in range(turns):
            strip = [
                packed_ref[turn, hour * rows + low : hour * rows + low + STRIP, :]
                for hour in range(hours)
            ]
            strip_ref[target, turn * hours * STRIP : (turn + 1) * hours * STRIP, :] = jnp.concatenate(
                strip, axis=0
            ).astype(bf16)


def advance_latitudes(hours, step, place, pieces, tables, gains, w_skip, w_mix, w_decode):
    turns, piece, channels = pieces[0].shape
    padded = round_up(piece, LANES)
    group = LANES // PACKED
    span = round_up(3 * step + STRIP * group, 8 * group)
    decode = jnp.pad(w_decode, ((0, 0), (0, LANES - w_decode.shape[1])))
    modes = gains.shape[0] // 2
    late = (gains,) + tables[2:] + (w_skip, w_mix, decode)
    spare = max(4 * (tables[0].shape[1] // 2), 2 * (tables[1].shape[0] // 2)) - modes
    results = pl.pallas_call(
        functools.partial(latitude_kernel, hours, turns, step),
        out_shape=tuple(
            jax.ShapeDtypeStruct((turns, piece, channels), jnp.bfloat16) for _ in pieces
        )
        + (jax.ShapeDtypeStruct((4, turns * hours * STRIP, LANES), jnp.bfloat16),),
        in_specs=[pl.BlockSpec(memory_space=pltpu.SMEM)]
        + [pl.BlockSpec(memory_space=pltpu.VMEM)] * 6
        + [pl.BlockSpec(memory_space=pl.ANY)] * len(late),
        scratch_shapes=[pltpu.VMEM(array.shape, array.dtype) for array in late]
        + [
            pltpu.SemaphoreType.DMA((len(late),)),
            pltpu.VMEM((4 * padded, turns * channels), jnp.bfloat16),
            pltpu.VMEM((channels // LANES, gains.shape[0] + spare, LANES), jnp.float32),
            pltpu.VMEM((turns, 2 * piece, LANES), jnp.float32),
            pltpu.VMEM((span, LANES), jnp.float32),
            pltpu.VMEM((turns, hours * span // group, LANES), jnp.float32),
        ],
        compiler_params=pltpu.CompilerParams(vmem_limit_bytes=VMEM),
        cost_estimate=pl.CostEstimate(
            flops=turns * 16 * 10**9,
            bytes_accessed=turns * 6 * 2**20,
            transcendentals=hours * turns * 4 * piece * channels,
        ),
        name="advance_latitudes",
    )(place, *pieces, *tables[:2], *late)
    return results[:4], results[4]


def collate_kernel(count, place_ref, *refs):
    far, out_ref, near, sems = refs[:count], refs[count], refs[count + 1 : -1], refs[-1]
    loads = [
        pltpu.make_async_copy(far[index], near[index], sems.at[0, index]) for index in range(count)
    ]
    stores = [
        pltpu.make_async_copy(
            near[index], out_ref.at[pl.ds(place_ref[index], near[index].shape[0])], sems.at[1, index]
        )
        for index in range(count)
    ]
    for load in loads:
        load.start()
    for load, store in zip(loads, stores):
        load.wait()
        store.start()
    for store in stores:
        store.wait()


def collate(place, pieces):
    count = len(pieces)
    turns, piece, channels = pieces[0].shape
    return pl.pallas_call(
        functools.partial(collate_kernel, count),
        out_shape=jax.ShapeDtypeStruct((count * turns, piece, channels), pieces[0].dtype),
        in_specs=[pl.BlockSpec(memory_space=pltpu.SMEM)]
        + [pl.BlockSpec(memory_space=pl.ANY)] * count,
        out_specs=pl.BlockSpec(memory_space=pl.ANY),
        scratch_shapes=[pltpu.VMEM(block.shape, block.dtype) for block in pieces]
        + [pltpu.SemaphoreType.DMA((2, count))],
        compiler_params=pltpu.CompilerParams(vmem_limit_bytes=VMEM),
        name="collate",
    )(place, *pieces)


def shift(block, axis, step):
    count = lax.axis_size(axis)
    return lax.ppermute(block, axis, [(source, (source + step) % count) for source in range(count)])


def global_hour(current, spec_filter, w_skip, w_mix, forward, inverse):
    longitude = lax.all_to_all(current, "col", split_axis=2, concat_axis=1, tiled=True)
    spectrum = jnp.einsum("alc,ml->amc", longitude, forward, preferred_element_type=jnp.float32)
    num_modes = spec_filter.shape[1]
    real_part = spectrum[:, :num_modes, :]
    imag_part = spectrum[:, num_modes:, :]
    filt_real = spec_filter[0][None]
    filt_imag = spec_filter[1][None]
    mixed = jnp.concatenate(
        [
            real_part * filt_real - imag_part * filt_imag,
            real_part * filt_imag + imag_part * filt_real,
        ],
        axis=1,
    ).astype(jnp.bfloat16)
    filtered = jnp.einsum("amc,lm->alc", mixed, inverse, preferred_element_type=jnp.float32).astype(
        jnp.bfloat16
    )
    spectral = lax.all_to_all(filtered, "col", split_axis=1, concat_axis=2, tiled=True)
    skipped = jnp.einsum("alc,cd->ald", current, w_skip, preferred_element_type=jnp.float32)
    activated = jax.nn.gelu(spectral.astype(jnp.float32) + skipped).astype(jnp.bfloat16)
    update = jnp.einsum("ald,de->ale", activated, w_mix, preferred_element_type=jnp.float32)
    return (current.astype(jnp.float32) + update).astype(jnp.bfloat16)


def window_extent(cells):
    return (cells + RIM - 1) // RATIO + 3 - (-RIM // RATIO)


def window_base():
    return -(-RIM // RATIO)


def global_by_latitude(
    hours, global_state, spec_filter, w_skip, w_mix, w_decode, box_lat0, box_lon0, rows_here,
    cols_here, prepare,
):
    count = lax.axis_size("col")
    me = lax.axis_index("col")
    lats_here, piece, _ = global_state.shape
    turns = lats_here // count
    tables = split_tables(piece * count, spec_filter.shape[1])
    owners = [(me - step) % count * turns for step in range(count)]
    def bands_of(turn):
        return [lax.dynamic_slice_in_dim(global_state, owner + turn, 1, 0) for owner in owners]

    bands, mine = lax.optimization_barrier((bands_of(0), filter_share(spec_filter)))
    received = [[shift(band, "col", -step) if step else band for step, band in enumerate(bands)]]
    wide = every_channel(mine)
    gains = spread(wide, PLANE).reshape(-1, wide.shape[1])
    rims, make_parts, weights = prepare(wide, gains)
    for turn in range(1, turns):
        bands, received[-1] = lax.optimization_barrier((bands_of(turn), received[-1]))
        received.append([shift(band, "col", -step) if step else band for step, band in enumerate(bands)])
    start = (box_lon0[0] - window_base() - me * piece) % (piece * count)
    place = jnp.stack([start // piece, (start // piece + 1) % count, start % piece]).astype(jnp.int32)
    outcome, strips, early = [], [], []
    for turn in range(turns):
        if turn > 0:
            received[turn], _ = lax.optimization_barrier((received[turn], (strips, rims)))
        blocks, strip = advance_latitudes(
            hours, cols_here // RATIO, place, received[turn], tables, gains, w_skip, w_mix, w_decode
        )
        if turn < turns - 1:
            early += [shift(blocks[step], "col", step) for step in range(1, count)]
        outcome.append(list(blocks))
        strips.append(strip)
    parts = make_parts(strips[-1])
    strips = jnp.concatenate(strips, axis=1)
    near = [
        lax.dynamic_index_in_dim(strips, (me - step) % count, 0, keepdims=False)
        for step in range(count)
    ]
    near, early = lax.optimization_barrier((near, early))
    near = [shift(strip, "col", -step) if step else strip for step, strip in enumerate(near)]
    got = spread(jnp.stack(near), PLANE)
    outcome, _ = lax.optimization_barrier((outcome, (near, parts)))
    plane = lax.axis_size(PLANE)
    got = got.reshape((plane * lats_here, -1, LANES))
    lat = box_lat0[0] - window_base() + lax.axis_index(PLANE) * (rows_here // RATIO)
    lat = jnp.clip(lat + jnp.arange(window_extent(rows_here), dtype=jnp.int32), 0, plane * lats_here - 1)
    band, lat = lat // lats_here, lat % lats_here
    pick = (band * count + (lat // turns - me) % count) * turns + lat % turns
    places, finals = [], []
    for turn, blocks in enumerate(outcome):
        for step, block in enumerate(blocks):
            if turn < turns - 1 and step:
                block = early[(count - 1) * turn + step - 1]
            elif step:
                block = shift(block, "col", step)
            places.append(owners[step] + turn)
            finals.append(block)

    def finish(after):
        blocks, after = lax.optimization_barrier((finals, after))
        return collate(jnp.stack(places).astype(jnp.int32), blocks), after

    return finish, got, pick.astype(jnp.int32), (parts, weights)


def global_by_channel(
    hours, global_state, spec_filter, w_skip, w_mix, w_decode, box_lat0, box_lon0, rows_here,
    cols_here, prepare,
):
    count = lax.axis_size("col")
    _, make_parts, weights = prepare(w_decode, w_decode)
    prepared = make_parts(w_decode), weights
    forward, inverse = fourier_tables(global_state.shape[1] * count, spec_filter.shape[1])
    base = window_base()
    high, wide = window_extent(rows_here), window_extent(cols_here)
    span = (count - 1) * (cols_here // RATIO) + wide
    lat_start = box_lat0[0] + lax.axis_index(PLANE) * (rows_here // RATIO)
    lon_start = box_lon0[0] + lax.axis_index("col") * (cols_here // RATIO)
    windows = []
    for _ in range(hours):
        global_state = global_hour(global_state, spec_filter, w_skip, w_mix, forward, inverse)
        coarse = jnp.einsum(
            "alc,ck->alk", global_state, w_decode, preferred_element_type=jnp.float32
        ).astype(jnp.bfloat16)
        coarse = lax.all_gather(coarse, "col", axis=1, tiled=True)
        coarse = jnp.pad(coarse, ((0, 0), (base, span), (0, 0)))
        coarse = lax.dynamic_slice_in_dim(coarse, box_lon0[0], base + span, 1)
        coarse = lax.all_gather(coarse, PLANE, axis=0, tiled=True)
        coarse = lax.dynamic_slice_in_dim(coarse, lon_start - box_lon0[0], wide, 1)
        coarse = jnp.pad(coarse, ((base, high), (0, 0), (0, 0)))
        coarse = lax.dynamic_slice_in_dim(coarse, lat_start, high, 0)
        windows.append(coarse)
    group = LANES // PACKED
    windows = jnp.stack(windows, axis=1)
    windows = jnp.pad(
        windows, ((0, 0), (0, 0), (0, STRIP * group - wide), (0, PACKED - windows.shape[3]))
    )
    windows = windows.reshape(high, hours * STRIP, LANES)
    return lambda after: (global_state, after), windows, jnp.arange(high, dtype=jnp.int32), prepared


def next_to(low, high, axis):
    count = lax.axis_size(axis)
    forward = [(i, i + 1) for i in range(count - 1)]
    backward = [(target, source) for source, target in forward]
    return lax.ppermute(low, axis, forward), lax.ppermute(high, axis, backward)


def grid_place(start_ref, total, base, extent):
    place = start_ref + base + lax.broadcasted_iota(jnp.int32, (extent, 1), 0)
    return (place >= 0) & (place < total)


def denoise_kernel(
    rows, cols, totals, variables, conds, width, place_ref, pick_ref, mid0_ref, mid1_ref, above_ref,
    below_ref, left_ref, right_ref, strip_ref, *refs
):
    far_refs, out_ref, refs = refs[:5], refs[5], refs[6:]
    near_refs, sems, refs = refs[:5], refs[5], refs[6:]
    first_w_ref, down_w_ref, up_w_ref, bridge_w_ref, last_w_ref = near_refs
    noisy_ref, noise_ref, blend_ref, own_ref, stack_ref, first_ref, pooled_ref, third_ref, pair_ref, spread_ref, window_ref = refs
    copies = [
        pltpu.make_async_copy(far, near, sems.at[index])
        for index, (far, near) in enumerate(zip(far_refs, near_refs))
    ]
    for copy in copies:
        copy.start()
    half = width // 2
    pad = (width - cols) // 2
    channels = mid0_ref.shape[2]
    f32, bf16 = jnp.float32, jnp.bfloat16

    inner = RIM - RIM_USED
    for ref, mid_ref, rim, part in ((noisy_ref, mid0_ref, RIM, 0), (noise_ref, mid1_ref, inner, RIM)):
        ref[0:rim, pad : pad + cols, :] = above_ref[part : part + rim]
        ref[rim : rim + rows, pad : pad + cols, :] = mid_ref[...]
        ref[rim + rows :, pad : pad + cols, :] = below_ref[part : part + rim]
        skip = RIM - rim
        for side_ref, low, to in ((left_ref, 0, pad - rim), (right_ref, pad + cols, 0)):
            side = side_ref[skip : skip + rows + 2 * rim].astype(f32)
            side = pltpu.roll(side, (to - part) % pad, 1)
            ref[:, low : low + pad, :] = side.astype(bf16)

    is_in = grid_place(place_ref[1], totals[1], -pad, width)
    col_in = is_in.astype(f32)
    base = window_base()
    col = lax.broadcasted_iota(jnp.int32, (width, 1), 0) - pad
    frac_col = ((col % RATIO).astype(f32) + 0.5) / RATIO
    col_base = jnp.where(is_in, (col + pad) // RATIO - pad // RATIO + base, FAR).astype(f32) + frac_col
    group = LANES // PACKED
    high = pick_ref.shape[0]
    point = lax.broadcasted_iota(jnp.int32, (1, group * high * STRIP), 1)
    point_lat = (point // STRIP % high).astype(f32)
    point_lon = (point % STRIP * group + point // (STRIP * high)).astype(f32)

    def blend(row):
        whole = row // RATIO
        frac_row = (row - whole * RATIO + 0.5) / RATIO
        there = place_ref[0] + row
        row_base = jnp.where((there >= 0) & (there < totals[0]), whole + base + frac_row, float(FAR))
        shifts = noisy_ref[row + RIM].astype(f32)
        lat = row_base + shifts[:, variables + conds : variables + conds + 1]
        lon = col_base + shifts[:, variables + conds + 1 : variables + conds + 2]
        weight_lat = jnp.maximum(1.0 - jnp.abs(point_lat - lat), 0.0)
        weight_lon = jnp.maximum(1.0 - jnp.abs(point_lon - lon), 0.0)
        return (weight_lat * weight_lon).astype(bf16)

    edges = [jnp.broadcast_to(col_in[low : low + pad], (pad, channels)) for low in (0, pad + cols)]
    lane = lax.broadcasted_iota(jnp.int32, (1, channels), 1)
    is_state = lane < variables
    is_cond = (lane >= variables) & (lane < variables + conds)
    strips = [strip_ref[pick_ref[index]].astype(f32) for index in range(high)]
    for hour in range(2):
        near = jnp.concatenate([s[hour * STRIP : (hour + 1) * STRIP] for s in strips], axis=0)
        for turn in range(LANES // PACKED):
            moved = pltpu.roll(near, (variables - turn * PACKED) % LANES, 1)
            window_ref[hour, turn * high * STRIP : (turn + 1) * high * STRIP, :] = jnp.where(
                is_cond, moved, 0.0
            ).astype(bf16)

    def flat(start, count, unit):
        return slice(start * unit, (start + count) * unit)

    def mask(value, row):
        low, mid, high = value[:pad], value[pad : pad + cols], value[pad + cols :]
        value = jnp.concatenate([low * edges[0], mid, high * edges[1]], axis=0)
        if 0 <= row < rows:
            return value
        there = place_ref[0] + row
        return value * jnp.where((there >= 0) & (there < totals[0]), 1.0, 0.0)

    def keep(ref, where, value):
        size = value.shape[0]
        ref[0, where, :] = pltpu.roll(value, 1, 0).astype(bf16)
        ref[1, where, :] = value.astype(bf16)
        ref[2, where, :] = pltpu.roll(value, size - 1, 0).astype(bf16)

    def pairs(ref, row, count):
        blocks = []
        for pair in range(count):
            taps = [
                ref[shift, flat(row + 2 * pair + step, 1, width), :]
                for step in range(4)
                for shift in range(3)
            ]
            blocks.append(jnp.concatenate(taps, axis=1))
        return jnp.concatenate(blocks, axis=0)

    def silu_of_half(half_value):
        return half_value + half_value * jnp.tanh(half_value)

    for hour in range(2):
        rim = RIM - RIM_USED * hour
        tall = rows + 2 * rim

        for row in range(0, tall, 2):
            here = flat(row, 2, width)
            if hour == 0:
                weights = jnp.concatenate([blend(row - RIM), blend(row + 1 - RIM)], axis=0)
                blend_ref[here, :] = weights
            else:
                weights = blend_ref[flat(row + RIM - rim, 2, width), :]
            cond = jnp.dot(weights, window_ref[hour], preferred_element_type=f32)
            if hour == 0:
                own = noisy_ref[row : row + 2].reshape(2 * width, channels).astype(f32)
                own_ref[here, :] = own
            else:
                own = own_ref[here, :]
            keep(stack_ref, here, jnp.where(is_state, own, cond))

        if hour == 0:
            copies[0].wait()
        for row in range(0, tall - 2, 8):
            value = jnp.dot(
                pairs(stack_ref, row, 4), first_w_ref[...], preferred_element_type=f32
            )
            for pair in range(4):
                top = row + 2 * pair
                here = flat(top // 2, 1, width)
                part = silu_of_half(value[pair * width : (pair + 1) * width])
                upper = mask(part[:, :channels], top - rim + 1)
                lower = mask(part[:, channels:], top - rim + 2)
                first_ref[here, :channels] = upper.astype(bf16)
                first_ref[here, channels:] = lower.astype(bf16)
                pair_ref[top // 2] = upper + lower
                even = pair_ref[top // 2, pl.ds(0, half, stride=2), :]
                odd = pair_ref[top // 2, pl.ds(1, half, stride=2), :]
                keep(pooled_ref, flat(top // 2, 1, half), even + odd)

        if hour == 0:
            for copy in copies[1:4]:
                copy.wait()
        half_rows = (tall - 2) // 2 - 2
        part = half_rows // 2
        for row in (0, part):
            taps = [
                pooled_ref[shift, flat(row + step, part, half), :]
                for step in range(3)
                for shift in range(3)
            ]
            second = jnp.dot(
                jnp.concatenate(taps, axis=1), down_w_ref[...], preferred_element_type=f32
            )
            lifted = jnp.dot(
                silu_of_half(second).astype(bf16), up_w_ref[...], preferred_element_type=f32
            )
            bridged = jnp.dot(
                first_ref[flat(row + 1, part, width), :], bridge_w_ref[...], preferred_element_type=f32
            )
            for step in range(part):
                own = lifted[step * half : (step + 1) * half]
                spread_ref[row + step, pl.ds(0, half, stride=2), :] = own
                spread_ref[row + step, pl.ds(1, half, stride=2), :] = own
                own = spread_ref[row + step]
                top = 2 * (row + step)
                for side in range(2):
                    value = bridged[
                        step * width : (step + 1) * width, side * channels : (side + 1) * channels
                    ]
                    value = mask(silu_of_half(value + own), top + side - rim + 3)
                    keep(third_ref, flat(top + side, 1, width), value)

        if hour == 0:
            copies[4].wait()
        skip = 1 if hour == 1 else 0
        count = (rows + 2 * (rim - RIM_USED)) // 2 if hour == 0 else rows // 2
        for first in range(0, count, 4):
            size = min(4, count - first)
            values = jnp.dot(
                pairs(third_ref, 2 * first + skip, size), last_w_ref[...], preferred_element_type=f32
            )
            for index in range(2 * size):
                pair, side = divmod(index, 2)
                row = 2 * first + index
                fresh = values[
                    pair * width : (pair + 1) * width, side * channels : (side + 1) * channels
                ]
                fresh = own_ref[flat(row + RIM_USED + skip, 1, width), :] + fresh
                if hour == 0:
                    fresh = fresh + noise_level * noise_ref[row].astype(f32)
                    own_ref[flat(row, 1, width), :] = mask(fresh, row - rim + RIM_USED)
                else:
                    out_ref[:, row * cols : (row + 1) * cols] = fresh[pad : pad + cols].T.astype(bf16)


def denoise(rows, cols, totals, variables, conds, place, pick, parts, strips, weights):
    mid0, _, _, _, left, _ = parts
    width, channels = cols + 2 * left.shape[1], mid0.shape[2]
    tall = rows + 2 * RIM
    most = (tall - 2) // 2
    points = LANES // PACKED * pick.shape[0] * STRIP
    bf16, f32 = jnp.bfloat16, jnp.float32
    return pl.pallas_call(
        functools.partial(denoise_kernel, rows, cols, totals, variables, conds, width),
        out_shape=jax.ShapeDtypeStruct((channels, rows * cols), bf16),
        in_specs=[pl.BlockSpec(memory_space=pltpu.SMEM)] * 2
        + [pl.BlockSpec(memory_space=pltpu.VMEM)] * 7
        + [pl.BlockSpec(memory_space=pl.ANY)] * len(weights),
        scratch_shapes=[pltpu.VMEM(array.shape, array.dtype) for array in weights]
        + [
            pltpu.SemaphoreType.DMA((len(weights),)),
            pltpu.VMEM((tall, width, channels), bf16),
            pltpu.VMEM((tall - 2 * RIM_USED, width, channels), bf16),
            pltpu.VMEM((tall * width, points), bf16),
            pltpu.VMEM((tall * width, channels), f32),
            pltpu.VMEM((3, tall * width, channels), bf16),
            pltpu.VMEM((most * width, 2 * channels), bf16),
            pltpu.VMEM((3, most * width // 2, channels), bf16),
            pltpu.VMEM((3, tall * width, channels), bf16),
            pltpu.VMEM((most, width, channels), f32),
            pltpu.VMEM((most, width, channels), f32),
            pltpu.VMEM((2, points, channels), bf16),
        ],
        compiler_params=pltpu.CompilerParams(vmem_limit_bytes=VMEM),
        cost_estimate=pl.CostEstimate(flops=10**6, bytes_accessed=10**5, transcendentals=0),
        name="denoise",
    )(place, pick, *parts, strips, *weights)


def conv_weight(weight, depth, width):
    out, _, given = weight.shape
    weight = jnp.pad(weight, ((0, width - out), (0, 0), (0, depth - given)))
    return jnp.transpose(weight, (1, 2, 0)).reshape(9 * depth, width)


def pair_weight(weight):
    row = weight.shape[0] // 3
    return jnp.concatenate(
        [jnp.pad(weight, ((0, row), (0, 0))), jnp.pad(weight, ((row, 0), (0, 0)))], axis=1
    )


def shards(
    global_state,
    spec_filter,
    w_skip,
    w_mix,
    w_decode,
    regional_state,
    noise_draws,
    w_first,
    w_down,
    w_up,
    w_bridge,
    w_last,
    box_lat0,
    box_lon0,
    stencil_lat,
    stencil_lon,
):
    hours = noise_draws.shape[0]
    rows_here, cols_here = regional_state.shape[1:]
    row_start = lax.axis_index(PLANE) * rows_here
    col_start = lax.axis_index("col") * cols_here
    total_rows = rows_here * lax.axis_size(PLANE)
    total_cols = cols_here * lax.axis_size("col")
    assert hours == 2

    variables = regional_state.shape[0]
    conds = w_decode.shape[1]
    lanes = variables + conds
    inner = RIM - RIM_USED
    high = window_extent(rows_here)
    place = jnp.stack([row_start, col_start]).astype(jnp.int32)
    totals = (total_rows, total_cols)

    def prepare(after, later):
        state, noise, _ = lax.optimization_barrier((regional_state, noise_draws, after))
        noisy = (
            state.astype(jnp.float32) + noise_level * noise[0].astype(jnp.float32)
        ).astype(jnp.bfloat16)
        lat_shift = stencil_lat - (row_start + jnp.arange(rows_here, dtype=jnp.int32))[:, None] // RATIO
        lon_shift = stencil_lon - (col_start + jnp.arange(cols_here, dtype=jnp.int32))[None, :] // RATIO
        cells = (rows_here, cols_here)
        mids = jnp.concatenate(
            [
                noisy,
                jnp.zeros((conds,) + cells, jnp.bfloat16),
                lat_shift.astype(jnp.bfloat16)[None],
                lon_shift.astype(jnp.bfloat16)[None],
                jnp.zeros((LANES - lanes - 2,) + cells, jnp.bfloat16),
                noise[1],
                jnp.zeros((LANES - variables,) + cells, jnp.bfloat16),
            ],
            axis=0,
        )
        mids = jnp.transpose(mids.reshape((2, LANES) + cells), (0, 2, 3, 1))
        mid0, mid1 = mids[0], mids[1]
        lows = jnp.concatenate([mid0[rows_here - RIM :], mid1[rows_here - inner :]], axis=0)
        highs = jnp.concatenate([mid0[:RIM], mid1[:inner]], axis=0)
        lows, highs, _ = lax.optimization_barrier((lows, highs, later))
        above, below = next_to(lows, highs, PLANE)

        def rim_cols(first, first_inner):
            wide, thin = slice(first, first + RIM), slice(first_inner, first_inner + inner)
            noise = jnp.concatenate([above[RIM:, thin], mid1[:, thin], below[RIM:, thin]], axis=0)
            noise = jnp.pad(
                noise, ((RIM_USED, RIM_USED), (0, RIM_COLS - RIM - inner), (0, 0))
            )
            return jnp.concatenate(
                [
                    jnp.concatenate([above[:RIM, wide], mid0[:, wide], below[:RIM, wide]], axis=0),
                    noise,
                ],
                axis=1,
            )

        def make_parts(after):
            lows, highs, _ = lax.optimization_barrier(
                (rim_cols(cols_here - RIM, cols_here - inner), rim_cols(0, 0), after)
            )
            return (mid0, mid1, above, below) + next_to(lows, highs, "col")

        weights = (
            pair_weight(conv_weight(0.5 * w_first, LANES, w_first.shape[0])),
            conv_weight(0.125 * w_down, w_down.shape[2], w_down.shape[0]),
            0.5 * w_up.T,
            0.5
            * jnp.concatenate(
                [jnp.pad(w_bridge.T, ((0, 0), (0, LANES))), jnp.pad(w_bridge.T, ((0, 0), (LANES, 0)))],
                axis=0,
            ),
            pair_weight(conv_weight(w_last, w_last.shape[2], LANES)),
        )
        return (above, below), make_parts, weights

    by_latitude = lax.axis_size("col") == 4 and global_state.shape[0] % 4 == 0
    global_steps = global_by_latitude if by_latitude else global_by_channel
    finish, strips, pick, (parts, weights) = global_steps(
        hours, global_state, spec_filter, w_skip, w_mix, w_decode, box_lat0, box_lon0,
        rows_here, cols_here, prepare,
    )
    regional_final = denoise(
        rows_here, cols_here, totals, variables, conds, place, pick, parts, strips, weights
    )
    regional_final = regional_final[:variables].reshape((variables, rows_here, cols_here))
    return finish(regional_final)


def solution(mesh):
    return jax.shard_map(
        shards,
        mesh=mesh,
        in_specs=(
            P(PLANE, "col", None),
            P(None, None, "col"),
            P(),
            P(),
            P(),
            P(None, PLANE, "col"),
            P(None, None, PLANE, "col"),
            P(),
            P(),
            P(),
            P(),
            P(),
            P(),
            P(),
            P(PLANE, "col"),
            P(PLANE, "col"),
        ),
        out_specs=(P(PLANE, "col", None), P(None, PLANE, "col")),
        check_vma=False,
    )
```
